32 devices in a mesh: dp: 2 (over y), fsdp: 8 (over z, core), seq: 2 (over x).
Axes of the slice: x: 2, y: 2, z: 4, core: 2. Of those that a mesh axis runs over, the one named last changes fastest.
Arguments:
- enc_ids: int32 [32, 512], P(('dp', 'fsdp'), 'seq'), may hold values from 0 to 32127
- span_mask: int32 [32, 512], P(('dp', 'fsdp'), 'seq'), may hold values 0 or 1
- segments: int32 [32, 512], P(('dp', 'fsdp'), 'seq'), may hold values from 0 to 3, never falling along the last dimension, each value on 1 to 384 neighbouring positions
- targets: int32 [32, 128], P(('dp', 'fsdp', 'seq')), may hold values from 0 to 32127
- loss_weights: int32 [32, 128], P(('dp', 'fsdp', 'seq')), may hold values from 0 to 1, as said below
- target_segments: int32 [32, 128], P(('dp', 'fsdp', 'seq')), may hold values from 0 to 3, as said below
- embedding: float32 [32128, 768], P('fsdp')
- emb_m: float32 [32128, 768], P('fsdp'), may hold values from -5.722046e-06 to 5.722046e-06
- emb_v: float32 [32128, 768], P('fsdp'), may hold values from 1.36141945e-14 to 5.4456778e-14
- gains: float32 [7, 768], replicated
- gain_m: float32 [7, 768], replicated, may hold values from -0.00012207031 to 0.00012207031
- gain_v: float32 [7, 768], replicated, may hold values from 5.4456778e-12 to 2.1782711e-11
- rel_bias: float32 [2, 32, 12], replicated, may hold values from -3 to 3
- rel_m: float32 [2, 32, 12], replicated, may hold values from -0.00012207031 to 0.00012207031
- rel_v: float32 [2, 32, 12], replicated, may hold values from 5.4456778e-12 to 2.1782711e-11
- enc_w: float32 [192, 36864], P('fsdp')
- enc_m: float32 [192, 36864], P('fsdp'), may hold values from -0.00010681152 to 0.00010681152
- enc_left: float32 [192, 36864], P('fsdp'), as said below
- enc_right: float32 [192, 36864], P('fsdp'), as said below
- enc_lroot: float32 [192, 36864], P('fsdp'), as said below
- enc_rroot: float32 [192, 36864], P('fsdp'), as said below
- dec_w: float32 [256, 36864], P('fsdp')
- dec_m: float32 [256, 36864], P('fsdp'), may hold values from -0.00010681152 to 0.00010681152
- dec_left: float32 [256, 36864], P('fsdp'), as said below
- dec_right: float32 [256, 36864], P('fsdp'), as said below
- dec_lroot: float32 [256, 36864], P('fsdp'), as said below
- dec_rroot: float32 [256, 36864], P('fsdp'), as said below
Outputs:
- loss_sum: float32 [], replicated
- loss_count: float32 [], replicated
- grad_norm: float32 [], replicated
- new_embedding: float32 [32128, 768], P('fsdp')
- new_emb_m: float32 [32128, 768], P('fsdp')
- new_emb_v: float32 [32128, 768], P('fsdp')
- new_gains: float32 [7, 768], replicated
- new_gain_m: float32 [7, 768], replicated
- new_gain_v: float32 [7, 768], replicated
- new_rel_bias: float32 [2, 32, 12], replicated
- new_rel_m: float32 [2, 32, 12], replicated
- new_rel_v: float32 [2, 32, 12], replicated
- new_enc_w: float32 [192, 36864], P('fsdp')
- new_enc_m: float32 [192, 36864], P('fsdp')
- new_enc_left: float32 [192, 36864], P('fsdp')
- new_enc_right: float32 [192, 36864], P('fsdp')
- new_dec_w: float32 [256, 36864], P('fsdp')
- new_dec_m: float32 [256, 36864], P('fsdp')
- new_dec_left: float32 [256, 36864], P('fsdp')
- new_dec_right: float32 [256, 36864], P('fsdp')
The draws below stay inside these ranges and needn't reach their ends.
Inputs may be any that keep to these rules, and one draw needn't show every extreme that they name: `loss_weights`: 0 or 1; the share of ones differs between rows. `target_segments`: never falling along a row; every row holds each of the numbers 0 to 3. `enc_left`: each block, read as a 192 x 192 matrix, is symmetric. `enc_right`: each block, read as a 192 x 192 matrix, is symmetric. `enc_lroot`: each block, read as a 192 x 192 matrix, is symmetric. `enc_rroot`: each block, read as a 192 x 192 matrix, is symmetric. `dec_left`: each block, read as a 192 x 192 matrix, is symmetric. `dec_right`: each block, read as a 192 x 192 matrix, is symmetric. `dec_lroot`: each block, read as a 192 x 192 matrix, is symmetric. `dec_rroot`: each block, read as a 192 x 192 matrix, is symmetric.
All inputs are finite; a program needn't handle non-finite values. No bound on the sum of `span_mask` on one device may be relied on, other than what follows from the above.
Results may differ from the reference program's by a relative error of at most 0.00355.
Values may be sent and summed in bfloat16 or wider, within the bound.
No kernel may reach another device: no remote copies, remote signals or barrier semaphores. Data moves between devices by JAX's collectives and lax.ppermute only.
A program may use at most 512 MiB of HBM per device.

```python
import math
import jax
import jax.numpy as jnp
import numpy as np
from jax import lax

D = 768
H = 12
DH = 64
FF = 3072
VOCAB = 32128
NBK = 32
REACH = 128
BLOCK = 192
L_ENC = 512
TGT = 128
SEQS = 2
STEP = 10
ROWS = 32
ENC_BLOCKS = 192
DEC_BLOCKS = 256
N_DP = 2
N_FSDP = 8
N_SEQ = 2


def grad_level():
    return 0.05 / (20.0 * D * D + 4.0 * D * FF + VOCAB * D) ** 0.5


def ramp_level(index, count):
    return (count - 1 + 2 * index, 3 * max(count - 1, 1))


def draw_loss_weights(key, part):
    rows_idx = np.arange(ROWS)
    group = rows_idx // SEQS
    dp_top, dp_low = ramp_level(group // N_FSDP, N_DP)
    fs_top, fs_low = ramp_level(group % N_FSDP, N_FSDP)
    sq_top, sq_low = ramp_level(rows_idx % SEQS // (SEQS // N_SEQ), N_SEQ)
    chance = 950 * dp_top * fs_top * sq_top // (dp_low * fs_low * sq_low)
    drawn = jax.random.randint(key, (ROWS, TGT), 0, 1000)
    return (drawn < jnp.asarray(chance, jnp.int32)[:, None]).astype(jnp.int32)


def draw_target_segments(key, part):
    row_keys = jax.random.split(jax.random.fold_in(key, 41), ROWS)

    def row_cuts(row_key):
        picks = jax.random.permutation(row_key, TGT - 1)[:3] + 1
        return jnp.sort(picks)
    cuts = jax.vmap(row_cuts)(row_keys)
    place = jnp.arange(TGT, dtype=jnp.int32)
    return jnp.sum((place[None, :, None] >= cuts[:, None, :]).astype(jnp.int32), axis=2).astype(jnp.int32)


def draw_embedding(key, part):
    place = jnp.arange(VOCAB, dtype=jnp.float32) / VOCAB
    spread = 1.0 + 2.0 * place
    base = jax.random.normal(key, (VOCAB, D))
    return (base * spread[:, None]).astype(jnp.float32)


def draw_gains(key, part):
    rising = 0.5 + jnp.arange(D, dtype=jnp.float32) / D
    noise = jnp.exp(0.15 * jax.random.normal(key, (7, D)))
    return (rising[None, :] * noise).astype(jnp.float32)


def block_scales(decoder):
    narrow = (8.0 * D) ** (-0.5)
    entries = D ** (-0.5)
    wide = 4.0 * D ** (-0.5)
    if decoder:
        plan = [(D, 3 * D, [narrow, narrow, entries]), (D, D, [wide]), (D, D, [narrow]), (D, 2 * D, [narrow, entries]), (D, D, [wide]), (D, FF, [entries]), (FF, D, [2.0 * FF ** (-0.5)])]
    else:
        plan = [(D, 3 * D, [narrow, narrow, entries]), (D, D, [wide]), (D, FF, [entries]), (FF, D, [2.0 * FF ** (-0.5)])]
    scales = []
    for height, breadth, regions in plan:
        for row_block in range(height // BLOCK):
            for col_block in range(breadth // BLOCK):
                scales.append(regions[col_block * BLOCK * len(regions) // breadth])
    return np.array(scales, np.float32)


def weight_blocks(key, decoder):
    scales = jnp.asarray(block_scales(decoder))
    amount = scales.shape[0]
    base = jax.random.normal(key, (amount, BLOCK * BLOCK))
    return (base * scales[:, None]).astype(jnp.float32)


def definite_blocks(key, amount, level, lowest, highest):
    first, second = jax.random.split(key)
    diagonal = level * jnp.exp(jax.random.uniform(first, (amount, BLOCK), minval=np.log(lowest), maxval=np.log(highest)))
    noise = jax.random.normal(second, (amount, BLOCK, BLOCK))
    noise = noise * (0.3 * level / BLOCK ** 0.5)
    noise = 0.5 * (noise + jnp.swapaxes(noise, 1, 2))
    identity = jnp.eye(BLOCK, dtype=jnp.float32)
    result = noise * (1.0 - identity) + diagonal[:, :, None] * identity
    return result.reshape(amount, BLOCK * BLOCK).astype(jnp.float32)


def stat_level():
    return 0.001 * BLOCK * grad_level() ** 2


def root_level():
    return grad_level() ** (-0.5)


def draw_enc_w(key, part):
    return weight_blocks(jax.random.fold_in(key, 11), False)


def draw_dec_w(key, part):
    return weight_blocks(jax.random.fold_in(key, 12), True)


def draw_enc_left(key, part):
    return definite_blocks(jax.random.fold_in(key, 21), ENC_BLOCKS, stat_level(), 1.0, 4.0)


def draw_enc_right(key, part):
    return definite_blocks(jax.random.fold_in(key, 22), ENC_BLOCKS, stat_level(), 1.0, 4.0)


def draw_enc_lroot(key, part):
    return definite_blocks(jax.random.fold_in(key, 23), ENC_BLOCKS, root_level(), 0.5, 2.0)


def draw_enc_rroot(key, part):
    return definite_blocks(jax.random.fold_in(key, 24), ENC_BLOCKS, root_level(), 0.5, 2.0)


def draw_dec_left(key, part):
    return definite_blocks(jax.random.fold_in(key, 31), DEC_BLOCKS, stat_level(), 1.0, 4.0)


def draw_dec_right(key, part):
    return definite_blocks(jax.random.fold_in(key, 32), DEC_BLOCKS, stat_level(), 1.0, 4.0)


def draw_dec_lroot(key, part):
    return definite_blocks(jax.random.fold_in(key, 33), DEC_BLOCKS, root_level(), 0.5, 2.0)


def draw_dec_rroot(key, part):
    return definite_blocks(jax.random.fold_in(key, 34), DEC_BLOCKS, root_level(), 0.5, 2.0)


def touch_ends(values, own_key, low, largest):
    index_at = [jax.random.randint(jax.random.fold_in(own_key, axis), (), 0, length) for axis, length in enumerate(values.shape)]
    widest = values.shape.index(max(values.shape))
    neighbour = index_at[:widest] + [(index_at[widest] + 1) % values.shape[widest]] + index_at[widest + 1:]
    return values.at[tuple(index_at)].set(low).at[tuple(neighbour)].set(largest)


def block_levels(stream_key, extent, pieces, low, largest):
    def one(position, blocks):
        heights = jax.random.uniform(jax.random.fold_in(jax.random.fold_in(stream_key, 6), position), (blocks,), jnp.float32, low / len(pieces), largest / len(pieces))
        return jnp.repeat(jnp.exp(heights), extent[position] // blocks).reshape((-1,) + (1,) * (len(extent) - position - 1))

    factor_of = one(*pieces[0])
    for cut in pieces[1:]:
        factor_of = factor_of * one(*cut)
    return factor_of


def cumulative_ranks(count, skew):
    weights = [(1 << 20) // math.isqrt(rank ** skew) + 1 for rank in range(1, count + 1)]
    deviation = 1 + sum(weights) // (1 << 30)
    return np.cumsum(np.array([max(1, weight // deviation) for weight in weights]))


def ranked(rng, extent, count, slope):
    grid = cumulative_ranks(count, slope)
    ticket = jax.random.randint(jax.random.fold_in(rng, 1), extent, 0, int(grid[count - 1]))
    rank = jnp.searchsorted(jnp.asarray(grid, jnp.int32), ticket, side="right")
    return jax.random.permutation(jax.random.fold_in(rng, 2), count)[rank].astype(jnp.int32)


def split_up(count, total, most, lean):
    portions = [(1 << 20) // math.isqrt(rank ** lean) + 1 for rank in range(2, count + 1)]
    spare, given = total - most - (count - 1), [1] * (count - 1)
    while spare > 0:
        free = [i for i in range(count - 1) if given[i] < most]
        pool, budget = sum([portions[i] for i in free]), spare
        for i in free:
            more = min(most - given[i], max(1, budget * portions[i] // pool), spare)
            given[i] = given[i] + more
            spare = spare - more
    return np.array([most] + given)


def ragged_sizes(stream_key, number_of, total, most, lean):
    if number_of == 2:
        one = jax.random.randint(stream_key, (), max(1, total - most), min(most, total - 1) + 1)
        return jnp.stack([one, total - one])
    tallies = jnp.asarray(split_up(number_of, total, most, lean), jnp.int32)
    twos = (number_of - 1) // 2
    source_of, taker = tallies[1:1 + 2 * twos:2], tallies[2:2 + 2 * twos:2]
    room = jnp.minimum(source_of - 1, most - taker)
    shifted = jax.random.randint(jax.random.fold_in(stream_key, 1), (twos,), 0, 1 << 20) % (room + 1)
    tallies = tallies.at[1:1 + 2 * twos:2].set(source_of - shifted).at[2:2 + 2 * twos:2].set(taker + shifted)
    return tallies[jax.random.permutation(jax.random.fold_in(stream_key, 2), number_of)]


def centred(rng, shape, scale, limit, pieces=(), kind=jnp.bfloat16):
    values = scale * jax.random.normal(rng, shape, jnp.float32)
    if pieces:
        values = values * block_levels(rng, shape, pieces, -0.22, 0.18)
    return jnp.clip(values, -limit, limit).astype(kind)


def setup_inputs(seed: int = 0) -> dict:
    arg_keys = jax.random.split(jax.random.key(seed), 28)
    enc_ids = touch_ends(ranked(arg_keys[0], (ROWS, L_ENC), VOCAB, 2), jax.random.fold_in(arg_keys[0], 3), 0, VOCAB - 1).astype(jnp.int32)
    span_mask = touch_ends((jax.random.randint(arg_keys[1], (ROWS, L_ENC), 0, 20) < 3).astype(jnp.int32), jax.random.fold_in(arg_keys[1], 1), 0, 1)
    segments = jax.vmap(lambda own: jnp.searchsorted(jnp.cumsum(ragged_sizes(own, 4, L_ENC, 3 * L_ENC // 4, 0)), jnp.arange(L_ENC), side="right"))(jax.random.split(arg_keys[2], ROWS)).reshape((ROWS, L_ENC)).astype(jnp.int32)
    targets = touch_ends(ranked(arg_keys[3], (ROWS, TGT), VOCAB, 2), jax.random.fold_in(arg_keys[3], 3), 0, VOCAB - 1).astype(jnp.int32)
    loss_weights = draw_loss_weights(jax.random.fold_in(arg_keys[27], 71), 0)
    target_segments = draw_target_segments(jax.random.fold_in(arg_keys[27], 71), 0)
    embedding = draw_embedding(jax.random.fold_in(arg_keys[27], 71), 0)
    emb_m = centred(arg_keys[7], (VOCAB, D), (0.00278 * (20 * D * D + 4 * D * FF + VOCAB * D) ** -0.5), 5.7220458984375e-06, ((0, 8),), jnp.float32)
    emb_v = jnp.clip(jnp.exp(math.log(5.445677817104283e-14) - 1.3862944 * jax.random.uniform(arg_keys[8], (VOCAB, D), jnp.float32) ** block_levels(arg_keys[8], (VOCAB, D), ((0, 8),), -0.2, 0.2)), 1.3614194542760708e-14, 5.445677817104283e-14)
    gains = draw_gains(jax.random.fold_in(arg_keys[27], 71), 0)
    gain_m = centred(arg_keys[10], (7, D), (0.0556 * (20 * D * D + 4 * D * FF + VOCAB * D) ** -0.5), 0.00012207031, (), jnp.float32)
    gain_v = jnp.clip(jnp.exp(jax.random.uniform(arg_keys[11], (7, D), jnp.float32, math.log(5.445677762894174e-12), math.log(2.1782711051576698e-11))), 5.445677762894174e-12, 2.1782711051576698e-11)
    rel_bias = centred(arg_keys[12], (2, NBK, H), 0.5, 3.0, (), jnp.float32)
    rel_m = centred(arg_keys[13], (2, NBK, H), (0.0556 * (20 * D * D + 4 * D * FF + VOCAB * D) ** -0.5), 0.00012207031, (), jnp.float32)
    rel_v = jnp.clip(jnp.exp(jax.random.uniform(arg_keys[14], (2, NBK, H), jnp.float32, math.log(5.445677762894174e-12), math.log(2.1782711051576698e-11))), 5.445677762894174e-12, 2.1782711051576698e-11)
    enc_w = draw_enc_w(jax.random.fold_in(arg_keys[27], 71), 0)
    enc_m = centred(arg_keys[16], (ENC_BLOCKS, BLOCK * BLOCK), (0.05 * (20 * D * D + 4 * D * FF + VOCAB * D) ** -0.5), 0.00010681152, ((0, 8),), jnp.float32)
    enc_left = draw_enc_left(jax.random.fold_in(arg_keys[27], 71), 0)
    enc_right = draw_enc_right(jax.random.fold_in(arg_keys[27], 71), 0)
    enc_lroot = draw_enc_lroot(jax.random.fold_in(arg_keys[27], 71), 0)
    enc_rroot = draw_enc_rroot(jax.random.fold_in(arg_keys[27], 71), 0)
    dec_w = draw_dec_w(jax.random.fold_in(arg_keys[27], 71), 0)
    dec_m = centred(arg_keys[22], (DEC_BLOCKS, BLOCK * BLOCK), (0.05 * (20 * D * D + 4 * D * FF + VOCAB * D) ** -0.5), 0.00010681152, ((0, 8),), jnp.float32)
    dec_left = draw_dec_left(jax.random.fold_in(arg_keys[27], 71), 0)
    dec_right = draw_dec_right(jax.random.fold_in(arg_keys[27], 71), 0)
    dec_lroot = draw_dec_lroot(jax.random.fold_in(arg_keys[27], 71), 0)
    dec_rroot = draw_dec_rroot(jax.random.fold_in(arg_keys[27], 71), 0)
    return dict(enc_ids=enc_ids, span_mask=span_mask, segments=segments, targets=targets, loss_weights=loss_weights, target_segments=target_segments, embedding=embedding, emb_m=emb_m, emb_v=emb_v, gains=gains, gain_m=gain_m, gain_v=gain_v, rel_bias=rel_bias, rel_m=rel_m, rel_v=rel_v, enc_w=enc_w, enc_m=enc_m, enc_left=enc_left, enc_right=enc_right, enc_lroot=enc_lroot, enc_rroot=enc_rroot, dec_w=dec_w, dec_m=dec_m, dec_left=dec_left, dec_right=dec_right, dec_lroot=dec_lroot, dec_rroot=dec_rroot)


norm_eps = 1e-06
neg_fill = -1000000000.0
sentinel_offset = 29
beta_first = 0.9
beta_second = 0.999
adam_eps = 1e-08
adam_rate = 0.5
shampoo_rate = 0.01
stat_decay = 0.999
weight_decay = 0.01
clip_limit = 0.05
highest = lax.Precision.HIGHEST

@jax.custom_vjp
def low(v):
    return lax.optimization_barrier(v.astype(jnp.bfloat16)).astype(jnp.float32)

@jax.custom_vjp
def low_back(v):
    return v

def low_keep(v):
    return (low(v), None)

def low_pass(kept, grad):
    return (grad,)

def back_keep(v):
    return (v, None)

def back_low(kept, grad):
    return (low(grad),)
low.defvjp(low_keep, low_pass)
low_back.defvjp(back_keep, back_low)

def bucket_edges(buckets, exact, reach):
    edges = list(range(1, exact))
    spread = buckets - exact
    for place in range(spread):
        edges.append(int(math.ceil(exact * (reach / exact) ** (place / spread) - 1e-09)))
    return edges

def position_buckets(query_pos, key_pos, causal):
    offset = key_pos[None, :] - query_pos[:, None]
    if causal:
        distance = jnp.maximum(-offset, 0)
        result = jnp.zeros(offset.shape, jnp.int32)
        edges = bucket_edges(NBK, NBK // 2, REACH)
    else:
        distance = jnp.abs(offset)
        result = jnp.where(offset > 0, NBK // 2, 0).astype(jnp.int32)
        edges = bucket_edges(NBK // 2, NBK // 4, REACH)
    for edge in edges:
        result = result + (distance >= edge).astype(jnp.int32)
    return result

def layer_shapes(decoder):
    if decoder:
        return [(D, 3 * D), (D, D), (D, D), (D, 2 * D), (D, D), (D, FF), (FF, D)]
    return [(D, 3 * D), (D, D), (D, FF), (FF, D)]

def as_blocks(flat):
    return flat.reshape(flat.shape[0], BLOCK, BLOCK)

def as_rows(blocks):
    return blocks.reshape(blocks.shape[0], BLOCK * BLOCK)

def unblock(blocks, shapes):
    matrix_list = []
    offset = 0
    for height, breadth in shapes:
        amount = height // BLOCK * (breadth // BLOCK)
        section = blocks[offset:offset + amount].reshape(height // BLOCK, breadth // BLOCK, BLOCK, BLOCK)
        matrix_list.append(section.transpose(0, 2, 1, 3).reshape(height, breadth))
        offset += amount
    return matrix_list

def rms(values, gain):
    return values * lax.rsqrt(lax.optimization_barrier(jnp.mean(values * values, axis=-1, keepdims=True)) + norm_eps) * gain

def both(values):
    return low_back(low(values))

def product(left, right):
    return jnp.matmul(left, right, precision=highest)

def heads(values):
    return values.reshape(values.shape[:-1] + (H, DH))

def attention(query, keys, values, bias, mask):
    scores = jnp.einsum('bqhe,bkhe->bhqk', query, keys, precision=highest) + bias
    scores = jnp.where(mask[:, None], low_back(scores), neg_fill)
    probs = jax.nn.softmax(scores, axis=-1)
    output = both(jnp.einsum('bhqk,bkhe->bqhe', low(probs), values, precision=highest))
    return output.reshape(output.shape[:-2] + (D,))

def feed_forward(hidden, gain, w_in, w_down):
    normed = low(rms(hidden, gain))
    inner = low_back(product(normed, w_in))
    active = low(jax.nn.gelu(inner))
    return hidden + low_back(product(active, w_down))

def self_block(hidden, gain, w_qkv, w_out, bias, mask):
    normed = low(rms(hidden, gain))
    qkv = both(product(normed, w_qkv))
    attended = attention(heads(qkv[..., :D]), heads(qkv[..., D:2 * D]), heads(qkv[..., 2 * D:]), bias, mask)
    return hidden + low_back(product(attended, w_out))

def group_loss(params, batch):
    table, gain_all, rel_all, enc_mats, dec_mats = params
    enc_in, segment_ids, dec_in, target_ids, weights, target_segs = batch
    row_count, enc_len = enc_in.shape
    dec_len = dec_in.shape[1]
    low_table = low(table)
    enc_low = [low(member) for member in enc_mats]
    dec_low = [low(member) for member in dec_mats]
    positions = jnp.arange(enc_len, dtype=jnp.int32)
    enc_bias = jnp.transpose(rel_all[0][position_buckets(positions, positions, False)], (2, 0, 1))
    enc_mask = segment_ids[:, :, None] == segment_ids[:, None, :]
    hidden = low_back(low_table[enc_in])
    hidden = self_block(hidden, gain_all[0], enc_low[0], enc_low[1], enc_bias, enc_mask)
    hidden = feed_forward(hidden, gain_all[1], enc_low[2], enc_low[3])
    encoded = low(rms(hidden, gain_all[2]))
    steps_pos = jnp.arange(dec_len, dtype=jnp.int32)
    dec_bias = jnp.transpose(rel_all[1][position_buckets(steps_pos, steps_pos, True)], (2, 0, 1))
    causal = (steps_pos[:, None] >= steps_pos[None, :])[None] & (target_segs[:, :, None] == target_segs[:, None, :])
    state = low_back(low_table[dec_in])
    state = self_block(state, gain_all[3], dec_low[0], dec_low[1], dec_bias, causal)
    normed = low(rms(state, gain_all[4]))
    query = heads(both(product(normed, dec_low[2])))
    pairs = both(product(encoded, dec_low[3]))
    cross_mask = target_segs[:, :, None] == segment_ids[:, None, :]
    attended = attention(query, heads(pairs[..., :D]), heads(pairs[..., D:]), jnp.zeros((), jnp.float32), cross_mask)
    state = state + low_back(product(attended, dec_low[4]))
    state = feed_forward(state, gain_all[5], dec_low[5], dec_low[6])
    final = low(rms(state, gain_all[6]) * D ** (-0.5))
    logits = low_back(jnp.einsum('btd,vd->btv', final, low_table, precision=highest))
    lse = jax.nn.logsumexp(logits, axis=-1)
    picked = jnp.take_along_axis(logits, target_ids[..., None], axis=-1)[..., 0]
    return jnp.sum(weights * (lse - picked))

def adam_update(weight, gradient, moment, second):
    moment = beta_first * moment + (1 - beta_first) * gradient
    second = beta_second * second + (1 - beta_second) * gradient * gradient
    corrected = moment / (1 - beta_first ** STEP)
    scaled = second / (1 - beta_second ** STEP)
    weight = weight - adam_rate * (corrected / (jnp.sqrt(scaled) + adam_eps) + weight_decay * weight)
    return (weight, moment, second)

def shampoo_update(weight, gradient, moment, left, right, left_root, right_root):
    weight, gradient, moment = (as_blocks(weight), as_blocks(gradient), as_blocks(moment))
    left, right, left_root, right_root = (as_blocks(left), as_blocks(right), as_blocks(left_root), as_blocks(right_root))
    left = stat_decay * left + (1 - stat_decay) * jnp.einsum('nij,nkj->nik', gradient, gradient, precision=highest)
    right = stat_decay * right + (1 - stat_decay) * jnp.einsum('nji,njk->nik', gradient, gradient, precision=highest)
    moment = beta_first * moment + (1 - beta_first) * gradient
    shaped = jnp.einsum('nij,njk->nik', left_root, moment, precision=highest)
    direction = jnp.einsum('nij,njk->nik', shaped, right_root, precision=highest)
    weight = weight - shampoo_rate * (direction + weight_decay * weight)
    return (as_rows(weight), as_rows(moment), as_rows(left), as_rows(right))

def reference(enc_ids, span_mask, segments, targets, loss_weights, target_segments, embedding, emb_m, emb_v, gains, gain_m, gain_v, rel_bias, rel_m, rel_v, enc_w, enc_m, enc_left, enc_right, enc_lroot, enc_rroot, dec_w, dec_m, dec_left, dec_right, dec_lroot, dec_rroot):
    enc_in = jnp.where(span_mask == 1, VOCAB - sentinel_offset, enc_ids).astype(jnp.int32)
    dec_in = jnp.concatenate([jnp.zeros((ROWS, 1), jnp.int32), targets[:, :-1]], axis=1).astype(jnp.int32)
    weights = loss_weights.astype(jnp.float32)
    groups = ROWS // SEQS
    batch = tuple((member.reshape((groups, SEQS) + member.shape[1:]) for member in (enc_in, segments, dec_in, targets, weights, target_segments)))

    def total_loss(params):
        table, gain_all, rel_all, enc_blocks, dec_blocks = params
        inner = (table, gain_all, rel_all, unblock(as_blocks(enc_blocks), layer_shapes(False)), unblock(as_blocks(dec_blocks), layer_shapes(True)))

        def add_group(running, item):
            return (running + jax.checkpoint(group_loss)(inner, item), None)
        result, unused = lax.scan(add_group, jnp.zeros((), jnp.float32), batch)
        return result
    params = (embedding, gains, rel_bias, enc_w, dec_w)
    loss_sum, pullback = jax.vjp(total_loss, params)
    grads = pullback(jnp.ones((), jnp.float32))[0]
    loss_count = jnp.maximum(jnp.sum(weights), 1.0)
    grads = [member / loss_count for member in grads]
    grad_norm = jnp.sqrt(sum((jnp.sum(member * member) for member in grads)))
    factor = jnp.minimum(1.0, clip_limit / grad_norm)
    emb_g, gain_g, rel_g, enc_g, dec_g = [member * factor for member in grads]
    new_emb = adam_update(embedding, emb_g, emb_m, emb_v)
    new_gain = adam_update(gains, gain_g, gain_m, gain_v)
    new_rel = adam_update(rel_bias, rel_g, rel_m, rel_v)
    new_enc = shampoo_update(enc_w, enc_g, enc_m, enc_left, enc_right, enc_lroot, enc_rroot)
    new_dec = shampoo_update(dec_w, dec_g, dec_m, dec_left, dec_right, dec_lroot, dec_rroot)
    return (loss_sum, loss_count, grad_norm, new_emb[0], new_emb[1], new_emb[2], new_gain[0], new_gain[1], new_gain[2], new_rel[0], new_rel[1], new_rel[2], new_enc[0], new_enc[1], new_enc[2], new_enc[3], new_dec[0], new_dec[1], new_dec[2], new_dec[3])
```

```python
import functools
import math

import jax
import jax.numpy as jnp
from jax import lax
from jax.experimental import pallas as pl
from jax.experimental.pallas import tpu as pltpu
from jax.sharding import PartitionSpec as P

D = 768
H = 12
DH = 64
FF = 3072
VOCAB = 32128
NBK = 32
REACH = 128
BLOCK = 192
STEP = 10
PAIR = 2 * BLOCK
TILE = 128
LANES = 128


norm_eps = 1e-06
neg_fill = -1000000000.0
sentinel_offset = 29
beta_first = 0.9
beta_second = 0.999
adam_eps = 1e-08
adam_rate = 0.5
shampoo_rate = 0.01
stat_decay = 0.999
weight_decay = 0.01
clip_limit = 0.05
highest = lax.Precision.HIGHEST


def bucket_edges(buckets, exact, reach):
    edges = list(range(1, exact))
    spread = buckets - exact
    for place in range(spread):
        edges.append(int(math.ceil(exact * (reach / exact) ** (place / spread) - 1e-09)))
    return edges


def offset_buckets(offset, causal):
    if causal:
        distance = jnp.maximum(-offset, 0)
        result = jnp.zeros(offset.shape, jnp.int32)
        edges = bucket_edges(NBK, NBK // 2, REACH)
    else:
        distance = jnp.abs(offset)
        result = jnp.where(offset > 0, NBK // 2, 0).astype(jnp.int32)
        edges = bucket_edges(NBK // 2, NBK // 4, REACH)
    for edge in edges:
        result = result + (distance >= edge).astype(jnp.int32)
    return result


def tile_reach(blocks):
    return min(blocks - 1, 2)


def tile_onehot(blocks, causal):
    reach = tile_reach(blocks)
    place = jnp.arange(TILE, dtype=jnp.int32)
    shift = jnp.arange(-reach, reach + 1, dtype=jnp.int32) * TILE
    offset = shift[:, None, None] + place[None, None, :] - place[None, :, None]
    buckets = offset_buckets(offset, causal).reshape(-1)
    return (jnp.arange(NBK, dtype=jnp.int32)[:, None] == buckets[None, :]).astype(jnp.float32)


def tile_bias(onehot, rel):
    flat = jnp.einsum("nh,np->hp", rel, onehot, precision=highest)
    return flat.reshape(H, -1, TILE, TILE)


def tile_bias_grad(onehot, grads):
    return jnp.einsum("np,hp->nh", onehot, grads.reshape(H, -1), precision=highest)


def head_lanes(half):
    lane = lax.broadcasted_iota(jnp.int32, (1, LANES), 1)
    return (lane // DH) == half


def block_scores(query, keys, bias_ref, half, row, row_segs, key_segs, causal):
    scores = lax.dot_general(query, keys, (((1,), (1,)), ((), ())), preferred_element_type=jnp.float32)
    width = keys.shape[0]
    if bias_ref is not None:
        reach = tile_reach(width // TILE)
        tiles = []
        for column in range(width // TILE):
            tiles.append(bias_ref[half, min(max(column - row, -reach), reach) + reach])
        scores = scores + (jnp.concatenate(tiles, axis=1) if len(tiles) > 1 else tiles[0])
    mask = row_segs == key_segs
    if causal:
        at_row = row * TILE + lax.broadcasted_iota(jnp.int32, scores.shape, 0)
        at_key = lax.broadcasted_iota(jnp.int32, scores.shape, 1)
        mask = mask & (at_row >= at_key)
    scores = jnp.where(mask, scores, neg_fill)
    raised = jnp.exp(scores - jnp.max(scores, axis=-1, keepdims=True))
    return raised * (1.0 / jnp.sum(raised, axis=-1, keepdims=True))


def attend_kernel(q_ref, k_ref, v_ref, *rest, biased, causal):
    bias_ref = rest[0] if biased else None
    sq_ref, sk_ref, o_ref = rest[-3:]
    keys = k_ref[0]
    values = v_ref[0]
    key_segs = sk_ref[0]
    for row in range(q_ref.shape[1] // TILE):
        part = pl.ds(row * TILE, TILE)
        query = q_ref[0, part, :]
        row_segs = sq_ref[0, part, :]
        result = None
        for half in range(2):
            lanes = head_lanes(half)
            probs = block_scores(
                jnp.where(lanes, query, 0), keys, bias_ref, half, row, row_segs, key_segs, causal
            )
            output = jnp.dot(
                probs.astype(jnp.bfloat16), values, preferred_element_type=jnp.float32
            )
            result = output if result is None else jnp.where(lanes, output, result)
        o_ref[0, part, :] = result.astype(jnp.bfloat16)


def attend_back_kernel(q_ref, k_ref, v_ref, g_ref, *rest, biased, causal):
    if biased:
        bias_ref, sq_ref, sk_ref, dq_ref, dk_ref, dv_ref, db_ref = rest
    else:
        sq_ref, sk_ref, dq_ref, dk_ref, dv_ref = rest
        bias_ref = db_ref = None
    keys = k_ref[0]
    values = v_ref[0]
    key_segs = sk_ref[0]
    width = keys.shape[0]
    if biased:

        @pl.when(pl.program_id(1) == 0)
        def _():
            db_ref[...] = jnp.zeros_like(db_ref)

    grad_keys = None
    grad_values = None
    for row in range(q_ref.shape[1] // TILE):
        part = pl.ds(row * TILE, TILE)
        query = q_ref[0, part, :]
        grad_out = g_ref[0, part, :]
        row_segs = sq_ref[0, part, :]
        grad_query = None
        for half in range(2):
            lanes = head_lanes(half)
            own_query = jnp.where(lanes, query, 0)
            own_grad = jnp.where(lanes, grad_out, 0)
            probs = block_scores(
                own_query, keys, bias_ref, half, row, row_segs, key_segs, causal
            )
            grad_probs = lax.dot_general(
                own_grad, values, (((1,), (1,)), ((), ())), preferred_element_type=jnp.float32
            )
            drop = jnp.sum(probs * grad_probs, axis=-1, keepdims=True)
            grad_scores = (probs * (grad_probs - drop)).astype(jnp.bfloat16)
            down = (((0,), (0,)), ((), ()))
            part_values = lax.dot_general(
                probs.astype(jnp.bfloat16), own_grad, down, preferred_element_type=jnp.float32
            )
            part_keys = lax.dot_general(
                grad_scores, own_query, down, preferred_element_type=jnp.float32
            )
            grad_values = part_values if grad_values is None else grad_values + part_values
            grad_keys = part_keys if grad_keys is None else grad_keys + part_keys
            own_grad_query = jnp.dot(grad_scores, keys, preferred_element_type=jnp.float32)
            grad_query = (
                own_grad_query if grad_query is None else jnp.where(lanes, own_grad_query, grad_query)
            )
            if biased:
                wide = grad_scores.astype(jnp.float32)
                reach = tile_reach(width // TILE)
                for column in range(width // TILE):
                    slot = min(max(column - row, -reach), reach) + reach
                    db_ref[half, slot] += wide[:, column * TILE : (column + 1) * TILE]
        dq_ref[0, part, :] = grad_query.astype(jnp.bfloat16)
    dk_ref[0] = grad_keys.astype(jnp.bfloat16)
    dv_ref[0] = grad_values.astype(jnp.bfloat16)


def attention_specs(query, keys, places, bias, row_segs, key_segs):
    q_at, k_at, v_at = places
    rows, nq = row_segs.shape
    nk = key_segs.shape[1]

    def panel(length, first):
        return pl.BlockSpec((1, length, LANES), lambda pair, row: (row, 0, first + pair))

    operands = [query, keys, keys]
    specs = [panel(nq, q_at), panel(nk, k_at), panel(nk, v_at)]
    tail = []
    tail_specs = []
    if bias is not None:
        tail.append(bias)
        tail_specs.append(
            pl.BlockSpec((2,) + bias.shape[1:], lambda pair, row: (pair, 0, 0, 0))
        )
    tail += [row_segs[:, :, None], key_segs[:, None, :]]
    tail_specs += [
        pl.BlockSpec((1, nq, 1), lambda pair, row: (row, 0, 0)),
        pl.BlockSpec((1, 1, nk), lambda pair, row: (row, 0, 0)),
    ]
    return operands, specs, tail, tail_specs, panel


def attention_cost(rows, nq, nk, products):
    return pl.CostEstimate(
        flops=2 * products * rows * H * nq * nk * LANES,
        bytes_accessed=2 * products * rows * (nq + nk) * D,
        transcendentals=rows * H * nq * nk,
    )


def attend(query, keys, places, bias, row_segs, key_segs, causal):
    rows, nq = row_segs.shape
    nk = key_segs.shape[1]
    operands, specs, tail, tail_specs, panel = attention_specs(
        query, keys, places, bias, row_segs, key_segs
    )
    return pl.pallas_call(
        functools.partial(attend_kernel, biased=bias is not None, causal=causal),
        out_shape=jax.ShapeDtypeStruct((rows, nq, D), jnp.bfloat16),
        grid=(H // 2, rows),
        in_specs=specs + tail_specs,
        out_specs=panel(nq, 0),
        cost_estimate=attention_cost(rows, nq, nk, 2),
        compiler_params=pltpu.CompilerParams(vmem_limit_bytes=32 << 20),
    )(*operands, *tail)


def attend_back(query, keys, places, bias, row_segs, key_segs, causal, grad_out):
    rows, nq = row_segs.shape
    nk = key_segs.shape[1]
    operands, specs, tail, tail_specs, panel = attention_specs(
        query, keys, places, bias, row_segs, key_segs
    )
    outs = [
        jax.ShapeDtypeStruct((rows, nq, D), jnp.bfloat16),
        jax.ShapeDtypeStruct((rows, nk, D), jnp.bfloat16),
        jax.ShapeDtypeStruct((rows, nk, D), jnp.bfloat16),
    ]
    out_specs = [panel(nq, 0), panel(nk, 0), panel(nk, 0)]
    if bias is not None:
        outs.append(jax.ShapeDtypeStruct(bias.shape, jnp.float32))
        out_specs.append(
            pl.BlockSpec((2,) + bias.shape[1:], lambda pair, row: (pair, 0, 0, 0))
        )
    return pl.pallas_call(
        functools.partial(attend_back_kernel, biased=bias is not None, causal=causal),
        out_shape=outs,
        grid=(H // 2, rows),
        in_specs=specs + [panel(nq, 0)] + tail_specs,
        out_specs=out_specs,
        cost_estimate=attention_cost(rows, nq, nk, 5),
        compiler_params=pltpu.CompilerParams(vmem_limit_bytes=32 << 20),
    )(*operands, grad_out, *tail)


def layer_shapes(decoder):
    if decoder:
        return [(D, 3 * D), (D, D), (D, D), (D, 2 * D), (D, D), (D, FF), (FF, D)]
    return [(D, 3 * D), (D, D), (D, FF), (FF, D)]


def as_blocks(flat):
    return flat.reshape(flat.shape[0], BLOCK, BLOCK)


def as_rows(blocks):
    return blocks.reshape(blocks.shape[0], BLOCK * BLOCK)


def as_pairs(blocks):
    amount = blocks.shape[0] // 2
    split = blocks.reshape(amount, 2, BLOCK, BLOCK)
    return jnp.concatenate([split[:, 0], split[:, 1]], axis=-1)


def from_pairs(pairs):
    amount = pairs.shape[0]
    split = jnp.stack([pairs[..., :BLOCK], pairs[..., BLOCK:]], axis=1)
    return split.reshape(2 * amount, BLOCK, BLOCK)


def matrices_of(pairs, shapes):
    matrix_list = []
    offset = 0
    for height, breadth in shapes:
        tall, wide = (height // BLOCK, breadth // PAIR)
        section = pairs[offset : offset + tall * wide].reshape(tall, wide, BLOCK, PAIR)
        matrix_list.append(section.transpose(0, 2, 1, 3).reshape(height, breadth))
        offset += tall * wide
    return matrix_list


def pairs_of(matrix):
    height, breadth = matrix.shape
    tiles = matrix.reshape(height // BLOCK, BLOCK, breadth // PAIR, PAIR)
    return tiles.transpose(0, 2, 1, 3).reshape(-1, BLOCK, PAIR)


def project(left, right):
    return jnp.matmul(left, right, preferred_element_type=jnp.float32)


def project_back(left, right):
    return jnp.einsum("btf,df->btd", left, right, preferred_element_type=jnp.float32)


def weight_grad(inputs, grads):
    return jnp.einsum("btd,btf->df", inputs, grads, preferred_element_type=jnp.float32)


def rms(values, gain):
    return values * lax.rsqrt(jnp.mean(values * values, axis=-1, keepdims=True) + norm_eps) * gain


def rms_back(values, gain, grad_out):
    inverse = lax.rsqrt(jnp.mean(values * values, axis=-1, keepdims=True) + norm_eps)
    normed = values * inverse
    grad_gain = jnp.sum(grad_out * normed, axis=(0, 1))
    grad_normed = grad_out * gain
    grad_values = inverse * (
        grad_normed - normed * jnp.mean(grad_normed * normed, axis=-1, keepdims=True)
    )
    return (grad_values, grad_gain)


def ff_forward(hidden, gain, w_in, w_down):
    normed = rms(hidden, gain).astype(jnp.bfloat16)
    inner = project(normed, w_in)
    active = jax.nn.gelu(inner).astype(jnp.bfloat16)
    return (hidden + project(active, w_down), (normed, inner, active))


def ff_back(hidden, gain, w_in, w_down, cache, grad_out):
    normed, inner, active = cache
    branch_grad = grad_out.astype(jnp.bfloat16)
    down_grad = weight_grad(active, branch_grad)
    grad_active = project_back(branch_grad, w_down)
    unused, gelu_back = jax.vjp(jax.nn.gelu, inner)
    grad_inner = gelu_back(grad_active)[0].astype(jnp.bfloat16)
    in_grad = weight_grad(normed, grad_inner)
    grad_part, grad_gain = rms_back(hidden, gain, project_back(grad_inner, w_in))
    return (grad_out + grad_part, grad_gain, in_grad, down_grad)


def table_rows(table, token_ids, vocab_first):
    local_ids = token_ids - vocab_first
    inside = (local_ids >= 0) & (local_ids < table.shape[0])
    picked = jnp.take(table, jnp.clip(local_ids, 0, table.shape[0] - 1), axis=0)
    return jnp.where(inside[..., None], picked, jnp.zeros((), table.dtype))


def table_grads(grads, token_ids, vocab_first, vocab_local, dense):
    local_ids = token_ids.reshape(-1) - vocab_first
    inside = (local_ids >= 0) & (local_ids < vocab_local)
    slots = jnp.where(inside, local_ids, vocab_local)
    length = -(-(vocab_local + 1) // 32) * 32
    summed = jax.ops.segment_sum(
        grads.reshape(-1, D).astype(jnp.float32), slots, num_segments=length
    )
    row = lax.broadcasted_iota(jnp.int32, (length, 1), 0)
    padded = jnp.pad(dense, ((0, length - vocab_local), (0, 0)))
    return jnp.where(row < vocab_local, summed + padded, 0.0)


REPLICAS = ("dp", "seq")
EVERYWHERE = ("fsdp", "dp", "seq")


def replica_rank():
    return lax.axis_index("dp") * lax.axis_size("seq") + lax.axis_index("seq")


def replica_count():
    return lax.axis_size("dp") * lax.axis_size("seq")


def gather_weights(master):
    amount = master.shape[0]
    parts = replica_count()
    if amount % (2 * parts):
        pairs = as_pairs(as_blocks(master.astype(jnp.bfloat16)))
        return lax.all_gather(pairs, "fsdp", axis=0, tiled=True)
    share = amount // parts
    own = lax.dynamic_slice_in_dim(master, replica_rank() * share, share, 0)
    pairs = as_pairs(as_blocks(own.astype(jnp.bfloat16)))
    return lax.all_gather(pairs, EVERYWHERE, axis=0, tiled=True)


def paired_mesh():
    return (
        lax.axis_size("dp") == 2 and lax.axis_size("seq") == 2 and lax.axis_size("fsdp") % 2 == 0
    )


def swap(values, axis):
    size = lax.axis_size(axis)
    return lax.ppermute(values, axis, [(place, place ^ 1) for place in range(size)])


def shift(values, step):
    size = lax.axis_size("fsdp")
    moves = [
        (place, place + 2 * step) for place in range(size) if 0 <= place + 2 * step < size
    ]
    return lax.ppermute(values, "fsdp", moves)


def choose(flag, if_set, if_clear):
    return jnp.where(flag == 1, if_set, if_clear)


def pick(values, place, axis):
    return lax.dynamic_index_in_dim(values, place, axis, False)


def narrow(values):
    return values.astype(jnp.bfloat16)


def wide(values):
    return values.astype(jnp.float32)


def agreed_scale(largest):
    for axis in ("seq", "dp"):
        largest = jnp.maximum(largest, swap(largest, axis))
    return 4096.0 / jnp.maximum(largest, 1e-30)


def placed(relative, first, second):
    def at(row, column):
        here = choose(second, relative[row][1 - column], relative[row][column])
        there = choose(second, relative[1 - row][1 - column], relative[1 - row][column])
        return choose(first, there, here)

    return [[at(0, 0), at(0, 1)], [at(1, 0), at(1, 1)]]


def reduce_blocks(pairs):
    if not paired_mesh():
        return lax.psum(
            lax.psum_scatter(pairs, "fsdp", scatter_dimension=0, tiled=True), REPLICAS
        )
    n_chips = lax.axis_size("fsdp") // 2
    core = lax.axis_index("fsdp") % 2
    chip = lax.axis_index("fsdp") // 2
    side, half = (lax.axis_index("dp"), lax.axis_index("seq"))
    amount = pairs.shape[0] // (2 * n_chips)
    quarter = amount // 4
    mid = BLOCK // 2
    pairs = pairs.reshape(n_chips, 2, amount, BLOCK, PAIR)
    chip_sum = wide(pick(pairs, core, 1)) + wide(swap(narrow(pick(pairs, 1 - core, 1)), "fsdp"))
    chip_sum = chip_sum.reshape(n_chips, 2, 2, quarter, BLOCK, PAIR)
    upper, lower = (chip_sum[..., :mid, :], chip_sum[..., mid:, :])
    upper = pick(upper, half, 2) + wide(swap(narrow(pick(upper, 1 - half, 2)), "seq"))
    lower = pick(lower, side, 1) + wide(swap(narrow(pick(lower, 1 - side, 1)), "dp"))
    upper = pick(upper, side, 1) + wide(swap(narrow(pick(upper, 1 - side, 1)), "dp"))
    lower = pick(lower, half, 1) + wide(swap(narrow(pick(lower, 1 - half, 1)), "seq"))
    line_sum = jnp.concatenate([upper, lower], axis=2)
    ahead = lax.dynamic_slice_in_dim(
        jnp.concatenate([line_sum, line_sum[:-1]], axis=0), chip, n_chips, 0
    )
    up = down = None
    for step in range(n_chips - 1, 0, -1):
        rising, falling = (ahead[step], ahead[n_chips - step])
        if up is not None:
            rising, falling = (rising + wide(up), falling + wide(down))
        up, down = (shift(narrow(rising), 1), shift(narrow(falling), -1))
    return ahead[0] + wide(up) + wide(down)


def share_blocks(own):
    side, half = (lax.axis_index("dp"), lax.axis_index("seq"))
    mid = BLOCK // 2
    scale = agreed_scale(jnp.max(jnp.abs(own)))
    own = lax.optimization_barrier((own * scale).astype(jnp.float16))
    upper, lower = (own[:, :mid], own[:, mid:])
    upper_side, lower_half = (swap(upper, "dp"), swap(lower, "seq"))
    upper_rest = swap(jnp.stack([upper, upper_side]), "seq")
    lower_rest = swap(jnp.stack([lower, lower_half]), "dp")
    relative = [
        [
            jnp.concatenate([upper, lower], axis=1),
            jnp.concatenate([upper_rest[0], lower_half], axis=1),
        ],
        [
            jnp.concatenate([upper_side, lower_rest[0]], axis=1),
            jnp.concatenate([upper_rest[1], lower_rest[1]], axis=1),
        ],
    ]
    whole = placed(relative, side, half)
    return wide(jnp.concatenate(whole[0] + whole[1], axis=0)) * (1.0 / scale)


def reduce_table(partial, bound):
    side, half = (lax.axis_index("dp"), lax.axis_index("seq"))
    scale = agreed_scale(bound)
    rows = partial.shape[0] // 4
    split = (partial * scale).reshape(2, 2, rows, D)

    def half_lanes(values, place):
        return lax.dynamic_slice_in_dim(values, place * (D // 2), D // 2, 1)

    def send(values, axis):
        return wide(swap(values.astype(jnp.float16), axis))

    top = pick(split[0], half, 0) + send(pick(split[0], 1 - half, 0), "seq")
    low = pick(split[1], side, 0) + send(pick(split[1], 1 - side, 0), "dp")
    top = half_lanes(top, side) + send(half_lanes(top, 1 - side), "dp")
    low = half_lanes(low, half) + send(half_lanes(low, 1 - half), "seq")
    return top, low, scale


def share_table(top, low, scale):
    side, half = (lax.axis_index("dp"), lax.axis_index("seq"))
    top = lax.optimization_barrier(top.astype(jnp.float16))
    low = lax.optimization_barrier(low.astype(jnp.float16))
    top_side, low_half = (swap(top, "dp"), swap(low, "seq"))
    top_rest = swap(jnp.stack([top, top_side]), "seq")
    low_rest = swap(jnp.stack([low, low_half]), "dp")
    top_all = placed([[top, top_side], [top_rest[0], top_rest[1]]], half, side)
    low_all = placed([[low, low_half], [low_rest[0], low_rest[1]]], side, half)
    rows = [jnp.concatenate(pieces, axis=1) for pieces in top_all + low_all]
    return wide(jnp.concatenate(rows, axis=0)) * (1.0 / scale)


def adam_update(weight, gradient, moment, second):
    moment = beta_first * moment + (1 - beta_first) * gradient
    second = beta_second * second + (1 - beta_second) * gradient * gradient
    corrected = moment / (1 - beta_first**STEP)
    scaled = second / (1 - beta_second**STEP)
    weight = weight - adam_rate * (
        corrected / (jnp.sqrt(scaled) + adam_eps) + weight_decay * weight
    )
    return (weight, moment, second)


def block_product(left, right, form):
    return jnp.einsum(form, left, right, precision=lax.Precision.HIGH)


def shampoo_ahead(moment, left_root, right_root):
    left_root, right_root = (as_blocks(left_root), as_blocks(right_root))
    shaped = block_product(left_root, as_blocks(moment), "nij,njk->nik")
    return (as_rows(block_product(shaped, right_root, "nij,njk->nik")), left_root, right_root)


def shampoo_products(gradient, left_root, right_root):
    shaped = block_product(left_root, gradient, "nij,njk->nik")
    return (
        as_rows(gradient),
        as_rows(block_product(shaped, right_root, "nij,njk->nik")),
        as_rows(block_product(gradient, gradient, "nij,nkj->nik")),
        as_rows(block_product(gradient, gradient, "nji,njk->nik")),
    )


def shampoo_update(weight, moment, left, right, ahead, products, factor):
    gradient, turned, left_square, right_square = products
    direction = beta_first * ahead + ((1 - beta_first) * factor) * turned
    square = (1 - stat_decay) * factor * factor
    return (
        weight - shampoo_rate * (direction + weight_decay * weight),
        beta_first * moment + ((1 - beta_first) * factor) * gradient,
        stat_decay * left + square * left_square,
        stat_decay * right + square * right_square,
    )


def on_device(
    enc_ids,
    span_mask,
    segments,
    targets,
    loss_weights,
    target_segments,
    embedding,
    emb_m,
    emb_v,
    gains,
    gain_m,
    gain_v,
    rel_bias,
    rel_m,
    rel_v,
    enc_w,
    enc_m,
    enc_left,
    enc_right,
    enc_lroot,
    enc_rroot,
    dec_w,
    dec_m,
    dec_left,
    dec_right,
    dec_lroot,
    dec_rroot,
):
    fsdp_rank = lax.axis_index("fsdp")
    seq_rank = lax.axis_index("seq")
    n_fsdp = lax.axis_size("fsdp")
    n_seq = lax.axis_size("seq")
    half_len = enc_ids.shape[1]
    rows, dec_len = targets.shape
    enc_len = half_len * n_seq
    enc_in = jnp.where(span_mask == 1, VOCAB - sentinel_offset, enc_ids)
    dec_in = jnp.concatenate([jnp.zeros((rows, 1), jnp.int32), targets[:, :-1]], axis=1)

    def by_rows(positions):
        return positions.reshape(n_seq, rows, half_len)

    message = jnp.concatenate(
        [by_rows(enc_in), by_rows(segments)], axis=2
    ).reshape(n_seq, -1)
    own = jnp.concatenate(
        [dec_in.reshape(-1), targets.reshape(-1), loss_weights.reshape(-1)]
    )
    message = jnp.concatenate([message.reshape(-1), own]).reshape(1, 1, -1)
    gathered = lax.all_gather(message, ("fsdp", "seq"), axis=0, tiled=True)
    gathered = gathered.reshape(n_fsdp, n_seq, -1)
    row_words = rows * 2 * half_len
    enc_words = lax.dynamic_slice_in_dim(gathered, seq_rank * row_words, row_words, 2)
    enc_words = enc_words.reshape(n_fsdp, n_seq, rows, 2, half_len).transpose(3, 0, 2, 1, 4)
    enc_words = enc_words.reshape(2, n_fsdp, rows * enc_len)
    all_enc = enc_words[0]
    row_segments = lax.dynamic_index_in_dim(enc_words[1], fsdp_rank, 0, False)
    row_segments = row_segments.reshape(rows, enc_len)
    dec_words = lax.dynamic_index_in_dim(gathered, seq_rank, 1, False)[:, n_seq * row_words :]
    dec_words = dec_words.reshape(n_fsdp, 3, rows * dec_len)
    all_dec, all_targets, all_weights = (dec_words[:, 0], dec_words[:, 1], dec_words[:, 2])
    all_tokens = jnp.concatenate([all_enc, all_dec], axis=1)

    table = embedding.astype(jnp.bfloat16)
    vocab_local = table.shape[0]
    vocab_first = fsdp_rank * vocab_local
    looked_up = lax.psum_scatter(
        table_rows(table, all_tokens, vocab_first), "fsdp", scatter_dimension=0, tiled=True
    ).reshape(-1, D)
    hidden0 = looked_up[: rows * enc_len].reshape(rows, enc_len, D).astype(jnp.float32)
    state0 = looked_up[rows * enc_len :].reshape(rows, dec_len, D).astype(jnp.float32)

    enc_mats = matrices_of(gather_weights(enc_w), layer_shapes(False))
    dec_mats = matrices_of(gather_weights(dec_w), layer_shapes(True))
    enc_onehot = tile_onehot(enc_len // TILE, False)
    dec_onehot = tile_onehot(dec_len // TILE, True)
    enc_bias = tile_bias(enc_onehot, rel_bias[0])
    dec_bias = tile_bias(dec_onehot, rel_bias[1])
    tile_at = D // LANES
    self_places = (0, tile_at, 2 * tile_at)
    cross_places = (0, 0, tile_at)

    normed0 = rms(hidden0, gains[0]).astype(jnp.bfloat16)
    enc_qkv = project(normed0, enc_mats[0]).astype(jnp.bfloat16)
    enc_attended = attend(
        enc_qkv, enc_qkv, self_places, enc_bias, row_segments, row_segments, False
    )
    hidden1 = hidden0 + project(enc_attended, enc_mats[1])
    hidden2, enc_cache = ff_forward(hidden1, gains[1], enc_mats[2], enc_mats[3])
    encoded = rms(hidden2, gains[2]).astype(jnp.bfloat16)
    pairs = project(encoded, dec_mats[3]).astype(jnp.bfloat16)

    normed3 = rms(state0, gains[3]).astype(jnp.bfloat16)
    self_qkv = project(normed3, dec_mats[0]).astype(jnp.bfloat16)
    self_attended = attend(
        self_qkv, self_qkv, self_places, dec_bias, target_segments, target_segments, True
    )
    state1 = state0 + project(self_attended, dec_mats[1])
    normed4 = rms(state1, gains[4]).astype(jnp.bfloat16)
    cross_query = project(normed4, dec_mats[2]).astype(jnp.bfloat16)
    cross_attended = attend(
        cross_query, pairs, cross_places, None, target_segments, row_segments, False
    )
    state2 = state1 + project(cross_attended, dec_mats[4])
    state3, dec_cache = ff_forward(state2, gains[5], dec_mats[5], dec_mats[6])
    out_scale = D ** (-0.5)
    final = (rms(state3, gains[6]) * out_scale).astype(jnp.bfloat16)

    all_final = lax.all_gather(final.reshape(rows * dec_len, D), "fsdp", axis=0, tiled=True)
    logits = jnp.einsum("nd,vd->nv", all_final, table, preferred_element_type=jnp.float32)
    local_ids = all_targets.reshape(-1) - vocab_first
    target_hot = local_ids[:, None] == jnp.arange(vocab_local, dtype=jnp.int32)[None, :]
    local_top = jnp.max(logits, axis=1)
    local_sum = jnp.sum(jnp.exp(logits - local_top[:, None]), axis=1)
    local_pick = jnp.sum(jnp.where(target_hot, logits, 0.0), axis=1)
    stats = lax.all_gather(
        jnp.stack([local_top, local_sum, local_pick])[None], "fsdp", axis=0, tiled=True
    )
    top_all = jnp.max(stats[:, 0], axis=0)
    sum_all = jnp.sum(stats[:, 1] * jnp.exp(stats[:, 0] - top_all), axis=0)
    pick_all = jnp.sum(stats[:, 2], axis=0)
    lse = top_all + jnp.log(sum_all)
    token_weights = all_weights.reshape(-1).astype(jnp.float32)
    group_loss = jnp.sum(token_weights * (lse - pick_all))
    group_count = jnp.sum(token_weights)
    grad_logits = (
        token_weights[:, None] * (jnp.exp(logits - lse[:, None]) - target_hot.astype(jnp.float32))
    ).astype(jnp.bfloat16)
    emb_grad = jnp.einsum("nv,nd->vd", grad_logits, all_final, preferred_element_type=jnp.float32)
    grad_final = lax.psum_scatter(
        jnp.dot(grad_logits, table, preferred_element_type=jnp.float32),
        "fsdp",
        scatter_dimension=0,
        tiled=True,
    ).reshape(rows, dec_len, D)

    grad_state3, gain_six = rms_back(state3, gains[6], grad_final * out_scale)
    grad_state2, gain_five, dec_in_grad, dec_down_grad = ff_back(
        state2, gains[5], dec_mats[5], dec_mats[6], dec_cache, grad_state3
    )
    branch_grad = grad_state2.astype(jnp.bfloat16)
    cross_out_grad = weight_grad(cross_attended, branch_grad)
    grad_cross = project_back(branch_grad, dec_mats[4]).astype(jnp.bfloat16)
    grad_cq, grad_ck, grad_cv = attend_back(
        cross_query, pairs, cross_places, None, target_segments, row_segments, False, grad_cross
    )
    grad_pairs = jnp.concatenate([grad_ck, grad_cv], axis=-1)
    cross_query_grad = weight_grad(normed4, grad_cq)
    grad_state1_part, gain_four = rms_back(state1, gains[4], project_back(grad_cq, dec_mats[2]))
    grad_state1 = grad_state2 + grad_state1_part
    cross_pair_grad = weight_grad(encoded, grad_pairs)
    grad_encoded = project_back(grad_pairs, dec_mats[3])
    branch_grad = grad_state1.astype(jnp.bfloat16)
    self_out_grad = weight_grad(self_attended, branch_grad)
    grad_self = project_back(branch_grad, dec_mats[1]).astype(jnp.bfloat16)
    grad_sq, grad_sk, grad_sv, dec_bias_grad = attend_back(
        self_qkv, self_qkv, self_places, dec_bias, target_segments, target_segments, True, grad_self
    )
    grad_sqkv = jnp.concatenate([grad_sq, grad_sk, grad_sv], axis=-1)
    self_qkv_grad = weight_grad(normed3, grad_sqkv)
    grad_state0_part, gain_three = rms_back(state0, gains[3], project_back(grad_sqkv, dec_mats[0]))
    grad_state0 = grad_state1 + grad_state0_part
    decoder_portion = jnp.concatenate(
        [
            pairs_of(matrix)
            for matrix in (
                self_qkv_grad,
                self_out_grad,
                cross_query_grad,
                cross_pair_grad,
                cross_out_grad,
                dec_in_grad,
                dec_down_grad,
            )
        ],
        axis=0,
    )
    dec_part = reduce_blocks(decoder_portion)

    grad_hidden2, gain_two = rms_back(hidden2, gains[2], grad_encoded)
    grad_hidden1, gain_one, encoder_input_gradient, encoder_down_gradient = ff_back(
        hidden1, gains[1], enc_mats[2], enc_mats[3], enc_cache, grad_hidden2
    )
    branch_grad = grad_hidden1.astype(jnp.bfloat16)
    encoder_output_gradient = weight_grad(enc_attended, branch_grad)
    grad_attn = project_back(branch_grad, enc_mats[1]).astype(jnp.bfloat16)
    grad_eq, grad_ek, grad_ev, enc_bias_grad = attend_back(
        enc_qkv, enc_qkv, self_places, enc_bias, row_segments, row_segments, False, grad_attn
    )
    grad_eqkv = jnp.concatenate([grad_eq, grad_ek, grad_ev], axis=-1)
    encoder_qkv_gradient = weight_grad(normed0, grad_eqkv)
    grad_hidden0_part, gain_zero = rms_back(hidden0, gains[0], project_back(grad_eqkv, enc_mats[0]))
    grad_hidden0 = grad_hidden1 + grad_hidden0_part
    encoder_portion = jnp.concatenate(
        [
            pairs_of(matrix)
            for matrix in (
                encoder_qkv_gradient,
                encoder_output_gradient,
                encoder_input_gradient,
                encoder_down_gradient,
            )
        ],
        axis=0,
    )
    enc_part = reduce_blocks(encoder_portion)

    back_rows = jnp.concatenate(
        [grad_hidden0.reshape(-1, D), grad_state0.reshape(-1, D)], axis=0
    ).astype(jnp.bfloat16)
    back_all = lax.all_gather(back_rows, "fsdp", axis=0, tiled=True)
    dense_bound = jnp.max(jnp.abs(emb_grad))
    bound = dense_bound + back_all.shape[0] * jnp.max(jnp.abs(back_all)).astype(jnp.float32)
    emb_grad = table_grads(back_all, all_tokens, vocab_first, vocab_local, emb_grad)
    gain_part = jnp.stack(
        [gain_zero, gain_one, gain_two, gain_three, gain_four, gain_five, gain_six]
    )
    rel_part = jnp.stack(
        [tile_bias_grad(enc_onehot, enc_bias_grad), tile_bias_grad(dec_onehot, dec_bias_grad)]
    )
    loss_part = jnp.where(fsdp_rank == 0, jnp.stack([group_loss, group_count]), 0.0)
    gain_total, rel_total, loss_total = lax.psum((gain_part, rel_part, loss_part), EVERYWHERE)
    loss_sum = loss_total[0]
    loss_count = jnp.maximum(loss_total[1], 1.0)
    share = 1.0 / loss_count
    gain_grad = gain_total * share
    rel_grad = rel_total * share

    if paired_mesh():
        dec_grad = from_pairs(share_blocks(dec_part) * share)
        enc_grad = from_pairs(share_blocks(enc_part) * share)
        top, low, scale = reduce_table(emb_grad, bound)
        squares = (
            jnp.sum(jnp.square(enc_part * share))
            + jnp.sum(jnp.square(dec_part * share))
            + jnp.sum(jnp.square(top * (share / scale)))
            + jnp.sum(jnp.square(low * (share / scale)))
        )
        squares_all = lax.psum(squares, EVERYWHERE)
        table_grad = share_table(top, low, scale)[:vocab_local] * share
    else:
        dec_whole, enc_whole = (dec_part * share, enc_part * share)
        dec_grad, enc_grad = (from_pairs(dec_whole), from_pairs(enc_whole))
        table_grad = lax.psum(emb_grad, REPLICAS)[:vocab_local] * share
        squares_all = lax.psum(
            jnp.sum(jnp.square(enc_whole))
            + jnp.sum(jnp.square(dec_whole))
            + jnp.sum(jnp.square(table_grad)),
            "fsdp",
        )

    enc_ahead, enc_lr, enc_rr = shampoo_ahead(enc_m, enc_lroot, enc_rroot)
    dec_ahead, dec_lr, dec_rr = shampoo_ahead(dec_m, dec_lroot, dec_rroot)
    dec_products = shampoo_products(dec_grad, dec_lr, dec_rr)
    enc_products = shampoo_products(enc_grad, enc_lr, enc_rr)
    grad_norm = jnp.sqrt(
        squares_all + jnp.sum(gain_grad * gain_grad) + jnp.sum(rel_grad * rel_grad)
    )
    factor = jnp.minimum(1.0, clip_limit / grad_norm)
    new_emb = adam_update(embedding, table_grad * factor, emb_m, emb_v)
    new_gain = adam_update(gains, gain_grad * factor, gain_m, gain_v)
    new_rel = adam_update(rel_bias, rel_grad * factor, rel_m, rel_v)
    new_enc = shampoo_update(enc_w, enc_m, enc_left, enc_right, enc_ahead, enc_products, factor)
    new_dec = shampoo_update(dec_w, dec_m, dec_left, dec_right, dec_ahead, dec_products, factor)
    return (
        loss_sum,
        loss_count,
        grad_norm,
        *new_emb,
        *new_gain,
        *new_rel,
        *new_enc,
        *new_dec,
    )


def solution(mesh):
    in_specs = (
        P(("dp", "fsdp"), "seq"),
        P(("dp", "fsdp"), "seq"),
        P(("dp", "fsdp"), "seq"),
        P(("dp", "fsdp", "seq"), None),
        P(("dp", "fsdp", "seq"), None),
        P(("dp", "fsdp", "seq"), None),
        P("fsdp", None),
        P("fsdp", None),
        P("fsdp", None),
        P(),
        P(),
        P(),
        P(),
        P(),
        P(),
        P("fsdp", None),
        P("fsdp", None),
        P("fsdp", None),
        P("fsdp", None),
        P("fsdp", None),
        P("fsdp", None),
        P("fsdp", None),
        P("fsdp", None),
        P("fsdp", None),
        P("fsdp", None),
        P("fsdp", None),
        P("fsdp", None),
    )
    out_specs = (
        P(),
        P(),
        P(),
        P("fsdp", None),
        P("fsdp", None),
        P("fsdp", None),
        P(),
        P(),
        P(),
        P(),
        P(),
        P(),
        P("fsdp", None),
        P("fsdp", None),
        P("fsdp", None),
        P("fsdp", None),
        P("fsdp", None),
        P("fsdp", None),
        P("fsdp", None),
        P("fsdp", None),
    )
    return jax.shard_map(
        on_device, mesh=mesh, in_specs=in_specs, out_specs=out_specs, check_vma=False
    )
```

```python
import functools
import math

import jax
import jax.numpy as jnp
from jax import lax
from jax.experimental import pallas as pl
from jax.experimental.pallas import tpu as pltpu
from jax.sharding import PartitionSpec as P

D = 768
H = 12
DH = 64
FF = 3072
VOCAB = 32128
NBK = 32
REACH = 128
BLOCK = 192
STEP = 10
PAIR = 2 * BLOCK
TILE = 128
LANES = 128


norm_eps = 1e-06
neg_fill = -1000000000.0
sentinel_offset = 29
beta_first = 0.9
beta_second = 0.999
adam_eps = 1e-08
adam_rate = 0.5
shampoo_rate = 0.01
stat_decay = 0.999
weight_decay = 0.01
clip_limit = 0.05
highest = lax.Precision.HIGHEST


def bucket_edges(buckets, exact, reach):
    edges = list(range(1, exact))
    spread = buckets - exact
    for place in range(spread):
        edges.append(int(math.ceil(exact * (reach / exact) ** (place / spread) - 1e-09)))
    return edges


def offset_buckets(offset, causal):
    if causal:
        distance = jnp.maximum(-offset, 0)
        result = jnp.zeros(offset.shape, jnp.int32)
        edges = bucket_edges(NBK, NBK // 2, REACH)
    else:
        distance = jnp.abs(offset)
        result = jnp.where(offset > 0, NBK // 2, 0).astype(jnp.int32)
        edges = bucket_edges(NBK // 2, NBK // 4, REACH)
    for edge in edges:
        result = result + (distance >= edge).astype(jnp.int32)
    return result


def tile_reach(blocks):
    return min(blocks - 1, 2)


def tile_onehot(blocks, causal):
    reach = tile_reach(blocks)
    place = jnp.arange(TILE, dtype=jnp.int32)
    shift = jnp.arange(-reach, reach + 1, dtype=jnp.int32) * TILE
    offset = shift[:, None, None] + place[None, None, :] - place[None, :, None]
    buckets = offset_buckets(offset, causal).reshape(-1)
    return (jnp.arange(NBK, dtype=jnp.int32)[:, None] == buckets[None, :]).astype(jnp.float32)


def tile_bias(onehot, rel):
    flat = jnp.einsum("nh,np->hp", rel, onehot, precision=highest)
    return flat.reshape(H, -1, TILE, TILE)


def tile_bias_grad(onehot, grads):
    return jnp.einsum("np,hp->nh", onehot, grads.reshape(H, -1), precision=highest)


def head_lanes(half):
    lane = lax.broadcasted_iota(jnp.int32, (1, LANES), 1)
    return (lane // DH) == half


def block_scores(query, keys, bias_ref, half, row, row_segs, key_segs, causal):
    scores = lax.dot_general(query, keys, (((1,), (1,)), ((), ())), preferred_element_type=jnp.float32)
    width = keys.shape[0]
    if bias_ref is not None:
        reach = tile_reach(width // TILE)
        tiles = []
        for column in range(width // TILE):
            tiles.append(bias_ref[half, min(max(column - row, -reach), reach) + reach])
        scores = scores + (jnp.concatenate(tiles, axis=1) if len(tiles) > 1 else tiles[0])
    mask = row_segs == key_segs
    if causal:
        at_row = row * TILE + lax.broadcasted_iota(jnp.int32, scores.shape, 0)
        at_key = lax.broadcasted_iota(jnp.int32, scores.shape, 1)
        mask = mask & (at_row >= at_key)
    scores = jnp.where(mask, scores, neg_fill)
    raised = jnp.exp(scores - jnp.max(scores, axis=-1, keepdims=True))
    return raised * (1.0 / jnp.sum(raised, axis=-1, keepdims=True))


def attend_kernel(q_ref, k_ref, v_ref, *rest, biased, causal):
    bias_ref = rest[0] if biased else None
    sq_ref, sk_ref, o_ref = rest[-3:]
    keys = k_ref[0]
    values = v_ref[0]
    key_segs = sk_ref[0]
    for row in range(q_ref.shape[1] // TILE):
        part = pl.ds(row * TILE, TILE)
        query = q_ref[0, part, :]
        row_segs = sq_ref[0, part, :]
        result = None
        for half in range(2):
            lanes = head_lanes(half)
            probs = block_scores(
                jnp.where(lanes, query, 0), keys, bias_ref, half, row, row_segs, key_segs, causal
            )
            output = jnp.dot(
                probs.astype(jnp.bfloat16), values, preferred_element_type=jnp.float32
            )
            result = output if result is None else jnp.where(lanes, output, result)
        o_ref[0, part, :] = result.astype(jnp.bfloat16)


def attend_back_kernel(q_ref, k_ref, v_ref, g_ref, *rest, biased, causal):
    if biased:
        bias_ref, sq_ref, sk_ref, dq_ref, dk_ref, dv_ref, db_ref = rest
    else:
        sq_ref, sk_ref, dq_ref, dk_ref, dv_ref = rest
        bias_ref = db_ref = None
    keys = k_ref[0]
    values = v_ref[0]
    key_segs = sk_ref[0]
    width = keys.shape[0]
    if biased:

        @pl.when(pl.program_id(1) == 0)
        def _():
            db_ref[...] = jnp.zeros_like(db_ref)

    grad_keys = None
    grad_values = None
    for row in range(q_ref.shape[1] // TILE):
        part = pl.ds(row * TILE, TILE)
        query = q_ref[0, part, :]
        grad_out = g_ref[0, part, :]
        row_segs = sq_ref[0, part, :]
        grad_query = None
        for half in range(2):
            lanes = head_lanes(half)
            own_query = jnp.where(lanes, query, 0)
            own_grad = jnp.where(lanes, grad_out, 0)
            probs = block_scores(
                own_query, keys, bias_ref, half, row, row_segs, key_segs, causal
            )
            grad_probs = lax.dot_general(
                own_grad, values, (((1,), (1,)), ((), ())), preferred_element_type=jnp.float32
            )
            drop = jnp.sum(probs * grad_probs, axis=-1, keepdims=True)
            grad_scores = (probs * (grad_probs - drop)).astype(jnp.bfloat16)
            down = (((0,), (0,)), ((), ()))
            part_values = lax.dot_general(
                probs.astype(jnp.bfloat16), own_grad, down, preferred_element_type=jnp.float32
            )
            part_keys = lax.dot_general(
                grad_scores, own_query, down, preferred_element_type=jnp.float32
            )
            grad_values = part_values if grad_values is None else grad_values + part_values
            grad_keys = part_keys if grad_keys is None else grad_keys + part_keys
            own_grad_query = jnp.dot(grad_scores, keys, preferred_element_type=jnp.float32)
            grad_query = (
                own_grad_query if grad_query is None else jnp.where(lanes, own_grad_query, grad_query)
            )
            if biased:
                wide = grad_scores.astype(jnp.float32)
                reach = tile_reach(width // TILE)
                for column in range(width // TILE):
                    slot = min(max(column - row, -reach), reach) + reach
                    db_ref[half, slot] += wide[:, column * TILE : (column + 1) * TILE]
        dq_ref[0, part, :] = grad_query.astype(jnp.bfloat16)
    dk_ref[0] = grad_keys.astype(jnp.bfloat16)
    dv_ref[0] = grad_values.astype(jnp.bfloat16)


def attention_specs(query, keys, places, bias, row_segs, key_segs):
    q_at, k_at, v_at = places
    rows, nq = row_segs.shape
    nk = key_segs.shape[1]

    def panel(length, first):
        return pl.BlockSpec((1, length, LANES), lambda pair, row: (row, 0, first + pair))

    operands = [query, keys, keys]
    specs = [panel(nq, q_at), panel(nk, k_at), panel(nk, v_at)]
    tail = []
    tail_specs = []
    if bias is not None:
        tail.append(bias)
        tail_specs.append(
            pl.BlockSpec((2,) + bias.shape[1:], lambda pair, row: (pair, 0, 0, 0))
        )
    tail += [row_segs[:, :, None], key_segs[:, None, :]]
    tail_specs += [
        pl.BlockSpec((1, nq, 1), lambda pair, row: (row, 0, 0)),
        pl.BlockSpec((1, 1, nk), lambda pair, row: (row, 0, 0)),
    ]
    return operands, specs, tail, tail_specs, panel


def attention_cost(rows, nq, nk, products):
    return pl.CostEstimate(
        flops=2 * products * rows * H * nq * nk * LANES,
        bytes_accessed=2 * products * rows * (nq + nk) * D,
        transcendentals=rows * H * nq * nk,
    )


def attend(query, keys, places, bias, row_segs, key_segs, causal):
    rows, nq = row_segs.shape
    nk = key_segs.shape[1]
    operands, specs, tail, tail_specs, panel = attention_specs(
        query, keys, places, bias, row_segs, key_segs
    )
    return pl.pallas_call(
        functools.partial(attend_kernel, biased=bias is not None, causal=causal),
        out_shape=jax.ShapeDtypeStruct((rows, nq, D), jnp.bfloat16),
        grid=(H // 2, rows),
        in_specs=specs + tail_specs,
        out_specs=panel(nq, 0),
        cost_estimate=attention_cost(rows, nq, nk, 2),
        compiler_params=pltpu.CompilerParams(vmem_limit_bytes=32 << 20),
    )(*operands, *tail)


def attend_back(query, keys, places, bias, row_segs, key_segs, causal, grad_out):
    rows, nq = row_segs.shape
    nk = key_segs.shape[1]
    operands, specs, tail, tail_specs, panel = attention_specs(
        query, keys, places, bias, row_segs, key_segs
    )
    outs = [
        jax.ShapeDtypeStruct((rows, nq, D), jnp.bfloat16),
        jax.ShapeDtypeStruct((rows, nk, D), jnp.bfloat16),
        jax.ShapeDtypeStruct((rows, nk, D), jnp.bfloat16),
    ]
    out_specs = [panel(nq, 0), panel(nk, 0), panel(nk, 0)]
    if bias is not None:
        outs.append(jax.ShapeDtypeStruct(bias.shape, jnp.float32))
        out_specs.append(
            pl.BlockSpec((2,) + bias.shape[1:], lambda pair, row: (pair, 0, 0, 0))
        )
    return pl.pallas_call(
        functools.partial(attend_back_kernel, biased=bias is not None, causal=causal),
        out_shape=outs,
        grid=(H // 2, rows),
        in_specs=specs + [panel(nq, 0)] + tail_specs,
        out_specs=out_specs,
        cost_estimate=attention_cost(rows, nq, nk, 5),
        compiler_params=pltpu.CompilerParams(vmem_limit_bytes=32 << 20),
    )(*operands, grad_out, *tail)


def layer_shapes(decoder):
    if decoder:
        return [(D, 3 * D), (D, D), (D, D), (D, 2 * D), (D, D), (D, FF), (FF, D)]
    return [(D, 3 * D), (D, D), (D, FF), (FF, D)]


def as_blocks(flat):
    return flat.reshape(flat.shape[0], BLOCK, BLOCK)


def as_rows(blocks):
    return blocks.reshape(blocks.shape[0], BLOCK * BLOCK)


def as_pairs(blocks):
    amount = blocks.shape[0] // 2
    split = blocks.reshape(amount, 2, BLOCK, BLOCK)
    return jnp.concatenate([split[:, 0], split[:, 1]], axis=-1)


def unpack_kernel(pairs_ref, out_ref):
    across = out_ref.shape[1] // PAIR
    for row in range(out_ref.shape[0] // BLOCK):
        for column in range(across):
            out_ref[row * BLOCK : (row + 1) * BLOCK, column * PAIR : (column + 1) * PAIR] = (
                pairs_ref[row * across + column]
            )


def matrices_of(pairs, shapes):
    matrix_list = []
    place = 0
    for height, breadth in shapes:
        group = 2 * breadth // PAIR
        first = place // group
        matrix_list.append(
            pl.pallas_call(
                unpack_kernel,
                out_shape=jax.ShapeDtypeStruct((height, breadth), pairs.dtype),
                grid=(height // PAIR,),
                in_specs=[
                    pl.BlockSpec(
                        (group, BLOCK, PAIR), lambda step, first=first: (first + step, 0, 0)
                    )
                ],
                out_specs=pl.BlockSpec((PAIR, breadth), lambda step: (step, 0)),
                cost_estimate=pl.CostEstimate(
                    flops=0, bytes_accessed=4 * height * breadth, transcendentals=0
                ),
                compiler_params=pltpu.CompilerParams(vmem_limit_bytes=32 << 20),
            )(pairs)
        )
        place += group * (height // PAIR)
    return matrix_list


def weight_grad_kernel(x_ref, g_ref, *rest):
    out_ref = rest[-1]
    across = out_ref.shape[0] // 2
    for column in range(across):
        product = lax.dot_general(
            x_ref[...],
            g_ref[:, column * PAIR : (column + 1) * PAIR],
            (((0,), (0,)), ((), ())),
            preferred_element_type=jnp.float32,
        )
        product = product.astype(jnp.bfloat16)
        out_ref[column] = product[:BLOCK]
        out_ref[across + column] = product[BLOCK:]


def weight_grads(operands):
    total = sum(x.shape[-1] * g.shape[-1] for x, g in operands) // (BLOCK * PAIR)
    pairs = None
    place = 0
    for x, g in operands:
        x = x.reshape(-1, x.shape[-1])
        g = g.reshape(-1, g.shape[-1])
        count, height = x.shape
        breadth = g.shape[1]
        group = 2 * breadth // PAIR
        first = place // group
        given = [] if pairs is None else [pairs]
        pairs = pl.pallas_call(
            weight_grad_kernel,
            out_shape=jax.ShapeDtypeStruct((total, BLOCK, PAIR), jnp.bfloat16),
            grid=(height // PAIR,),
            in_specs=[
                pl.BlockSpec((count, PAIR), lambda step: (0, step)),
                pl.BlockSpec((count, breadth), lambda step: (0, 0)),
            ]
            + [pl.BlockSpec(memory_space=pl.ANY)] * len(given),
            out_specs=pl.BlockSpec(
                (group, BLOCK, PAIR), lambda step, first=first: (first + step, 0, 0)
            ),
            input_output_aliases={2: 0} if given else {},
            cost_estimate=pl.CostEstimate(
                flops=2 * count * height * breadth,
                bytes_accessed=2 * (count * (height + breadth) + height * breadth),
                transcendentals=0,
            ),
            compiler_params=pltpu.CompilerParams(vmem_limit_bytes=40 << 20),
        )(x, g, *given)
        place += group * (height // PAIR)
    return pairs


def split_float(values):
    high = values.astype(jnp.bfloat16)
    return high, (values - high.astype(jnp.float32)).astype(jnp.bfloat16)


def full_product(left, right, contract):
    def part(first, second):
        return lax.dot_general(
            first, second, (contract, ((), ())), preferred_element_type=jnp.float32
        )

    return (
        part(left[0], right[1]) + part(left[1], right[0]) + part(left[0], right[0])
    )


ROW_COL = ((1,), (0,))
ROW_ROW = ((1,), (1,))
COL_COL = ((0,), (0,))


def turned_product(left_root, middle, right_root):
    shaped = full_product(split_float(left_root), middle, ROW_COL)
    return full_product(split_float(shaped), split_float(right_root), ROW_COL)


def ahead_kernel(m_ref, lr_ref, rr_ref, o_ref):
    for place in range(m_ref.shape[0]):
        o_ref[place] = turned_product(lr_ref[place], split_float(m_ref[place]), rr_ref[place])


def products_kernel(g_ref, lr_ref, rr_ref, g_out, turned_out, left_out, right_out):
    for place in range(2):
        block = g_ref[0, :, place * BLOCK : (place + 1) * BLOCK]
        g_out[place] = block
        halves = split_float(block)
        turned_out[place] = turned_product(lr_ref[place], halves, rr_ref[place])
        left_out[place] = full_product(halves, halves, ROW_ROW)
        right_out[place] = full_product(halves, halves, COL_COL)


def block_cost(amount, products, arrays):
    return pl.CostEstimate(
        flops=6 * products * amount * BLOCK**3,
        bytes_accessed=4 * arrays * amount * BLOCK * BLOCK,
        transcendentals=0,
    )


def shampoo_ahead(moment, left_root, right_root):
    blocks = [as_blocks(moment), as_blocks(left_root), as_blocks(right_root)]
    amount = moment.shape[0]
    spec = pl.BlockSpec((2, BLOCK, BLOCK), lambda pair: (pair, 0, 0))
    ahead = pl.pallas_call(
        ahead_kernel,
        out_shape=jax.ShapeDtypeStruct((amount, BLOCK, BLOCK), jnp.float32),
        grid=(amount // 2,),
        in_specs=[spec] * 3,
        out_specs=spec,
        cost_estimate=block_cost(amount, 2, 4),
        compiler_params=pltpu.CompilerParams(vmem_limit_bytes=32 << 20),
    )(*blocks)
    return as_rows(ahead), blocks[1], blocks[2]


def shampoo_products(pairs, left_root, right_root):
    amount = left_root.shape[0]
    spec = pl.BlockSpec((2, BLOCK, BLOCK), lambda pair: (pair, 0, 0))
    results = pl.pallas_call(
        products_kernel,
        out_shape=[jax.ShapeDtypeStruct((amount, BLOCK, BLOCK), jnp.float32)] * 4,
        grid=(amount // 2,),
        in_specs=[pl.BlockSpec((1, BLOCK, PAIR), lambda pair: (pair, 0, 0)), spec, spec],
        out_specs=[spec] * 4,
        cost_estimate=block_cost(amount, 4, 7),
        compiler_params=pltpu.CompilerParams(vmem_limit_bytes=32 << 20),
    )(pairs, left_root, right_root)
    return [as_rows(result) for result in results]


def project(left, right):
    return jnp.matmul(left, right, preferred_element_type=jnp.float32)


def project_back(left, right):
    return jnp.einsum("btf,df->btd", left, right, preferred_element_type=jnp.float32)


def rms(values, gain):
    return values * lax.rsqrt(jnp.mean(values * values, axis=-1, keepdims=True) + norm_eps) * gain


def rms_back(values, gain, grad_out):
    inverse = lax.rsqrt(jnp.mean(values * values, axis=-1, keepdims=True) + norm_eps)
    normed = values * inverse
    grad_gain = jnp.sum(grad_out * normed, axis=(0, 1))
    grad_normed = grad_out * gain
    grad_values = inverse * (
        grad_normed - normed * jnp.mean(grad_normed * normed, axis=-1, keepdims=True)
    )
    return (grad_values, grad_gain)


def ff_forward(hidden, gain, w_in, w_down):
    normed = rms(hidden, gain).astype(jnp.bfloat16)
    inner = project(normed, w_in)
    active = jax.nn.gelu(inner).astype(jnp.bfloat16)
    return (hidden + project(active, w_down), (normed, inner, active))


def ff_back(hidden, gain, w_in, w_down, cache, grad_out):
    normed, inner, active = cache
    branch_grad = grad_out.astype(jnp.bfloat16)
    grad_active = project_back(branch_grad, w_down)
    unused, gelu_back = jax.vjp(jax.nn.gelu, inner)
    grad_inner = gelu_back(grad_active)[0].astype(jnp.bfloat16)
    grad_part, grad_gain = rms_back(hidden, gain, project_back(grad_inner, w_in))
    return (grad_out + grad_part, grad_gain, (normed, grad_inner), (active, branch_grad))


def table_rows(table, token_ids, vocab_first):
    local_ids = token_ids - vocab_first
    inside = (local_ids >= 0) & (local_ids < table.shape[0])
    picked = jnp.take(table, jnp.clip(local_ids, 0, table.shape[0] - 1), axis=0)
    return jnp.where(inside[..., None], picked, jnp.zeros((), table.dtype))


def table_grads(grads, token_ids, vocab_first, dense):
    vocab_local = dense.shape[0]
    local_ids = token_ids.reshape(-1) - vocab_first
    inside = (local_ids >= 0) & (local_ids < vocab_local)
    slots = jnp.where(inside, local_ids, vocab_local)
    return dense.at[slots].add(grads.astype(jnp.float32), mode="drop")


REPLICAS = ("dp", "seq")
EVERYWHERE = ("fsdp", "dp", "seq")


def replica_rank():
    return lax.axis_index("dp") * lax.axis_size("seq") + lax.axis_index("seq")


def replica_count():
    return lax.axis_size("dp") * lax.axis_size("seq")


def own_weights(master):
    share = master.shape[0] // replica_count()
    if master.shape[0] % (2 * replica_count()) == 0:
        master = lax.dynamic_slice_in_dim(master, replica_rank() * share, share, 0)
    return as_pairs(as_blocks(master.astype(jnp.bfloat16)))


def gather_weights(pairs, amount):
    split = amount % (2 * replica_count()) == 0
    return lax.all_gather(pairs, EVERYWHERE if split else "fsdp", axis=0, tiled=True)


def paired_mesh():
    return (
        lax.axis_size("dp") == 2 and lax.axis_size("seq") == 2 and lax.axis_size("fsdp") % 2 == 0
    )


def swap(values, axis):
    size = lax.axis_size(axis)
    return lax.ppermute(values, axis, [(place, place ^ 1) for place in range(size)])


def shift(values, step):
    size = lax.axis_size("fsdp")
    moves = [
        (place, place + 2 * step) for place in range(size) if 0 <= place + 2 * step < size
    ]
    return lax.ppermute(values, "fsdp", moves)


def choose(flag, if_set, if_clear):
    return jnp.where(flag == 1, if_set, if_clear)


def pick(values, place, axis):
    return lax.dynamic_index_in_dim(values, place, axis, False)


def narrow(values):
    return values.astype(jnp.bfloat16)


def wide(values):
    return values.astype(jnp.float32)


def agreed_scale(largest):
    for axis in ("seq", "dp"):
        largest = jnp.maximum(largest, swap(largest, axis))
    return 4096.0 / jnp.maximum(largest, 1e-30)


def placed(relative, first, second):
    def at(row, column):
        here = choose(second, relative[row][1 - column], relative[row][column])
        there = choose(second, relative[1 - row][1 - column], relative[1 - row][column])
        return choose(first, there, here)

    return [[at(0, 0), at(0, 1)], [at(1, 0), at(1, 1)]]


def sum_small(values):
    size = lax.axis_size("fsdp")
    if not paired_mesh() or size & (size - 1):
        return lax.psum(values, EVERYWHERE)
    values = values + swap(values, "seq")
    values = values + swap(values, "dp")
    step = 1
    while step < size:
        moves = [(place, place ^ step) for place in range(size)]
        values = values + lax.ppermute(values, "fsdp", moves)
        step *= 2
    return values


def reduce_blocks(pairs):
    if not paired_mesh():
        return lax.psum(
            lax.psum_scatter(wide(pairs), "fsdp", scatter_dimension=0, tiled=True), REPLICAS
        )
    n_chips = lax.axis_size("fsdp") // 2
    core = lax.axis_index("fsdp") % 2
    chip = lax.axis_index("fsdp") // 2
    side, half = (lax.axis_index("dp"), lax.axis_index("seq"))
    amount = pairs.shape[0] // (2 * n_chips)
    quarter = amount // 4
    mid = BLOCK // 2
    pairs = pairs.reshape(n_chips, 2, amount, BLOCK, PAIR)
    chip_sum = wide(pick(pairs, core, 1)) + wide(swap(pick(pairs, 1 - core, 1), "fsdp"))
    chip_sum = chip_sum.reshape(n_chips, 2, 2, quarter, BLOCK, PAIR)
    upper, lower = (chip_sum[..., :mid, :], chip_sum[..., mid:, :])
    upper = pick(upper, half, 2) + wide(swap(narrow(pick(upper, 1 - half, 2)), "seq"))
    lower = pick(lower, side, 1) + wide(swap(narrow(pick(lower, 1 - side, 1)), "dp"))
    upper = pick(upper, side, 1) + wide(swap(narrow(pick(upper, 1 - side, 1)), "dp"))
    lower = pick(lower, half, 1) + wide(swap(narrow(pick(lower, 1 - half, 1)), "seq"))
    line_sum = jnp.concatenate([upper, lower], axis=2)
    ahead = lax.dynamic_slice_in_dim(
        jnp.concatenate([line_sum, line_sum[:-1]], axis=0), chip, n_chips, 0
    )
    up = down = None
    for step in range(n_chips - 1, 0, -1):
        rising, falling = (ahead[step], ahead[n_chips - step])
        if up is not None:
            rising, falling = (rising + wide(up), falling + wide(down))
        up, down = (shift(narrow(rising), 1), shift(narrow(falling), -1))
    return ahead[0] + wide(up) + wide(down)


def share_blocks(own):
    side, half = (lax.axis_index("dp"), lax.axis_index("seq"))
    mid = BLOCK // 2
    scale = agreed_scale(jnp.max(jnp.abs(own)))
    own = lax.optimization_barrier((own * scale).astype(jnp.float16))
    upper, lower = (own[:, :mid], own[:, mid:])
    upper_side, lower_half = (swap(upper, "dp"), swap(lower, "seq"))
    upper_rest = swap(jnp.stack([upper, upper_side]), "seq")
    lower_rest = swap(jnp.stack([lower, lower_half]), "dp")
    relative = [
        [
            jnp.concatenate([upper, lower], axis=1),
            jnp.concatenate([upper_rest[0], lower_half], axis=1),
        ],
        [
            jnp.concatenate([upper_side, lower_rest[0]], axis=1),
            jnp.concatenate([upper_rest[1], lower_rest[1]], axis=1),
        ],
    ]
    whole = placed(relative, side, half)
    return wide(jnp.concatenate(whole[0] + whole[1], axis=0)) * (1.0 / scale)


def window_rows(half_rows):
    return -(-half_rows // 16) * 8


def reduce_table(partial, bound):
    side, half = (lax.axis_index("dp"), lax.axis_index("seq"))
    scale = agreed_scale(bound)
    half_rows = partial.shape[0] // 2
    window = window_rows(half_rows)

    def rows_of(first, place):
        start = first + place * (half_rows - window)
        return lax.dynamic_slice_in_dim(partial, start, window, 0) * scale

    def half_lanes(values, place):
        return lax.dynamic_slice_in_dim(values, place * (D // 2), D // 2, 1)

    def send(values, axis):
        return wide(swap(values.astype(jnp.float16), axis))

    top = rows_of(0, half) + send(rows_of(0, 1 - half), "seq")
    low = rows_of(half_rows, side) + send(rows_of(half_rows, 1 - side), "dp")
    top = half_lanes(top, side) + send(half_lanes(top, 1 - side), "dp")
    low = half_lanes(low, half) + send(half_lanes(low, 1 - half), "seq")
    return top, low, scale


def table_squares(top, low, half_rows):
    side, half = (lax.axis_index("dp"), lax.axis_index("seq"))
    again = 2 * window_rows(half_rows) - half_rows
    row = lax.broadcasted_iota(jnp.int32, (top.shape[0], 1), 0)
    return jnp.sum(jnp.where(row >= again * half, top * top, 0.0)) + jnp.sum(
        jnp.where(row >= again * side, low * low, 0.0)
    )


def share_table(top, low, scale, half_rows):
    side, half = (lax.axis_index("dp"), lax.axis_index("seq"))
    again = 2 * window_rows(half_rows) - half_rows
    top = lax.optimization_barrier(top.astype(jnp.float16))
    low = lax.optimization_barrier(low.astype(jnp.float16))
    top_side, low_half = (swap(top, "dp"), swap(low, "seq"))
    top_rest = (swap(top, "seq"), swap(top_side, "seq"))
    low_rest = (swap(low, "dp"), swap(low_half, "dp"))
    top_all = placed([[top, top_side], top_rest], half, side)
    low_all = placed([[low, low_half], low_rest], side, half)
    rows = []
    for first, second in (top_all, low_all):
        rows.append(jnp.concatenate(first, axis=1))
        rows.append(jnp.concatenate(second, axis=1)[again:])
    return wide(jnp.concatenate(rows, axis=0)) * (1.0 / scale)


def adam_update(weight, gradient, moment, second):
    moment = beta_first * moment + (1 - beta_first) * gradient
    second = beta_second * second + (1 - beta_second) * gradient * gradient
    corrected = moment / (1 - beta_first**STEP)
    scaled = second / (1 - beta_second**STEP)
    weight = weight - adam_rate * (
        corrected / (jnp.sqrt(scaled) + adam_eps) + weight_decay * weight
    )
    return (weight, moment, second)


def shampoo_update(weight, moment, left, right, ahead, products, factor):
    gradient, turned, left_square, right_square = products
    direction = beta_first * ahead + ((1 - beta_first) * factor) * turned
    square = (1 - stat_decay) * factor * factor
    return (
        weight - shampoo_rate * (direction + weight_decay * weight),
        beta_first * moment + ((1 - beta_first) * factor) * gradient,
        stat_decay * left + square * left_square,
        stat_decay * right + square * right_square,
    )


def on_device(
    enc_ids,
    span_mask,
    segments,
    targets,
    loss_weights,
    target_segments,
    embedding,
    emb_m,
    emb_v,
    gains,
    gain_m,
    gain_v,
    rel_bias,
    rel_m,
    rel_v,
    enc_w,
    enc_m,
    enc_left,
    enc_right,
    enc_lroot,
    enc_rroot,
    dec_w,
    dec_m,
    dec_left,
    dec_right,
    dec_lroot,
    dec_rroot,
):
    fsdp_rank = lax.axis_index("fsdp")
    seq_rank = lax.axis_index("seq")
    n_fsdp = lax.axis_size("fsdp")
    n_seq = lax.axis_size("seq")
    half_len = enc_ids.shape[1]
    rows, dec_len = targets.shape
    enc_len = half_len * n_seq
    enc_in = jnp.where(span_mask == 1, VOCAB - sentinel_offset, enc_ids)
    dec_in = jnp.concatenate([jnp.zeros((rows, 1), jnp.int32), targets[:, :-1]], axis=1)

    def by_rows(positions):
        return positions.reshape(n_seq, rows, half_len)

    message = jnp.concatenate(
        [by_rows(enc_in), by_rows(segments)], axis=2
    ).reshape(n_seq, -1)
    own = jnp.concatenate(
        [dec_in.reshape(-1), targets.reshape(-1), loss_weights.reshape(-1)]
    )
    message = jnp.concatenate([message.reshape(-1), own]).reshape(1, 1, -1)
    enc_pairs, dec_pairs, message = lax.optimization_barrier(
        (own_weights(enc_w), own_weights(dec_w), message)
    )
    enc_pairs = gather_weights(enc_pairs, enc_w.shape[0])
    dec_pairs = gather_weights(dec_pairs, dec_w.shape[0])
    gathered = lax.all_gather(message, ("fsdp", "seq"), axis=0, tiled=True)
    gathered = gathered.reshape(n_fsdp, n_seq, -1)
    row_words = rows * 2 * half_len
    enc_words = lax.dynamic_slice_in_dim(gathered, seq_rank * row_words, row_words, 2)
    enc_words = enc_words.reshape(n_fsdp, n_seq, rows, 2, half_len).transpose(3, 0, 2, 1, 4)
    enc_words = enc_words.reshape(2, n_fsdp, rows * enc_len)
    all_enc = enc_words[0]
    row_segments = lax.dynamic_index_in_dim(enc_words[1], fsdp_rank, 0, False)
    row_segments = row_segments.reshape(rows, enc_len)
    dec_words = lax.dynamic_index_in_dim(gathered, seq_rank, 1, False)[:, n_seq * row_words :]
    dec_words = dec_words.reshape(n_fsdp, 3, rows * dec_len)
    all_dec, all_targets, all_weights = (dec_words[:, 0], dec_words[:, 1], dec_words[:, 2])
    all_tokens = jnp.concatenate([all_enc, all_dec], axis=1)

    table = embedding.astype(jnp.bfloat16)
    vocab_local = table.shape[0]
    vocab_first = fsdp_rank * vocab_local
    looked_up = lax.psum_scatter(
        table_rows(table, all_tokens, vocab_first), "fsdp", scatter_dimension=0, tiled=True
    ).reshape(-1, D)
    hidden0 = looked_up[: rows * enc_len].reshape(rows, enc_len, D).astype(jnp.float32)
    state0 = looked_up[rows * enc_len :].reshape(rows, dec_len, D).astype(jnp.float32)

    enc_mats = matrices_of(enc_pairs, layer_shapes(False))
    dec_mats = matrices_of(dec_pairs, layer_shapes(True))
    enc_onehot = tile_onehot(enc_len // TILE, False)
    dec_onehot = tile_onehot(dec_len // TILE, True)
    enc_bias = tile_bias(enc_onehot, rel_bias[0])
    dec_bias = tile_bias(dec_onehot, rel_bias[1])
    tile_at = D // LANES
    self_places = (0, tile_at, 2 * tile_at)
    cross_places = (0, 0, tile_at)

    normed0 = rms(hidden0, gains[0]).astype(jnp.bfloat16)
    enc_qkv = project(normed0, enc_mats[0]).astype(jnp.bfloat16)
    enc_attended = attend(
        enc_qkv, enc_qkv, self_places, enc_bias, row_segments, row_segments, False
    )
    hidden1 = hidden0 + project(enc_attended, enc_mats[1])
    hidden2, enc_cache = ff_forward(hidden1, gains[1], enc_mats[2], enc_mats[3])
    encoded = rms(hidden2, gains[2]).astype(jnp.bfloat16)
    pairs = project(encoded, dec_mats[3]).astype(jnp.bfloat16)

    normed3 = rms(state0, gains[3]).astype(jnp.bfloat16)
    self_qkv = project(normed3, dec_mats[0]).astype(jnp.bfloat16)
    self_attended = attend(
        self_qkv, self_qkv, self_places, dec_bias, target_segments, target_segments, True
    )
    state1 = state0 + project(self_attended, dec_mats[1])
    normed4 = rms(state1, gains[4]).astype(jnp.bfloat16)
    cross_query = project(normed4, dec_mats[2]).astype(jnp.bfloat16)
    cross_attended = attend(
        cross_query, pairs, cross_places, None, target_segments, row_segments, False
    )
    state2 = state1 + project(cross_attended, dec_mats[4])
    state3, dec_cache = ff_forward(state2, gains[5], dec_mats[5], dec_mats[6])
    out_scale = D ** (-0.5)
    final = (rms(state3, gains[6]) * out_scale).astype(jnp.bfloat16)

    all_final = lax.all_gather(final.reshape(rows * dec_len, D), "fsdp", axis=0, tiled=True)
    logits = jnp.einsum("nd,vd->nv", all_final, table, preferred_element_type=jnp.float32)
    local_ids = all_targets.reshape(-1) - vocab_first
    target_hot = local_ids[:, None] == jnp.arange(vocab_local, dtype=jnp.int32)[None, :]
    local_top = jnp.max(logits, axis=1)
    local_sum = jnp.sum(jnp.exp(logits - local_top[:, None]), axis=1)
    local_pick = jnp.sum(jnp.where(target_hot, logits, 0.0), axis=1)
    stats = lax.all_gather(
        jnp.stack([local_top, local_sum, local_pick])[None], "fsdp", axis=0, tiled=True
    )
    top_all = jnp.max(stats[:, 0], axis=0)
    sum_all = jnp.sum(stats[:, 1] * jnp.exp(stats[:, 0] - top_all), axis=0)
    pick_all = jnp.sum(stats[:, 2], axis=0)
    lse = top_all + jnp.log(sum_all)
    token_weights = all_weights.reshape(-1).astype(jnp.float32)
    group_loss = jnp.sum(token_weights * (lse - pick_all))
    group_count = jnp.sum(token_weights)
    grad_logits = (
        token_weights[:, None] * (jnp.exp(logits - lse[:, None]) - target_hot.astype(jnp.float32))
    ).astype(jnp.bfloat16)
    emb_grad = jnp.einsum("nv,nd->vd", grad_logits, all_final, preferred_element_type=jnp.float32)
    grad_final = lax.psum_scatter(
        jnp.dot(grad_logits, table, preferred_element_type=jnp.float32),
        "fsdp",
        scatter_dimension=0,
        tiled=True,
    ).reshape(rows, dec_len, D)

    grad_state3, gain_six = rms_back(state3, gains[6], grad_final * out_scale)
    grad_state2, gain_five, dec_in_grad, dec_down_grad = ff_back(
        state2, gains[5], dec_mats[5], dec_mats[6], dec_cache, grad_state3
    )
    branch_grad = grad_state2.astype(jnp.bfloat16)
    cross_out_grad = (cross_attended, branch_grad)
    grad_cross = project_back(branch_grad, dec_mats[4]).astype(jnp.bfloat16)
    grad_cq, grad_ck, grad_cv = attend_back(
        cross_query, pairs, cross_places, None, target_segments, row_segments, False, grad_cross
    )
    grad_pairs = jnp.concatenate([grad_ck, grad_cv], axis=-1)
    cross_query_grad = (normed4, grad_cq)
    grad_state1_part, gain_four = rms_back(state1, gains[4], project_back(grad_cq, dec_mats[2]))
    grad_state1 = grad_state2 + grad_state1_part
    cross_pair_grad = (encoded, grad_pairs)
    grad_encoded = project_back(grad_pairs, dec_mats[3])
    branch_grad = grad_state1.astype(jnp.bfloat16)
    self_out_grad = (self_attended, branch_grad)
    grad_self = project_back(branch_grad, dec_mats[1]).astype(jnp.bfloat16)
    grad_sq, grad_sk, grad_sv, dec_bias_grad = attend_back(
        self_qkv, self_qkv, self_places, dec_bias, target_segments, target_segments, True, grad_self
    )
    grad_sqkv = jnp.concatenate([grad_sq, grad_sk, grad_sv], axis=-1)
    self_qkv_grad = (normed3, grad_sqkv)
    grad_state0_part, gain_three = rms_back(state0, gains[3], project_back(grad_sqkv, dec_mats[0]))
    grad_state0 = grad_state1 + grad_state0_part
    decoder_portion = weight_grads(
        [
            self_qkv_grad,
            self_out_grad,
            cross_query_grad,
            cross_pair_grad,
            cross_out_grad,
            dec_in_grad,
            dec_down_grad,
        ]
    )
    dec_part = reduce_blocks(decoder_portion)

    grad_hidden2, gain_two = rms_back(hidden2, gains[2], grad_encoded)
    grad_hidden1, gain_one, encoder_input_gradient, encoder_down_gradient = ff_back(
        hidden1, gains[1], enc_mats[2], enc_mats[3], enc_cache, grad_hidden2
    )
    branch_grad = grad_hidden1.astype(jnp.bfloat16)
    encoder_output_gradient = (enc_attended, branch_grad)
    grad_attn = project_back(branch_grad, enc_mats[1]).astype(jnp.bfloat16)
    grad_eq, grad_ek, grad_ev, enc_bias_grad = attend_back(
        enc_qkv, enc_qkv, self_places, enc_bias, row_segments, row_segments, False, grad_attn
    )
    grad_eqkv = jnp.concatenate([grad_eq, grad_ek, grad_ev], axis=-1)
    encoder_qkv_gradient = (normed0, grad_eqkv)
    grad_hidden0_part, gain_zero = rms_back(hidden0, gains[0], project_back(grad_eqkv, enc_mats[0]))
    grad_hidden0 = grad_hidden1 + grad_hidden0_part
    encoder_portion = weight_grads(
        [
            encoder_qkv_gradient,
            encoder_output_gradient,
            encoder_input_gradient,
            encoder_down_gradient,
        ]
    )
    enc_part = reduce_blocks(encoder_portion)

    back_rows = jnp.concatenate(
        [grad_hidden0.reshape(-1, D), grad_state0.reshape(-1, D)], axis=0
    ).astype(jnp.bfloat16)
    back_all = lax.all_gather(back_rows, "fsdp", axis=0, tiled=True)
    dense_bound = jnp.max(jnp.abs(emb_grad))
    bound = dense_bound + back_all.shape[0] * jnp.max(jnp.abs(back_all)).astype(jnp.float32)
    emb_grad = table_grads(back_all, all_tokens, vocab_first, emb_grad)
    gain_part = jnp.stack(
        [gain_zero, gain_one, gain_two, gain_three, gain_four, gain_five, gain_six]
    )
    rel_part = jnp.stack(
        [tile_bias_grad(enc_onehot, enc_bias_grad), tile_bias_grad(dec_onehot, dec_bias_grad)]
    )
    loss_part = jnp.where(fsdp_rank == 0, jnp.stack([group_loss, group_count]), 0.0)
    small = jnp.concatenate(
        [gain_part.reshape(-1), rel_part.reshape(-1), loss_part, jnp.zeros(126, jnp.float32)]
    )
    small = sum_small(small.reshape(-1, LANES)).reshape(-1)
    gain_total = small[: 7 * D].reshape(7, D)
    rel_total = small[7 * D : 7 * D + 2 * NBK * H].reshape(2, NBK, H)
    loss_total = small[7 * D + 2 * NBK * H :]
    loss_sum = loss_total[0]
    loss_count = jnp.maximum(loss_total[1], 1.0)
    share = 1.0 / loss_count
    gain_grad = gain_total * share
    rel_grad = rel_total * share

    if paired_mesh():
        dec_grad = share_blocks(dec_part) * share
        enc_grad = share_blocks(enc_part) * share
        half_rows = vocab_local // 2
        top, low, scale = reduce_table(emb_grad, bound)
        squares = (
            jnp.sum(jnp.square(enc_part * share))
            + jnp.sum(jnp.square(dec_part * share))
            + table_squares(top * (share / scale), low * (share / scale), half_rows)
        )
        squares_all = sum_small(squares)
        table_grad = share_table(top, low, scale, half_rows) * share
    else:
        dec_grad, enc_grad = (dec_part * share, enc_part * share)
        table_grad = lax.psum(emb_grad, REPLICAS) * share
        squares_all = lax.psum(
            jnp.sum(jnp.square(enc_grad))
            + jnp.sum(jnp.square(dec_grad))
            + jnp.sum(jnp.square(table_grad)),
            "fsdp",
        )

    enc_ahead, enc_lr, enc_rr = shampoo_ahead(enc_m, enc_lroot, enc_rroot)
    dec_ahead, dec_lr, dec_rr = shampoo_ahead(dec_m, dec_lroot, dec_rroot)
    dec_products = shampoo_products(dec_grad, dec_lr, dec_rr)
    enc_products = shampoo_products(enc_grad, enc_lr, enc_rr)
    grad_norm = jnp.sqrt(
        squares_all + jnp.sum(gain_grad * gain_grad) + jnp.sum(rel_grad * rel_grad)
    )
    factor = jnp.minimum(1.0, clip_limit / grad_norm)
    new_emb = adam_update(embedding, table_grad * factor, emb_m, emb_v)
    new_gain = adam_update(gains, gain_grad * factor, gain_m, gain_v)
    new_rel = adam_update(rel_bias, rel_grad * factor, rel_m, rel_v)
    new_enc = shampoo_update(enc_w, enc_m, enc_left, enc_right, enc_ahead, enc_products, factor)
    new_dec = shampoo_update(dec_w, dec_m, dec_left, dec_right, dec_ahead, dec_products, factor)
    return (
        loss_sum,
        loss_count,
        grad_norm,
        *new_emb,
        *new_gain,
        *new_rel,
        *new_enc,
        *new_dec,
    )


def solution(mesh):
    in_specs = (
        P(("dp", "fsdp"), "seq"),
        P(("dp", "fsdp"), "seq"),
        P(("dp", "fsdp"), "seq"),
        P(("dp", "fsdp", "seq"), None),
        P(("dp", "fsdp", "seq"), None),
        P(("dp", "fsdp", "seq"), None),
        P("fsdp", None),
        P("fsdp", None),
        P("fsdp", None),
        P(),
        P(),
        P(),
        P(),
        P(),
        P(),
        P("fsdp", None),
        P("fsdp", None),
        P("fsdp", None),
        P("fsdp", None),
        P("fsdp", None),
        P("fsdp", None),
        P("fsdp", None),
        P("fsdp", None),
        P("fsdp", None),
        P("fsdp", None),
        P("fsdp", None),
        P("fsdp", None),
    )
    out_specs = (
        P(),
        P(),
        P(),
        P("fsdp", None),
        P("fsdp", None),
        P("fsdp", None),
        P(),
        P(),
        P(),
        P(),
        P(),
        P(),
        P("fsdp", None),
        P("fsdp", None),
        P("fsdp", None),
        P("fsdp", None),
        P("fsdp", None),
        P("fsdp", None),
        P("fsdp", None),
        P("fsdp", None),
    )
    return jax.shard_map(
        on_device, mesh=mesh, in_specs=in_specs, out_specs=out_specs, check_vma=False
    )
```

```python
import functools
import math

import jax
import jax.numpy as jnp
from jax import lax
from jax.experimental import pallas as pl
from jax.experimental.pallas import tpu as pltpu
from jax.sharding import PartitionSpec as P

D = 768
H = 12
DH = 64
FF = 3072
VOCAB = 32128
NBK = 32
REACH = 128
BLOCK = 192
STEP = 10
PAIR = 2 * BLOCK
TILE = 128
LANES = 128


norm_eps = 1e-06
neg_fill = -1000000000.0
sentinel_offset = 29
beta_first = 0.9
beta_second = 0.999
adam_eps = 1e-08
adam_rate = 0.5
shampoo_rate = 0.01
stat_decay = 0.999
weight_decay = 0.01
clip_limit = 0.05
highest = lax.Precision.HIGHEST


def bucket_edges(buckets, exact, reach):
    edges = list(range(1, exact))
    spread = buckets - exact
    for place in range(spread):
        edges.append(int(math.ceil(exact * (reach / exact) ** (place / spread) - 1e-09)))
    return edges


def offset_buckets(offset, causal):
    if causal:
        distance = jnp.maximum(-offset, 0)
        result = jnp.zeros(offset.shape, jnp.int32)
        edges = bucket_edges(NBK, NBK // 2, REACH)
    else:
        distance = jnp.abs(offset)
        result = jnp.where(offset > 0, NBK // 2, 0).astype(jnp.int32)
        edges = bucket_edges(NBK // 2, NBK // 4, REACH)
    for edge in edges:
        result = result + (distance >= edge).astype(jnp.int32)
    return result


def tile_reach(blocks):
    return min(blocks - 1, 2)


def tile_onehot(blocks, causal):
    reach = tile_reach(blocks)
    place = jnp.arange(TILE, dtype=jnp.int32)
    shift = jnp.arange(-reach, reach + 1, dtype=jnp.int32) * TILE
    offset = shift[:, None, None] + place[None, None, :] - place[None, :, None]
    buckets = offset_buckets(offset, causal).reshape(-1)
    return (jnp.arange(NBK, dtype=jnp.int32)[:, None] == buckets[None, :]).astype(jnp.float32)


def tile_bias(onehot, rel):
    flat = jnp.einsum("nh,np->hp", rel, onehot, precision=highest)
    return flat.reshape(H, -1, TILE, TILE)


def tile_bias_grad(onehot, grads):
    return jnp.einsum("np,hp->nh", onehot, grads.reshape(H, -1), precision=highest)


def head_lanes(half):
    lane = lax.broadcasted_iota(jnp.int32, (1, LANES), 1)
    return (lane // DH) == half


def block_scores(query, keys, bias_ref, half, row, row_segs, key_segs, causal):
    scores = lax.dot_general(query, keys, (((1,), (1,)), ((), ())), preferred_element_type=jnp.float32)
    width = keys.shape[0]
    if bias_ref is not None:
        reach = tile_reach(width // TILE)
        tiles = []
        for column in range(width // TILE):
            tiles.append(bias_ref[half, min(max(column - row, -reach), reach) + reach])
        scores = scores + (jnp.concatenate(tiles, axis=1) if len(tiles) > 1 else tiles[0])
    mask = row_segs == key_segs
    if causal:
        at_row = row * TILE + lax.broadcasted_iota(jnp.int32, scores.shape, 0)
        at_key = lax.broadcasted_iota(jnp.int32, scores.shape, 1)
        mask = mask & (at_row >= at_key)
    scores = jnp.where(mask, scores, neg_fill)
    raised = jnp.exp(scores - jnp.max(scores, axis=-1, keepdims=True))
    return raised * (1.0 / jnp.sum(raised, axis=-1, keepdims=True))


def attend_kernel(q_ref, k_ref, v_ref, *rest, biased, causal):
    bias_ref = rest[0] if biased else None
    sq_ref, sk_ref, o_ref = rest[-3:]
    keys = k_ref[0]
    values = v_ref[0]
    key_segs = sk_ref[0]
    for row in range(q_ref.shape[1] // TILE):
        part = pl.ds(row * TILE, TILE)
        query = q_ref[0, part, :]
        row_segs = sq_ref[0, part, :]
        result = None
        for half in range(2):
            lanes = head_lanes(half)
            probs = block_scores(
                jnp.where(lanes, query, 0), keys, bias_ref, half, row, row_segs, key_segs, causal
            )
            output = jnp.dot(
                probs.astype(jnp.bfloat16), values, preferred_element_type=jnp.float32
            )
            result = output if result is None else jnp.where(lanes, output, result)
        o_ref[0, part, :] = result.astype(jnp.bfloat16)


def attend_back_kernel(q_ref, k_ref, v_ref, g_ref, *rest, biased, causal):
    if biased:
        bias_ref, sq_ref, sk_ref, dq_ref, dk_ref, dv_ref, db_ref = rest
    else:
        sq_ref, sk_ref, dq_ref, dk_ref, dv_ref = rest
        bias_ref = db_ref = None
    keys = k_ref[0]
    values = v_ref[0]
    key_segs = sk_ref[0]
    width = keys.shape[0]
    if biased:

        @pl.when(pl.program_id(1) == 0)
        def _():
            db_ref[...] = jnp.zeros_like(db_ref)

    grad_keys = None
    grad_values = None
    for row in range(q_ref.shape[1] // TILE):
        part = pl.ds(row * TILE, TILE)
        query = q_ref[0, part, :]
        grad_out = g_ref[0, part, :]
        row_segs = sq_ref[0, part, :]
        grad_query = None
        for half in range(2):
            lanes = head_lanes(half)
            own_query = jnp.where(lanes, query, 0)
            own_grad = jnp.where(lanes, grad_out, 0)
            probs = block_scores(
                own_query, keys, bias_ref, half, row, row_segs, key_segs, causal
            )
            grad_probs = lax.dot_general(
                own_grad, values, (((1,), (1,)), ((), ())), preferred_element_type=jnp.float32
            )
            drop = jnp.sum(probs * grad_probs, axis=-1, keepdims=True)
            grad_scores = (probs * (grad_probs - drop)).astype(jnp.bfloat16)
            down = (((0,), (0,)), ((), ()))
            part_values = lax.dot_general(
                probs.astype(jnp.bfloat16), own_grad, down, preferred_element_type=jnp.float32
            )
            part_keys = lax.dot_general(
                grad_scores, own_query, down, preferred_element_type=jnp.float32
            )
            grad_values = part_values if grad_values is None else grad_values + part_values
            grad_keys = part_keys if grad_keys is None else grad_keys + part_keys
            own_grad_query = jnp.dot(grad_scores, keys, preferred_element_type=jnp.float32)
            grad_query = (
                own_grad_query if grad_query is None else jnp.where(lanes, own_grad_query, grad_query)
            )
            if biased:
                wide = grad_scores.astype(jnp.float32)
                reach = tile_reach(width // TILE)
                for column in range(width // TILE):
                    slot = min(max(column - row, -reach), reach) + reach
                    db_ref[half, slot] += wide[:, column * TILE : (column + 1) * TILE]
        dq_ref[0, part, :] = grad_query.astype(jnp.bfloat16)
    dk_ref[0] = grad_keys.astype(jnp.bfloat16)
    dv_ref[0] = grad_values.astype(jnp.bfloat16)


def attention_specs(query, keys, places, bias, row_segs, key_segs):
    q_at, k_at, v_at = places
    rows, nq = row_segs.shape
    nk = key_segs.shape[1]

    def panel(length, first):
        return pl.BlockSpec((1, length, LANES), lambda pair, row: (row, 0, first + pair))

    operands = [query, keys, keys]
    specs = [panel(nq, q_at), panel(nk, k_at), panel(nk, v_at)]
    tail = []
    tail_specs = []
    if bias is not None:
        tail.append(bias)
        tail_specs.append(
            pl.BlockSpec((2,) + bias.shape[1:], lambda pair, row: (pair, 0, 0, 0))
        )
    tail += [row_segs[:, :, None], key_segs[:, None, :]]
    tail_specs += [
        pl.BlockSpec((1, nq, 1), lambda pair, row: (row, 0, 0)),
        pl.BlockSpec((1, 1, nk), lambda pair, row: (row, 0, 0)),
    ]
    return operands, specs, tail, tail_specs, panel


def attention_cost(rows, nq, nk, products):
    return pl.CostEstimate(
        flops=2 * products * rows * H * nq * nk * LANES,
        bytes_accessed=2 * products * rows * (nq + nk) * D,
        transcendentals=rows * H * nq * nk,
    )


def attend(query, keys, places, bias, row_segs, key_segs, causal):
    rows, nq = row_segs.shape
    nk = key_segs.shape[1]
    operands, specs, tail, tail_specs, panel = attention_specs(
        query, keys, places, bias, row_segs, key_segs
    )
    return pl.pallas_call(
        functools.partial(attend_kernel, biased=bias is not None, causal=causal),
        out_shape=jax.ShapeDtypeStruct((rows, nq, D), jnp.bfloat16),
        grid=(H // 2, rows),
        in_specs=specs + tail_specs,
        out_specs=panel(nq, 0),
        cost_estimate=attention_cost(rows, nq, nk, 2),
        compiler_params=pltpu.CompilerParams(vmem_limit_bytes=32 << 20),
    )(*operands, *tail)


def attend_back(query, keys, places, bias, row_segs, key_segs, causal, grad_out):
    rows, nq = row_segs.shape
    nk = key_segs.shape[1]
    operands, specs, tail, tail_specs, panel = attention_specs(
        query, keys, places, bias, row_segs, key_segs
    )
    outs = [
        jax.ShapeDtypeStruct((rows, nq, D), jnp.bfloat16),
        jax.ShapeDtypeStruct((rows, nk, D), jnp.bfloat16),
        jax.ShapeDtypeStruct((rows, nk, D), jnp.bfloat16),
    ]
    out_specs = [panel(nq, 0), panel(nk, 0), panel(nk, 0)]
    if bias is not None:
        outs.append(jax.ShapeDtypeStruct(bias.shape, jnp.float32))
        out_specs.append(
            pl.BlockSpec((2,) + bias.shape[1:], lambda pair, row: (pair, 0, 0, 0))
        )
    return pl.pallas_call(
        functools.partial(attend_back_kernel, biased=bias is not None, causal=causal),
        out_shape=outs,
        grid=(H // 2, rows),
        in_specs=specs + [panel(nq, 0)] + tail_specs,
        out_specs=out_specs,
        cost_estimate=attention_cost(rows, nq, nk, 5),
        compiler_params=pltpu.CompilerParams(vmem_limit_bytes=32 << 20),
    )(*operands, grad_out, *tail)


def layer_shapes(decoder):
    if decoder:
        return [(D, 3 * D), (D, D), (D, D), (D, 2 * D), (D, D), (D, FF), (FF, D)]
    return [(D, 3 * D), (D, D), (D, FF), (FF, D)]


def as_blocks(flat):
    return flat.reshape(flat.shape[0], BLOCK, BLOCK)


def as_rows(blocks):
    return blocks.reshape(blocks.shape[0], BLOCK * BLOCK)


def as_pairs(blocks):
    amount = blocks.shape[0] // 2
    split = blocks.reshape(amount, 2, BLOCK, BLOCK)
    return jnp.concatenate([split[:, 0], split[:, 1]], axis=-1)


def unpack_kernel(pairs_ref, out_ref):
    across = out_ref.shape[1] // PAIR
    for row in range(out_ref.shape[0] // BLOCK):
        for column in range(across):
            out_ref[row * BLOCK : (row + 1) * BLOCK, column * PAIR : (column + 1) * PAIR] = (
                pairs_ref[row * across + column]
            )


def matrices_of(pairs, shapes):
    matrix_list = []
    place = 0
    for height, breadth in shapes:
        group = 2 * breadth // PAIR
        first = place // group
        matrix_list.append(
            pl.pallas_call(
                unpack_kernel,
                out_shape=jax.ShapeDtypeStruct((height, breadth), pairs.dtype),
                grid=(height // PAIR,),
                in_specs=[
                    pl.BlockSpec(
                        (group, BLOCK, PAIR), lambda step, first=first: (first + step, 0, 0)
                    )
                ],
                out_specs=pl.BlockSpec((PAIR, breadth), lambda step: (step, 0)),
                cost_estimate=pl.CostEstimate(
                    flops=0, bytes_accessed=4 * height * breadth, transcendentals=0
                ),
                compiler_params=pltpu.CompilerParams(vmem_limit_bytes=32 << 20),
            )(pairs)
        )
        place += group * (height // PAIR)
    return matrix_list


def weight_grad_kernel(x_ref, g_ref, *rest):
    out_ref = rest[-1]
    across = out_ref.shape[0] // 2
    for column in range(across):
        product = lax.dot_general(
            x_ref[...],
            g_ref[:, column * PAIR : (column + 1) * PAIR],
            (((0,), (0,)), ((), ())),
            preferred_element_type=jnp.float32,
        )
        product = product.astype(jnp.bfloat16)
        out_ref[column] = product[:BLOCK]
        out_ref[across + column] = product[BLOCK:]


def weight_grads(operands):
    total = sum(x.shape[-1] * g.shape[-1] for x, g in operands) // (BLOCK * PAIR)
    pairs = None
    place = 0
    for x, g in operands:
        x = x.reshape(-1, x.shape[-1])
        g = g.reshape(-1, g.shape[-1])
        count, height = x.shape
        breadth = g.shape[1]
        group = 2 * breadth // PAIR
        first = place // group
        given = [] if pairs is None else [pairs]
        pairs = pl.pallas_call(
            weight_grad_kernel,
            out_shape=jax.ShapeDtypeStruct((total, BLOCK, PAIR), jnp.bfloat16),
            grid=(height // PAIR,),
            in_specs=[
                pl.BlockSpec((count, PAIR), lambda step: (0, step)),
                pl.BlockSpec((count, breadth), lambda step: (0, 0)),
            ]
            + [pl.BlockSpec(memory_space=pl.ANY)] * len(given),
            out_specs=pl.BlockSpec(
                (group, BLOCK, PAIR), lambda step, first=first: (first + step, 0, 0)
            ),
            input_output_aliases={2: 0} if given else {},
            cost_estimate=pl.CostEstimate(
                flops=2 * count * height * breadth,
                bytes_accessed=2 * (count * (height + breadth) + height * breadth),
                transcendentals=0,
            ),
            compiler_params=pltpu.CompilerParams(vmem_limit_bytes=40 << 20),
        )(x, g, *given)
        place += group * (height // PAIR)
    return pairs


def split_float(values):
    high = values.astype(jnp.bfloat16)
    return high, (values - high.astype(jnp.float32)).astype(jnp.bfloat16)


def full_product(left, right, contract):
    def part(first, second):
        return lax.dot_general(
            first, second, (contract, ((), ())), preferred_element_type=jnp.float32
        )

    return (
        part(left[0], right[1]) + part(left[1], right[0]) + part(left[0], right[0])
    )


ROW_COL = ((1,), (0,))
ROW_ROW = ((1,), (1,))
COL_COL = ((0,), (0,))


def turned_product(left_root, middle, right_root):
    shaped = full_product(split_float(left_root), middle, ROW_COL)
    return full_product(split_float(shaped), split_float(right_root), ROW_COL)


def ahead_kernel(m_ref, lr_ref, rr_ref, o_ref):
    for place in range(m_ref.shape[0]):
        o_ref[place] = turned_product(lr_ref[place], split_float(m_ref[place]), rr_ref[place])


def products_kernel(g_ref, lr_ref, rr_ref, g_out, turned_out, left_out, right_out):
    for place in range(2):
        block = g_ref[0, :, place * BLOCK : (place + 1) * BLOCK]
        g_out[place] = block
        halves = split_float(block)
        turned_out[place] = turned_product(lr_ref[place], halves, rr_ref[place])
        left_out[place] = full_product(halves, halves, ROW_ROW)
        right_out[place] = full_product(halves, halves, COL_COL)


def block_cost(amount, products, arrays):
    return pl.CostEstimate(
        flops=6 * products * amount * BLOCK**3,
        bytes_accessed=4 * arrays * amount * BLOCK * BLOCK,
        transcendentals=0,
    )


def shampoo_ahead(moment, left_root, right_root):
    blocks = [as_blocks(moment), as_blocks(left_root), as_blocks(right_root)]
    amount = moment.shape[0]
    spec = pl.BlockSpec((2, BLOCK, BLOCK), lambda pair: (pair, 0, 0))
    ahead = pl.pallas_call(
        ahead_kernel,
        out_shape=jax.ShapeDtypeStruct((amount, BLOCK, BLOCK), jnp.float32),
        grid=(amount // 2,),
        in_specs=[spec] * 3,
        out_specs=spec,
        cost_estimate=block_cost(amount, 2, 4),
        compiler_params=pltpu.CompilerParams(vmem_limit_bytes=32 << 20),
    )(*blocks)
    return as_rows(ahead), blocks[1], blocks[2]


def shampoo_products(pairs, left_root, right_root):
    amount = left_root.shape[0]
    spec = pl.BlockSpec((2, BLOCK, BLOCK), lambda pair: (pair, 0, 0))
    results = pl.pallas_call(
        products_kernel,
        out_shape=[jax.ShapeDtypeStruct((amount, BLOCK, BLOCK), jnp.float32)] * 4,
        grid=(amount // 2,),
        in_specs=[pl.BlockSpec((1, BLOCK, PAIR), lambda pair: (pair, 0, 0)), spec, spec],
        out_specs=[spec] * 4,
        cost_estimate=block_cost(amount, 4, 7),
        compiler_params=pltpu.CompilerParams(vmem_limit_bytes=32 << 20),
    )(pairs, left_root, right_root)
    return [as_rows(result) for result in results]


def project(left, right):
    return jnp.matmul(left, right, preferred_element_type=jnp.float32)


def project_back(left, right):
    return jnp.einsum("btf,df->btd", left, right, preferred_element_type=jnp.float32)


def rms(values, gain):
    return values * lax.rsqrt(jnp.mean(values * values, axis=-1, keepdims=True) + norm_eps) * gain


def rms_back(values, gain, grad_out):
    inverse = lax.rsqrt(jnp.mean(values * values, axis=-1, keepdims=True) + norm_eps)
    normed = values * inverse
    grad_gain = jnp.sum(grad_out * normed, axis=(0, 1))
    grad_normed = grad_out * gain
    grad_values = inverse * (
        grad_normed - normed * jnp.mean(grad_normed * normed, axis=-1, keepdims=True)
    )
    return (grad_values, grad_gain)


def ff_forward(hidden, gain, w_in, w_down):
    normed = rms(hidden, gain).astype(jnp.bfloat16)
    inner = project(normed, w_in)
    active = jax.nn.gelu(inner).astype(jnp.bfloat16)
    return (hidden + project(active, w_down), (normed, inner, active))


def ff_back(hidden, gain, w_in, w_down, cache, grad_out):
    normed, inner, active = cache
    branch_grad = grad_out.astype(jnp.bfloat16)
    grad_active = project_back(branch_grad, w_down)
    unused, gelu_back = jax.vjp(jax.nn.gelu, inner)
    grad_inner = gelu_back(grad_active)[0].astype(jnp.bfloat16)
    grad_part, grad_gain = rms_back(hidden, gain, project_back(grad_inner, w_in))
    return (grad_out + grad_part, grad_gain, (normed, grad_inner), (active, branch_grad))


def table_rows(table, token_ids, vocab_first):
    local_ids = token_ids - vocab_first
    inside = (local_ids >= 0) & (local_ids < table.shape[0])
    picked = jnp.take(table, jnp.clip(local_ids, 0, table.shape[0] - 1), axis=0)
    return jnp.where(inside[..., None], picked, jnp.zeros((), table.dtype))


def table_grads(grads, token_ids, vocab_first, dense):
    vocab_local = dense.shape[0]
    local_ids = token_ids.reshape(-1) - vocab_first
    inside = (local_ids >= 0) & (local_ids < vocab_local)
    slots = jnp.where(inside, local_ids, vocab_local)
    return dense.at[slots].add(grads.astype(jnp.float32), mode="drop")


REPLICAS = ("dp", "seq")
EVERYWHERE = ("fsdp", "dp", "seq")


def replica_rank():
    return lax.axis_index("dp") * lax.axis_size("seq") + lax.axis_index("seq")


def replica_count():
    return lax.axis_size("dp") * lax.axis_size("seq")


def paired_mesh():
    return (
        lax.axis_size("dp") == 2 and lax.axis_size("seq") == 2 and lax.axis_size("fsdp") % 2 == 0
    )


def swap(values, axis):
    size = lax.axis_size(axis)
    return lax.ppermute(values, axis, [(place, place ^ 1) for place in range(size)])


def shift(values, step):
    size = lax.axis_size("fsdp")
    moves = [
        (place, place + 2 * step) for place in range(size) if 0 <= place + 2 * step < size
    ]
    return lax.ppermute(values, "fsdp", moves)


def choose(flag, if_set, if_clear):
    return jnp.where(flag == 1, if_set, if_clear)


def pick(values, place, axis):
    return lax.dynamic_index_in_dim(values, place, axis, False)


def narrow(values):
    return values.astype(jnp.bfloat16)


def wide(values):
    return values.astype(jnp.float32)


def agreed_scale(largest):
    for axis in ("seq", "dp"):
        largest = jnp.maximum(largest, swap(largest, axis))
    return 4096.0 / jnp.maximum(largest, 1e-30)


def placed(relative, first, second):
    def at(row, column):
        here = choose(second, relative[row][1 - column], relative[row][column])
        there = choose(second, relative[1 - row][1 - column], relative[1 - row][column])
        return choose(first, there, here)

    return [[at(0, 0), at(0, 1)], [at(1, 0), at(1, 1)]]


def own_weights(master):
    share = master.shape[0] // replica_count()
    if master.shape[0] % (2 * replica_count()) == 0:
        master = lax.dynamic_slice_in_dim(master, replica_rank() * share, share, 0)
    return as_pairs(as_blocks(master.astype(jnp.bfloat16)))


def along_chips(own):
    n_chips = lax.axis_size("fsdp") // 2
    rising = falling = own
    pieces = [own]
    for _ in range(n_chips - 1):
        rising, falling = (shift(rising, 1), shift(falling, -1))
        pieces = [rising] + pieces + [falling]
    first = n_chips - 1 - lax.axis_index("fsdp") // 2
    return lax.dynamic_slice_in_dim(jnp.stack(pieces), first, n_chips, 0)


def gather_weights(pairs, amount, shapes):
    if not paired_mesh():
        split = amount % (2 * replica_count()) == 0
        everything = lax.all_gather(pairs, EVERYWHERE if split else "fsdp", axis=0, tiled=True)
        return matrices_of(everything, shapes)
    line = along_chips(pairs)
    mid = BLOCK // 2
    upper, lower = (line[:, :, :mid], line[:, :, mid:])
    upper_side, lower_half = (swap(upper, "dp"), swap(lower, "seq"))
    upper_half, lower_side = (swap(upper, "seq"), swap(lower, "dp"))
    pieces = [
        upper,
        lower,
        upper_half,
        lower_half,
        upper_side,
        lower_side,
        swap(upper_side, "seq"),
        swap(lower_half, "dp"),
    ]
    pieces += [swap(piece, "fsdp") for piece in pieces]
    return assembled(pieces, shapes)


def assemble_kernel(place_ref, *refs, shapes):
    pieces, outs = (refs[:16], refs[16 : 16 + len(shapes)])
    buffer, in_sems, out_sems = refs[16 + len(shapes) :]
    core, side, half = (place_ref[0], place_ref[1], place_ref[2])
    n_chips, quarter, mid, _ = pieces[0].shape
    copies = []
    for index, piece in enumerate(pieces):
        owner = ((side ^ (index // 4 % 2)) * 2 + (half ^ (index // 2 % 2))) * quarter
        for chip in range(n_chips):
            first = (2 * chip + (core ^ (index // 8))) * (4 * quarter) + owner
            copies.append(
                pltpu.make_async_copy(
                    piece.at[chip],
                    buffer.at[pl.ds(first, quarter), pl.ds((index % 2) * mid, mid), :],
                    in_sems.at[index, chip],
                )
            )
    for copy in copies:
        copy.start()
    for copy in copies:
        copy.wait()
    copies = []
    for out_ref, (height, breadth) in zip(outs, shapes):
        for row in range(height // BLOCK):
            for column in range(breadth // PAIR):
                copies.append(
                    pltpu.make_async_copy(
                        buffer.at[len(copies)],
                        out_ref.at[pl.ds(row * BLOCK, BLOCK), pl.ds(column * PAIR, PAIR)],
                        out_sems.at[len(copies)],
                    )
                )
    for copy in copies:
        copy.start()
    for copy in copies:
        copy.wait()


def own_place():
    return jnp.stack(
        [lax.axis_index("fsdp") % 2, lax.axis_index("dp"), lax.axis_index("seq")]
    ).astype(jnp.int32)


def assembled(pieces, shapes):
    n_chips, quarter, mid, _ = pieces[0].shape
    total = 8 * n_chips * quarter
    return pl.pallas_call(
        functools.partial(assemble_kernel, shapes=shapes),
        out_shape=[jax.ShapeDtypeStruct(shape, jnp.bfloat16) for shape in shapes],
        in_specs=[pl.BlockSpec(memory_space=pltpu.SMEM)]
        + [pl.BlockSpec(memory_space=pl.ANY)] * len(pieces),
        out_specs=[pl.BlockSpec(memory_space=pl.ANY)] * len(shapes),
        scratch_shapes=[
            pltpu.VMEM((total, BLOCK, PAIR), jnp.bfloat16),
            pltpu.SemaphoreType.DMA((len(pieces), n_chips)),
            pltpu.SemaphoreType.DMA((total,)),
        ],
        cost_estimate=pl.CostEstimate(
            flops=0, bytes_accessed=4 * total * BLOCK * PAIR, transcendentals=0
        ),
        compiler_params=pltpu.CompilerParams(vmem_limit_bytes=30 << 20),
    )(own_place(), *pieces)


def fold_kernel(place_ref, own_ref, got_ref, keep_up, send_up, keep_low, send_low):
    total = wide(own_ref[0]) + wide(got_ref[0])
    mid = BLOCK // 2
    upper, lower = (total[:, :mid], total[:, mid:])
    other_side, other_half = (pl.program_id(1), pl.program_id(2))

    @pl.when(other_half == 0)
    def _():
        keep_up[0, 0] = upper

    @pl.when(other_half == 1)
    def _():
        send_up[0, 0] = narrow(upper)

    @pl.when(other_side == 0)
    def _():
        keep_low[0, 0] = lower

    @pl.when(other_side == 1)
    def _():
        send_low[0, 0] = narrow(lower)


def fold_cores(pairs, got, n_chips, quarter):
    mid = BLOCK // 2

    def quarter_of(place, other_side, other_half):
        return (place[1] ^ other_side) * 2 + (place[2] ^ other_half)

    whole = (1, quarter, BLOCK, PAIR)
    part = (1, 1, quarter, mid, PAIR)
    halves = (n_chips, 2, quarter, mid, PAIR)

    def up_at(chip, other_side, other_half, place):
        return (chip, place[1] ^ other_side, 0, 0, 0)

    def keep_low_at(chip, other_side, other_half, place):
        return (chip, jnp.where(other_side == 0, place[2] ^ other_half, place[2] ^ 1), 0, 0, 0)

    def send_low_at(chip, other_side, other_half, place):
        return (chip, jnp.where(other_side == 1, place[2] ^ other_half, place[2]), 0, 0, 0)

    return pl.pallas_call(
        fold_kernel,
        out_shape=[
            jax.ShapeDtypeStruct(halves, kind)
            for kind in (jnp.float32, jnp.bfloat16, jnp.float32, jnp.bfloat16)
        ],
        grid_spec=pltpu.PrefetchScalarGridSpec(
            num_scalar_prefetch=1,
            grid=(n_chips, 2, 2),
            in_specs=[
                pl.BlockSpec(
                    whole,
                    lambda chip, side, half, place: (
                        (2 * chip + place[0]) * 4 + quarter_of(place, side, half),
                        0,
                        0,
                        0,
                    ),
                ),
                pl.BlockSpec(
                    whole,
                    lambda chip, side, half, place: (
                        chip * 4 + quarter_of(place, side, half),
                        0,
                        0,
                        0,
                    ),
                ),
            ],
            out_specs=[
                pl.BlockSpec(part, up_at),
                pl.BlockSpec(part, up_at),
                pl.BlockSpec(part, keep_low_at),
                pl.BlockSpec(part, send_low_at),
            ],
        ),
        cost_estimate=pl.CostEstimate(
            flops=pairs.size // 2, bytes_accessed=5 * pairs.size, transcendentals=0
        ),
        compiler_params=pltpu.CompilerParams(vmem_limit_bytes=32 << 20),
    )(
        own_place(),
        pairs.reshape(-1, quarter, BLOCK, PAIR),
        got.reshape(-1, quarter, BLOCK, PAIR),
    )


def sum_small(values):
    size = lax.axis_size("fsdp")
    if not paired_mesh() or size & (size - 1):
        return lax.psum(values, EVERYWHERE)
    values = values + swap(values, "seq")
    values = values + swap(values, "dp")
    step = 1
    while step < size:
        moves = [(place, place ^ step) for place in range(size)]
        values = values + lax.ppermute(values, "fsdp", moves)
        step *= 2
    return values


def reduce_blocks(pairs):
    if not paired_mesh():
        return lax.psum(
            lax.psum_scatter(wide(pairs), "fsdp", scatter_dimension=0, tiled=True), REPLICAS
        )
    n_chips = lax.axis_size("fsdp") // 2
    core = lax.axis_index("fsdp") % 2
    chip = lax.axis_index("fsdp") // 2
    side, half = (lax.axis_index("dp"), lax.axis_index("seq"))
    amount = pairs.shape[0] // (2 * n_chips)
    quarter = amount // 4
    split = pairs.reshape(n_chips, 2, amount, BLOCK, PAIR)
    got = swap(pick(split, 1 - core, 1), "fsdp")
    upper, upper_sent, lower, lower_sent = fold_cores(pairs, got, n_chips, quarter)
    upper = upper + wide(swap(upper_sent, "seq"))
    lower = lower + wide(swap(lower_sent, "dp"))
    upper = pick(upper, side, 1) + wide(swap(narrow(pick(upper, 1 - side, 1)), "dp"))
    lower = pick(lower, half, 1) + wide(swap(narrow(pick(lower, 1 - half, 1)), "seq"))
    line_sum = jnp.concatenate([upper, lower], axis=2)
    ahead = lax.dynamic_slice_in_dim(
        jnp.concatenate([line_sum, line_sum[:-1]], axis=0), chip, n_chips, 0
    )
    up = down = None
    for step in range(n_chips - 1, 0, -1):
        rising, falling = (ahead[step], ahead[n_chips - step])
        if up is not None:
            rising, falling = (rising + wide(up), falling + wide(down))
        up, down = (shift(narrow(rising), 1), shift(narrow(falling), -1))
    return ahead[0] + wide(up) + wide(down)


def share_blocks(own):
    side, half = (lax.axis_index("dp"), lax.axis_index("seq"))
    mid = BLOCK // 2
    scale = agreed_scale(jnp.max(jnp.abs(own)))
    own = lax.optimization_barrier((own * scale).astype(jnp.float16))
    upper, lower = (own[:, :mid], own[:, mid:])
    upper_side, lower_half = (swap(upper, "dp"), swap(lower, "seq"))
    upper_rest = swap(jnp.stack([upper, upper_side]), "seq")
    lower_rest = swap(jnp.stack([lower, lower_half]), "dp")
    relative = [
        [
            jnp.concatenate([upper, lower], axis=1),
            jnp.concatenate([upper_rest[0], lower_half], axis=1),
        ],
        [
            jnp.concatenate([upper_side, lower_rest[0]], axis=1),
            jnp.concatenate([upper_rest[1], lower_rest[1]], axis=1),
        ],
    ]
    whole = placed(relative, side, half)
    return wide(jnp.concatenate(whole[0] + whole[1], axis=0)) * (1.0 / scale)


def window_rows(half_rows):
    return -(-half_rows // 16) * 8


def reduce_table(partial, bound):
    side, half = (lax.axis_index("dp"), lax.axis_index("seq"))
    scale = agreed_scale(bound)
    half_rows = partial.shape[0] // 2
    window = window_rows(half_rows)

    def rows_of(first, place):
        start = first + place * (half_rows - window)
        return lax.dynamic_slice_in_dim(partial, start, window, 0) * scale

    def half_lanes(values, place):
        return lax.dynamic_slice_in_dim(values, place * (D // 2), D // 2, 1)

    def send(values, axis):
        return wide(swap(values.astype(jnp.float16), axis))

    top = rows_of(0, half) + send(rows_of(0, 1 - half), "seq")
    low = rows_of(half_rows, side) + send(rows_of(half_rows, 1 - side), "dp")
    top = half_lanes(top, side) + send(half_lanes(top, 1 - side), "dp")
    low = half_lanes(low, half) + send(half_lanes(low, 1 - half), "seq")
    return top, low, scale


def table_squares(top, low, half_rows):
    side, half = (lax.axis_index("dp"), lax.axis_index("seq"))
    again = 2 * window_rows(half_rows) - half_rows
    row = lax.broadcasted_iota(jnp.int32, (top.shape[0], 1), 0)
    return jnp.sum(jnp.where(row >= again * half, top * top, 0.0)) + jnp.sum(
        jnp.where(row >= again * side, low * low, 0.0)
    )


def share_table(top, low, scale, half_rows):
    side, half = (lax.axis_index("dp"), lax.axis_index("seq"))
    again = 2 * window_rows(half_rows) - half_rows
    top = lax.optimization_barrier(top.astype(jnp.float16))
    low = lax.optimization_barrier(low.astype(jnp.float16))
    top_side, low_half = (swap(top, "dp"), swap(low, "seq"))
    top_rest = (swap(top, "seq"), swap(top_side, "seq"))
    low_rest = (swap(low, "dp"), swap(low_half, "dp"))
    top_all = placed([[top, top_side], top_rest], half, side)
    low_all = placed([[low, low_half], low_rest], side, half)
    rows = []
    for first, second in (top_all, low_all):
        rows.append(jnp.concatenate(first, axis=1))
        rows.append(jnp.concatenate(second, axis=1)[again:])
    return wide(jnp.concatenate(rows, axis=0)) * (1.0 / scale)


def adam_update(weight, gradient, moment, second):
    moment = beta_first * moment + (1 - beta_first) * gradient
    second = beta_second * second + (1 - beta_second) * gradient * gradient
    corrected = moment / (1 - beta_first**STEP)
    scaled = second / (1 - beta_second**STEP)
    weight = weight - adam_rate * (
        corrected / (jnp.sqrt(scaled) + adam_eps) + weight_decay * weight
    )
    return (weight, moment, second)


def shampoo_update(weight, moment, left, right, ahead, products, factor):
    gradient, turned, left_square, right_square = products
    direction = beta_first * ahead + ((1 - beta_first) * factor) * turned
    square = (1 - stat_decay) * factor * factor
    return (
        weight - shampoo_rate * (direction + weight_decay * weight),
        beta_first * moment + ((1 - beta_first) * factor) * gradient,
        stat_decay * left + square * left_square,
        stat_decay * right + square * right_square,
    )


def on_device(
    enc_ids,
    span_mask,
    segments,
    targets,
    loss_weights,
    target_segments,
    embedding,
    emb_m,
    emb_v,
    gains,
    gain_m,
    gain_v,
    rel_bias,
    rel_m,
    rel_v,
    enc_w,
    enc_m,
    enc_left,
    enc_right,
    enc_lroot,
    enc_rroot,
    dec_w,
    dec_m,
    dec_left,
    dec_right,
    dec_lroot,
    dec_rroot,
):
    fsdp_rank = lax.axis_index("fsdp")
    seq_rank = lax.axis_index("seq")
    n_fsdp = lax.axis_size("fsdp")
    n_seq = lax.axis_size("seq")
    half_len = enc_ids.shape[1]
    rows, dec_len = targets.shape
    enc_len = half_len * n_seq
    enc_in = jnp.where(span_mask == 1, VOCAB - sentinel_offset, enc_ids)
    dec_in = jnp.concatenate([jnp.zeros((rows, 1), jnp.int32), targets[:, :-1]], axis=1)

    halves = jnp.stack([enc_in, segments]).reshape(2, n_seq, rows, half_len)
    if n_seq == 2:
        kept = pick(halves, seq_rank, 1)
        got = swap(pick(halves, 1 - seq_rank, 1), "seq")
        parts = (choose(seq_rank, got, kept), choose(seq_rank, kept, got))
        row_words = jnp.stack(parts, axis=2)
    else:
        row_words = lax.all_to_all(halves, "seq", 1, 1, tiled=True).transpose(0, 2, 1, 3)
    row_words = row_words.reshape(2, rows, enc_len)
    row_segments = row_words[1]
    message = jnp.concatenate(
        [
            row_words[0].reshape(-1),
            dec_in.reshape(-1),
            targets.reshape(-1),
            loss_weights.reshape(-1),
        ]
    ).reshape(1, -1)
    enc_pairs, dec_pairs, message = lax.optimization_barrier(
        (own_weights(enc_w), own_weights(dec_w), message)
    )
    enc_mats = gather_weights(enc_pairs, enc_w.shape[0], layer_shapes(False))
    dec_mats = gather_weights(dec_pairs, dec_w.shape[0], layer_shapes(True))
    gathered = lax.all_gather(message, "fsdp", axis=0, tiled=True)
    all_enc = gathered[:, : rows * enc_len]
    rest = gathered[:, rows * enc_len :].reshape(n_fsdp, 3, rows * dec_len)
    all_dec, all_targets, all_weights = (rest[:, 0], rest[:, 1], rest[:, 2])
    all_tokens = jnp.concatenate([all_enc, all_dec], axis=1)

    table = embedding.astype(jnp.bfloat16)
    vocab_local = table.shape[0]
    vocab_first = fsdp_rank * vocab_local
    looked_up = lax.psum_scatter(
        table_rows(table, all_tokens, vocab_first), "fsdp", scatter_dimension=0, tiled=True
    ).reshape(-1, D)
    enc_ready = shampoo_ahead(enc_m, enc_lroot, enc_rroot)
    dec_ready = shampoo_ahead(dec_m, dec_lroot, dec_rroot)
    looked_up, enc_ready, dec_ready = lax.optimization_barrier((looked_up, enc_ready, dec_ready))
    enc_ahead, enc_lr, enc_rr = enc_ready
    dec_ahead, dec_lr, dec_rr = dec_ready
    hidden0 = looked_up[: rows * enc_len].reshape(rows, enc_len, D).astype(jnp.float32)
    state0 = looked_up[rows * enc_len :].reshape(rows, dec_len, D).astype(jnp.float32)

    enc_onehot = tile_onehot(enc_len // TILE, False)
    dec_onehot = tile_onehot(dec_len // TILE, True)
    enc_bias = tile_bias(enc_onehot, rel_bias[0])
    dec_bias = tile_bias(dec_onehot, rel_bias[1])
    tile_at = D // LANES
    self_places = (0, tile_at, 2 * tile_at)
    cross_places = (0, 0, tile_at)

    normed0 = rms(hidden0, gains[0]).astype(jnp.bfloat16)
    enc_qkv = project(normed0, enc_mats[0]).astype(jnp.bfloat16)
    enc_attended = attend(
        enc_qkv, enc_qkv, self_places, enc_bias, row_segments, row_segments, False
    )
    hidden1 = hidden0 + project(enc_attended, enc_mats[1])
    hidden2, enc_cache = ff_forward(hidden1, gains[1], enc_mats[2], enc_mats[3])
    encoded = rms(hidden2, gains[2]).astype(jnp.bfloat16)
    pairs = project(encoded, dec_mats[3]).astype(jnp.bfloat16)

    normed3 = rms(state0, gains[3]).astype(jnp.bfloat16)
    self_qkv = project(normed3, dec_mats[0]).astype(jnp.bfloat16)
    self_attended = attend(
        self_qkv, self_qkv, self_places, dec_bias, target_segments, target_segments, True
    )
    state1 = state0 + project(self_attended, dec_mats[1])
    normed4 = rms(state1, gains[4]).astype(jnp.bfloat16)
    cross_query = project(normed4, dec_mats[2]).astype(jnp.bfloat16)
    cross_attended = attend(
        cross_query, pairs, cross_places, None, target_segments, row_segments, False
    )
    state2 = state1 + project(cross_attended, dec_mats[4])
    state3, dec_cache = ff_forward(state2, gains[5], dec_mats[5], dec_mats[6])
    out_scale = D ** (-0.5)
    final = (rms(state3, gains[6]) * out_scale).astype(jnp.bfloat16)

    all_final = lax.all_gather(final.reshape(rows * dec_len, D), "fsdp", axis=0, tiled=True)
    logits = jnp.einsum("nd,vd->nv", all_final, table, preferred_element_type=jnp.float32)
    local_ids = all_targets.reshape(-1) - vocab_first
    target_hot = local_ids[:, None] == jnp.arange(vocab_local, dtype=jnp.int32)[None, :]
    local_top = jnp.max(logits, axis=1)
    local_sum = jnp.sum(jnp.exp(logits - local_top[:, None]), axis=1)
    local_pick = jnp.sum(jnp.where(target_hot, logits, 0.0), axis=1)
    stats = lax.all_gather(
        jnp.stack([local_top, local_sum, local_pick])[None], "fsdp", axis=0, tiled=True
    )
    top_all = jnp.max(stats[:, 0], axis=0)
    sum_all = jnp.sum(stats[:, 1] * jnp.exp(stats[:, 0] - top_all), axis=0)
    pick_all = jnp.sum(stats[:, 2], axis=0)
    lse = top_all + jnp.log(sum_all)
    token_weights = all_weights.reshape(-1).astype(jnp.float32)
    group_loss = jnp.sum(token_weights * (lse - pick_all))
    group_count = jnp.sum(token_weights)
    grad_logits = (
        token_weights[:, None] * (jnp.exp(logits - lse[:, None]) - target_hot.astype(jnp.float32))
    ).astype(jnp.bfloat16)
    emb_grad = jnp.einsum("nv,nd->vd", grad_logits, all_final, preferred_element_type=jnp.float32)
    grad_final = lax.psum_scatter(
        jnp.dot(grad_logits, table, preferred_element_type=jnp.float32),
        "fsdp",
        scatter_dimension=0,
        tiled=True,
    ).reshape(rows, dec_len, D)

    grad_state3, gain_six = rms_back(state3, gains[6], grad_final * out_scale)
    grad_state2, gain_five, dec_in_grad, dec_down_grad = ff_back(
        state2, gains[5], dec_mats[5], dec_mats[6], dec_cache, grad_state3
    )
    branch_grad = grad_state2.astype(jnp.bfloat16)
    cross_out_grad = (cross_attended, branch_grad)
    grad_cross = project_back(branch_grad, dec_mats[4]).astype(jnp.bfloat16)
    grad_cq, grad_ck, grad_cv = attend_back(
        cross_query, pairs, cross_places, None, target_segments, row_segments, False, grad_cross
    )
    grad_pairs = jnp.concatenate([grad_ck, grad_cv], axis=-1)
    cross_query_grad = (normed4, grad_cq)
    grad_state1_part, gain_four = rms_back(state1, gains[4], project_back(grad_cq, dec_mats[2]))
    grad_state1 = grad_state2 + grad_state1_part
    cross_pair_grad = (encoded, grad_pairs)
    grad_encoded = project_back(grad_pairs, dec_mats[3])
    branch_grad = grad_state1.astype(jnp.bfloat16)
    self_out_grad = (self_attended, branch_grad)
    grad_self = project_back(branch_grad, dec_mats[1]).astype(jnp.bfloat16)
    grad_sq, grad_sk, grad_sv, dec_bias_grad = attend_back(
        self_qkv, self_qkv, self_places, dec_bias, target_segments, target_segments, True, grad_self
    )
    grad_sqkv = jnp.concatenate([grad_sq, grad_sk, grad_sv], axis=-1)
    self_qkv_grad = (normed3, grad_sqkv)
    grad_state0_part, gain_three = rms_back(state0, gains[3], project_back(grad_sqkv, dec_mats[0]))
    grad_state0 = grad_state1 + grad_state0_part
    decoder_portion = weight_grads(
        [
            self_qkv_grad,
            self_out_grad,
            cross_query_grad,
            cross_pair_grad,
            cross_out_grad,
            dec_in_grad,
            dec_down_grad,
        ]
    )
    dec_part = reduce_blocks(decoder_portion)

    grad_hidden2, gain_two = rms_back(hidden2, gains[2], grad_encoded)
    grad_hidden1, gain_one, encoder_input_gradient, encoder_down_gradient = ff_back(
        hidden1, gains[1], enc_mats[2], enc_mats[3], enc_cache, grad_hidden2
    )
    branch_grad = grad_hidden1.astype(jnp.bfloat16)
    encoder_output_gradient = (enc_attended, branch_grad)
    grad_attn = project_back(branch_grad, enc_mats[1]).astype(jnp.bfloat16)
    grad_eq, grad_ek, grad_ev, enc_bias_grad = attend_back(
        enc_qkv, enc_qkv, self_places, enc_bias, row_segments, row_segments, False, grad_attn
    )
    grad_eqkv = jnp.concatenate([grad_eq, grad_ek, grad_ev], axis=-1)
    encoder_qkv_gradient = (normed0, grad_eqkv)
    grad_hidden0_part, gain_zero = rms_back(hidden0, gains[0], project_back(grad_eqkv, enc_mats[0]))
    grad_hidden0 = grad_hidden1 + grad_hidden0_part
    encoder_portion = weight_grads(
        [
            encoder_qkv_gradient,
            encoder_output_gradient,
            encoder_input_gradient,
            encoder_down_gradient,
        ]
    )
    enc_part = reduce_blocks(encoder_portion)

    back_rows = jnp.concatenate(
        [grad_hidden0.reshape(-1, D), grad_state0.reshape(-1, D)], axis=0
    ).astype(jnp.bfloat16)
    back_all = lax.all_gather(back_rows, "fsdp", axis=0, tiled=True)
    dense_bound = jnp.max(jnp.abs(emb_grad))
    bound = dense_bound + back_all.shape[0] * jnp.max(jnp.abs(back_all)).astype(jnp.float32)
    emb_grad = table_grads(back_all, all_tokens, vocab_first, emb_grad)
    gain_part = jnp.stack(
        [gain_zero, gain_one, gain_two, gain_three, gain_four, gain_five, gain_six]
    )
    rel_part = jnp.stack(
        [tile_bias_grad(enc_onehot, enc_bias_grad), tile_bias_grad(dec_onehot, dec_bias_grad)]
    )
    loss_part = jnp.where(fsdp_rank == 0, jnp.stack([group_loss, group_count]), 0.0)
    small = jnp.concatenate(
        [gain_part.reshape(-1), rel_part.reshape(-1), loss_part, jnp.zeros(126, jnp.float32)]
    )
    small = sum_small(small.reshape(-1, LANES)).reshape(-1)
    gain_total = small[: 7 * D].reshape(7, D)
    rel_total = small[7 * D : 7 * D + 2 * NBK * H].reshape(2, NBK, H)
    loss_total = small[7 * D + 2 * NBK * H :]
    loss_sum = loss_total[0]
    loss_count = jnp.maximum(loss_total[1], 1.0)
    share = 1.0 / loss_count
    gain_grad = gain_total * share
    rel_grad = rel_total * share

    if paired_mesh():
        dec_grad = share_blocks(dec_part) * share
        enc_grad = share_blocks(enc_part) * share
        half_rows = vocab_local // 2
        top, low, scale = reduce_table(emb_grad, bound)
        squares = (
            jnp.sum(jnp.square(enc_part * share))
            + jnp.sum(jnp.square(dec_part * share))
            + table_squares(top * (share / scale), low * (share / scale), half_rows)
        )
        squares_all = sum_small(squares)
        table_grad = share_table(top, low, scale, half_rows) * share
    else:
        dec_grad, enc_grad = (dec_part * share, enc_part * share)
        table_grad = lax.psum(emb_grad, REPLICAS) * share
        squares_all = lax.psum(
            jnp.sum(jnp.square(enc_grad))
            + jnp.sum(jnp.square(dec_grad))
            + jnp.sum(jnp.square(table_grad)),
            "fsdp",
        )

    dec_products = shampoo_products(dec_grad, dec_lr, dec_rr)
    enc_products = shampoo_products(enc_grad, enc_lr, enc_rr)
    dec_products, enc_products = lax.optimization_barrier((dec_products, enc_products))
    grad_norm = jnp.sqrt(
        squares_all + jnp.sum(gain_grad * gain_grad) + jnp.sum(rel_grad * rel_grad)
    )
    factor = jnp.minimum(1.0, clip_limit / grad_norm)
    new_emb = adam_update(embedding, table_grad * factor, emb_m, emb_v)
    new_gain = adam_update(gains, gain_grad * factor, gain_m, gain_v)
    new_rel = adam_update(rel_bias, rel_grad * factor, rel_m, rel_v)
    new_enc = shampoo_update(enc_w, enc_m, enc_left, enc_right, enc_ahead, enc_products, factor)
    new_dec = shampoo_update(dec_w, dec_m, dec_left, dec_right, dec_ahead, dec_products, factor)
    return (
        loss_sum,
        loss_count,
        grad_norm,
        *new_emb,
        *new_gain,
        *new_rel,
        *new_enc,
        *new_dec,
    )


def solution(mesh):
    in_specs = (
        P(("dp", "fsdp"), "seq"),
        P(("dp", "fsdp"), "seq"),
        P(("dp", "fsdp"), "seq"),
        P(("dp", "fsdp", "seq"), None),
        P(("dp", "fsdp", "seq"), None),
        P(("dp", "fsdp", "seq"), None),
        P("fsdp", None),
        P("fsdp", None),
        P("fsdp", None),
        P(),
        P(),
        P(),
        P(),
        P(),
        P(),
        P("fsdp", None),
        P("fsdp", None),
        P("fsdp", None),
        P("fsdp", None),
        P("fsdp", None),
        P("fsdp", None),
        P("fsdp", None),
        P("fsdp", None),
        P("fsdp", None),
        P("fsdp", None),
        P("fsdp", None),
        P("fsdp", None),
    )
    out_specs = (
        P(),
        P(),
        P(),
        P("fsdp", None),
        P("fsdp", None),
        P("fsdp", None),
        P(),
        P(),
        P(),
        P(),
        P(),
        P(),
        P("fsdp", None),
        P("fsdp", None),
        P("fsdp", None),
        P("fsdp", None),
        P("fsdp", None),
        P("fsdp", None),
        P("fsdp", None),
        P("fsdp", None),
    )
    return jax.shard_map(
        on_device, mesh=mesh, in_specs=in_specs, out_specs=out_specs, check_vma=False
    )
```

```python
import functools
import math

import jax
import jax.numpy as jnp
from jax import lax
from jax.experimental import pallas as pl
from jax.experimental.pallas import tpu as pltpu
from jax.sharding import PartitionSpec as P

D = 768
H = 12
DH = 64
FF = 3072
VOCAB = 32128
NBK = 32
REACH = 128
BLOCK = 192
STEP = 10
PAIR = 2 * BLOCK
TILE = 128
LANES = 128


norm_eps = 1e-06
neg_fill = -1000000000.0
sentinel_offset = 29
beta_first = 0.9
beta_second = 0.999
adam_eps = 1e-08
adam_rate = 0.5
shampoo_rate = 0.01
stat_decay = 0.999
weight_decay = 0.01
clip_limit = 0.05
highest = lax.Precision.HIGHEST


def bucket_edges(buckets, exact, reach):
    edges = list(range(1, exact))
    spread = buckets - exact
    for place in range(spread):
        edges.append(int(math.ceil(exact * (reach / exact) ** (place / spread) - 1e-09)))
    return edges


def offset_buckets(offset, causal):
    if causal:
        distance = jnp.maximum(-offset, 0)
        result = jnp.zeros(offset.shape, jnp.int32)
        edges = bucket_edges(NBK, NBK // 2, REACH)
    else:
        distance = jnp.abs(offset)
        result = jnp.where(offset > 0, NBK // 2, 0).astype(jnp.int32)
        edges = bucket_edges(NBK // 2, NBK // 4, REACH)
    for edge in edges:
        result = result + (distance >= edge).astype(jnp.int32)
    return result


def tile_reach(blocks):
    return min(blocks - 1, 2)


def tile_onehot(blocks, causal):
    reach = tile_reach(blocks)
    place = jnp.arange(TILE, dtype=jnp.int32)
    shift = jnp.arange(-reach, reach + 1, dtype=jnp.int32) * TILE
    offset = shift[:, None, None] + place[None, None, :] - place[None, :, None]
    buckets = offset_buckets(offset, causal).reshape(-1)
    return (jnp.arange(NBK, dtype=jnp.int32)[:, None] == buckets[None, :]).astype(jnp.float32)


def tile_bias(onehot, rel):
    flat = jnp.einsum("nh,np->hp", rel, onehot, precision=highest)
    return flat.reshape(H, -1, TILE, TILE)


def tile_bias_grad(onehot, grads):
    return jnp.einsum("np,hp->nh", onehot, grads.reshape(H, -1), precision=highest)


def head_lanes(half):
    lane = lax.broadcasted_iota(jnp.int32, (1, LANES), 1)
    return (lane // DH) == half


def block_scores(query, keys, bias_ref, half, row, row_segs, key_segs, causal):
    scores = lax.dot_general(query, keys, (((1,), (1,)), ((), ())), preferred_element_type=jnp.float32)
    width = keys.shape[0]
    if bias_ref is not None:
        reach = tile_reach(width // TILE)
        tiles = []
        for column in range(width // TILE):
            tiles.append(bias_ref[half, min(max(column - row, -reach), reach) + reach])
        scores = scores + (jnp.concatenate(tiles, axis=1) if len(tiles) > 1 else tiles[0])
    mask = row_segs == key_segs
    if causal:
        at_row = row * TILE + lax.broadcasted_iota(jnp.int32, scores.shape, 0)
        at_key = lax.broadcasted_iota(jnp.int32, scores.shape, 1)
        mask = mask & (at_row >= at_key)
    scores = jnp.where(mask, scores, neg_fill)
    raised = jnp.exp(scores - jnp.max(scores, axis=-1, keepdims=True))
    return raised * (1.0 / jnp.sum(raised, axis=-1, keepdims=True))


def attend_kernel(q_ref, k_ref, v_ref, *rest, biased, causal):
    bias_ref = rest[0] if biased else None
    sq_ref, sk_ref, o_ref = rest[-3:]
    keys = k_ref[0]
    values = v_ref[0]
    key_segs = sk_ref[0]
    for row in range(q_ref.shape[1] // TILE):
        part = pl.ds(row * TILE, TILE)
        query = q_ref[0, part, :]
        row_segs = sq_ref[0, part, :]
        result = None
        for half in range(2):
            lanes = head_lanes(half)
            probs = block_scores(
                jnp.where(lanes, query, 0), keys, bias_ref, half, row, row_segs, key_segs, causal
            )
            output = jnp.dot(
                probs.astype(jnp.bfloat16), values, preferred_element_type=jnp.float32
            )
            result = output if result is None else jnp.where(lanes, output, result)
        o_ref[0, part, :] = result.astype(jnp.bfloat16)


def attend_back_kernel(q_ref, k_ref, v_ref, g_ref, *rest, biased, causal):
    if biased:
        bias_ref, sq_ref, sk_ref, dq_ref, dk_ref, dv_ref, db_ref = rest
    else:
        sq_ref, sk_ref, dq_ref, dk_ref, dv_ref = rest
        bias_ref = db_ref = None
    keys = k_ref[0]
    values = v_ref[0]
    key_segs = sk_ref[0]
    width = keys.shape[0]
    if biased:

        @pl.when(pl.program_id(1) == 0)
        def _():
            db_ref[...] = jnp.zeros_like(db_ref)

    grad_keys = None
    grad_values = None
    for row in range(q_ref.shape[1] // TILE):
        part = pl.ds(row * TILE, TILE)
        query = q_ref[0, part, :]
        grad_out = g_ref[0, part, :]
        row_segs = sq_ref[0, part, :]
        grad_query = None
        for half in range(2):
            lanes = head_lanes(half)
            own_query = jnp.where(lanes, query, 0)
            own_grad = jnp.where(lanes, grad_out, 0)
            probs = block_scores(
                own_query, keys, bias_ref, half, row, row_segs, key_segs, causal
            )
            grad_probs = lax.dot_general(
                own_grad, values, (((1,), (1,)), ((), ())), preferred_element_type=jnp.float32
            )
            drop = jnp.sum(probs * grad_probs, axis=-1, keepdims=True)
            grad_scores = (probs * (grad_probs - drop)).astype(jnp.bfloat16)
            down = (((0,), (0,)), ((), ()))
            part_values = lax.dot_general(
                probs.astype(jnp.bfloat16), own_grad, down, preferred_element_type=jnp.float32
            )
            part_keys = lax.dot_general(
                grad_scores, own_query, down, preferred_element_type=jnp.float32
            )
            grad_values = part_values if grad_values is None else grad_values + part_values
            grad_keys = part_keys if grad_keys is None else grad_keys + part_keys
            own_grad_query = jnp.dot(grad_scores, keys, preferred_element_type=jnp.float32)
            grad_query = (
                own_grad_query if grad_query is None else jnp.where(lanes, own_grad_query, grad_query)
            )
            if biased:
                wide = grad_scores.astype(jnp.float32)
                reach = tile_reach(width // TILE)
                for column in range(width // TILE):
                    slot = min(max(column - row, -reach), reach) + reach
                    db_ref[half, slot] += wide[:, column * TILE : (column + 1) * TILE]
        dq_ref[0, part, :] = grad_query.astype(jnp.bfloat16)
    dk_ref[0] = grad_keys.astype(jnp.bfloat16)
    dv_ref[0] = grad_values.astype(jnp.bfloat16)


def attention_specs(query, keys, places, bias, row_segs, key_segs):
    q_at, k_at, v_at = places
    rows, nq = row_segs.shape
    nk = key_segs.shape[1]

    def panel(length, first):
        return pl.BlockSpec((1, length, LANES), lambda pair, row: (row, 0, first + pair))

    operands = [query, keys, keys]
    specs = [panel(nq, q_at), panel(nk, k_at), panel(nk, v_at)]
    tail = []
    tail_specs = []
    if bias is not None:
        tail.append(bias)
        tail_specs.append(
            pl.BlockSpec((2,) + bias.shape[1:], lambda pair, row: (pair, 0, 0, 0))
        )
    tail += [row_segs[:, :, None], key_segs[:, None, :]]
    tail_specs += [
        pl.BlockSpec((1, nq, 1), lambda pair, row: (row, 0, 0)),
        pl.BlockSpec((1, 1, nk), lambda pair, row: (row, 0, 0)),
    ]
    return operands, specs, tail, tail_specs, panel


def attention_cost(rows, nq, nk, products):
    return pl.CostEstimate(
        flops=2 * products * rows * H * nq * nk * LANES,
        bytes_accessed=2 * products * rows * (nq + nk) * D,
        transcendentals=rows * H * nq * nk,
    )


def attend(query, keys, places, bias, row_segs, key_segs, causal):
    rows, nq = row_segs.shape
    nk = key_segs.shape[1]
    operands, specs, tail, tail_specs, panel = attention_specs(
        query, keys, places, bias, row_segs, key_segs
    )
    return pl.pallas_call(
        functools.partial(attend_kernel, biased=bias is not None, causal=causal),
        out_shape=jax.ShapeDtypeStruct((rows, nq, D), jnp.bfloat16),
        grid=(H // 2, rows),
        in_specs=specs + tail_specs,
        out_specs=panel(nq, 0),
        cost_estimate=attention_cost(rows, nq, nk, 2),
        compiler_params=pltpu.CompilerParams(vmem_limit_bytes=32 << 20),
    )(*operands, *tail)


def attend_back(query, keys, places, bias, row_segs, key_segs, causal, grad_out):
    rows, nq = row_segs.shape
    nk = key_segs.shape[1]
    operands, specs, tail, tail_specs, panel = attention_specs(
        query, keys, places, bias, row_segs, key_segs
    )
    outs = [
        jax.ShapeDtypeStruct((rows, nq, D), jnp.bfloat16),
        jax.ShapeDtypeStruct((rows, nk, D), jnp.bfloat16),
        jax.ShapeDtypeStruct((rows, nk, D), jnp.bfloat16),
    ]
    out_specs = [panel(nq, 0), panel(nk, 0), panel(nk, 0)]
    if bias is not None:
        outs.append(jax.ShapeDtypeStruct(bias.shape, jnp.float32))
        out_specs.append(
            pl.BlockSpec((2,) + bias.shape[1:], lambda pair, row: (pair, 0, 0, 0))
        )
    return pl.pallas_call(
        functools.partial(attend_back_kernel, biased=bias is not None, causal=causal),
        out_shape=outs,
        grid=(H // 2, rows),
        in_specs=specs + [panel(nq, 0)] + tail_specs,
        out_specs=out_specs,
        cost_estimate=attention_cost(rows, nq, nk, 5),
        compiler_params=pltpu.CompilerParams(vmem_limit_bytes=32 << 20),
    )(*operands, grad_out, *tail)


def layer_shapes(decoder):
    if decoder:
        return [(D, 3 * D), (D, D), (D, D), (D, 2 * D), (D, D), (D, FF), (FF, D)]
    return [(D, 3 * D), (D, D), (D, FF), (FF, D)]


def as_blocks(flat):
    if flat.ndim == 3:
        return flat
    return flat.reshape(flat.shape[0], BLOCK, BLOCK)


def as_rows(blocks):
    return blocks.reshape(blocks.shape[0], BLOCK * BLOCK)


def as_pairs(blocks):
    amount = blocks.shape[0] // 2
    split = blocks.reshape(amount, 2, BLOCK, BLOCK)
    return jnp.concatenate([split[:, 0], split[:, 1]], axis=-1)


def unpack_kernel(pairs_ref, out_ref):
    across = out_ref.shape[1] // PAIR
    for row in range(out_ref.shape[0] // BLOCK):
        for column in range(across):
            out_ref[row * BLOCK : (row + 1) * BLOCK, column * PAIR : (column + 1) * PAIR] = (
                pairs_ref[row * across + column]
            )


def matrices_of(pairs, shapes):
    matrix_list = []
    place = 0
    for height, breadth in shapes:
        group = 2 * breadth // PAIR
        first = place // group
        matrix_list.append(
            pl.pallas_call(
                unpack_kernel,
                out_shape=jax.ShapeDtypeStruct((height, breadth), pairs.dtype),
                grid=(height // PAIR,),
                in_specs=[
                    pl.BlockSpec(
                        (group, BLOCK, PAIR), lambda step, first=first: (first + step, 0, 0)
                    )
                ],
                out_specs=pl.BlockSpec((PAIR, breadth), lambda step: (step, 0)),
                cost_estimate=pl.CostEstimate(
                    flops=0, bytes_accessed=4 * height * breadth, transcendentals=0
                ),
                compiler_params=pltpu.CompilerParams(vmem_limit_bytes=32 << 20),
            )(pairs)
        )
        place += group * (height // PAIR)
    return matrix_list


def weight_grad_kernel(x_ref, g_ref, *rest):
    out_ref = rest[-1]
    across = out_ref.shape[0] // 2
    for column in range(across):
        product = lax.dot_general(
            x_ref[...],
            g_ref[:, column * PAIR : (column + 1) * PAIR],
            (((0,), (0,)), ((), ())),
            preferred_element_type=jnp.float32,
        )
        product = product.astype(jnp.bfloat16)
        out_ref[column] = product[:BLOCK]
        out_ref[across + column] = product[BLOCK:]


def weight_grads(operands):
    total = sum(x.shape[-1] * g.shape[-1] for x, g in operands) // (BLOCK * PAIR)
    pairs = None
    place = 0
    for x, g in operands:
        x = x.reshape(-1, x.shape[-1])
        g = g.reshape(-1, g.shape[-1])
        count, height = x.shape
        breadth = g.shape[1]
        group = 2 * breadth // PAIR
        first = place // group
        given = [] if pairs is None else [pairs]
        pairs = pl.pallas_call(
            weight_grad_kernel,
            out_shape=jax.ShapeDtypeStruct((total, BLOCK, PAIR), jnp.bfloat16),
            grid=(height // PAIR,),
            in_specs=[
                pl.BlockSpec((count, PAIR), lambda step: (0, step)),
                pl.BlockSpec((count, breadth), lambda step: (0, 0)),
            ]
            + [pl.BlockSpec(memory_space=pl.ANY)] * len(given),
            out_specs=pl.BlockSpec(
                (group, BLOCK, PAIR), lambda step, first=first: (first + step, 0, 0)
            ),
            input_output_aliases={2: 0} if given else {},
            cost_estimate=pl.CostEstimate(
                flops=2 * count * height * breadth,
                bytes_accessed=2 * (count * (height + breadth) + height * breadth),
                transcendentals=0,
            ),
            compiler_params=pltpu.CompilerParams(vmem_limit_bytes=40 << 20),
        )(x, g, *given)
        place += group * (height // PAIR)
    return pairs


def split_float(values):
    high = values.astype(jnp.bfloat16)
    return high, (values - high.astype(jnp.float32)).astype(jnp.bfloat16)


def full_product(left, right, contract):
    def part(first, second):
        return lax.dot_general(
            first, second, (contract, ((), ())), preferred_element_type=jnp.float32
        )

    return (
        part(left[0], right[1]) + part(left[1], right[0]) + part(left[0], right[0])
    )


ROW_COL = ((1,), (0,))
ROW_ROW = ((1,), (1,))
COL_COL = ((0,), (0,))


def turned_product(left_root, middle, right_root):
    shaped = full_product(split_float(left_root), middle, ROW_COL)
    return full_product(split_float(shaped), split_float(right_root), ROW_COL)


def ahead_kernel(m_ref, lr_ref, rr_ref, o_ref):
    for place in range(m_ref.shape[0]):
        o_ref[place] = turned_product(lr_ref[place], split_float(m_ref[place]), rr_ref[place])


def products_kernel(g_ref, lr_ref, rr_ref, g_out, turned_out, left_out, right_out):
    for place in range(2):
        block = g_ref[0, :, place * BLOCK : (place + 1) * BLOCK]
        g_out[place] = block
        halves = split_float(block)
        turned_out[place] = turned_product(lr_ref[place], halves, rr_ref[place])
        left_out[place] = full_product(halves, halves, ROW_ROW)
        right_out[place] = full_product(halves, halves, COL_COL)


def block_cost(amount, products, arrays):
    return pl.CostEstimate(
        flops=6 * products * amount * BLOCK**3,
        bytes_accessed=4 * arrays * amount * BLOCK * BLOCK,
        transcendentals=0,
    )


def shampoo_ahead(moment, left_root, right_root):
    blocks = [as_blocks(member) for member in (moment, left_root, right_root)]
    amount = moment.shape[0]
    spec = pl.BlockSpec((2, BLOCK, BLOCK), lambda pair: (pair, 0, 0))
    ahead = pl.pallas_call(
        ahead_kernel,
        out_shape=jax.ShapeDtypeStruct((amount, BLOCK, BLOCK), jnp.float32),
        grid=(amount // 2,),
        in_specs=[spec] * 3,
        out_specs=spec,
        cost_estimate=block_cost(amount, 2, 4),
        compiler_params=pltpu.CompilerParams(vmem_limit_bytes=32 << 20),
    )(*blocks)
    return as_rows(ahead), blocks[1], blocks[2]


def shampoo_products(pairs, left_root, right_root):
    amount = left_root.shape[0]
    spec = pl.BlockSpec((2, BLOCK, BLOCK), lambda pair: (pair, 0, 0))
    results = pl.pallas_call(
        products_kernel,
        out_shape=[jax.ShapeDtypeStruct((amount, BLOCK, BLOCK), jnp.float32)] * 4,
        grid=(amount // 2,),
        in_specs=[pl.BlockSpec((1, BLOCK, PAIR), lambda pair: (pair, 0, 0)), spec, spec],
        out_specs=[spec] * 4,
        cost_estimate=block_cost(amount, 4, 7),
        compiler_params=pltpu.CompilerParams(vmem_limit_bytes=32 << 20),
    )(pairs, left_root, right_root)
    return [as_rows(result) for result in results]


def project(left, right):
    return jnp.matmul(left, right, preferred_element_type=jnp.float32)


def project_back(left, right):
    return jnp.einsum("btf,df->btd", left, right, preferred_element_type=jnp.float32)


def rms(values, gain):
    return values * lax.rsqrt(jnp.mean(values * values, axis=-1, keepdims=True) + norm_eps) * gain


def rms_back(values, gain, grad_out):
    inverse = lax.rsqrt(jnp.mean(values * values, axis=-1, keepdims=True) + norm_eps)
    normed = values * inverse
    grad_gain = jnp.sum(grad_out * normed, axis=(0, 1))
    grad_normed = grad_out * gain
    grad_values = inverse * (
        grad_normed - normed * jnp.mean(grad_normed * normed, axis=-1, keepdims=True)
    )
    return (grad_values, grad_gain)


def ff_forward(hidden, gain, w_in, w_down):
    normed = rms(hidden, gain).astype(jnp.bfloat16)
    inner = project(normed, w_in)
    active = jax.nn.gelu(inner).astype(jnp.bfloat16)
    return (hidden + project(active, w_down), (normed, inner, active))


def ff_back(hidden, gain, w_in, w_down, cache, grad_out):
    normed, inner, active = cache
    branch_grad = grad_out.astype(jnp.bfloat16)
    grad_active = project_back(branch_grad, w_down)
    unused, gelu_back = jax.vjp(jax.nn.gelu, inner)
    grad_inner = gelu_back(grad_active)[0].astype(jnp.bfloat16)
    grad_part, grad_gain = rms_back(hidden, gain, project_back(grad_inner, w_in))
    return (grad_out + grad_part, grad_gain, (normed, grad_inner), (active, branch_grad))


def table_rows(table, token_ids, vocab_first):
    local_ids = token_ids - vocab_first
    inside = (local_ids >= 0) & (local_ids < table.shape[0])
    picked = jnp.take(table, jnp.clip(local_ids, 0, table.shape[0] - 1), axis=0)
    return jnp.where(inside[..., None], picked, jnp.zeros((), table.dtype))


def table_grads(grads, token_ids, vocab_first, dense):
    vocab_local = dense.shape[0]
    local_ids = token_ids.reshape(-1) - vocab_first
    inside = (local_ids >= 0) & (local_ids < vocab_local)
    slots = jnp.where(inside, local_ids, vocab_local)
    return dense.at[slots].add(grads.astype(jnp.float32), mode="drop")


REPLICAS = ("dp", "seq")
EVERYWHERE = ("fsdp", "dp", "seq")


def replica_rank():
    return lax.axis_index("dp") * lax.axis_size("seq") + lax.axis_index("seq")


def replica_count():
    return lax.axis_size("dp") * lax.axis_size("seq")


def paired_mesh():
    return (
        lax.axis_size("dp") == 2 and lax.axis_size("seq") == 2 and lax.axis_size("fsdp") % 2 == 0
    )


def swap(values, axis):
    size = lax.axis_size(axis)
    return lax.ppermute(values, axis, [(place, place ^ 1) for place in range(size)])


def shift(values, step):
    size = lax.axis_size("fsdp")
    moves = [
        (place, place + 2 * step) for place in range(size) if 0 <= place + 2 * step < size
    ]
    return lax.ppermute(values, "fsdp", moves)


def choose(flag, if_set, if_clear):
    return jnp.where(flag == 1, if_set, if_clear)


def pick(values, place, axis):
    return lax.dynamic_index_in_dim(values, place, axis, False)


def narrow(values):
    return values.astype(jnp.bfloat16)


def wide(values):
    return values.astype(jnp.float32)


def placed(relative, first, second):
    def at(row, column):
        here = choose(second, relative[row][1 - column], relative[row][column])
        there = choose(second, relative[1 - row][1 - column], relative[1 - row][column])
        return choose(first, there, here)

    return [[at(0, 0), at(0, 1)], [at(1, 0), at(1, 1)]]


def own_weights(master):
    share = master.shape[0] // replica_count()
    if master.shape[0] % (2 * replica_count()) == 0:
        master = lax.dynamic_slice_in_dim(master, replica_rank() * share, share, 0)
    return as_pairs(as_blocks(master.astype(jnp.bfloat16)))


def hold(values):
    return lax.optimization_barrier(values)


def gathered_weights(pairs, amount):
    split = amount % (2 * replica_count()) == 0
    return lax.all_gather(pairs, EVERYWHERE if split else "fsdp", axis=0, tiled=True)


def own_place():
    return jnp.stack(
        [lax.axis_index("fsdp") % 2, lax.axis_index("dp"), lax.axis_index("seq")]
    ).astype(jnp.int32)


def fold_kernel(place_ref, own_ref, got_ref, keep_up, send_up, keep_low, send_low):
    total = wide(own_ref[0]) + wide(got_ref[0])
    mid = BLOCK // 2
    upper, lower = (total[:, :mid], total[:, mid:])
    other_side, other_half = (pl.program_id(1), pl.program_id(2))

    @pl.when(other_half == 0)
    def _():
        keep_up[0, 0] = upper

    @pl.when(other_half == 1)
    def _():
        send_up[0, 0] = narrow(upper)

    @pl.when(other_side == 0)
    def _():
        keep_low[0, 0] = lower

    @pl.when(other_side == 1)
    def _():
        send_low[0, 0] = narrow(lower)


def fold_cores(pairs, got, n_chips, quarter):
    mid = BLOCK // 2

    def quarter_of(place, other_side, other_half):
        return (place[1] ^ other_side) * 2 + (place[2] ^ other_half)

    whole = (1, quarter, BLOCK, PAIR)
    part = (1, 1, quarter, mid, PAIR)
    halves = (n_chips, 2, quarter, mid, PAIR)

    def up_at(chip, other_side, other_half, place):
        return (chip, place[1] ^ other_side, 0, 0, 0)

    def keep_low_at(chip, other_side, other_half, place):
        return (chip, jnp.where(other_side == 0, place[2] ^ other_half, place[2] ^ 1), 0, 0, 0)

    def send_low_at(chip, other_side, other_half, place):
        return (chip, jnp.where(other_side == 1, place[2] ^ other_half, place[2]), 0, 0, 0)

    return pl.pallas_call(
        fold_kernel,
        out_shape=[
            jax.ShapeDtypeStruct(halves, kind)
            for kind in (jnp.float32, jnp.bfloat16, jnp.float32, jnp.bfloat16)
        ],
        grid_spec=pltpu.PrefetchScalarGridSpec(
            num_scalar_prefetch=1,
            grid=(n_chips, 2, 2),
            in_specs=[
                pl.BlockSpec(
                    whole,
                    lambda chip, side, half, place: (
                        (2 * chip + place[0]) * 4 + quarter_of(place, side, half),
                        0,
                        0,
                        0,
                    ),
                ),
                pl.BlockSpec(
                    whole,
                    lambda chip, side, half, place: (
                        chip * 4 + quarter_of(place, side, half),
                        0,
                        0,
                        0,
                    ),
                ),
            ],
            out_specs=[
                pl.BlockSpec(part, up_at),
                pl.BlockSpec(part, up_at),
                pl.BlockSpec(part, keep_low_at),
                pl.BlockSpec(part, send_low_at),
            ],
        ),
        cost_estimate=pl.CostEstimate(
            flops=pairs.size // 2, bytes_accessed=5 * pairs.size, transcendentals=0
        ),
        compiler_params=pltpu.CompilerParams(vmem_limit_bytes=32 << 20),
    )(
        own_place(),
        pairs.reshape(-1, quarter, BLOCK, PAIR),
        got.reshape(-1, quarter, BLOCK, PAIR),
    )


def sum_replicas(values):
    values = values + swap(values, "seq")
    return values + swap(values, "dp")


def sum_line(values):
    size = lax.axis_size("fsdp")
    if size & (size - 1):
        return lax.psum(values, "fsdp")
    step = 1
    while step < size:
        moves = [(place, place ^ step) for place in range(size)]
        values = values + lax.ppermute(values, "fsdp", moves)
        step *= 2
    return values


def summed_blocks(pairs):
    shard = lax.psum_scatter(wide(pairs), "fsdp", scatter_dimension=0, tiled=True)
    return lax.psum(shard, REPLICAS)


def swap_halves(pairs):
    n_chips = lax.axis_size("fsdp") // 2
    core = lax.axis_index("fsdp") % 2
    split = pairs.reshape(n_chips, 2, -1, BLOCK, PAIR)
    return swap(pick(split, 1 - core, 1), "fsdp")


def fold_blocks(pairs, got):
    n_chips = lax.axis_size("fsdp") // 2
    return fold_cores(pairs, got, n_chips, pairs.shape[0] // (8 * n_chips))


def near_sums(folded):
    return [folded[0], swap(folded[1], "seq"), folded[2], swap(folded[3], "dp")]


def far_sums(near):
    side, half = (lax.axis_index("dp"), lax.axis_index("seq"))
    upper = near[0] + wide(near[1])
    lower = near[2] + wide(near[3])
    return [
        pick(upper, side, 1),
        swap(narrow(pick(upper, 1 - side, 1)), "dp"),
        pick(lower, half, 1),
        swap(narrow(pick(lower, 1 - half, 1)), "seq"),
    ]


def line_sums(far):
    size = lax.axis_size("fsdp")
    line = narrow(jnp.concatenate([far[0] + wide(far[1]), far[2] + wide(far[3])], axis=2))
    cores = [list(range(core, size, 2)) for core in range(2)]
    return lax.all_to_all(line, "fsdp", 0, 0, axis_index_groups=cores, tiled=True)


def line_total(arrived):
    return jnp.sum(wide(arrived), axis=0)


def share_blocks(own):
    return wide(lax.all_gather(narrow(own), REPLICAS, axis=0, tiled=True))


def window_rows(half_rows):
    return -(-half_rows // 16) * 8


def half_lanes(values, place):
    return lax.dynamic_slice_in_dim(values, place * (D // 2), D // 2, 1)


SCALE_ROWS = 8


def scale_of(power):
    return jnp.exp2(power.astype(jnp.float32))


def scaled_swap(values, power, axis):
    mark = jnp.full((SCALE_ROWS, values.shape[1]), power, jnp.float16)
    message = jnp.concatenate([values.astype(jnp.float16), mark], axis=0)
    got = swap(message, axis)
    return got[:-SCALE_ROWS], got[-1, 0].astype(jnp.float32)


def joined(values, power, got):
    others, other_power = got
    least = jnp.minimum(power, other_power)
    return (
        values * scale_of(least - power) + wide(others) * scale_of(least - other_power),
        least,
    )


def near_table(partial, bound):
    side, half = (lax.axis_index("dp"), lax.axis_index("seq"))
    half_rows = partial.shape[0] // 2
    window = window_rows(half_rows)
    power = jnp.clip(12.0 - jnp.ceil(jnp.log2(jnp.maximum(bound, 1e-37))), -120.0, 120.0)

    def rows_of(first, place):
        start = first + place * (half_rows - window)
        return lax.dynamic_slice_in_dim(partial, start, window, 0) * scale_of(power)

    return [
        rows_of(0, half),
        scaled_swap(rows_of(0, 1 - half), power, "seq"),
        rows_of(half_rows, side),
        scaled_swap(rows_of(half_rows, 1 - side), power, "dp"),
        power,
    ]


def far_table(near):
    side, half = (lax.axis_index("dp"), lax.axis_index("seq"))
    top, top_power = joined(near[0], near[4], near[1])
    low, low_power = joined(near[2], near[4], near[3])
    return [
        half_lanes(top, side),
        top_power,
        scaled_swap(half_lanes(top, 1 - side), top_power, "dp"),
        half_lanes(low, half),
        low_power,
        scaled_swap(half_lanes(low, 1 - half), low_power, "seq"),
    ]


def table_total(far):
    top, power = joined(*far[:3])
    low, _ = joined(*far[3:])
    return top, low, scale_of(power)


def table_squares(top, low, half_rows):
    side, half = (lax.axis_index("dp"), lax.axis_index("seq"))
    again = 2 * window_rows(half_rows) - half_rows
    row = lax.broadcasted_iota(jnp.int32, (top.shape[0], 1), 0)
    return jnp.sum(jnp.where(row >= again * half, top * top, 0.0)) + jnp.sum(
        jnp.where(row >= again * side, low * low, 0.0)
    )


def share_near(top, low):
    top = hold(top.astype(jnp.float16))
    low = hold(low.astype(jnp.float16))
    return [jnp.stack([top, swap(top, "dp")]), jnp.stack([low, swap(low, "seq")])]


def share_far(near):
    return [swap(near[0], "seq"), swap(near[1], "dp")]


def placed_table(near, far, scale, half_rows):
    side, half = (lax.axis_index("dp"), lax.axis_index("seq"))
    again = 2 * window_rows(half_rows) - half_rows
    top_all = placed([near[0], far[0]], half, side)
    low_all = placed([near[1], far[1]], side, half)
    rows = []
    for first, second in (top_all, low_all):
        rows.append(jnp.concatenate(first, axis=1))
        rows.append(jnp.concatenate(second, axis=1)[again:])
    return wide(jnp.concatenate(rows, axis=0)) * (1.0 / scale)


def adam_update(weight, gradient, moment, second):
    moment = beta_first * moment + (1 - beta_first) * gradient
    second = beta_second * second + (1 - beta_second) * gradient * gradient
    corrected = moment / (1 - beta_first**STEP)
    scaled = second / (1 - beta_second**STEP)
    weight = weight - adam_rate * (
        corrected / (jnp.sqrt(scaled) + adam_eps) + weight_decay * weight
    )
    return (weight, moment, second)


def shampoo_update(weight, moment, left, right, ahead, products, factor):
    gradient, turned, left_square, right_square = products
    direction = beta_first * ahead + ((1 - beta_first) * factor) * turned
    square = (1 - stat_decay) * factor * factor
    return (
        weight - shampoo_rate * (direction + weight_decay * weight),
        beta_first * moment + ((1 - beta_first) * factor) * gradient,
        stat_decay * left + square * left_square,
        stat_decay * right + square * right_square,
    )


def on_device(
    enc_ids,
    span_mask,
    segments,
    targets,
    loss_weights,
    target_segments,
    embedding,
    emb_m,
    emb_v,
    gains,
    gain_m,
    gain_v,
    rel_bias,
    rel_m,
    rel_v,
    enc_w,
    enc_m,
    enc_left,
    enc_right,
    enc_lroot,
    enc_rroot,
    dec_w,
    dec_m,
    dec_left,
    dec_right,
    dec_lroot,
    dec_rroot,
):
    fsdp_rank = lax.axis_index("fsdp")
    seq_rank = lax.axis_index("seq")
    n_fsdp = lax.axis_size("fsdp")
    n_seq = lax.axis_size("seq")
    half_len = enc_ids.shape[1]
    rows, dec_len = targets.shape
    enc_len = half_len * n_seq
    enc_in = jnp.where(span_mask == 1, VOCAB - sentinel_offset, enc_ids)
    dec_in = jnp.concatenate([jnp.zeros((rows, 1), jnp.int32), targets[:, :-1]], axis=1)

    paired = paired_mesh()

    halves = jnp.stack([enc_in, segments]).reshape(2, n_seq, rows, half_len)
    enc_own, dec_own, table = (own_weights(enc_w), own_weights(dec_w), narrow(embedding))
    if n_seq == 2:
        kept = pick(halves, seq_rank, 1)
        got = swap(pick(halves, 1 - seq_rank, 1), "seq")
        got, enc_own, dec_own = hold((got, enc_own, dec_own))
        parts = (choose(seq_rank, got, kept), choose(seq_rank, kept, got))
        row_words = jnp.stack(parts, axis=2)
    else:
        row_words = lax.all_to_all(halves, "seq", 1, 1, tiled=True).transpose(0, 2, 1, 3)
    row_words = row_words.reshape(2, rows, enc_len)
    row_segments = row_words[1]
    message = jnp.concatenate(
        [
            row_words[0].reshape(-1),
            dec_in.reshape(-1),
            targets.reshape(-1),
            loss_weights.reshape(-1),
        ]
    ).reshape(1, -1)
    enc_pairs = gathered_weights(enc_own, enc_w.shape[0])
    gathered = lax.all_gather(message, "fsdp", axis=0, tiled=True)
    all_enc = gathered[:, : rows * enc_len]
    rest = gathered[:, rows * enc_len :].reshape(n_fsdp, 3, rows * dec_len)
    all_dec, all_targets, all_weights = (rest[:, 0], rest[:, 1], rest[:, 2])
    all_tokens = jnp.concatenate([all_enc, all_dec], axis=1)
    vocab_local = table.shape[0]
    vocab_first = fsdp_rank * vocab_local
    found = table_rows(table, all_tokens, vocab_first)
    found, enc_pairs, dec_own = hold((found, enc_pairs, dec_own))
    looked_up = lax.psum_scatter(found, "fsdp", scatter_dimension=0, tiled=True).reshape(-1, D)
    dec_pairs = gathered_weights(dec_own, dec_w.shape[0])
    enc_mats = matrices_of(enc_pairs, layer_shapes(False))
    enc_onehot = tile_onehot(enc_len // TILE, False)
    dec_onehot = tile_onehot(dec_len // TILE, True)
    looked_up, enc_mats, enc_bias, dec_bias = hold(
        (looked_up, enc_mats, tile_bias(enc_onehot, rel_bias[0]), tile_bias(dec_onehot, rel_bias[1]))
    )
    hidden0 = looked_up[: rows * enc_len].reshape(rows, enc_len, D).astype(jnp.float32)
    state0 = looked_up[rows * enc_len :].reshape(rows, dec_len, D).astype(jnp.float32)

    tile_at = D // LANES
    self_places = (0, tile_at, 2 * tile_at)
    cross_places = (0, 0, tile_at)

    normed0 = rms(hidden0, gains[0]).astype(jnp.bfloat16)
    enc_qkv = project(normed0, enc_mats[0]).astype(jnp.bfloat16)
    enc_attended = attend(
        enc_qkv, enc_qkv, self_places, enc_bias, row_segments, row_segments, False
    )
    hidden1 = hidden0 + project(enc_attended, enc_mats[1])
    hidden2, enc_cache = ff_forward(hidden1, gains[1], enc_mats[2], enc_mats[3])
    encoded = rms(hidden2, gains[2]).astype(jnp.bfloat16)
    count = jnp.sum(all_weights).astype(jnp.float32)
    if paired:
        count = count + swap(count, "seq")
        count = count + swap(count, "dp")
    else:
        count = lax.psum(count, REPLICAS)
    encoded, count, dec_pairs = hold((encoded, count, dec_pairs))
    share = 1.0 / jnp.maximum(count, 1.0)
    dec_mats = matrices_of(dec_pairs, layer_shapes(True))
    pairs = project(encoded, dec_mats[3]).astype(jnp.bfloat16)

    normed3 = rms(state0, gains[3]).astype(jnp.bfloat16)
    self_qkv = project(normed3, dec_mats[0]).astype(jnp.bfloat16)
    self_attended = attend(
        self_qkv, self_qkv, self_places, dec_bias, target_segments, target_segments, True
    )
    state1 = state0 + project(self_attended, dec_mats[1])
    normed4 = rms(state1, gains[4]).astype(jnp.bfloat16)
    cross_query = project(normed4, dec_mats[2]).astype(jnp.bfloat16)
    cross_attended = attend(
        cross_query, pairs, cross_places, None, target_segments, row_segments, False
    )
    state2 = state1 + project(cross_attended, dec_mats[4])
    state3, dec_cache = ff_forward(state2, gains[5], dec_mats[5], dec_mats[6])
    out_scale = D ** (-0.5)
    final = (rms(state3, gains[6]) * out_scale).astype(jnp.bfloat16)

    all_final = lax.all_gather(final.reshape(rows * dec_len, D), "fsdp", axis=0, tiled=True)
    logits = jnp.einsum("nd,vd->nv", all_final, table, preferred_element_type=jnp.float32)
    local_ids = all_targets.reshape(-1) - vocab_first
    target_hot = local_ids[:, None] == jnp.arange(vocab_local, dtype=jnp.int32)[None, :]
    local_top = jnp.max(logits, axis=1)
    local_sum = jnp.sum(jnp.exp(logits - local_top[:, None]), axis=1)
    local_pick = jnp.sum(jnp.where(target_hot, logits, 0.0), axis=1)
    stats = lax.all_gather(
        jnp.stack([local_top, local_sum, local_pick])[None], "fsdp", axis=0, tiled=True
    )
    top_all = jnp.max(stats[:, 0], axis=0)
    sum_all = jnp.sum(stats[:, 1] * jnp.exp(stats[:, 0] - top_all), axis=0)
    pick_all = jnp.sum(stats[:, 2], axis=0)
    lse = top_all + jnp.log(sum_all)
    token_weights = all_weights.reshape(-1).astype(jnp.float32)
    group_loss = jnp.sum(token_weights * (lse - pick_all))
    grad_logits = (
        token_weights[:, None] * (jnp.exp(logits - lse[:, None]) - target_hot.astype(jnp.float32))
    ).astype(jnp.bfloat16)
    grad_final = lax.psum_scatter(
        jnp.dot(grad_logits, table, preferred_element_type=jnp.float32),
        "fsdp",
        scatter_dimension=0,
        tiled=True,
    ).reshape(rows, dec_len, D)
    dense_grad = jnp.einsum("nv,nd->vd", grad_logits, all_final, preferred_element_type=jnp.float32)
    grad_final, dense_grad, dense_bound = hold(
        (grad_final, dense_grad, jnp.max(jnp.abs(dense_grad)))
    )

    grad_state3, gain_six = rms_back(state3, gains[6], grad_final * out_scale)
    grad_state2, gain_five, dec_in_grad, dec_down_grad = ff_back(
        state2, gains[5], dec_mats[5], dec_mats[6], dec_cache, grad_state3
    )
    branch_grad = grad_state2.astype(jnp.bfloat16)
    cross_out_grad = (cross_attended, branch_grad)
    grad_cross = project_back(branch_grad, dec_mats[4]).astype(jnp.bfloat16)
    grad_cq, grad_ck, grad_cv = attend_back(
        cross_query, pairs, cross_places, None, target_segments, row_segments, False, grad_cross
    )
    grad_pairs = jnp.concatenate([grad_ck, grad_cv], axis=-1)
    cross_query_grad = (normed4, grad_cq)
    grad_state1_part, gain_four = rms_back(state1, gains[4], project_back(grad_cq, dec_mats[2]))
    grad_state1 = grad_state2 + grad_state1_part
    cross_pair_grad = (encoded, grad_pairs)
    grad_encoded = project_back(grad_pairs, dec_mats[3])
    branch_grad = grad_state1.astype(jnp.bfloat16)
    self_out_grad = (self_attended, branch_grad)
    grad_self = project_back(branch_grad, dec_mats[1]).astype(jnp.bfloat16)
    grad_sq, grad_sk, grad_sv, dec_bias_grad = attend_back(
        self_qkv, self_qkv, self_places, dec_bias, target_segments, target_segments, True, grad_self
    )
    grad_sqkv = jnp.concatenate([grad_sq, grad_sk, grad_sv], axis=-1)
    self_qkv_grad = (normed3, grad_sqkv)
    grad_state0_part, gain_three = rms_back(state0, gains[3], project_back(grad_sqkv, dec_mats[0]))
    grad_state0 = grad_state1 + grad_state0_part
    decoder_portion = weight_grads(
        [
            self_qkv_grad,
            self_out_grad,
            cross_query_grad,
            cross_pair_grad,
            cross_out_grad,
            dec_in_grad,
            dec_down_grad,
        ]
    )
    if paired:
        dec_got = swap_halves(decoder_portion)

    grad_hidden2, gain_two = rms_back(hidden2, gains[2], grad_encoded)
    grad_hidden1, gain_one, encoder_input_gradient, encoder_down_gradient = ff_back(
        hidden1, gains[1], enc_mats[2], enc_mats[3], enc_cache, grad_hidden2
    )
    branch_grad = grad_hidden1.astype(jnp.bfloat16)
    encoder_output_gradient = (enc_attended, branch_grad)
    grad_attn = project_back(branch_grad, enc_mats[1]).astype(jnp.bfloat16)
    if paired:
        dec_got, decoder_portion, grad_attn = hold((dec_got, decoder_portion, grad_attn))
        dec_folded = fold_blocks(decoder_portion, dec_got)
        dec_folded, grad_attn = hold((dec_folded, grad_attn))
        dec_close = near_sums(dec_folded)
    grad_eq, grad_ek, grad_ev, enc_bias_grad = attend_back(
        enc_qkv, enc_qkv, self_places, enc_bias, row_segments, row_segments, False, grad_attn
    )
    grad_eqkv = jnp.concatenate([grad_eq, grad_ek, grad_ev], axis=-1)
    encoder_qkv_gradient = (normed0, grad_eqkv)
    grad_hidden0_part, gain_zero = rms_back(hidden0, gains[0], project_back(grad_eqkv, enc_mats[0]))
    grad_hidden0 = grad_hidden1 + grad_hidden0_part
    back_rows = jnp.concatenate(
        [grad_hidden0.reshape(-1, D), grad_state0.reshape(-1, D)], axis=0
    ).astype(jnp.bfloat16)
    if paired:
        dec_close, back_rows, grad_eqkv = hold((dec_close, back_rows, grad_eqkv))
        encoder_qkv_gradient = (normed0, grad_eqkv)
        dec_far_sums = far_sums(dec_close)
    back_all = lax.all_gather(back_rows, "fsdp", axis=0, tiled=True)
    encoder_portion = weight_grads(
        [
            encoder_qkv_gradient,
            encoder_output_gradient,
            encoder_input_gradient,
            encoder_down_gradient,
        ]
    )
    if paired:
        encoder_portion, dec_far_sums = hold((encoder_portion, dec_far_sums))
        enc_got = swap_halves(encoder_portion)
        enc_got, encoder_portion, enc_roots = hold(
            (enc_got, encoder_portion, (enc_m, enc_lroot, enc_rroot))
        )
        enc_folded = hold(fold_blocks(encoder_portion, enc_got))
        enc_close = near_sums(enc_folded)
        enc_ready = shampoo_ahead(*enc_roots)
        back_all, enc_close, enc_ready, dec_far_sums = hold(
            (back_all, enc_close, enc_ready, dec_far_sums)
        )
        dec_arrived = line_sums(dec_far_sums)
        enc_far_sums = far_sums(enc_close)
        bound = dense_bound + back_all.shape[0] * jnp.max(jnp.abs(back_all)).astype(jnp.float32)
    else:
        enc_ready = shampoo_ahead(enc_m, enc_lroot, enc_rroot)
        dec_ready = shampoo_ahead(dec_m, dec_lroot, dec_rroot)
    emb_grad = table_grads(back_all, all_tokens, vocab_first, dense_grad)
    gain_part = jnp.stack(
        [gain_zero, gain_one, gain_two, gain_three, gain_four, gain_five, gain_six]
    )
    rel_part = jnp.stack(
        [tile_bias_grad(enc_onehot, enc_bias_grad), tile_bias_grad(dec_onehot, dec_bias_grad)]
    )
    small = [
        gain_part.reshape(-1),
        rel_part.reshape(-1),
        jnp.where(fsdp_rank == 0, group_loss, 0.0).reshape(1),
    ]
    if paired:
        half_rows = vocab_local // 2
        dec_arrived, enc_far_sums, emb_grad, bound, dec_roots = hold(
            (dec_arrived, enc_far_sums, emb_grad, bound, (dec_m, dec_lroot, dec_rroot))
        )
        table_close = near_table(emb_grad, bound)
        enc_arrived = line_sums(enc_far_sums)
        dec_own_sum = line_total(dec_arrived)
        dec_grad = share_blocks(dec_own_sum) * share
        dec_ready = shampoo_ahead(*dec_roots)
        table_close, dec_ready, dec_grad, enc_arrived = hold(
            (table_close, dec_ready, dec_grad, enc_arrived)
        )
        table_far = far_table(table_close)
        dec_products = shampoo_products(dec_grad, *dec_ready[1:])
        enc_own_sum = line_total(enc_arrived)
        enc_grad = share_blocks(enc_own_sum) * share
        table_far, dec_products = hold((table_far, dec_products))
        top, low, scale = table_total(table_far)
        squares = (
            jnp.sum(jnp.square(enc_own_sum * share))
            + jnp.sum(jnp.square(dec_own_sum * share))
            + table_squares(top * (share / scale), low * (share / scale), half_rows)
        )
    else:
        dec_grad = summed_blocks(decoder_portion) * share
        enc_grad = summed_blocks(encoder_portion) * share
        dec_products = shampoo_products(dec_grad, *dec_ready[1:])
        enc_products = shampoo_products(enc_grad, *enc_ready[1:])
        table_grad = lax.psum(emb_grad, REPLICAS) * share
        squares = (
            jnp.sum(jnp.square(enc_grad))
            + jnp.sum(jnp.square(dec_grad))
            + jnp.sum(jnp.square(table_grad))
        ) / replica_count()
    small = jnp.concatenate(small + [squares.reshape(1), jnp.zeros(126, jnp.float32)])
    small = small.reshape(-1, LANES)
    if paired:
        small, top, low, enc_grad = hold((sum_replicas(small), top, low, enc_grad))
        table_near = share_near(top, low)
        small = sum_line(small)
        enc_products = shampoo_products(enc_grad, *enc_ready[1:])
        table_near, small, enc_products = hold((table_near, small, enc_products))
        table_grad = placed_table(table_near, share_far(table_near), scale, half_rows) * share
    else:
        small = lax.psum(small, EVERYWHERE)
    small = small.reshape(-1)
    gain_grad = small[: 7 * D].reshape(7, D) * share
    rel_grad = small[7 * D : 7 * D + 2 * NBK * H].reshape(2, NBK, H) * share
    loss_sum = small[7 * D + 2 * NBK * H]
    squares_all = small[7 * D + 2 * NBK * H + 1]
    loss_count = jnp.maximum(count, 1.0)
    if paired:
        dec_ahead, enc_ahead = (dec_ready[0], enc_ready[0])
    else:
        dec_products, enc_products = hold((dec_products, enc_products))
        dec_ahead, enc_ahead = (dec_ready[0], enc_ready[0])
    grad_norm = jnp.sqrt(
        squares_all + jnp.sum(gain_grad * gain_grad) + jnp.sum(rel_grad * rel_grad)
    )
    factor = jnp.minimum(1.0, clip_limit / grad_norm)
    new_emb = adam_update(embedding, table_grad * factor, emb_m, emb_v)
    new_gain = adam_update(gains, gain_grad * factor, gain_m, gain_v)
    new_rel = adam_update(rel_bias, rel_grad * factor, rel_m, rel_v)
    new_enc = shampoo_update(enc_w, enc_m, enc_left, enc_right, enc_ahead, enc_products, factor)
    new_dec = shampoo_update(dec_w, dec_m, dec_left, dec_right, dec_ahead, dec_products, factor)
    return (
        loss_sum,
        loss_count,
        grad_norm,
        *new_emb,
        *new_gain,
        *new_rel,
        *new_enc,
        *new_dec,
    )


def solution(mesh):
    in_specs = (
        P(("dp", "fsdp"), "seq"),
        P(("dp", "fsdp"), "seq"),
        P(("dp", "fsdp"), "seq"),
        P(("dp", "fsdp", "seq"), None),
        P(("dp", "fsdp", "seq"), None),
        P(("dp", "fsdp", "seq"), None),
        P("fsdp", None),
        P("fsdp", None),
        P("fsdp", None),
        P(),
        P(),
        P(),
        P(),
        P(),
        P(),
        P("fsdp", None),
        P("fsdp", None),
        P("fsdp", None),
        P("fsdp", None),
        P("fsdp", None),
        P("fsdp", None),
        P("fsdp", None),
        P("fsdp", None),
        P("fsdp", None),
        P("fsdp", None),
        P("fsdp", None),
        P("fsdp", None),
    )
    out_specs = (
        P(),
        P(),
        P(),
        P("fsdp", None),
        P("fsdp", None),
        P("fsdp", None),
        P(),
        P(),
        P(),
        P(),
        P(),
        P(),
        P("fsdp", None),
        P("fsdp", None),
        P("fsdp", None),
        P("fsdp", None),
        P("fsdp", None),
        P("fsdp", None),
        P("fsdp", None),
        P("fsdp", None),
    )
    return jax.shard_map(
        on_device, mesh=mesh, in_specs=in_specs, out_specs=out_specs, check_vma=False
    )
```

```python
import functools
import math

import jax
import jax.numpy as jnp
from jax import lax
from jax.experimental import pallas as pl
from jax.experimental.pallas import tpu as pltpu
from jax.sharding import PartitionSpec as P

D = 768
H = 12
DH = 64
FF = 3072
VOCAB = 32128
NBK = 32
REACH = 128
BLOCK = 192
STEP = 10
PAIR = 2 * BLOCK
TILE = 128
LANES = 128


norm_eps = 1e-06
neg_fill = -1000000000.0
sentinel_offset = 29
beta_first = 0.9
beta_second = 0.999
adam_eps = 1e-08
adam_rate = 0.5
shampoo_rate = 0.01
stat_decay = 0.999
weight_decay = 0.01
clip_limit = 0.05
highest = lax.Precision.HIGHEST


def bucket_edges(buckets, exact, reach):
    edges = list(range(1, exact))
    spread = buckets - exact
    for place in range(spread):
        edges.append(int(math.ceil(exact * (reach / exact) ** (place / spread) - 1e-09)))
    return edges


def offset_buckets(offset, causal):
    if causal:
        distance = jnp.maximum(-offset, 0)
        result = jnp.zeros(offset.shape, jnp.int32)
        edges = bucket_edges(NBK, NBK // 2, REACH)
    else:
        distance = jnp.abs(offset)
        result = jnp.where(offset > 0, NBK // 2, 0).astype(jnp.int32)
        edges = bucket_edges(NBK // 2, NBK // 4, REACH)
    for edge in edges:
        result = result + (distance >= edge).astype(jnp.int32)
    return result


def tile_reach(blocks):
    return min(blocks - 1, 2)


def tile_onehot(blocks, causal):
    reach = tile_reach(blocks)
    place = jnp.arange(TILE, dtype=jnp.int32)
    shift = jnp.arange(-reach, reach + 1, dtype=jnp.int32) * TILE
    offset = shift[:, None, None] + place[None, None, :] - place[None, :, None]
    buckets = offset_buckets(offset, causal).reshape(-1)
    return (jnp.arange(NBK, dtype=jnp.int32)[:, None] == buckets[None, :]).astype(jnp.float32)


def tile_bias(onehot, rel):
    flat = jnp.einsum("nh,np->hp", rel, onehot, precision=highest)
    return flat.reshape(H, -1, TILE, TILE)


def tile_bias_grad(onehot, grads):
    return jnp.einsum("np,hp->nh", onehot, grads.reshape(H, -1), precision=highest)


def head_lanes(half):
    lane = lax.broadcasted_iota(jnp.int32, (1, LANES), 1)
    return (lane // DH) == half


def block_scores(query, keys, bias_ref, half, row, row_segs, key_segs, causal):
    scores = lax.dot_general(query, keys, (((1,), (1,)), ((), ())), preferred_element_type=jnp.float32)
    width = keys.shape[0]
    if bias_ref is not None:
        reach = tile_reach(width // TILE)
        tiles = []
        for column in range(width // TILE):
            tiles.append(bias_ref[half, min(max(column - row, -reach), reach) + reach])
        scores = scores + (jnp.concatenate(tiles, axis=1) if len(tiles) > 1 else tiles[0])
    mask = row_segs == key_segs
    if causal:
        at_row = row * TILE + lax.broadcasted_iota(jnp.int32, scores.shape, 0)
        at_key = lax.broadcasted_iota(jnp.int32, scores.shape, 1)
        mask = mask & (at_row >= at_key)
    scores = jnp.where(mask, scores, neg_fill)
    raised = jnp.exp(scores - jnp.max(scores, axis=-1, keepdims=True))
    return raised * (1.0 / jnp.sum(raised, axis=-1, keepdims=True))


def attend_kernel(q_ref, k_ref, v_ref, *rest, biased, causal):
    bias_ref = rest[0] if biased else None
    sq_ref, sk_ref, o_ref = rest[-3:]
    keys = k_ref[0]
    values = v_ref[0]
    key_segs = sk_ref[0]
    for row in range(q_ref.shape[1] // TILE):
        part = pl.ds(row * TILE, TILE)
        query = q_ref[0, part, :]
        row_segs = sq_ref[0, part, :]
        result = None
        for half in range(2):
            lanes = head_lanes(half)
            probs = block_scores(
                jnp.where(lanes, query, 0), keys, bias_ref, half, row, row_segs, key_segs, causal
            )
            output = jnp.dot(
                probs.astype(jnp.bfloat16), values, preferred_element_type=jnp.float32
            )
            result = output if result is None else jnp.where(lanes, output, result)
        o_ref[0, part, :] = result.astype(jnp.bfloat16)


def attend_back_kernel(q_ref, k_ref, v_ref, g_ref, *rest, biased, causal):
    if biased:
        bias_ref, sq_ref, sk_ref, dq_ref, dk_ref, dv_ref, db_ref = rest
    else:
        sq_ref, sk_ref, dq_ref, dk_ref, dv_ref = rest
        bias_ref = db_ref = None
    keys = k_ref[0]
    values = v_ref[0]
    key_segs = sk_ref[0]
    width = keys.shape[0]
    if biased:

        @pl.when(pl.program_id(1) == 0)
        def _():
            db_ref[...] = jnp.zeros_like(db_ref)

    grad_keys = None
    grad_values = None
    for row in range(q_ref.shape[1] // TILE):
        part = pl.ds(row * TILE, TILE)
        query = q_ref[0, part, :]
        grad_out = g_ref[0, part, :]
        row_segs = sq_ref[0, part, :]
        grad_query = None
        for half in range(2):
            lanes = head_lanes(half)
            own_query = jnp.where(lanes, query, 0)
            own_grad = jnp.where(lanes, grad_out, 0)
            probs = block_scores(
                own_query, keys, bias_ref, half, row, row_segs, key_segs, causal
            )
            grad_probs = lax.dot_general(
                own_grad, values, (((1,), (1,)), ((), ())), preferred_element_type=jnp.float32
            )
            drop = jnp.sum(probs * grad_probs, axis=-1, keepdims=True)
            grad_scores = (probs * (grad_probs - drop)).astype(jnp.bfloat16)
            down = (((0,), (0,)), ((), ()))
            part_values = lax.dot_general(
                probs.astype(jnp.bfloat16), own_grad, down, preferred_element_type=jnp.float32
            )
            part_keys = lax.dot_general(
                grad_scores, own_query, down, preferred_element_type=jnp.float32
            )
            grad_values = part_values if grad_values is None else grad_values + part_values
            grad_keys = part_keys if grad_keys is None else grad_keys + part_keys
            own_grad_query = jnp.dot(grad_scores, keys, preferred_element_type=jnp.float32)
            grad_query = (
                own_grad_query if grad_query is None else jnp.where(lanes, own_grad_query, grad_query)
            )
            if biased:
                wide = grad_scores.astype(jnp.float32)
                reach = tile_reach(width // TILE)
                for column in range(width // TILE):
                    slot = min(max(column - row, -reach), reach) + reach
                    db_ref[half, slot] += wide[:, column * TILE : (column + 1) * TILE]
        dq_ref[0, part, :] = grad_query.astype(jnp.bfloat16)
    dk_ref[0] = grad_keys.astype(jnp.bfloat16)
    dv_ref[0] = grad_values.astype(jnp.bfloat16)


def attention_specs(query, keys, places, bias, row_segs, key_segs):
    q_at, k_at, v_at = places
    rows, nq = row_segs.shape
    nk = key_segs.shape[1]

    def panel(length, first):
        return pl.BlockSpec((1, length, LANES), lambda pair, row: (row, 0, first + pair))

    operands = [query, keys, keys]
    specs = [panel(nq, q_at), panel(nk, k_at), panel(nk, v_at)]
    tail = []
    tail_specs = []
    if bias is not None:
        tail.append(bias)
        tail_specs.append(
            pl.BlockSpec((2,) + bias.shape[1:], lambda pair, row: (pair, 0, 0, 0))
        )
    tail += [row_segs[:, :, None], key_segs[:, None, :]]
    tail_specs += [
        pl.BlockSpec((1, nq, 1), lambda pair, row: (row, 0, 0)),
        pl.BlockSpec((1, 1, nk), lambda pair, row: (row, 0, 0)),
    ]
    return operands, specs, tail, tail_specs, panel


def attention_cost(rows, nq, nk, products):
    return pl.CostEstimate(
        flops=2 * products * rows * H * nq * nk * LANES,
        bytes_accessed=2 * products * rows * (nq + nk) * D,
        transcendentals=rows * H * nq * nk,
    )


def attend(query, keys, places, bias, row_segs, key_segs, causal):
    rows, nq = row_segs.shape
    nk = key_segs.shape[1]
    operands, specs, tail, tail_specs, panel = attention_specs(
        query, keys, places, bias, row_segs, key_segs
    )
    return pl.pallas_call(
        functools.partial(attend_kernel, biased=bias is not None, causal=causal),
        out_shape=jax.ShapeDtypeStruct((rows, nq, D), jnp.bfloat16),
        grid=(H // 2, rows),
        in_specs=specs + tail_specs,
        out_specs=panel(nq, 0),
        cost_estimate=attention_cost(rows, nq, nk, 2),
        compiler_params=pltpu.CompilerParams(vmem_limit_bytes=32 << 20),
    )(*operands, *tail)


def attend_back(query, keys, places, bias, row_segs, key_segs, causal, grad_out):
    rows, nq = row_segs.shape
    nk = key_segs.shape[1]
    operands, specs, tail, tail_specs, panel = attention_specs(
        query, keys, places, bias, row_segs, key_segs
    )
    outs = [
        jax.ShapeDtypeStruct((rows, nq, D), jnp.bfloat16),
        jax.ShapeDtypeStruct((rows, nk, D), jnp.bfloat16),
        jax.ShapeDtypeStruct((rows, nk, D), jnp.bfloat16),
    ]
    out_specs = [panel(nq, 0), panel(nk, 0), panel(nk, 0)]
    if bias is not None:
        outs.append(jax.ShapeDtypeStruct(bias.shape, jnp.float32))
        out_specs.append(
            pl.BlockSpec((2,) + bias.shape[1:], lambda pair, row: (pair, 0, 0, 0))
        )
    return pl.pallas_call(
        functools.partial(attend_back_kernel, biased=bias is not None, causal=causal),
        out_shape=outs,
        grid=(H // 2, rows),
        in_specs=specs + [panel(nq, 0)] + tail_specs,
        out_specs=out_specs,
        cost_estimate=attention_cost(rows, nq, nk, 5),
        compiler_params=pltpu.CompilerParams(vmem_limit_bytes=32 << 20),
    )(*operands, grad_out, *tail)


def layer_shapes(decoder):
    if decoder:
        return [(D, 3 * D), (D, D), (D, D), (D, 2 * D), (D, D), (D, FF), (FF, D)]
    return [(D, 3 * D), (D, D), (D, FF), (FF, D)]


def as_blocks(flat):
    if flat.ndim == 3:
        return flat
    return flat.reshape(flat.shape[0], BLOCK, BLOCK)


def as_rows(blocks):
    return blocks.reshape(blocks.shape[0], BLOCK * BLOCK)


def as_pairs(blocks):
    amount = blocks.shape[0] // 2
    split = blocks.reshape(amount, 2, BLOCK, BLOCK)
    return jnp.concatenate([split[:, 0], split[:, 1]], axis=-1)


def unpack_kernel(pairs_ref, out_ref):
    across = out_ref.shape[1] // PAIR
    for row in range(out_ref.shape[0] // BLOCK):
        for column in range(across):
            out_ref[row * BLOCK : (row + 1) * BLOCK, column * PAIR : (column + 1) * PAIR] = (
                pairs_ref[row * across + column]
            )


def matrices_of(pairs, shapes):
    matrix_list = []
    place = 0
    for height, breadth in shapes:
        group = 2 * breadth // PAIR
        first = place // group
        matrix_list.append(
            pl.pallas_call(
                unpack_kernel,
                out_shape=jax.ShapeDtypeStruct((height, breadth), pairs.dtype),
                grid=(height // PAIR,),
                in_specs=[
                    pl.BlockSpec(
                        (group, BLOCK, PAIR), lambda step, first=first: (first + step, 0, 0)
                    )
                ],
                out_specs=pl.BlockSpec((PAIR, breadth), lambda step: (step, 0)),
                cost_estimate=pl.CostEstimate(
                    flops=0, bytes_accessed=4 * height * breadth, transcendentals=0
                ),
                compiler_params=pltpu.CompilerParams(vmem_limit_bytes=32 << 20),
            )(pairs)
        )
        place += group * (height // PAIR)
    return matrix_list


def weight_grad_kernel(x_ref, g_ref, *rest):
    out_ref = rest[-1]
    across = out_ref.shape[0] // 2
    for column in range(across):
        product = lax.dot_general(
            x_ref[...],
            g_ref[:, column * PAIR : (column + 1) * PAIR],
            (((0,), (0,)), ((), ())),
            preferred_element_type=jnp.float32,
        )
        product = product.astype(jnp.bfloat16)
        out_ref[column] = product[:BLOCK]
        out_ref[across + column] = product[BLOCK:]


def weight_grads(operands):
    total = sum(x.shape[-1] * g.shape[-1] for x, g in operands) // (BLOCK * PAIR)
    pairs = None
    place = 0
    for x, g in operands:
        x = x.reshape(-1, x.shape[-1])
        g = g.reshape(-1, g.shape[-1])
        count, height = x.shape
        breadth = g.shape[1]
        group = 2 * breadth // PAIR
        first = place // group
        given = [] if pairs is None else [pairs]
        pairs = pl.pallas_call(
            weight_grad_kernel,
            out_shape=jax.ShapeDtypeStruct((total, BLOCK, PAIR), jnp.bfloat16),
            grid=(height // PAIR,),
            in_specs=[
                pl.BlockSpec((count, PAIR), lambda step: (0, step)),
                pl.BlockSpec((count, breadth), lambda step: (0, 0)),
            ]
            + [pl.BlockSpec(memory_space=pl.ANY)] * len(given),
            out_specs=pl.BlockSpec(
                (group, BLOCK, PAIR), lambda step, first=first: (first + step, 0, 0)
            ),
            input_output_aliases={2: 0} if given else {},
            cost_estimate=pl.CostEstimate(
                flops=2 * count * height * breadth,
                bytes_accessed=2 * (count * (height + breadth) + height * breadth),
                transcendentals=0,
            ),
            compiler_params=pltpu.CompilerParams(vmem_limit_bytes=40 << 20),
        )(x, g, *given)
        place += group * (height // PAIR)
    return pairs


def split_float(values):
    high = values.astype(jnp.bfloat16)
    return high, (values - high.astype(jnp.float32)).astype(jnp.bfloat16)


def full_product(left, right, contract):
    def part(first, second):
        return lax.dot_general(
            first, second, (contract, ((), ())), preferred_element_type=jnp.float32
        )

    return (
        part(left[0], right[1]) + part(left[1], right[0]) + part(left[0], right[0])
    )


ROW_COL = ((1,), (0,))
ROW_ROW = ((1,), (1,))
COL_COL = ((0,), (0,))


def turned_product(left_root, middle, right_root):
    shaped = full_product(split_float(left_root), middle, ROW_COL)
    return full_product(split_float(shaped), split_float(right_root), ROW_COL)


def ahead_kernel(m_ref, lr_ref, rr_ref, o_ref):
    for place in range(m_ref.shape[0]):
        o_ref[place] = turned_product(lr_ref[place], split_float(m_ref[place]), rr_ref[place])


def products_kernel(g_ref, lr_ref, rr_ref, g_out, turned_out, left_out, right_out):
    for place in range(2):
        block = g_ref[0, :, place * BLOCK : (place + 1) * BLOCK]
        g_out[place] = block
        halves = split_float(block)
        turned_out[place] = turned_product(lr_ref[place], halves, rr_ref[place])
        left_out[place] = full_product(halves, halves, ROW_ROW)
        right_out[place] = full_product(halves, halves, COL_COL)


def block_cost(amount, products, arrays):
    return pl.CostEstimate(
        flops=6 * products * amount * BLOCK**3,
        bytes_accessed=4 * arrays * amount * BLOCK * BLOCK,
        transcendentals=0,
    )


def shampoo_ahead(moment, left_root, right_root):
    blocks = [as_blocks(member) for member in (moment, left_root, right_root)]
    amount = moment.shape[0]
    spec = pl.BlockSpec((2, BLOCK, BLOCK), lambda pair: (pair, 0, 0))
    ahead = pl.pallas_call(
        ahead_kernel,
        out_shape=jax.ShapeDtypeStruct((amount, BLOCK, BLOCK), jnp.float32),
        grid=(amount // 2,),
        in_specs=[spec] * 3,
        out_specs=spec,
        cost_estimate=block_cost(amount, 2, 4),
        compiler_params=pltpu.CompilerParams(vmem_limit_bytes=52 << 20),
    )(*blocks)
    return ahead, blocks[1], blocks[2]


def shampoo_products(pairs, left_root, right_root):
    amount = left_root.shape[0]
    spec = pl.BlockSpec((2, BLOCK, BLOCK), lambda pair: (pair, 0, 0))
    results = pl.pallas_call(
        products_kernel,
        out_shape=[jax.ShapeDtypeStruct((amount, BLOCK, BLOCK), jnp.float32)] * 4,
        grid=(amount // 2,),
        in_specs=[pl.BlockSpec((1, BLOCK, PAIR), lambda pair: (pair, 0, 0)), spec, spec],
        out_specs=[spec] * 4,
        cost_estimate=block_cost(amount, 4, 7),
        compiler_params=pltpu.CompilerParams(vmem_limit_bytes=52 << 20),
    )(pairs, left_root, right_root)
    return [as_rows(result) for result in results]


def project(left, right):
    return jnp.matmul(left, right, preferred_element_type=jnp.float32)


def project_back(left, right):
    return jnp.einsum("btf,df->btd", left, right, preferred_element_type=jnp.float32)


def rms(values, gain):
    return values * lax.rsqrt(jnp.mean(values * values, axis=-1, keepdims=True) + norm_eps) * gain


def rms_back(values, gain, grad_out):
    inverse = lax.rsqrt(jnp.mean(values * values, axis=-1, keepdims=True) + norm_eps)
    normed = values * inverse
    grad_gain = jnp.sum(grad_out * normed, axis=(0, 1))
    grad_normed = grad_out * gain
    grad_values = inverse * (
        grad_normed - normed * jnp.mean(grad_normed * normed, axis=-1, keepdims=True)
    )
    return (grad_values, grad_gain)


def ff_forward(hidden, gain, w_in, w_down):
    normed = rms(hidden, gain).astype(jnp.bfloat16)
    inner = project(normed, w_in)
    active = jax.nn.gelu(inner).astype(jnp.bfloat16)
    return (hidden + project(active, w_down), (normed, inner, active))


def ff_back(hidden, gain, w_in, w_down, cache, grad_out):
    normed, inner, active = cache
    branch_grad = grad_out.astype(jnp.bfloat16)
    grad_active = project_back(branch_grad, w_down)
    unused, gelu_back = jax.vjp(jax.nn.gelu, inner)
    grad_inner = gelu_back(grad_active)[0].astype(jnp.bfloat16)
    grad_part, grad_gain = rms_back(hidden, gain, project_back(grad_inner, w_in))
    return (grad_out + grad_part, grad_gain, (normed, grad_inner), (active, branch_grad))


def table_rows(table, token_ids, vocab_first):
    local_ids = token_ids - vocab_first
    inside = (local_ids >= 0) & (local_ids < table.shape[0])
    picked = jnp.take(table, jnp.clip(local_ids, 0, table.shape[0] - 1), axis=0)
    return jnp.where(inside[..., None], picked, jnp.zeros((), table.dtype))


def table_grads(grads, token_ids, vocab_first, dense):
    vocab_local = dense.shape[0]
    local_ids = token_ids.reshape(-1) - vocab_first
    inside = (local_ids >= 0) & (local_ids < vocab_local)
    slots = jnp.where(inside, local_ids, vocab_local)
    return dense.at[slots].add(grads.astype(jnp.float32), mode="drop")


REPLICAS = ("dp", "seq")
EVERYWHERE = ("fsdp", "dp", "seq")


def replica_rank():
    return lax.axis_index("dp") * lax.axis_size("seq") + lax.axis_index("seq")


def replica_count():
    return lax.axis_size("dp") * lax.axis_size("seq")


def paired_mesh():
    return (
        lax.axis_size("dp") == 2 and lax.axis_size("seq") == 2 and lax.axis_size("fsdp") % 2 == 0
    )


def swap(values, axis):
    size = lax.axis_size(axis)
    return lax.ppermute(values, axis, [(place, place ^ 1) for place in range(size)])


def shift(values, step):
    size = lax.axis_size("fsdp")
    moves = [
        (place, place + 2 * step) for place in range(size) if 0 <= place + 2 * step < size
    ]
    return lax.ppermute(values, "fsdp", moves)


def choose(flag, if_set, if_clear):
    return jnp.where(flag == 1, if_set, if_clear)


def pick(values, place, axis):
    return lax.dynamic_index_in_dim(values, place, axis, False)


def narrow(values):
    return values.astype(jnp.bfloat16)


def wide(values):
    return values.astype(jnp.float32)


def placed(relative, first, second):
    def at(row, column):
        here = choose(second, relative[row][1 - column], relative[row][column])
        there = choose(second, relative[1 - row][1 - column], relative[1 - row][column])
        return choose(first, there, here)

    return [[at(0, 0), at(0, 1)], [at(1, 0), at(1, 1)]]


def own_weights(master):
    share = master.shape[0] // replica_count()
    if master.shape[0] % (2 * replica_count()) == 0:
        master = lax.dynamic_slice_in_dim(master, replica_rank() * share, share, 0)
    return as_pairs(as_blocks(master.astype(jnp.bfloat16)))


def hold(values):
    return lax.optimization_barrier(values)


def chip_groups():
    return [list(range(core, lax.axis_size("fsdp"), 2)) for core in range(2)]


def along_line(own):
    n_chips = lax.axis_size("fsdp") // 2
    copies = jnp.broadcast_to(own[None], (n_chips,) + own.shape)
    return lax.all_to_all(copies, "fsdp", 0, 0, axis_index_groups=chip_groups(), tiled=True)


def exchange_near(line):
    mid = BLOCK // 2
    upper, lower = (line[:, :, :mid], line[:, :, mid:])
    return [upper, lower, swap(upper, "seq"), swap(lower, "dp")]


def exchange_far(near):
    upper, lower, upper_half, lower_side = near
    return [
        swap(jnp.stack([lower, lower_side]), "seq"),
        swap(jnp.stack([upper, upper_half]), "dp"),
    ]


def swap_cores(pieces):
    return [swap(piece, "fsdp") for piece in pieces]


def assemble_kernel(place_ref, *refs, shapes):
    outs = refs[12 : 12 + len(shapes)]
    buffer, in_sems, out_sems = refs[12 + len(shapes) :]
    core, side, half = (place_ref[0], place_ref[1], place_ref[2])
    n_chips, quarter, mid, _ = refs[0].shape
    copies = []
    for other in range(2):
        upper, lower, upper_half, lower_side, by_half, by_side = refs[6 * other : 6 * other + 6]
        pieces = [
            (upper, lower),
            (upper_half, by_half.at[0]),
            (by_side.at[0], lower_side),
            (by_side.at[1], by_half.at[1]),
        ]
        for place, both in enumerate(pieces):
            owner = ((side ^ (place // 2)) * 2 + (half ^ (place % 2))) * quarter
            for low, piece in enumerate(both):
                for chip in range(n_chips):
                    first = (2 * chip + (core ^ other)) * (4 * quarter) + owner
                    copies.append(
                        pltpu.make_async_copy(
                            piece.at[chip],
                            buffer.at[pl.ds(first, quarter), pl.ds(low * mid, mid), :],
                            in_sems.at[len(copies)],
                        )
                    )
    for copy in copies:
        copy.start()
    for copy in copies:
        copy.wait()
    copies = []
    for out_ref, (height, breadth) in zip(outs, shapes):
        for row in range(height // BLOCK):
            for column in range(breadth // PAIR):
                copies.append(
                    pltpu.make_async_copy(
                        buffer.at[len(copies)],
                        out_ref.at[pl.ds(row * BLOCK, BLOCK), pl.ds(column * PAIR, PAIR)],
                        out_sems.at[len(copies)],
                    )
                )
    for copy in copies:
        copy.start()
    for copy in copies:
        copy.wait()


def assembled(pieces, shapes):
    n_chips, quarter, mid, _ = pieces[0].shape
    total = 8 * n_chips * quarter
    return pl.pallas_call(
        functools.partial(assemble_kernel, shapes=shapes),
        out_shape=[jax.ShapeDtypeStruct(shape, jnp.bfloat16) for shape in shapes],
        in_specs=[pl.BlockSpec(memory_space=pltpu.SMEM)]
        + [pl.BlockSpec(memory_space=pl.ANY)] * len(pieces),
        out_specs=[pl.BlockSpec(memory_space=pl.ANY)] * len(shapes),
        scratch_shapes=[
            pltpu.VMEM((total, BLOCK, PAIR), jnp.bfloat16),
            pltpu.SemaphoreType.DMA((16 * n_chips,)),
            pltpu.SemaphoreType.DMA((total,)),
        ],
        cost_estimate=pl.CostEstimate(
            flops=0, bytes_accessed=4 * total * BLOCK * PAIR, transcendentals=0
        ),
        compiler_params=pltpu.CompilerParams(vmem_limit_bytes=30 << 20),
    )(own_place(), *pieces)


def gathered_weights(pairs, amount):
    split = amount % (2 * replica_count()) == 0
    return lax.all_gather(pairs, EVERYWHERE if split else "fsdp", axis=0, tiled=True)


def own_place():
    return jnp.stack(
        [lax.axis_index("fsdp") % 2, lax.axis_index("dp"), lax.axis_index("seq")]
    ).astype(jnp.int32)


def fold_kernel(place_ref, own_ref, got_ref, keep_up, send_up, keep_low, send_low):
    total = wide(own_ref[0]) + wide(got_ref[0])
    mid = BLOCK // 2
    upper, lower = (total[:, :mid], total[:, mid:])
    other_side, other_half = (pl.program_id(1), pl.program_id(2))

    @pl.when(other_half == 0)
    def _():
        keep_up[0, 0] = upper

    @pl.when(other_half == 1)
    def _():
        send_up[0, 0] = narrow(upper)

    @pl.when(other_side == 0)
    def _():
        keep_low[0, 0] = lower

    @pl.when(other_side == 1)
    def _():
        send_low[0, 0] = narrow(lower)


def fold_cores(pairs, got, n_chips, quarter):
    mid = BLOCK // 2

    def quarter_of(place, other_side, other_half):
        return (place[1] ^ other_side) * 2 + (place[2] ^ other_half)

    whole = (1, quarter, BLOCK, PAIR)
    part = (1, 1, quarter, mid, PAIR)
    halves = (n_chips, 2, quarter, mid, PAIR)

    def up_at(chip, other_side, other_half, place):
        return (chip, place[1] ^ other_side, 0, 0, 0)

    def keep_low_at(chip, other_side, other_half, place):
        return (chip, jnp.where(other_side == 0, place[2] ^ other_half, place[2] ^ 1), 0, 0, 0)

    def send_low_at(chip, other_side, other_half, place):
        return (chip, jnp.where(other_side == 1, place[2] ^ other_half, place[2]), 0, 0, 0)

    return pl.pallas_call(
        fold_kernel,
        out_shape=[
            jax.ShapeDtypeStruct(halves, kind)
            for kind in (jnp.float32, jnp.bfloat16, jnp.float32, jnp.bfloat16)
        ],
        grid_spec=pltpu.PrefetchScalarGridSpec(
            num_scalar_prefetch=1,
            grid=(n_chips, 2, 2),
            in_specs=[
                pl.BlockSpec(
                    whole,
                    lambda chip, side, half, place: (
                        (2 * chip + place[0]) * 4 + quarter_of(place, side, half),
                        0,
                        0,
                        0,
                    ),
                ),
                pl.BlockSpec(
                    whole,
                    lambda chip, side, half, place: (
                        chip * 4 + quarter_of(place, side, half),
                        0,
                        0,
                        0,
                    ),
                ),
            ],
            out_specs=[
                pl.BlockSpec(part, up_at),
                pl.BlockSpec(part, up_at),
                pl.BlockSpec(part, keep_low_at),
                pl.BlockSpec(part, send_low_at),
            ],
        ),
        cost_estimate=pl.CostEstimate(
            flops=pairs.size // 2, bytes_accessed=5 * pairs.size, transcendentals=0
        ),
        compiler_params=pltpu.CompilerParams(vmem_limit_bytes=32 << 20),
    )(
        own_place(),
        pairs.reshape(-1, quarter, BLOCK, PAIR),
        got.reshape(-1, quarter, BLOCK, PAIR),
    )


def sum_replicas(values):
    values = values + swap(values, "seq")
    return values + swap(values, "dp")


def sum_line(values):
    size = lax.axis_size("fsdp")
    if size & (size - 1):
        return lax.psum(values, "fsdp")
    step = 1
    while step < size:
        moves = [(place, place ^ step) for place in range(size)]
        values = values + lax.ppermute(values, "fsdp", moves)
        step *= 2
    return values


def summed_blocks(pairs):
    shard = lax.psum_scatter(wide(pairs), "fsdp", scatter_dimension=0, tiled=True)
    return lax.psum(shard, REPLICAS)


def swap_halves(pairs):
    n_chips = lax.axis_size("fsdp") // 2
    core = lax.axis_index("fsdp") % 2
    split = pairs.reshape(n_chips, 2, -1, BLOCK, PAIR)
    return swap(pick(split, 1 - core, 1), "fsdp")


def fold_blocks(pairs, got):
    n_chips = lax.axis_size("fsdp") // 2
    return fold_cores(pairs, got, n_chips, pairs.shape[0] // (8 * n_chips))


def near_sums(folded):
    return [folded[0], swap(folded[1], "seq"), folded[2], swap(folded[3], "dp")]


def far_sums(near):
    side, half = (lax.axis_index("dp"), lax.axis_index("seq"))
    upper = near[0] + wide(near[1])
    lower = near[2] + wide(near[3])
    return [
        pick(upper, side, 1),
        swap(narrow(pick(upper, 1 - side, 1)), "dp"),
        pick(lower, half, 1),
        swap(narrow(pick(lower, 1 - half, 1)), "seq"),
    ]


def line_sums(far):
    line = narrow(jnp.concatenate([far[0] + wide(far[1]), far[2] + wide(far[3])], axis=2))
    return lax.all_to_all(line, "fsdp", 0, 0, axis_index_groups=chip_groups(), tiled=True)


def line_total(arrived):
    return jnp.sum(wide(arrived), axis=0)


def share_blocks(own):
    return wide(lax.all_gather(narrow(own), REPLICAS, axis=0, tiled=True))


def window_rows(half_rows):
    return -(-half_rows // 16) * 8


def half_lanes(values, place):
    return lax.dynamic_slice_in_dim(values, place * (D // 2), D // 2, 1)


SCALE_ROWS = 8


def scale_of(power):
    return jnp.exp2(power.astype(jnp.float32))


def message_of(values, power):
    mark = jnp.full((SCALE_ROWS, values.shape[1]), power, jnp.float16)
    return jnp.concatenate([values.astype(jnp.float16), mark], axis=0)


def scaled_swap(message, axis):
    got = swap(message, axis)
    return got[:-SCALE_ROWS], got[-1, 0].astype(jnp.float32)


def joined(values, power, got):
    others, other_power = got
    least = jnp.minimum(power, other_power)
    return (
        values * scale_of(least - power) + wide(others) * scale_of(least - other_power),
        least,
    )


def near_parts(partial, bound):
    side, half = (lax.axis_index("dp"), lax.axis_index("seq"))
    half_rows = partial.shape[0] // 2
    window = window_rows(half_rows)
    power = jnp.clip(12.0 - jnp.ceil(jnp.log2(jnp.maximum(bound, 1e-37))), -120.0, 120.0)

    def rows_of(first, place):
        start = first + place * (half_rows - window)
        return lax.dynamic_slice_in_dim(partial, start, window, 0) * scale_of(power)

    return [
        rows_of(0, half),
        message_of(rows_of(0, 1 - half), power),
        rows_of(half_rows, side),
        message_of(rows_of(half_rows, 1 - side), power),
        power,
    ]


def near_table(parts):
    top, top_sent, low, low_sent, power = parts
    return [top, scaled_swap(top_sent, "seq"), low, scaled_swap(low_sent, "dp"), power]


def far_table(near):
    side, half = (lax.axis_index("dp"), lax.axis_index("seq"))
    top, top_power = joined(near[0], near[4], near[1])
    low, low_power = joined(near[2], near[4], near[3])
    return [
        half_lanes(top, side),
        top_power,
        scaled_swap(message_of(half_lanes(top, 1 - side), top_power), "dp"),
        half_lanes(low, half),
        low_power,
        scaled_swap(message_of(half_lanes(low, 1 - half), low_power), "seq"),
    ]


def table_total(far):
    top, power = joined(*far[:3])
    low, _ = joined(*far[3:])
    return top, low, scale_of(power)


def table_squares(top, low, half_rows):
    side, half = (lax.axis_index("dp"), lax.axis_index("seq"))
    again = 2 * window_rows(half_rows) - half_rows
    row = lax.broadcasted_iota(jnp.int32, (top.shape[0], 1), 0)
    return jnp.sum(jnp.where(row >= again * half, top * top, 0.0)) + jnp.sum(
        jnp.where(row >= again * side, low * low, 0.0)
    )


def share_near(top, low):
    top = hold(top.astype(jnp.float16))
    low = hold(low.astype(jnp.float16))
    return [jnp.stack([top, swap(top, "dp")]), jnp.stack([low, swap(low, "seq")])]


def share_far(near):
    return [swap(near[0], "seq"), swap(near[1], "dp")]


def placed_table(near, far, scale, half_rows):
    side, half = (lax.axis_index("dp"), lax.axis_index("seq"))
    again = 2 * window_rows(half_rows) - half_rows
    top_all = placed([near[0], far[0]], half, side)
    low_all = placed([near[1], far[1]], side, half)
    rows = []
    for first, second in (top_all, low_all):
        rows.append(jnp.concatenate(first, axis=1))
        rows.append(jnp.concatenate(second, axis=1)[again:])
    return wide(jnp.concatenate(rows, axis=0)) * (1.0 / scale)


def adam_update(weight, gradient, moment, second):
    moment = beta_first * moment + (1 - beta_first) * gradient
    second = beta_second * second + (1 - beta_second) * gradient * gradient
    corrected = moment / (1 - beta_first**STEP)
    scaled = second / (1 - beta_second**STEP)
    weight = weight - adam_rate * (
        corrected / (jnp.sqrt(scaled) + adam_eps) + weight_decay * weight
    )
    return (weight, moment, second)


def shampoo_update(weight, moment, left, right, ahead, products, factor):
    gradient, turned, left_square, right_square = products
    direction = beta_first * ahead + ((1 - beta_first) * factor) * turned
    square = (1 - stat_decay) * factor * factor
    return (
        weight - shampoo_rate * (direction + weight_decay * weight),
        beta_first * moment + ((1 - beta_first) * factor) * gradient,
        stat_decay * left + square * left_square,
        stat_decay * right + square * right_square,
    )


def on_device(
    enc_ids,
    span_mask,
    segments,
    targets,
    loss_weights,
    target_segments,
    embedding,
    emb_m,
    emb_v,
    gains,
    gain_m,
    gain_v,
    rel_bias,
    rel_m,
    rel_v,
    enc_w,
    enc_m,
    enc_left,
    enc_right,
    enc_lroot,
    enc_rroot,
    dec_w,
    dec_m,
    dec_left,
    dec_right,
    dec_lroot,
    dec_rroot,
):
    fsdp_rank = lax.axis_index("fsdp")
    seq_rank = lax.axis_index("seq")
    n_fsdp = lax.axis_size("fsdp")
    n_seq = lax.axis_size("seq")
    half_len = enc_ids.shape[1]
    rows, dec_len = targets.shape
    enc_len = half_len * n_seq
    enc_in = jnp.where(span_mask == 1, VOCAB - sentinel_offset, enc_ids)
    dec_in = jnp.concatenate([jnp.zeros((rows, 1), jnp.int32), targets[:, :-1]], axis=1)

    paired = paired_mesh()

    halves = jnp.stack([enc_in, segments]).reshape(2, n_seq, rows, half_len)
    enc_own, dec_own, table = (own_weights(enc_w), own_weights(dec_w), narrow(embedding))
    if n_seq == 2:
        kept = pick(halves, seq_rank, 1)
        got = swap(pick(halves, 1 - seq_rank, 1), "seq")
        got, enc_own, dec_own = hold((got, enc_own, dec_own))
        parts = (choose(seq_rank, got, kept), choose(seq_rank, kept, got))
        row_words = jnp.stack(parts, axis=2)
    else:
        row_words = lax.all_to_all(halves, "seq", 1, 1, tiled=True).transpose(0, 2, 1, 3)
    row_words = row_words.reshape(2, rows, enc_len)
    row_segments = row_words[1]
    message = jnp.concatenate(
        [
            row_words[0].reshape(-1),
            dec_in.reshape(-1),
            targets.reshape(-1),
            loss_weights.reshape(-1),
        ]
    ).reshape(1, -1)
    enc_pairs = gathered_weights(enc_own, enc_w.shape[0])
    gathered = lax.all_gather(message, "fsdp", axis=0, tiled=True)
    gathered, dec_own = hold((gathered, dec_own))
    if paired:
        dec_line = along_line(dec_own)
    all_enc = gathered[:, : rows * enc_len]
    rest = gathered[:, rows * enc_len :].reshape(n_fsdp, 3, rows * dec_len)
    all_dec, all_targets, all_weights = (rest[:, 0], rest[:, 1], rest[:, 2])
    all_tokens = jnp.concatenate([all_enc, all_dec], axis=1)
    vocab_local = table.shape[0]
    vocab_first = fsdp_rank * vocab_local
    found = table_rows(table, all_tokens, vocab_first)
    enc_roots = (enc_m, enc_lroot, enc_rroot)
    dec_roots = (dec_m, dec_lroot, dec_rroot)
    found, enc_roots = hold((found, enc_roots))
    enc_ready = shampoo_ahead(*enc_roots)
    enc_ready, dec_roots = hold((enc_ready, dec_roots))
    dec_ready = shampoo_ahead(*dec_roots)
    enc_onehot = tile_onehot(enc_len // TILE, False)
    dec_onehot = tile_onehot(dec_len // TILE, True)
    if paired:
        found, enc_pairs, enc_ready, dec_line, rel_tiles, dec_ready = hold(
            (found, enc_pairs, enc_ready, dec_line, rel_bias, dec_ready)
        )
    else:
        found, enc_pairs, rel_tiles = hold((found, enc_pairs, rel_bias))
    looked_up = lax.psum_scatter(found, "fsdp", scatter_dimension=0, tiled=True).reshape(-1, D)
    enc_mats = matrices_of(enc_pairs, layer_shapes(False))
    enc_bias = tile_bias(enc_onehot, rel_tiles[0])
    dec_bias = tile_bias(dec_onehot, rel_tiles[1])
    if paired:
        dec_near = exchange_near(dec_line)
        enc_ahead, dec_ahead = (as_rows(enc_ready[0]), as_rows(dec_ready[0]))
        dec_near, enc_mats, enc_bias, dec_bias, enc_ahead = hold(
            (dec_near, enc_mats, enc_bias, dec_bias, enc_ahead)
        )
        dec_far = exchange_far(dec_near)
        dec_cores = swap_cores(dec_near)
        looked_up, dec_far, dec_cores, dec_ahead = hold((looked_up, dec_far, dec_cores, dec_ahead))
        dec_cores = dec_cores + swap_cores(dec_far)
    else:
        dec_mats = matrices_of(gathered_weights(dec_own, dec_w.shape[0]), layer_shapes(True))
        enc_ahead, dec_ahead = (as_rows(enc_ready[0]), as_rows(dec_ready[0]))
    hidden0 = looked_up[: rows * enc_len].reshape(rows, enc_len, D).astype(jnp.float32)
    state0 = looked_up[rows * enc_len :].reshape(rows, dec_len, D).astype(jnp.float32)

    tile_at = D // LANES
    self_places = (0, tile_at, 2 * tile_at)
    cross_places = (0, 0, tile_at)

    normed0 = rms(hidden0, gains[0]).astype(jnp.bfloat16)
    enc_qkv = project(normed0, enc_mats[0]).astype(jnp.bfloat16)
    enc_attended = attend(
        enc_qkv, enc_qkv, self_places, enc_bias, row_segments, row_segments, False
    )
    hidden1 = hidden0 + project(enc_attended, enc_mats[1])
    hidden2, enc_cache = ff_forward(hidden1, gains[1], enc_mats[2], enc_mats[3])
    encoded = rms(hidden2, gains[2]).astype(jnp.bfloat16)
    if paired:
        encoded, dec_cores = hold((encoded, dec_cores))
        dec_mats = assembled(dec_near + dec_far + dec_cores, layer_shapes(True))
    pairs = project(encoded, dec_mats[3]).astype(jnp.bfloat16)

    normed3 = rms(state0, gains[3]).astype(jnp.bfloat16)
    self_qkv = project(normed3, dec_mats[0]).astype(jnp.bfloat16)
    self_attended = attend(
        self_qkv, self_qkv, self_places, dec_bias, target_segments, target_segments, True
    )
    state1 = state0 + project(self_attended, dec_mats[1])
    normed4 = rms(state1, gains[4]).astype(jnp.bfloat16)
    cross_query = project(normed4, dec_mats[2]).astype(jnp.bfloat16)
    cross_attended = attend(
        cross_query, pairs, cross_places, None, target_segments, row_segments, False
    )
    state2 = state1 + project(cross_attended, dec_mats[4])
    state3, dec_cache = ff_forward(state2, gains[5], dec_mats[5], dec_mats[6])
    out_scale = D ** (-0.5)
    final = (rms(state3, gains[6]) * out_scale).astype(jnp.bfloat16)

    all_final = lax.all_gather(final.reshape(rows * dec_len, D), "fsdp", axis=0, tiled=True)
    logits = jnp.einsum("nd,vd->nv", all_final, table, preferred_element_type=jnp.float32)
    local_ids = all_targets.reshape(-1) - vocab_first
    target_hot = local_ids[:, None] == jnp.arange(vocab_local, dtype=jnp.int32)[None, :]
    local_top = jnp.max(logits, axis=1)
    local_sum = jnp.sum(jnp.exp(logits - local_top[:, None]), axis=1)
    local_pick = jnp.sum(jnp.where(target_hot, logits, 0.0), axis=1)
    stats = lax.all_gather(
        jnp.stack([local_top, local_sum, local_pick])[None], "fsdp", axis=0, tiled=True
    )
    top_all = jnp.max(stats[:, 0], axis=0)
    sum_all = jnp.sum(stats[:, 1] * jnp.exp(stats[:, 0] - top_all), axis=0)
    pick_all = jnp.sum(stats[:, 2], axis=0)
    lse = top_all + jnp.log(sum_all)
    token_weights = all_weights.reshape(-1).astype(jnp.float32)
    group_loss = jnp.sum(token_weights * (lse - pick_all))
    grad_logits = (
        token_weights[:, None] * (jnp.exp(logits - lse[:, None]) - target_hot.astype(jnp.float32))
    ).astype(jnp.bfloat16)
    grad_final = lax.psum_scatter(
        jnp.dot(grad_logits, table, preferred_element_type=jnp.float32),
        "fsdp",
        scatter_dimension=0,
        tiled=True,
    ).reshape(rows, dec_len, D)
    count = jnp.sum(all_weights).astype(jnp.float32)
    if paired:
        count, _ = hold((count, group_loss))
        count = count + swap(count, "seq")
        count = count + swap(count, "dp")
    else:
        count = lax.psum(count, REPLICAS)
    share = 1.0 / jnp.maximum(count, 1.0)
    dense_grad = jnp.einsum("nv,nd->vd", grad_logits, all_final, preferred_element_type=jnp.float32)
    grad_final, dense_grad, dense_bound, share = hold(
        (grad_final, dense_grad, jnp.max(jnp.abs(dense_grad)), share)
    )

    grad_state3, gain_six = rms_back(state3, gains[6], grad_final * out_scale)
    grad_state2, gain_five, dec_in_grad, dec_down_grad = ff_back(
        state2, gains[5], dec_mats[5], dec_mats[6], dec_cache, grad_state3
    )
    branch_grad = grad_state2.astype(jnp.bfloat16)
    cross_out_grad = (cross_attended, branch_grad)
    grad_cross = project_back(branch_grad, dec_mats[4]).astype(jnp.bfloat16)
    grad_cq, grad_ck, grad_cv = attend_back(
        cross_query, pairs, cross_places, None, target_segments, row_segments, False, grad_cross
    )
    grad_pairs = jnp.concatenate([grad_ck, grad_cv], axis=-1)
    cross_query_grad = (normed4, grad_cq)
    grad_state1_part, gain_four = rms_back(state1, gains[4], project_back(grad_cq, dec_mats[2]))
    grad_state1 = grad_state2 + grad_state1_part
    cross_pair_grad = (encoded, grad_pairs)
    grad_encoded = project_back(grad_pairs, dec_mats[3])
    branch_grad = grad_state1.astype(jnp.bfloat16)
    self_out_grad = (self_attended, branch_grad)
    grad_self = project_back(branch_grad, dec_mats[1]).astype(jnp.bfloat16)
    grad_sq, grad_sk, grad_sv, dec_bias_grad = attend_back(
        self_qkv, self_qkv, self_places, dec_bias, target_segments, target_segments, True, grad_self
    )
    grad_sqkv = jnp.concatenate([grad_sq, grad_sk, grad_sv], axis=-1)
    self_qkv_grad = (normed3, grad_sqkv)
    grad_state0_part, gain_three = rms_back(state0, gains[3], project_back(grad_sqkv, dec_mats[0]))
    grad_state0 = grad_state1 + grad_state0_part
    decoder_portion = weight_grads(
        [
            self_qkv_grad,
            self_out_grad,
            cross_query_grad,
            cross_pair_grad,
            cross_out_grad,
            dec_in_grad,
            dec_down_grad,
        ]
    )
    if paired:
        dec_got = swap_halves(decoder_portion)

    grad_hidden2, gain_two = rms_back(hidden2, gains[2], grad_encoded)
    grad_hidden1, gain_one, encoder_input_gradient, encoder_down_gradient = ff_back(
        hidden1, gains[1], enc_mats[2], enc_mats[3], enc_cache, grad_hidden2
    )
    branch_grad = grad_hidden1.astype(jnp.bfloat16)
    encoder_output_gradient = (enc_attended, branch_grad)
    grad_attn = project_back(branch_grad, enc_mats[1]).astype(jnp.bfloat16)
    if paired:
        dec_got, decoder_portion, grad_attn = hold((dec_got, decoder_portion, grad_attn))
        dec_folded = fold_blocks(decoder_portion, dec_got)
        dec_folded, grad_attn = hold((dec_folded, grad_attn))
        dec_close = near_sums(dec_folded)
    grad_eq, grad_ek, grad_ev, enc_bias_grad = attend_back(
        enc_qkv, enc_qkv, self_places, enc_bias, row_segments, row_segments, False, grad_attn
    )
    grad_eqkv = jnp.concatenate([grad_eq, grad_ek, grad_ev], axis=-1)
    encoder_qkv_gradient = (normed0, grad_eqkv)
    grad_hidden0_part, gain_zero = rms_back(hidden0, gains[0], project_back(grad_eqkv, enc_mats[0]))
    grad_hidden0 = grad_hidden1 + grad_hidden0_part
    back_rows = jnp.concatenate(
        [grad_hidden0.reshape(-1, D), grad_state0.reshape(-1, D)], axis=0
    ).astype(jnp.bfloat16)
    if paired:
        dec_close, back_rows, grad_eqkv = hold((dec_close, back_rows, grad_eqkv))
        encoder_qkv_gradient = (normed0, grad_eqkv)
        dec_far_sums = far_sums(dec_close)
    back_all = lax.all_gather(back_rows, "fsdp", axis=0, tiled=True)
    encoder_portion = weight_grads(
        [
            encoder_qkv_gradient,
            encoder_output_gradient,
            encoder_input_gradient,
            encoder_down_gradient,
        ]
    )
    if paired:
        encoder_portion, dec_far_sums = hold((encoder_portion, dec_far_sums))
        enc_got = swap_halves(encoder_portion)
        enc_got, encoder_portion = hold((enc_got, encoder_portion))
        enc_folded = hold(fold_blocks(encoder_portion, enc_got))
        enc_close = near_sums(enc_folded)
        back_all, enc_folded, dec_far_sums = hold((back_all, enc_folded, dec_far_sums))
        dec_arrived = line_sums(dec_far_sums)
        bound = dense_bound + back_all.shape[0] * jnp.max(jnp.abs(back_all)).astype(jnp.float32)
    emb_grad = table_grads(back_all, all_tokens, vocab_first, dense_grad)
    gain_part = jnp.stack(
        [gain_zero, gain_one, gain_two, gain_three, gain_four, gain_five, gain_six]
    )
    rel_part = jnp.stack(
        [tile_bias_grad(enc_onehot, enc_bias_grad), tile_bias_grad(dec_onehot, dec_bias_grad)]
    )
    small = [
        gain_part.reshape(-1),
        rel_part.reshape(-1),
        jnp.where(fsdp_rank == 0, group_loss, 0.0).reshape(1),
    ]
    if paired:
        half_rows = vocab_local // 2
        dec_arrived, enc_close, emb_grad, bound = hold((dec_arrived, enc_close, emb_grad, bound))
        enc_far_sums = far_sums(enc_close)
        dec_own_sum = line_total(dec_arrived)
        dec_grad = share_blocks(dec_own_sum) * share
        table_parts = near_parts(emb_grad, bound)
        enc_far_sums, table_parts = hold((enc_far_sums, table_parts))
        table_close = near_table(table_parts)
        enc_arrived = line_sums(enc_far_sums)
        table_close, dec_grad = hold((table_close, dec_grad))
        table_far = far_table(table_close)
        dec_products = shampoo_products(dec_grad, *dec_ready[1:])
        table_far, dec_products, enc_arrived = hold((table_far, dec_products, enc_arrived))
        enc_own_sum = line_total(enc_arrived)
        enc_grad = share_blocks(enc_own_sum) * share
        top, low, scale = table_total(table_far)
        squares = (
            jnp.sum(jnp.square(enc_own_sum * share))
            + jnp.sum(jnp.square(dec_own_sum * share))
            + table_squares(top * (share / scale), low * (share / scale), half_rows)
        )
    else:
        dec_grad = summed_blocks(decoder_portion) * share
        enc_grad = summed_blocks(encoder_portion) * share
        dec_products = shampoo_products(dec_grad, *dec_ready[1:])
        enc_products = shampoo_products(enc_grad, *enc_ready[1:])
        table_grad = lax.psum(emb_grad, REPLICAS) * share
        squares = (
            jnp.sum(jnp.square(enc_grad))
            + jnp.sum(jnp.square(dec_grad))
            + jnp.sum(jnp.square(table_grad))
        ) / replica_count()
    small = jnp.concatenate(small + [squares.reshape(1), jnp.zeros(126, jnp.float32)])
    small = small.reshape(-1, LANES)
    if paired:
        small, top, low, enc_grad = hold((sum_replicas(small), top, low, enc_grad))
        table_near = share_near(top, low)
        small = sum_line(small)
        enc_products = shampoo_products(enc_grad, *enc_ready[1:])
        table_near, small, enc_products = hold((table_near, small, enc_products))
        table_grad = placed_table(table_near, share_far(table_near), scale, half_rows) * share
    else:
        small = lax.psum(small, EVERYWHERE)
    small = small.reshape(-1)
    gain_grad = small[: 7 * D].reshape(7, D) * share
    rel_grad = small[7 * D : 7 * D + 2 * NBK * H].reshape(2, NBK, H) * share
    loss_sum = small[7 * D + 2 * NBK * H]
    squares_all = small[7 * D + 2 * NBK * H + 1]
    loss_count = jnp.maximum(count, 1.0)
    if not paired:
        dec_products, enc_products = hold((dec_products, enc_products))
    grad_norm = jnp.sqrt(
        squares_all + jnp.sum(gain_grad * gain_grad) + jnp.sum(rel_grad * rel_grad)
    )
    factor = jnp.minimum(1.0, clip_limit / grad_norm)
    new_emb = adam_update(embedding, table_grad * factor, emb_m, emb_v)
    new_gain = adam_update(gains, gain_grad * factor, gain_m, gain_v)
    new_rel = adam_update(rel_bias, rel_grad * factor, rel_m, rel_v)
    new_enc = shampoo_update(enc_w, enc_m, enc_left, enc_right, enc_ahead, enc_products, factor)
    new_dec = shampoo_update(dec_w, dec_m, dec_left, dec_right, dec_ahead, dec_products, factor)
    return (
        loss_sum,
        loss_count,
        grad_norm,
        *new_emb,
        *new_gain,
        *new_rel,
        *new_enc,
        *new_dec,
    )


def solution(mesh):
    in_specs = (
        P(("dp", "fsdp"), "seq"),
        P(("dp", "fsdp"), "seq"),
        P(("dp", "fsdp"), "seq"),
        P(("dp", "fsdp", "seq"), None),
        P(("dp", "fsdp", "seq"), None),
        P(("dp", "fsdp", "seq"), None),
        P("fsdp", None),
        P("fsdp", None),
        P("fsdp", None),
        P(),
        P(),
        P(),
        P(),
        P(),
        P(),
        P("fsdp", None),
        P("fsdp", None),
        P("fsdp", None),
        P("fsdp", None),
        P("fsdp", None),
        P("fsdp", None),
        P("fsdp", None),
        P("fsdp", None),
        P("fsdp", None),
        P("fsdp", None),
        P("fsdp", None),
        P("fsdp", None),
    )
    out_specs = (
        P(),
        P(),
        P(),
        P("fsdp", None),
        P("fsdp", None),
        P("fsdp", None),
        P(),
        P(),
        P(),
        P(),
        P(),
        P(),
        P("fsdp", None),
        P("fsdp", None),
        P("fsdp", None),
        P("fsdp", None),
        P("fsdp", None),
        P("fsdp", None),
        P("fsdp", None),
        P("fsdp", None),
    )
    return jax.shard_map(
        on_device, mesh=mesh, in_specs=in_specs, out_specs=out_specs, check_vma=False
    )
```

```python
import functools
import math

import jax
import jax.numpy as jnp
from jax import lax
from jax.experimental import pallas as pl
from jax.experimental.pallas import tpu as pltpu
from jax.sharding import PartitionSpec as P

D = 768
H = 12
DH = 64
FF = 3072
VOCAB = 32128
NBK = 32
REACH = 128
BLOCK = 192
STEP = 10
PAIR = 2 * BLOCK
TILE = 128
LANES = 128


norm_eps = 1e-06
neg_fill = -1000000000.0
sentinel_offset = 29
beta_first = 0.9
beta_second = 0.999
adam_eps = 1e-08
adam_rate = 0.5
shampoo_rate = 0.01
stat_decay = 0.999
weight_decay = 0.01
clip_limit = 0.05
highest = lax.Precision.HIGHEST


def bucket_edges(buckets, exact, reach):
    edges = list(range(1, exact))
    spread = buckets - exact
    for place in range(spread):
        edges.append(int(math.ceil(exact * (reach / exact) ** (place / spread) - 1e-09)))
    return edges


def offset_buckets(offset, causal):
    if causal:
        distance = jnp.maximum(-offset, 0)
        result = jnp.zeros(offset.shape, jnp.int32)
        edges = bucket_edges(NBK, NBK // 2, REACH)
    else:
        distance = jnp.abs(offset)
        result = jnp.where(offset > 0, NBK // 2, 0).astype(jnp.int32)
        edges = bucket_edges(NBK // 2, NBK // 4, REACH)
    for edge in edges:
        result = result + (distance >= edge).astype(jnp.int32)
    return result


def tile_reach(blocks):
    return min(blocks - 1, 2)


def tile_onehot(blocks, causal):
    reach = tile_reach(blocks)
    place = jnp.arange(TILE, dtype=jnp.int32)
    shift = jnp.arange(-reach, reach + 1, dtype=jnp.int32) * TILE
    offset = shift[:, None, None] + place[None, None, :] - place[None, :, None]
    buckets = offset_buckets(offset, causal).reshape(-1)
    return (jnp.arange(NBK, dtype=jnp.int32)[:, None] == buckets[None, :]).astype(jnp.float32)


def tile_bias(onehot, rel):
    flat = jnp.einsum("nh,np->hp", rel, onehot, precision=highest)
    return flat.reshape(H, -1, TILE, TILE)


def tile_bias_grad(onehot, grads):
    return jnp.einsum("np,hp->nh", onehot, grads.reshape(H, -1), precision=highest)


def head_lanes(half):
    lane = lax.broadcasted_iota(jnp.int32, (1, LANES), 1)
    return (lane // DH) == half


def both_heads(values):
    return jnp.concatenate([jnp.where(head_lanes(half), values, 0) for half in range(2)], axis=0)


def own_lanes(stacked):
    return jnp.where(head_lanes(0), stacked[:TILE], stacked[TILE:])


def block_probs(stacked, keys, bias_ref, row, row_segs, key_segs, causal):
    scores = lax.dot_general(
        stacked, keys, (((1,), (1,)), ((), ())), preferred_element_type=jnp.float32
    )
    width = keys.shape[0]
    mask = row_segs == key_segs
    if causal:
        at_row = row * TILE + lax.broadcasted_iota(jnp.int32, (TILE, width), 0)
        at_key = lax.broadcasted_iota(jnp.int32, (TILE, width), 1)
        mask = mask & (at_row >= at_key)
    probs = []
    for half in range(2):
        own = scores[half * TILE : (half + 1) * TILE]
        if bias_ref is not None:
            reach = tile_reach(width // TILE)
            tiles = []
            for column in range(width // TILE):
                tiles.append(bias_ref[half, min(max(column - row, -reach), reach) + reach])
            own = own + (jnp.concatenate(tiles, axis=1) if len(tiles) > 1 else tiles[0])
        own = jnp.where(mask, own, neg_fill)
        raised = jnp.exp(own - jnp.max(own, axis=-1, keepdims=True))
        probs.append(raised * (1.0 / jnp.sum(raised, axis=-1, keepdims=True)))
    return jnp.concatenate(probs, axis=0)


def attend_kernel(q_ref, k_ref, v_ref, *rest, biased, causal):
    bias_ref = rest[0] if biased else None
    sq_ref, sk_ref, o_ref = rest[-3:]
    keys = k_ref[0]
    values = v_ref[0]
    key_segs = sk_ref[0]
    for row in range(q_ref.shape[1] // TILE):
        part = pl.ds(row * TILE, TILE)
        probs = block_probs(
            both_heads(q_ref[0, part, :]), keys, bias_ref, row, sq_ref[0, part, :], key_segs, causal
        )
        output = jnp.dot(probs.astype(jnp.bfloat16), values, preferred_element_type=jnp.float32)
        o_ref[0, part, :] = own_lanes(output).astype(jnp.bfloat16)


def attend_back_kernel(q_ref, k_ref, v_ref, g_ref, *rest, biased, causal):
    if biased:
        bias_ref, sq_ref, sk_ref, dq_ref, dk_ref, dv_ref, db_ref = rest
    else:
        sq_ref, sk_ref, dq_ref, dk_ref, dv_ref = rest
        bias_ref = db_ref = None
    keys = k_ref[0]
    values = v_ref[0]
    key_segs = sk_ref[0]
    width = keys.shape[0]
    if biased:

        @pl.when(pl.program_id(1) == 0)
        def _():
            db_ref[...] = jnp.zeros_like(db_ref)

    grad_keys = None
    grad_values = None
    down = (((0,), (0,)), ((), ()))
    for row in range(q_ref.shape[1] // TILE):
        part = pl.ds(row * TILE, TILE)
        query = both_heads(q_ref[0, part, :])
        grad_out = both_heads(g_ref[0, part, :])
        probs = block_probs(
            query, keys, bias_ref, row, sq_ref[0, part, :], key_segs, causal
        )
        grad_probs = lax.dot_general(
            grad_out, values, (((1,), (1,)), ((), ())), preferred_element_type=jnp.float32
        )
        drop = jnp.sum(probs * grad_probs, axis=-1, keepdims=True)
        grad_scores = (probs * (grad_probs - drop)).astype(jnp.bfloat16)
        part_values = lax.dot_general(
            probs.astype(jnp.bfloat16), grad_out, down, preferred_element_type=jnp.float32
        )
        part_keys = lax.dot_general(grad_scores, query, down, preferred_element_type=jnp.float32)
        grad_values = part_values if grad_values is None else grad_values + part_values
        grad_keys = part_keys if grad_keys is None else grad_keys + part_keys
        grad_query = jnp.dot(grad_scores, keys, preferred_element_type=jnp.float32)
        dq_ref[0, part, :] = own_lanes(grad_query).astype(jnp.bfloat16)
        if biased:
            broad = grad_scores.astype(jnp.float32)
            reach = tile_reach(width // TILE)
            for half in range(2):
                for column in range(width // TILE):
                    slot = min(max(column - row, -reach), reach) + reach
                    db_ref[half, slot] += broad[
                        half * TILE : (half + 1) * TILE, column * TILE : (column + 1) * TILE
                    ]
    dk_ref[0] = grad_keys.astype(jnp.bfloat16)
    dv_ref[0] = grad_values.astype(jnp.bfloat16)


def attention_specs(query, keys, places, bias, row_segs, key_segs):
    q_at, k_at, v_at = places
    rows, nq = row_segs.shape
    nk = key_segs.shape[1]

    def panel(length, first):
        return pl.BlockSpec((1, length, LANES), lambda pair, row: (row, 0, first + pair))

    operands = [query, keys, keys]
    specs = [panel(nq, q_at), panel(nk, k_at), panel(nk, v_at)]
    tail = []
    tail_specs = []
    if bias is not None:
        tail.append(bias)
        tail_specs.append(
            pl.BlockSpec((2,) + bias.shape[1:], lambda pair, row: (pair, 0, 0, 0))
        )
    tail += [row_segs[:, :, None], key_segs[:, None, :]]
    tail_specs += [
        pl.BlockSpec((1, nq, 1), lambda pair, row: (row, 0, 0)),
        pl.BlockSpec((1, 1, nk), lambda pair, row: (row, 0, 0)),
    ]
    return operands, specs, tail, tail_specs, panel


def attention_cost(rows, nq, nk, products):
    return pl.CostEstimate(
        flops=2 * products * rows * H * nq * nk * LANES,
        bytes_accessed=2 * products * rows * (nq + nk) * D,
        transcendentals=rows * H * nq * nk,
    )


def attend(query, keys, places, bias, row_segs, key_segs, causal):
    rows, nq = row_segs.shape
    nk = key_segs.shape[1]
    operands, specs, tail, tail_specs, panel = attention_specs(
        query, keys, places, bias, row_segs, key_segs
    )
    return pl.pallas_call(
        functools.partial(attend_kernel, biased=bias is not None, causal=causal),
        out_shape=jax.ShapeDtypeStruct((rows, nq, D), jnp.bfloat16),
        grid=(H // 2, rows),
        in_specs=specs + tail_specs,
        out_specs=panel(nq, 0),
        cost_estimate=attention_cost(rows, nq, nk, 2),
        compiler_params=pltpu.CompilerParams(vmem_limit_bytes=32 << 20),
    )(*operands, *tail)


def attend_back(query, keys, places, bias, row_segs, key_segs, causal, grad_out):
    rows, nq = row_segs.shape
    nk = key_segs.shape[1]
    operands, specs, tail, tail_specs, panel = attention_specs(
        query, keys, places, bias, row_segs, key_segs
    )
    outs = [
        jax.ShapeDtypeStruct((rows, nq, D), jnp.bfloat16),
        jax.ShapeDtypeStruct((rows, nk, D), jnp.bfloat16),
        jax.ShapeDtypeStruct((rows, nk, D), jnp.bfloat16),
    ]
    out_specs = [panel(nq, 0), panel(nk, 0), panel(nk, 0)]
    if bias is not None:
        outs.append(jax.ShapeDtypeStruct(bias.shape, jnp.float32))
        out_specs.append(
            pl.BlockSpec((2,) + bias.shape[1:], lambda pair, row: (pair, 0, 0, 0))
        )
    return pl.pallas_call(
        functools.partial(attend_back_kernel, biased=bias is not None, causal=causal),
        out_shape=outs,
        grid=(H // 2, rows),
        in_specs=specs + [panel(nq, 0)] + tail_specs,
        out_specs=out_specs,
        cost_estimate=attention_cost(rows, nq, nk, 5),
        compiler_params=pltpu.CompilerParams(vmem_limit_bytes=32 << 20),
    )(*operands, grad_out, *tail)


def layer_shapes(decoder):
    if decoder:
        return [(D, 3 * D), (D, D), (D, D), (D, 2 * D), (D, D), (D, FF), (FF, D)]
    return [(D, 3 * D), (D, D), (D, FF), (FF, D)]


def as_blocks(flat):
    if flat.ndim == 3:
        return flat
    return flat.reshape(flat.shape[0], BLOCK, BLOCK)


def as_rows(blocks):
    return blocks.reshape(blocks.shape[0], BLOCK * BLOCK)


def as_pairs(blocks):
    amount = blocks.shape[0] // 2
    split = blocks.reshape(amount, 2, BLOCK, BLOCK)
    return jnp.concatenate([split[:, 0], split[:, 1]], axis=-1)


def unpack_kernel(pairs_ref, out_ref):
    across = out_ref.shape[1] // PAIR
    for row in range(out_ref.shape[0] // BLOCK):
        for column in range(across):
            out_ref[row * BLOCK : (row + 1) * BLOCK, column * PAIR : (column + 1) * PAIR] = (
                pairs_ref[row * across + column]
            )


def matrices_of(pairs, shapes):
    matrix_list = []
    place = 0
    for height, breadth in shapes:
        group = 2 * breadth // PAIR
        first = place // group
        matrix_list.append(
            pl.pallas_call(
                unpack_kernel,
                out_shape=jax.ShapeDtypeStruct((height, breadth), pairs.dtype),
                grid=(height // PAIR,),
                in_specs=[
                    pl.BlockSpec(
                        (group, BLOCK, PAIR), lambda step, first=first: (first + step, 0, 0)
                    )
                ],
                out_specs=pl.BlockSpec((PAIR, breadth), lambda step: (step, 0)),
                cost_estimate=pl.CostEstimate(
                    flops=0, bytes_accessed=4 * height * breadth, transcendentals=0
                ),
                compiler_params=pltpu.CompilerParams(vmem_limit_bytes=32 << 20),
            )(pairs)
        )
        place += group * (height // PAIR)
    return matrix_list


def weight_grad_kernel(x_ref, g_ref, *rest):
    out_ref = rest[-1]
    across = out_ref.shape[0] // 2
    for column in range(across):
        product = lax.dot_general(
            x_ref[...],
            g_ref[:, column * PAIR : (column + 1) * PAIR],
            (((0,), (0,)), ((), ())),
            preferred_element_type=jnp.float32,
        )
        product = product.astype(jnp.bfloat16)
        out_ref[column] = product[:BLOCK]
        out_ref[across + column] = product[BLOCK:]


def weight_grads(operands):
    total = sum(x.shape[-1] * g.shape[-1] for x, g in operands) // (BLOCK * PAIR)
    pairs = None
    place = 0
    for x, g in operands:
        x = x.reshape(-1, x.shape[-1])
        g = g.reshape(-1, g.shape[-1])
        count, height = x.shape
        breadth = g.shape[1]
        group = 2 * breadth // PAIR
        first = place // group
        given = [] if pairs is None else [pairs]
        pairs = pl.pallas_call(
            weight_grad_kernel,
            out_shape=jax.ShapeDtypeStruct((total, BLOCK, PAIR), jnp.bfloat16),
            grid=(height // PAIR,),
            in_specs=[
                pl.BlockSpec((count, PAIR), lambda step: (0, step)),
                pl.BlockSpec((count, breadth), lambda step: (0, 0)),
            ]
            + [pl.BlockSpec(memory_space=pl.ANY)] * len(given),
            out_specs=pl.BlockSpec(
                (group, BLOCK, PAIR), lambda step, first=first: (first + step, 0, 0)
            ),
            input_output_aliases={2: 0} if given else {},
            cost_estimate=pl.CostEstimate(
                flops=2 * count * height * breadth,
                bytes_accessed=2 * (count * (height + breadth) + height * breadth),
                transcendentals=0,
            ),
            compiler_params=pltpu.CompilerParams(vmem_limit_bytes=40 << 20),
        )(x, g, *given)
        place += group * (height // PAIR)
    return pairs


def split_float(values):
    high = values.astype(jnp.bfloat16)
    return high, (values - high.astype(jnp.float32)).astype(jnp.bfloat16)


def full_product(left, right, contract):
    def part(first, second):
        return lax.dot_general(
            first, second, (contract, ((), ())), preferred_element_type=jnp.float32
        )

    return (
        part(left[0], right[1]) + part(left[1], right[0]) + part(left[0], right[0])
    )


ROW_COL = ((1,), (0,))
ROW_ROW = ((1,), (1,))
COL_COL = ((0,), (0,))


def turned_product(left_root, middle, right_root):
    shaped = full_product(split_float(left_root), middle, ROW_COL)
    return full_product(split_float(shaped), split_float(right_root), ROW_COL)


def ahead_kernel(m_ref, lr_ref, rr_ref, o_ref):
    for place in range(m_ref.shape[0]):
        o_ref[place] = turned_product(lr_ref[place], split_float(m_ref[place]), rr_ref[place])


def products_kernel(g_ref, lr_ref, rr_ref, g_out, turned_out, left_out, right_out):
    for place in range(2):
        block = g_ref[0, :, place * BLOCK : (place + 1) * BLOCK]
        g_out[place] = block
        halves = split_float(block)
        turned_out[place] = turned_product(lr_ref[place], halves, rr_ref[place])
        left_out[place] = full_product(halves, halves, ROW_ROW)
        right_out[place] = full_product(halves, halves, COL_COL)


def block_cost(amount, products, arrays):
    return pl.CostEstimate(
        flops=6 * products * amount * BLOCK**3,
        bytes_accessed=4 * arrays * amount * BLOCK * BLOCK,
        transcendentals=0,
    )


def shampoo_ahead(moment, left_root, right_root):
    blocks = [as_blocks(member) for member in (moment, left_root, right_root)]
    amount = moment.shape[0]
    spec = pl.BlockSpec((2, BLOCK, BLOCK), lambda pair: (pair, 0, 0))
    ahead = pl.pallas_call(
        ahead_kernel,
        out_shape=jax.ShapeDtypeStruct((amount, BLOCK, BLOCK), jnp.float32),
        grid=(amount // 2,),
        in_specs=[spec] * 3,
        out_specs=spec,
        cost_estimate=block_cost(amount, 2, 4),
        compiler_params=pltpu.CompilerParams(vmem_limit_bytes=52 << 20),
    )(*blocks)
    return ahead, blocks[1], blocks[2]


def shampoo_products(pairs, left_root, right_root):
    amount = left_root.shape[0]
    spec = pl.BlockSpec((2, BLOCK, BLOCK), lambda pair: (pair, 0, 0))
    results = pl.pallas_call(
        products_kernel,
        out_shape=[jax.ShapeDtypeStruct((amount, BLOCK, BLOCK), jnp.float32)] * 4,
        grid=(amount // 2,),
        in_specs=[pl.BlockSpec((1, BLOCK, PAIR), lambda pair: (pair, 0, 0)), spec, spec],
        out_specs=[spec] * 4,
        cost_estimate=block_cost(amount, 4, 7),
        compiler_params=pltpu.CompilerParams(vmem_limit_bytes=52 << 20),
    )(pairs, left_root, right_root)
    return results


def rows_of_all(results):
    return [as_rows(result) for result in results]


def project(left, right):
    return jnp.matmul(left, right, preferred_element_type=jnp.float32)


def project_back(left, right):
    return jnp.einsum("btf,df->btd", left, right, preferred_element_type=jnp.float32)


def rms(values, gain):
    return values * lax.rsqrt(jnp.mean(values * values, axis=-1, keepdims=True) + norm_eps) * gain


def rms_back(values, gain, grad_out):
    inverse = lax.rsqrt(jnp.mean(values * values, axis=-1, keepdims=True) + norm_eps)
    normed = values * inverse
    grad_gain = jnp.sum(grad_out * normed, axis=(0, 1))
    grad_normed = grad_out * gain
    grad_values = inverse * (
        grad_normed - normed * jnp.mean(grad_normed * normed, axis=-1, keepdims=True)
    )
    return (grad_values, grad_gain)


def ff_forward(hidden, gain, w_in, w_down):
    normed = rms(hidden, gain).astype(jnp.bfloat16)
    inner = project(normed, w_in)
    active = jax.nn.gelu(inner).astype(jnp.bfloat16)
    return (hidden + project(active, w_down), (normed, inner, active))


def ff_back(hidden, gain, w_in, w_down, cache, grad_out):
    normed, inner, active = cache
    branch_grad = grad_out.astype(jnp.bfloat16)
    grad_active = project_back(branch_grad, w_down)
    unused, gelu_back = jax.vjp(jax.nn.gelu, inner)
    grad_inner = gelu_back(grad_active)[0].astype(jnp.bfloat16)
    grad_part, grad_gain = rms_back(hidden, gain, project_back(grad_inner, w_in))
    return (grad_out + grad_part, grad_gain, (normed, grad_inner), (active, branch_grad))


def table_rows(table, token_ids, vocab_first):
    local_ids = token_ids - vocab_first
    inside = (local_ids >= 0) & (local_ids < table.shape[0])
    picked = jnp.take(table, jnp.clip(local_ids, 0, table.shape[0] - 1), axis=0)
    return jnp.where(inside[..., None], picked, jnp.zeros((), table.dtype))


def table_grads(grads, token_ids, vocab_first, dense):
    vocab_local = dense.shape[0]
    local_ids = token_ids.reshape(-1) - vocab_first
    inside = (local_ids >= 0) & (local_ids < vocab_local)
    slots = jnp.where(inside, local_ids, vocab_local)
    return dense.at[slots].add(grads.astype(jnp.float32), mode="drop")


REPLICAS = ("dp", "seq")
EVERYWHERE = ("fsdp", "dp", "seq")


def replica_rank():
    return lax.axis_index("dp") * lax.axis_size("seq") + lax.axis_index("seq")


def replica_count():
    return lax.axis_size("dp") * lax.axis_size("seq")


def paired_mesh():
    return (
        lax.axis_size("dp") == 2 and lax.axis_size("seq") == 2 and lax.axis_size("fsdp") % 2 == 0
    )


def swap(values, axis):
    size = lax.axis_size(axis)
    return lax.ppermute(values, axis, [(place, place ^ 1) for place in range(size)])


def shift(values, step):
    size = lax.axis_size("fsdp")
    moves = [
        (place, place + 2 * step) for place in range(size) if 0 <= place + 2 * step < size
    ]
    return lax.ppermute(values, "fsdp", moves)


def choose(flag, if_set, if_clear):
    return jnp.where(flag == 1, if_set, if_clear)


def pick(values, place, axis):
    return lax.dynamic_index_in_dim(values, place, axis, False)


def narrow(values):
    return values.astype(jnp.bfloat16)


def wide(values):
    return values.astype(jnp.float32)


def placed(relative, first, second):
    def at(row, column):
        here = choose(second, relative[row][1 - column], relative[row][column])
        there = choose(second, relative[1 - row][1 - column], relative[1 - row][column])
        return choose(first, there, here)

    return [[at(0, 0), at(0, 1)], [at(1, 0), at(1, 1)]]


def own_weights(master):
    share = master.shape[0] // replica_count()
    if master.shape[0] % (2 * replica_count()) == 0:
        master = lax.dynamic_slice_in_dim(master, replica_rank() * share, share, 0)
    return as_pairs(as_blocks(master.astype(jnp.bfloat16)))


def hold(values):
    return lax.optimization_barrier(values)


def chip_groups():
    return [list(range(core, lax.axis_size("fsdp"), 2)) for core in range(2)]


def along_line(own):
    n_chips = lax.axis_size("fsdp") // 2
    copies = jnp.broadcast_to(own[None], (n_chips,) + own.shape)
    return lax.all_to_all(copies, "fsdp", 0, 0, axis_index_groups=chip_groups(), tiled=True)


def exchange_near(line):
    mid = BLOCK // 2
    upper, lower = (line[:, :, :mid], line[:, :, mid:])
    return [upper, lower, swap(upper, "seq"), swap(lower, "dp")]


def exchange_far(near):
    upper, lower, upper_half, lower_side = near
    return [
        swap(jnp.stack([lower, lower_side]), "seq"),
        swap(jnp.stack([upper, upper_half]), "dp"),
    ]


def swap_cores(pieces):
    return [swap(piece, "fsdp") for piece in pieces]


def assemble_kernel(place_ref, *refs, shapes):
    outs = refs[12 : 12 + len(shapes)]
    buffer, in_sems, out_sems = refs[12 + len(shapes) :]
    core, side, half = (place_ref[0], place_ref[1], place_ref[2])
    n_chips, quarter, mid, _ = refs[0].shape
    copies = []
    for other in range(2):
        upper, lower, upper_half, lower_side, by_half, by_side = refs[6 * other : 6 * other + 6]
        pieces = [
            (upper, lower),
            (upper_half, by_half.at[0]),
            (by_side.at[0], lower_side),
            (by_side.at[1], by_half.at[1]),
        ]
        for place, both in enumerate(pieces):
            owner = ((side ^ (place // 2)) * 2 + (half ^ (place % 2))) * quarter
            for low, piece in enumerate(both):
                for chip in range(n_chips):
                    first = (2 * chip + (core ^ other)) * (4 * quarter) + owner
                    copies.append(
                        pltpu.make_async_copy(
                            piece.at[chip],
                            buffer.at[pl.ds(first, quarter), pl.ds(low * mid, mid), :],
                            in_sems.at[len(copies)],
                        )
                    )
    for copy in copies:
        copy.start()
    for copy in copies:
        copy.wait()
    copies = []
    for out_ref, (height, breadth) in zip(outs, shapes):
        for row in range(height // BLOCK):
            for column in range(breadth // PAIR):
                copies.append(
                    pltpu.make_async_copy(
                        buffer.at[len(copies)],
                        out_ref.at[pl.ds(row * BLOCK, BLOCK), pl.ds(column * PAIR, PAIR)],
                        out_sems.at[len(copies)],
                    )
                )
    for copy in copies:
        copy.start()
    for copy in copies:
        copy.wait()


def assembled(pieces, shapes):
    n_chips, quarter, mid, _ = pieces[0].shape
    total = 8 * n_chips * quarter
    return pl.pallas_call(
        functools.partial(assemble_kernel, shapes=shapes),
        out_shape=[jax.ShapeDtypeStruct(shape, jnp.bfloat16) for shape in shapes],
        in_specs=[pl.BlockSpec(memory_space=pltpu.SMEM)]
        + [pl.BlockSpec(memory_space=pl.ANY)] * len(pieces),
        out_specs=[pl.BlockSpec(memory_space=pl.ANY)] * len(shapes),
        scratch_shapes=[
            pltpu.VMEM((total, BLOCK, PAIR), jnp.bfloat16),
            pltpu.SemaphoreType.DMA((16 * n_chips,)),
            pltpu.SemaphoreType.DMA((total,)),
        ],
        cost_estimate=pl.CostEstimate(
            flops=0, bytes_accessed=4 * total * BLOCK * PAIR, transcendentals=0
        ),
        compiler_params=pltpu.CompilerParams(vmem_limit_bytes=30 << 20),
    )(own_place(), *pieces)


def gathered_weights(pairs, amount):
    split = amount % (2 * replica_count()) == 0
    return lax.all_gather(pairs, EVERYWHERE if split else "fsdp", axis=0, tiled=True)


def own_place():
    return jnp.stack(
        [lax.axis_index("fsdp") % 2, lax.axis_index("dp"), lax.axis_index("seq")]
    ).astype(jnp.int32)


def fold_kernel(place_ref, own_ref, got_ref, keep_up, send_up, keep_low, send_low):
    total = wide(own_ref[0]) + wide(got_ref[0])
    mid = BLOCK // 2
    upper, lower = (total[:, :mid], total[:, mid:])
    other_side, other_half = (pl.program_id(1), pl.program_id(2))

    @pl.when(other_half == 0)
    def _():
        keep_up[0, 0] = upper

    @pl.when(other_half == 1)
    def _():
        send_up[0, 0] = narrow(upper)

    @pl.when(other_side == 0)
    def _():
        keep_low[0, 0] = lower

    @pl.when(other_side == 1)
    def _():
        send_low[0, 0] = narrow(lower)


def fold_cores(pairs, got, n_chips, quarter):
    mid = BLOCK // 2

    def quarter_of(place, other_side, other_half):
        return (place[1] ^ other_side) * 2 + (place[2] ^ other_half)

    whole = (1, quarter, BLOCK, PAIR)
    part = (1, 1, quarter, mid, PAIR)
    halves = (n_chips, 2, quarter, mid, PAIR)

    def up_at(chip, other_side, other_half, place):
        return (chip, place[1] ^ other_side, 0, 0, 0)

    def keep_low_at(chip, other_side, other_half, place):
        return (chip, jnp.where(other_side == 0, place[2] ^ other_half, place[2] ^ 1), 0, 0, 0)

    def send_low_at(chip, other_side, other_half, place):
        return (chip, jnp.where(other_side == 1, place[2] ^ other_half, place[2]), 0, 0, 0)

    return pl.pallas_call(
        fold_kernel,
        out_shape=[
            jax.ShapeDtypeStruct(halves, kind)
            for kind in (jnp.float32, jnp.bfloat16, jnp.float32, jnp.bfloat16)
        ],
        grid_spec=pltpu.PrefetchScalarGridSpec(
            num_scalar_prefetch=1,
            grid=(n_chips, 2, 2),
            in_specs=[
                pl.BlockSpec(
                    whole,
                    lambda chip, side, half, place: (
                        (2 * chip + place[0]) * 4 + quarter_of(place, side, half),
                        0,
                        0,
                        0,
                    ),
                ),
                pl.BlockSpec(
                    whole,
                    lambda chip, side, half, place: (
                        chip * 4 + quarter_of(place, side, half),
                        0,
                        0,
                        0,
                    ),
                ),
            ],
            out_specs=[
                pl.BlockSpec(part, up_at),
                pl.BlockSpec(part, up_at),
                pl.BlockSpec(part, keep_low_at),
                pl.BlockSpec(part, send_low_at),
            ],
        ),
        cost_estimate=pl.CostEstimate(
            flops=pairs.size // 2, bytes_accessed=5 * pairs.size, transcendentals=0
        ),
        compiler_params=pltpu.CompilerParams(vmem_limit_bytes=32 << 20),
    )(
        own_place(),
        pairs.reshape(-1, quarter, BLOCK, PAIR),
        got.reshape(-1, quarter, BLOCK, PAIR),
    )


def sum_replicas(values):
    values = values + swap(values, "seq")
    return values + swap(values, "dp")


def sum_line(values):
    size = lax.axis_size("fsdp")
    if size & (size - 1):
        return lax.psum(values, "fsdp")
    step = 1
    while step < size:
        moves = [(place, place ^ step) for place in range(size)]
        values = values + lax.ppermute(values, "fsdp", moves)
        step *= 2
    return values


def summed_blocks(pairs):
    shard = lax.psum_scatter(wide(pairs), "fsdp", scatter_dimension=0, tiled=True)
    return lax.psum(shard, REPLICAS)


def swap_halves(pairs):
    n_chips = lax.axis_size("fsdp") // 2
    core = lax.axis_index("fsdp") % 2
    split = pairs.reshape(n_chips, 2, -1, BLOCK, PAIR)
    return swap(pick(split, 1 - core, 1), "fsdp")


def fold_blocks(pairs, got):
    n_chips = lax.axis_size("fsdp") // 2
    return fold_cores(pairs, got, n_chips, pairs.shape[0] // (8 * n_chips))


def near_sums(folded):
    return [folded[0], swap(folded[1], "seq"), folded[2], swap(folded[3], "dp")]


def far_sums(near):
    side, half = (lax.axis_index("dp"), lax.axis_index("seq"))
    upper = near[0] + wide(near[1])
    lower = near[2] + wide(near[3])
    return [
        pick(upper, side, 1),
        swap(narrow(pick(upper, 1 - side, 1)), "dp"),
        pick(lower, half, 1),
        swap(narrow(pick(lower, 1 - half, 1)), "seq"),
    ]


def line_sums(far):
    line = narrow(jnp.concatenate([far[0] + wide(far[1]), far[2] + wide(far[3])], axis=2))
    return lax.all_to_all(line, "fsdp", 0, 0, axis_index_groups=chip_groups(), tiled=True)


def line_total(arrived):
    return jnp.sum(wide(arrived), axis=0)


def share_blocks(own):
    return wide(lax.all_gather(narrow(own), REPLICAS, axis=0, tiled=True))


def window_rows(half_rows):
    return -(-half_rows // 16) * 8


def half_lanes(values, place):
    return lax.dynamic_slice_in_dim(values, place * (D // 2), D // 2, 1)


SCALE_ROWS = 8


def scale_of(power):
    return jnp.exp2(power.astype(jnp.float32))


def message_of(values, power):
    mark = jnp.full((SCALE_ROWS, values.shape[1]), power, jnp.float16)
    return jnp.concatenate([values.astype(jnp.float16), mark], axis=0)


def scaled_swap(message, axis):
    got = swap(message, axis)
    return got[:-SCALE_ROWS], got[-1, 0].astype(jnp.float32)


def joined(values, power, got):
    others, other_power = got
    least = jnp.minimum(power, other_power)
    return (
        values * scale_of(least - power) + wide(others) * scale_of(least - other_power),
        least,
    )


def near_parts(partial, bound):
    side, half = (lax.axis_index("dp"), lax.axis_index("seq"))
    half_rows = partial.shape[0] // 2
    window = window_rows(half_rows)
    power = jnp.clip(12.0 - jnp.ceil(jnp.log2(jnp.maximum(bound, 1e-37))), -120.0, 120.0)

    def rows_of(first, place):
        start = first + place * (half_rows - window)
        return lax.dynamic_slice_in_dim(partial, start, window, 0) * scale_of(power)

    return [
        rows_of(0, half),
        message_of(rows_of(0, 1 - half), power),
        rows_of(half_rows, side),
        message_of(rows_of(half_rows, 1 - side), power),
        power,
    ]


def near_table(parts):
    top, top_sent, low, low_sent, power = parts
    return [top, scaled_swap(top_sent, "seq"), low, scaled_swap(low_sent, "dp"), power]


def far_table(near):
    side, half = (lax.axis_index("dp"), lax.axis_index("seq"))
    top, top_power = joined(near[0], near[4], near[1])
    low, low_power = joined(near[2], near[4], near[3])
    return [
        half_lanes(top, side),
        top_power,
        scaled_swap(message_of(half_lanes(top, 1 - side), top_power), "dp"),
        half_lanes(low, half),
        low_power,
        scaled_swap(message_of(half_lanes(low, 1 - half), low_power), "seq"),
    ]


def table_total(far):
    top, power = joined(*far[:3])
    low, _ = joined(*far[3:])
    return top, low, scale_of(power)


def table_squares(top, low, half_rows):
    side, half = (lax.axis_index("dp"), lax.axis_index("seq"))
    again = 2 * window_rows(half_rows) - half_rows
    row = lax.broadcasted_iota(jnp.int32, (top.shape[0], 1), 0)
    return jnp.sum(jnp.where(row >= again * half, top * top, 0.0)) + jnp.sum(
        jnp.where(row >= again * side, low * low, 0.0)
    )


def share_near(top, low):
    top = hold(top.astype(jnp.float16))
    low = hold(low.astype(jnp.float16))
    return [jnp.stack([top, swap(top, "dp")]), jnp.stack([low, swap(low, "seq")])]


def share_far(near):
    return [swap(near[0], "seq"), swap(near[1], "dp")]


def placed_table(near, far, scale, half_rows):
    side, half = (lax.axis_index("dp"), lax.axis_index("seq"))
    again = 2 * window_rows(half_rows) - half_rows
    top_all = placed([near[0], far[0]], half, side)
    low_all = placed([near[1], far[1]], side, half)
    rows = []
    for first, second in (top_all, low_all):
        rows.append(jnp.concatenate(first, axis=1))
        rows.append(jnp.concatenate(second, axis=1)[again:])
    return wide(jnp.concatenate(rows, axis=0)) * (1.0 / scale)


def adam_update(weight, gradient, moment, second):
    moment = beta_first * moment + (1 - beta_first) * gradient
    second = beta_second * second + (1 - beta_second) * gradient * gradient
    corrected = moment / (1 - beta_first**STEP)
    scaled = second / (1 - beta_second**STEP)
    weight = weight - adam_rate * (
        corrected / (jnp.sqrt(scaled) + adam_eps) + weight_decay * weight
    )
    return (weight, moment, second)


def shampoo_update(weight, moment, left, right, ahead, products, factor):
    gradient, turned, left_square, right_square = products
    direction = beta_first * ahead + ((1 - beta_first) * factor) * turned
    square = (1 - stat_decay) * factor * factor
    return (
        weight - shampoo_rate * (direction + weight_decay * weight),
        beta_first * moment + ((1 - beta_first) * factor) * gradient,
        stat_decay * left + square * left_square,
        stat_decay * right + square * right_square,
    )


def on_device(
    enc_ids,
    span_mask,
    segments,
    targets,
    loss_weights,
    target_segments,
    embedding,
    emb_m,
    emb_v,
    gains,
    gain_m,
    gain_v,
    rel_bias,
    rel_m,
    rel_v,
    enc_w,
    enc_m,
    enc_left,
    enc_right,
    enc_lroot,
    enc_rroot,
    dec_w,
    dec_m,
    dec_left,
    dec_right,
    dec_lroot,
    dec_rroot,
):
    fsdp_rank = lax.axis_index("fsdp")
    seq_rank = lax.axis_index("seq")
    n_fsdp = lax.axis_size("fsdp")
    n_seq = lax.axis_size("seq")
    half_len = enc_ids.shape[1]
    rows, dec_len = targets.shape
    enc_len = half_len * n_seq
    enc_in = jnp.where(span_mask == 1, VOCAB - sentinel_offset, enc_ids)
    dec_in = jnp.concatenate([jnp.zeros((rows, 1), jnp.int32), targets[:, :-1]], axis=1)

    paired = paired_mesh()

    halves = jnp.stack([enc_in, segments]).reshape(2, n_seq, rows, half_len)
    enc_own, dec_own, table = (own_weights(enc_w), own_weights(dec_w), narrow(embedding))
    if n_seq == 2:
        kept = pick(halves, seq_rank, 1)
        got = swap(pick(halves, 1 - seq_rank, 1), "seq")
        got, enc_own, dec_own = hold((got, enc_own, dec_own))
        parts = (choose(seq_rank, got, kept), choose(seq_rank, kept, got))
        row_words = jnp.stack(parts, axis=2)
    else:
        row_words = lax.all_to_all(halves, "seq", 1, 1, tiled=True).transpose(0, 2, 1, 3)
    row_words = row_words.reshape(2, rows, enc_len)
    row_segments = row_words[1]
    message = jnp.concatenate(
        [
            row_words[0].reshape(-1),
            dec_in.reshape(-1),
            targets.reshape(-1),
            loss_weights.reshape(-1),
        ]
    ).reshape(1, -1)
    enc_pairs = gathered_weights(enc_own, enc_w.shape[0])
    gathered = lax.all_gather(message, "fsdp", axis=0, tiled=True)
    gathered, dec_own = hold((gathered, dec_own))
    if paired:
        dec_line = along_line(dec_own)
    all_enc = gathered[:, : rows * enc_len]
    rest = gathered[:, rows * enc_len :].reshape(n_fsdp, 3, rows * dec_len)
    all_dec, all_targets, all_weights = (rest[:, 0], rest[:, 1], rest[:, 2])
    all_tokens = jnp.concatenate([all_enc, all_dec], axis=1)
    vocab_local = table.shape[0]
    vocab_first = fsdp_rank * vocab_local
    found = table_rows(table, all_tokens, vocab_first)
    enc_roots = (enc_m, enc_lroot, enc_rroot)
    dec_roots = (dec_m, dec_lroot, dec_rroot)
    found, enc_roots = hold((found, enc_roots))
    enc_ready = shampoo_ahead(*enc_roots)
    enc_ready, dec_roots = hold((enc_ready, dec_roots))
    dec_ready = shampoo_ahead(*dec_roots)
    enc_onehot = tile_onehot(enc_len // TILE, False)
    dec_onehot = tile_onehot(dec_len // TILE, True)
    if paired:
        found, enc_pairs, enc_ready, dec_line, rel_tiles, dec_ready = hold(
            (found, enc_pairs, enc_ready, dec_line, rel_bias, dec_ready)
        )
    else:
        found, enc_pairs, rel_tiles = hold((found, enc_pairs, rel_bias))
    looked_up = lax.psum_scatter(found, "fsdp", scatter_dimension=0, tiled=True).reshape(-1, D)
    enc_mats = matrices_of(enc_pairs, layer_shapes(False))
    enc_bias = tile_bias(enc_onehot, rel_tiles[0])
    dec_bias = tile_bias(dec_onehot, rel_tiles[1])
    if paired:
        dec_near = exchange_near(dec_line)
        enc_ahead, dec_ahead = (as_rows(enc_ready[0]), as_rows(dec_ready[0]))
        dec_near, enc_mats, enc_bias, dec_bias, enc_ahead = hold(
            (dec_near, enc_mats, enc_bias, dec_bias, enc_ahead)
        )
        dec_far = exchange_far(dec_near)
        dec_cores = swap_cores(dec_near)
        looked_up, dec_far, dec_cores, dec_ahead = hold((looked_up, dec_far, dec_cores, dec_ahead))
        dec_cores = dec_cores + swap_cores(dec_far)
    else:
        dec_mats = matrices_of(gathered_weights(dec_own, dec_w.shape[0]), layer_shapes(True))
        enc_ahead, dec_ahead = (as_rows(enc_ready[0]), as_rows(dec_ready[0]))
    hidden0 = looked_up[: rows * enc_len].reshape(rows, enc_len, D).astype(jnp.float32)
    state0 = looked_up[rows * enc_len :].reshape(rows, dec_len, D).astype(jnp.float32)

    tile_at = D // LANES
    self_places = (0, tile_at, 2 * tile_at)
    cross_places = (0, 0, tile_at)

    normed0 = rms(hidden0, gains[0]).astype(jnp.bfloat16)
    enc_qkv = project(normed0, enc_mats[0]).astype(jnp.bfloat16)
    enc_attended = attend(
        enc_qkv, enc_qkv, self_places, enc_bias, row_segments, row_segments, False
    )
    hidden1 = hidden0 + project(enc_attended, enc_mats[1])
    hidden2, enc_cache = ff_forward(hidden1, gains[1], enc_mats[2], enc_mats[3])
    encoded = rms(hidden2, gains[2]).astype(jnp.bfloat16)
    if paired:
        encoded, dec_cores = hold((encoded, dec_cores))
        dec_mats = assembled(dec_near + dec_far + dec_cores, layer_shapes(True))
    pairs = project(encoded, dec_mats[3]).astype(jnp.bfloat16)

    normed3 = rms(state0, gains[3]).astype(jnp.bfloat16)
    self_qkv = project(normed3, dec_mats[0]).astype(jnp.bfloat16)
    self_attended = attend(
        self_qkv, self_qkv, self_places, dec_bias, target_segments, target_segments, True
    )
    state1 = state0 + project(self_attended, dec_mats[1])
    normed4 = rms(state1, gains[4]).astype(jnp.bfloat16)
    cross_query = project(normed4, dec_mats[2]).astype(jnp.bfloat16)
    cross_attended = attend(
        cross_query, pairs, cross_places, None, target_segments, row_segments, False
    )
    state2 = state1 + project(cross_attended, dec_mats[4])
    state3, dec_cache = ff_forward(state2, gains[5], dec_mats[5], dec_mats[6])
    out_scale = D ** (-0.5)
    final = (rms(state3, gains[6]) * out_scale).astype(jnp.bfloat16)

    count = jnp.sum(all_weights).astype(jnp.float32)
    final, count = hold((final, count))
    all_final = lax.all_gather(final.reshape(rows * dec_len, D), "fsdp", axis=0, tiled=True)
    if paired:
        count = count + swap(count, "seq")
        count = count + swap(count, "dp")
    else:
        count = lax.psum(count, REPLICAS)
    all_final, count = hold((all_final, count))
    share = 1.0 / jnp.maximum(count, 1.0)
    logits = jnp.einsum("nd,vd->nv", all_final, table, preferred_element_type=jnp.float32)
    local_ids = all_targets.reshape(-1) - vocab_first
    target_hot = local_ids[:, None] == jnp.arange(vocab_local, dtype=jnp.int32)[None, :]
    local_top = jnp.max(logits, axis=1)
    local_sum = jnp.sum(jnp.exp(logits - local_top[:, None]), axis=1)
    local_pick = jnp.sum(jnp.where(target_hot, logits, 0.0), axis=1)
    stats = lax.all_gather(
        jnp.stack([local_top, local_sum, local_pick])[None], "fsdp", axis=0, tiled=True
    )
    top_all = jnp.max(stats[:, 0], axis=0)
    sum_all = jnp.sum(stats[:, 1] * jnp.exp(stats[:, 0] - top_all), axis=0)
    pick_all = jnp.sum(stats[:, 2], axis=0)
    lse = top_all + jnp.log(sum_all)
    token_weights = all_weights.reshape(-1).astype(jnp.float32)
    group_loss = jnp.sum(token_weights * (lse - pick_all))
    grad_logits = (
        token_weights[:, None] * (jnp.exp(logits - lse[:, None]) - target_hot.astype(jnp.float32))
    ).astype(jnp.bfloat16)
    grad_final = lax.psum_scatter(
        jnp.dot(grad_logits, table, preferred_element_type=jnp.float32),
        "fsdp",
        scatter_dimension=0,
        tiled=True,
    ).reshape(rows, dec_len, D)
    dense_grad = jnp.einsum("nv,nd->vd", grad_logits, all_final, preferred_element_type=jnp.float32)
    grad_final, dense_grad, dense_bound = hold(
        (grad_final, dense_grad, jnp.max(jnp.abs(dense_grad)))
    )

    grad_state3, gain_six = rms_back(state3, gains[6], grad_final * out_scale)
    grad_state2, gain_five, dec_in_grad, dec_down_grad = ff_back(
        state2, gains[5], dec_mats[5], dec_mats[6], dec_cache, grad_state3
    )
    branch_grad = grad_state2.astype(jnp.bfloat16)
    cross_out_grad = (cross_attended, branch_grad)
    grad_cross = project_back(branch_grad, dec_mats[4]).astype(jnp.bfloat16)
    grad_cq, grad_ck, grad_cv = attend_back(
        cross_query, pairs, cross_places, None, target_segments, row_segments, False, grad_cross
    )
    grad_pairs = jnp.concatenate([grad_ck, grad_cv], axis=-1)
    cross_query_grad = (normed4, grad_cq)
    grad_state1_part, gain_four = rms_back(state1, gains[4], project_back(grad_cq, dec_mats[2]))
    grad_state1 = grad_state2 + grad_state1_part
    cross_pair_grad = (encoded, grad_pairs)
    grad_encoded = project_back(grad_pairs, dec_mats[3])
    branch_grad = grad_state1.astype(jnp.bfloat16)
    self_out_grad = (self_attended, branch_grad)
    grad_self = project_back(branch_grad, dec_mats[1]).astype(jnp.bfloat16)
    grad_sq, grad_sk, grad_sv, dec_bias_grad = attend_back(
        self_qkv, self_qkv, self_places, dec_bias, target_segments, target_segments, True, grad_self
    )
    grad_sqkv = jnp.concatenate([grad_sq, grad_sk, grad_sv], axis=-1)
    self_qkv_grad = (normed3, grad_sqkv)
    grad_state0_part, gain_three = rms_back(state0, gains[3], project_back(grad_sqkv, dec_mats[0]))
    grad_state0 = grad_state1 + grad_state0_part
    decoder_portion = weight_grads(
        [
            self_qkv_grad,
            self_out_grad,
            cross_query_grad,
            cross_pair_grad,
            cross_out_grad,
            dec_in_grad,
            dec_down_grad,
        ]
    )
    if paired:
        dec_got = swap_halves(decoder_portion)

    grad_hidden2, gain_two = rms_back(hidden2, gains[2], grad_encoded)
    grad_hidden1, gain_one, encoder_input_gradient, encoder_down_gradient = ff_back(
        hidden1, gains[1], enc_mats[2], enc_mats[3], enc_cache, grad_hidden2
    )
    branch_grad = grad_hidden1.astype(jnp.bfloat16)
    encoder_output_gradient = (enc_attended, branch_grad)
    grad_attn = project_back(branch_grad, enc_mats[1]).astype(jnp.bfloat16)
    if paired:
        dec_got, decoder_portion, grad_attn = hold((dec_got, decoder_portion, grad_attn))
        dec_folded = fold_blocks(decoder_portion, dec_got)
        dec_folded, grad_attn = hold((dec_folded, grad_attn))
        dec_close = near_sums(dec_folded)
    grad_eq, grad_ek, grad_ev, enc_bias_grad = attend_back(
        enc_qkv, enc_qkv, self_places, enc_bias, row_segments, row_segments, False, grad_attn
    )
    grad_eqkv = jnp.concatenate([grad_eq, grad_ek, grad_ev], axis=-1)
    encoder_qkv_gradient = (normed0, grad_eqkv)
    grad_hidden0_part, gain_zero = rms_back(hidden0, gains[0], project_back(grad_eqkv, enc_mats[0]))
    grad_hidden0 = grad_hidden1 + grad_hidden0_part
    back_rows = jnp.concatenate(
        [grad_hidden0.reshape(-1, D), grad_state0.reshape(-1, D)], axis=0
    ).astype(jnp.bfloat16)
    if paired:
        dec_close, back_rows, grad_eqkv = hold((dec_close, back_rows, grad_eqkv))
        encoder_qkv_gradient = (normed0, grad_eqkv)
        dec_far_sums = far_sums(dec_close)
    back_all = lax.all_gather(back_rows, "fsdp", axis=0, tiled=True)
    encoder_portion = weight_grads(
        [
            encoder_qkv_gradient,
            encoder_output_gradient,
            encoder_input_gradient,
            encoder_down_gradient,
        ]
    )
    if paired:
        encoder_portion, dec_far_sums = hold((encoder_portion, dec_far_sums))
        enc_got = swap_halves(encoder_portion)
        enc_got, encoder_portion = hold((enc_got, encoder_portion))
        enc_folded = hold(fold_blocks(encoder_portion, enc_got))
        enc_close = near_sums(enc_folded)
        back_all, enc_folded, dec_far_sums = hold((back_all, enc_folded, dec_far_sums))
        dec_arrived = line_sums(dec_far_sums)
        bound = dense_bound + back_all.shape[0] * jnp.max(jnp.abs(back_all)).astype(jnp.float32)
    emb_grad = table_grads(back_all, all_tokens, vocab_first, dense_grad)
    gain_part = jnp.stack(
        [gain_zero, gain_one, gain_two, gain_three, gain_four, gain_five, gain_six]
    )
    rel_part = jnp.stack(
        [tile_bias_grad(enc_onehot, enc_bias_grad), tile_bias_grad(dec_onehot, dec_bias_grad)]
    )
    small = jnp.concatenate(
        [
            gain_part.reshape(-1),
            rel_part.reshape(-1),
            jnp.where(fsdp_rank == 0, group_loss, 0.0).reshape(1),
        ]
    )
    if paired:
        half_rows = vocab_local // 2
        dec_arrived, enc_close, emb_grad, bound = hold((dec_arrived, enc_close, emb_grad, bound))
        enc_far_sums = far_sums(enc_close)
        dec_own_sum = line_total(dec_arrived)
        dec_grad = share_blocks(dec_own_sum) * share
        table_parts = near_parts(emb_grad, bound)
        enc_far_sums, table_parts = hold((enc_far_sums, table_parts))
        table_close = near_table(table_parts)
        enc_arrived = line_sums(enc_far_sums)
        table_close, dec_grad, small = hold((table_close, dec_grad, small))
        table_far = far_table(table_close)
        dec_products = shampoo_products(dec_grad, *dec_ready[1:])
        table_far, dec_products, enc_arrived = hold((table_far, dec_products, enc_arrived))
        enc_own_sum = line_total(enc_arrived)
        enc_grad = share_blocks(enc_own_sum) * share
        top, low, scale = table_total(table_far)
        squares = (
            jnp.sum(jnp.square(enc_own_sum * share))
            + jnp.sum(jnp.square(dec_own_sum * share))
            + table_squares(top * (share / scale), low * (share / scale), half_rows)
        )
    else:
        dec_grad = summed_blocks(decoder_portion) * share
        enc_grad = summed_blocks(encoder_portion) * share
        dec_products = rows_of_all(shampoo_products(dec_grad, *dec_ready[1:]))
        enc_products = rows_of_all(shampoo_products(enc_grad, *enc_ready[1:]))
        table_grad = lax.psum(emb_grad, REPLICAS) * share
        squares = (
            jnp.sum(jnp.square(enc_grad))
            + jnp.sum(jnp.square(dec_grad))
            + jnp.sum(jnp.square(table_grad))
        ) / replica_count()
    small = jnp.concatenate([small, squares.reshape(1), jnp.zeros(126, jnp.float32)])
    small = small.reshape(-1, LANES)
    if paired:
        small, top, low, dec_products = hold((sum_replicas(small), top, low, dec_products))
        table_near = share_near(top, low)
        small = sum_line(small)
        dec_products, enc_grad = hold((rows_of_all(dec_products), enc_grad))
        enc_products = shampoo_products(enc_grad, *enc_ready[1:])
        table_near, small, enc_products = hold((table_near, small, enc_products))
        enc_products = hold(rows_of_all(enc_products))
        table_grad = placed_table(table_near, share_far(table_near), scale, half_rows) * share
    else:
        small = lax.psum(small, EVERYWHERE)
    small = small.reshape(-1)
    gain_grad = small[: 7 * D].reshape(7, D) * share
    rel_grad = small[7 * D : 7 * D + 2 * NBK * H].reshape(2, NBK, H) * share
    loss_sum = small[7 * D + 2 * NBK * H]
    squares_all = small[7 * D + 2 * NBK * H + 1]
    loss_count = jnp.maximum(count, 1.0)
    if not paired:
        dec_products, enc_products = hold((dec_products, enc_products))
    grad_norm = jnp.sqrt(
        squares_all + jnp.sum(gain_grad * gain_grad) + jnp.sum(rel_grad * rel_grad)
    )
    factor = jnp.minimum(1.0, clip_limit / grad_norm)
    new_emb = adam_update(embedding, table_grad * factor, emb_m, emb_v)
    new_gain = adam_update(gains, gain_grad * factor, gain_m, gain_v)
    new_rel = adam_update(rel_bias, rel_grad * factor, rel_m, rel_v)
    new_enc = shampoo_update(enc_w, enc_m, enc_left, enc_right, enc_ahead, enc_products, factor)
    new_dec = shampoo_update(dec_w, dec_m, dec_left, dec_right, dec_ahead, dec_products, factor)
    return (
        loss_sum,
        loss_count,
        grad_norm,
        *new_emb,
        *new_gain,
        *new_rel,
        *new_enc,
        *new_dec,
    )


def solution(mesh):
    in_specs = (
        P(("dp", "fsdp"), "seq"),
        P(("dp", "fsdp"), "seq"),
        P(("dp", "fsdp"), "seq"),
        P(("dp", "fsdp", "seq"), None),
        P(("dp", "fsdp", "seq"), None),
        P(("dp", "fsdp", "seq"), None),
        P("fsdp", None),
        P("fsdp", None),
        P("fsdp", None),
        P(),
        P(),
        P(),
        P(),
        P(),
        P(),
        P("fsdp", None),
        P("fsdp", None),
        P("fsdp", None),
        P("fsdp", None),
        P("fsdp", None),
        P("fsdp", None),
        P("fsdp", None),
        P("fsdp", None),
        P("fsdp", None),
        P("fsdp", None),
        P("fsdp", None),
        P("fsdp", None),
    )
    out_specs = (
        P(),
        P(),
        P(),
        P("fsdp", None),
        P("fsdp", None),
        P("fsdp", None),
        P(),
        P(),
        P(),
        P(),
        P(),
        P(),
        P("fsdp", None),
        P("fsdp", None),
        P("fsdp", None),
        P("fsdp", None),
        P("fsdp", None),
        P("fsdp", None),
        P("fsdp", None),
        P("fsdp", None),
    )
    return jax.shard_map(
        on_device, mesh=mesh, in_specs=in_specs, out_specs=out_specs, check_vma=False
    )
```

```python
import functools
import math

import jax
import jax.numpy as jnp
from jax import lax
from jax.experimental import pallas as pl
from jax.experimental.pallas import tpu as pltpu
from jax.sharding import PartitionSpec as P

D = 768
H = 12
DH = 64
FF = 3072
VOCAB = 32128
NBK = 32
REACH = 128
BLOCK = 192
STEP = 10
PAIR = 2 * BLOCK
TILE = 128
LANES = 128


norm_eps = 1e-06
neg_fill = -1000000000.0
sentinel_offset = 29
beta_first = 0.9
beta_second = 0.999
adam_eps = 1e-08
adam_rate = 0.5
shampoo_rate = 0.01
stat_decay = 0.999
weight_decay = 0.01
clip_limit = 0.05
highest = lax.Precision.HIGHEST


def bucket_edges(buckets, exact, reach):
    edges = list(range(1, exact))
    spread = buckets - exact
    for place in range(spread):
        edges.append(int(math.ceil(exact * (reach / exact) ** (place / spread) - 1e-09)))
    return edges


def offset_buckets(offset, causal):
    if causal:
        distance = jnp.maximum(-offset, 0)
        result = jnp.zeros(offset.shape, jnp.int32)
        edges = bucket_edges(NBK, NBK // 2, REACH)
    else:
        distance = jnp.abs(offset)
        result = jnp.where(offset > 0, NBK // 2, 0).astype(jnp.int32)
        edges = bucket_edges(NBK // 2, NBK // 4, REACH)
    for edge in edges:
        result = result + (distance >= edge).astype(jnp.int32)
    return result


def tile_reach(blocks):
    return min(blocks - 1, 2)


def tile_onehot(blocks, causal):
    reach = tile_reach(blocks)
    place = jnp.arange(TILE, dtype=jnp.int32)
    shift = jnp.arange(-reach, reach + 1, dtype=jnp.int32) * TILE
    offset = shift[:, None, None] + place[None, None, :] - place[None, :, None]
    buckets = offset_buckets(offset, causal).reshape(-1)
    return (jnp.arange(NBK, dtype=jnp.int32)[:, None] == buckets[None, :]).astype(jnp.float32)


def tile_bias(onehot, rel):
    flat = jnp.einsum("nh,np->hp", rel, onehot, precision=highest)
    return flat.reshape(H, -1, TILE, TILE)


def tile_bias_grad(onehot, grads):
    return jnp.einsum("np,hp->nh", onehot, grads.reshape(H, -1), precision=highest)


def head_lanes(half):
    lane = lax.broadcasted_iota(jnp.int32, (1, LANES), 1)
    return (lane // DH) == half


def both_heads(values):
    return jnp.concatenate([jnp.where(head_lanes(half), values, 0) for half in range(2)], axis=0)


def own_lanes(stacked):
    return jnp.where(head_lanes(0), stacked[:TILE], stacked[TILE:])


def block_probs(stacked, keys, bias_ref, row, row_segs, key_segs, causal):
    scores = lax.dot_general(
        stacked, keys, (((1,), (1,)), ((), ())), preferred_element_type=jnp.float32
    )
    width = keys.shape[0]
    mask = row_segs == key_segs
    if causal:
        at_row = row * TILE + lax.broadcasted_iota(jnp.int32, (TILE, width), 0)
        at_key = lax.broadcasted_iota(jnp.int32, (TILE, width), 1)
        mask = mask & (at_row >= at_key)
    probs = []
    for half in range(2):
        own = scores[half * TILE : (half + 1) * TILE]
        if bias_ref is not None:
            reach = tile_reach(width // TILE)
            tiles = []
            for column in range(width // TILE):
                tiles.append(bias_ref[half, min(max(column - row, -reach), reach) + reach])
            own = own + (jnp.concatenate(tiles, axis=1) if len(tiles) > 1 else tiles[0])
        own = jnp.where(mask, own, neg_fill)
        raised = jnp.exp(own - jnp.max(own, axis=-1, keepdims=True))
        probs.append(raised * (1.0 / jnp.sum(raised, axis=-1, keepdims=True)))
    return jnp.concatenate(probs, axis=0)


def attend_kernel(q_ref, k_ref, v_ref, *rest, biased, causal):
    bias_ref = rest[0] if biased else None
    sq_ref, sk_ref, o_ref = rest[-3:]
    keys = k_ref[0]
    values = v_ref[0]
    key_segs = sk_ref[0]
    for row in range(q_ref.shape[1] // TILE):
        part = pl.ds(row * TILE, TILE)
        probs = block_probs(
            both_heads(q_ref[0, part, :]), keys, bias_ref, row, sq_ref[0, part, :], key_segs, causal
        )
        output = jnp.dot(probs.astype(jnp.bfloat16), values, preferred_element_type=jnp.float32)
        o_ref[0, part, :] = own_lanes(output).astype(jnp.bfloat16)


def attend_back_kernel(q_ref, k_ref, v_ref, g_ref, *rest, biased, causal):
    if biased:
        bias_ref, sq_ref, sk_ref, dq_ref, dk_ref, dv_ref, db_ref = rest
    else:
        sq_ref, sk_ref, dq_ref, dk_ref, dv_ref = rest
        bias_ref = db_ref = None
    keys = k_ref[0]
    values = v_ref[0]
    key_segs = sk_ref[0]
    width = keys.shape[0]
    if biased:

        @pl.when(pl.program_id(1) == 0)
        def _():
            db_ref[...] = jnp.zeros_like(db_ref)

    grad_keys = None
    grad_values = None
    down = (((0,), (0,)), ((), ()))
    for row in range(q_ref.shape[1] // TILE):
        part = pl.ds(row * TILE, TILE)
        query = both_heads(q_ref[0, part, :])
        grad_out = both_heads(g_ref[0, part, :])
        probs = block_probs(
            query, keys, bias_ref, row, sq_ref[0, part, :], key_segs, causal
        )
        grad_probs = lax.dot_general(
            grad_out, values, (((1,), (1,)), ((), ())), preferred_element_type=jnp.float32
        )
        drop = jnp.sum(probs * grad_probs, axis=-1, keepdims=True)
        grad_scores = (probs * (grad_probs - drop)).astype(jnp.bfloat16)
        part_values = lax.dot_general(
            probs.astype(jnp.bfloat16), grad_out, down, preferred_element_type=jnp.float32
        )
        part_keys = lax.dot_general(grad_scores, query, down, preferred_element_type=jnp.float32)
        grad_values = part_values if grad_values is None else grad_values + part_values
        grad_keys = part_keys if grad_keys is None else grad_keys + part_keys
        grad_query = jnp.dot(grad_scores, keys, preferred_element_type=jnp.float32)
        dq_ref[0, part, :] = own_lanes(grad_query).astype(jnp.bfloat16)
        if biased:
            broad = grad_scores.astype(jnp.float32)
            reach = tile_reach(width // TILE)
            for half in range(2):
                for column in range(width // TILE):
                    slot = min(max(column - row, -reach), reach) + reach
                    db_ref[half, slot] += broad[
                        half * TILE : (half + 1) * TILE, column * TILE : (column + 1) * TILE
                    ]
    dk_ref[0] = grad_keys.astype(jnp.bfloat16)
    dv_ref[0] = grad_values.astype(jnp.bfloat16)


def attention_specs(query, keys, places, bias, row_segs, key_segs):
    q_at, k_at, v_at = places
    rows, nq = row_segs.shape
    nk = key_segs.shape[1]

    def panel(length, first):
        return pl.BlockSpec((1, length, LANES), lambda pair, row: (row, 0, first + pair))

    operands = [query, keys, keys]
    specs = [panel(nq, q_at), panel(nk, k_at), panel(nk, v_at)]
    tail = []
    tail_specs = []
    if bias is not None:
        tail.append(bias)
        tail_specs.append(
            pl.BlockSpec((2,) + bias.shape[1:], lambda pair, row: (pair, 0, 0, 0))
        )
    tail += [row_segs[:, :, None], key_segs[:, None, :]]
    tail_specs += [
        pl.BlockSpec((1, nq, 1), lambda pair, row: (row, 0, 0)),
        pl.BlockSpec((1, 1, nk), lambda pair, row: (row, 0, 0)),
    ]
    return operands, specs, tail, tail_specs, panel


def attention_cost(rows, nq, nk, products):
    return pl.CostEstimate(
        flops=2 * products * rows * H * nq * nk * LANES,
        bytes_accessed=2 * products * rows * (nq + nk) * D,
        transcendentals=rows * H * nq * nk,
    )


def attend(query, keys, places, bias, row_segs, key_segs, causal):
    rows, nq = row_segs.shape
    nk = key_segs.shape[1]
    operands, specs, tail, tail_specs, panel = attention_specs(
        query, keys, places, bias, row_segs, key_segs
    )
    return pl.pallas_call(
        functools.partial(attend_kernel, biased=bias is not None, causal=causal),
        out_shape=jax.ShapeDtypeStruct((rows, nq, D), jnp.bfloat16),
        grid=(H // 2, rows),
        in_specs=specs + tail_specs,
        out_specs=panel(nq, 0),
        cost_estimate=attention_cost(rows, nq, nk, 2),
        compiler_params=pltpu.CompilerParams(vmem_limit_bytes=32 << 20),
    )(*operands, *tail)


def attend_back(query, keys, places, bias, row_segs, key_segs, causal, grad_out):
    rows, nq = row_segs.shape
    nk = key_segs.shape[1]
    operands, specs, tail, tail_specs, panel = attention_specs(
        query, keys, places, bias, row_segs, key_segs
    )
    outs = [
        jax.ShapeDtypeStruct((rows, nq, D), jnp.bfloat16),
        jax.ShapeDtypeStruct((rows, nk, D), jnp.bfloat16),
        jax.ShapeDtypeStruct((rows, nk, D), jnp.bfloat16),
    ]
    out_specs = [panel(nq, 0), panel(nk, 0), panel(nk, 0)]
    if bias is not None:
        outs.append(jax.ShapeDtypeStruct(bias.shape, jnp.float32))
        out_specs.append(
            pl.BlockSpec((2,) + bias.shape[1:], lambda pair, row: (pair, 0, 0, 0))
        )
    return pl.pallas_call(
        functools.partial(attend_back_kernel, biased=bias is not None, causal=causal),
        out_shape=outs,
        grid=(H // 2, rows),
        in_specs=specs + [panel(nq, 0)] + tail_specs,
        out_specs=out_specs,
        cost_estimate=attention_cost(rows, nq, nk, 5),
        compiler_params=pltpu.CompilerParams(vmem_limit_bytes=32 << 20),
    )(*operands, grad_out, *tail)


def layer_shapes(decoder):
    if decoder:
        return [(D, 3 * D), (D, D), (D, D), (D, 2 * D), (D, D), (D, FF), (FF, D)]
    return [(D, 3 * D), (D, D), (D, FF), (FF, D)]


def as_blocks(flat):
    if flat.ndim == 3:
        return flat
    return flat.reshape(flat.shape[0], BLOCK, BLOCK)


def as_rows(blocks):
    return blocks.reshape(blocks.shape[0], BLOCK * BLOCK)


def as_pairs(blocks):
    amount = blocks.shape[0] // 2
    split = blocks.reshape(amount, 2, BLOCK, BLOCK)
    return jnp.concatenate([split[:, 0], split[:, 1]], axis=-1)


def unpack_kernel(pairs_ref, out_ref):
    across = out_ref.shape[1] // PAIR
    for row in range(out_ref.shape[0] // BLOCK):
        for column in range(across):
            out_ref[row * BLOCK : (row + 1) * BLOCK, column * PAIR : (column + 1) * PAIR] = (
                pairs_ref[row * across + column]
            )


def matrices_of(pairs, shapes):
    matrix_list = []
    place = 0
    for height, breadth in shapes:
        group = 2 * breadth // PAIR
        first = place // group
        matrix_list.append(
            pl.pallas_call(
                unpack_kernel,
                out_shape=jax.ShapeDtypeStruct((height, breadth), pairs.dtype),
                grid=(height // PAIR,),
                in_specs=[
                    pl.BlockSpec(
                        (group, BLOCK, PAIR), lambda step, first=first: (first + step, 0, 0)
                    )
                ],
                out_specs=pl.BlockSpec((PAIR, breadth), lambda step: (step, 0)),
                cost_estimate=pl.CostEstimate(
                    flops=0, bytes_accessed=4 * height * breadth, transcendentals=0
                ),
                compiler_params=pltpu.CompilerParams(vmem_limit_bytes=32 << 20),
            )(pairs)
        )
        place += group * (height // PAIR)
    return matrix_list


def weight_grad_kernel(x_ref, g_ref, *rest):
    out_ref = rest[-1]
    across = out_ref.shape[0] // 2
    for column in range(across):
        product = lax.dot_general(
            x_ref[...],
            g_ref[:, column * PAIR : (column + 1) * PAIR],
            (((0,), (0,)), ((), ())),
            preferred_element_type=jnp.float32,
        )
        product = product.astype(jnp.bfloat16)
        out_ref[column] = product[:BLOCK]
        out_ref[across + column] = product[BLOCK:]


def weight_grads(operands):
    total = sum(x.shape[-1] * g.shape[-1] for x, g in operands) // (BLOCK * PAIR)
    pairs = None
    place = 0
    for x, g in operands:
        x = x.reshape(-1, x.shape[-1])
        g = g.reshape(-1, g.shape[-1])
        count, height = x.shape
        breadth = g.shape[1]
        group = 2 * breadth // PAIR
        first = place // group
        given = [] if pairs is None else [pairs]
        pairs = pl.pallas_call(
            weight_grad_kernel,
            out_shape=jax.ShapeDtypeStruct((total, BLOCK, PAIR), jnp.bfloat16),
            grid=(height // PAIR,),
            in_specs=[
                pl.BlockSpec((count, PAIR), lambda step: (0, step)),
                pl.BlockSpec((count, breadth), lambda step: (0, 0)),
            ]
            + [pl.BlockSpec(memory_space=pl.ANY)] * len(given),
            out_specs=pl.BlockSpec(
                (group, BLOCK, PAIR), lambda step, first=first: (first + step, 0, 0)
            ),
            input_output_aliases={2: 0} if given else {},
            cost_estimate=pl.CostEstimate(
                flops=2 * count * height * breadth,
                bytes_accessed=2 * (count * (height + breadth) + height * breadth),
                transcendentals=0,
            ),
            compiler_params=pltpu.CompilerParams(vmem_limit_bytes=40 << 20),
        )(x, g, *given)
        place += group * (height // PAIR)
    return pairs


def split_float(values):
    high = values.astype(jnp.bfloat16)
    return high, (values - high.astype(jnp.float32)).astype(jnp.bfloat16)


def full_product(left, right, contract):
    def part(first, second):
        return lax.dot_general(
            first, second, (contract, ((), ())), preferred_element_type=jnp.float32
        )

    return (
        part(left[0], right[1]) + part(left[1], right[0]) + part(left[0], right[0])
    )


ROW_COL = ((1,), (0,))
ROW_ROW = ((1,), (1,))
COL_COL = ((0,), (0,))


def turned_product(left_root, middle, right_root):
    shaped = full_product(split_float(left_root), middle, ROW_COL)
    return full_product(split_float(shaped), split_float(right_root), ROW_COL)


def ahead_kernel(m_ref, lr_ref, rr_ref, o_ref):
    for place in range(m_ref.shape[0]):
        o_ref[place] = turned_product(lr_ref[place], split_float(m_ref[place]), rr_ref[place])


def products_kernel(rest_ref, g_ref, lr_ref, rr_ref, g_out, turned_out, left_out, right_out):
    rest = rest_ref[0]

    def single(first, second, contract):
        return lax.dot_general(
            first, second, (contract, ((), ())), preferred_element_type=jnp.float32
        )

    for place in range(2):
        block = g_ref[0, :, place * BLOCK : (place + 1) * BLOCK]
        g_out[place] = block.astype(jnp.float32) * rest
        high, low = split_float(lr_ref[place])
        shaped = single(low, block, ROW_COL) + single(high, block, ROW_COL)
        turned_out[place] = rest * full_product(
            split_float(shaped), split_float(rr_ref[place]), ROW_COL
        )
        left_out[place] = (rest * rest) * single(block, block, ROW_ROW)
        right_out[place] = (rest * rest) * single(block, block, COL_COL)


def block_cost(amount, products, arrays):
    return pl.CostEstimate(
        flops=6 * products * amount * BLOCK**3,
        bytes_accessed=4 * arrays * amount * BLOCK * BLOCK,
        transcendentals=0,
    )


def shampoo_ahead(moment, left_root, right_root):
    blocks = [as_blocks(member) for member in (moment, left_root, right_root)]
    amount = moment.shape[0]
    spec = pl.BlockSpec((2, BLOCK, BLOCK), lambda pair: (pair, 0, 0))
    ahead = pl.pallas_call(
        ahead_kernel,
        out_shape=jax.ShapeDtypeStruct((amount, BLOCK, BLOCK), jnp.float32),
        grid=(amount // 2,),
        in_specs=[spec] * 3,
        out_specs=spec,
        cost_estimate=block_cost(amount, 2, 4),
        compiler_params=pltpu.CompilerParams(vmem_limit_bytes=52 << 20),
    )(*blocks)
    return ahead, blocks[1], blocks[2]


def shampoo_products(pairs, share, left_root, right_root):
    amount = left_root.shape[0]
    power = jnp.exp2(jnp.floor(jnp.log2(share)))
    pairs = narrow(wide(pairs) * power)
    spec = pl.BlockSpec((2, BLOCK, BLOCK), lambda pair: (pair, 0, 0))
    results = pl.pallas_call(
        products_kernel,
        out_shape=[jax.ShapeDtypeStruct((amount, BLOCK, BLOCK), jnp.float32)] * 4,
        grid=(amount // 2,),
        in_specs=[
            pl.BlockSpec(memory_space=pltpu.SMEM),
            pl.BlockSpec((1, BLOCK, PAIR), lambda pair: (pair, 0, 0)),
            spec,
            spec,
        ],
        out_specs=[spec] * 4,
        cost_estimate=block_cost(amount, 3, 7),
        compiler_params=pltpu.CompilerParams(vmem_limit_bytes=52 << 20),
    )((share / power).reshape(1), pairs, left_root, right_root)
    return results


def rows_of_all(results):
    return [as_rows(result) for result in results]


def project(left, right):
    return jnp.matmul(left, right, preferred_element_type=jnp.float32)


def project_back(left, right):
    return jnp.einsum("btf,df->btd", left, right, preferred_element_type=jnp.float32)


def rms(values, gain):
    return values * lax.rsqrt(jnp.mean(values * values, axis=-1, keepdims=True) + norm_eps) * gain


def rms_back(values, gain, grad_out):
    inverse = lax.rsqrt(jnp.mean(values * values, axis=-1, keepdims=True) + norm_eps)
    normed = values * inverse
    grad_gain = jnp.sum(grad_out * normed, axis=(0, 1))
    grad_normed = grad_out * gain
    grad_values = inverse * (
        grad_normed - normed * jnp.mean(grad_normed * normed, axis=-1, keepdims=True)
    )
    return (grad_values, grad_gain)


def ff_forward(hidden, gain, w_in, w_down):
    normed = rms(hidden, gain).astype(jnp.bfloat16)
    inner = project(normed, w_in)
    active = jax.nn.gelu(inner).astype(jnp.bfloat16)
    return (hidden + project(active, w_down), (normed, inner, active))


def ff_back(hidden, gain, w_in, w_down, cache, grad_out):
    normed, inner, active = cache
    branch_grad = grad_out.astype(jnp.bfloat16)
    grad_active = project_back(branch_grad, w_down)
    unused, gelu_back = jax.vjp(jax.nn.gelu, inner)
    grad_inner = gelu_back(grad_active)[0].astype(jnp.bfloat16)
    grad_part, grad_gain = rms_back(hidden, gain, project_back(grad_inner, w_in))
    return (grad_out + grad_part, grad_gain, (normed, grad_inner), (active, branch_grad))


def table_rows(table, token_ids, vocab_first):
    local_ids = token_ids - vocab_first
    inside = (local_ids >= 0) & (local_ids < table.shape[0])
    picked = jnp.take(table, jnp.clip(local_ids, 0, table.shape[0] - 1), axis=0)
    return jnp.where(inside[..., None], picked, jnp.zeros((), table.dtype))


def table_grads(grads, token_ids, vocab_first, dense):
    vocab_local = dense.shape[0]
    local_ids = token_ids.reshape(-1) - vocab_first
    inside = (local_ids >= 0) & (local_ids < vocab_local)
    slots = jnp.where(inside, local_ids, vocab_local)
    return dense.at[slots].add(grads.astype(jnp.float32), mode="drop")


REPLICAS = ("dp", "seq")
EVERYWHERE = ("fsdp", "dp", "seq")


def replica_rank():
    return lax.axis_index("dp") * lax.axis_size("seq") + lax.axis_index("seq")


def replica_count():
    return lax.axis_size("dp") * lax.axis_size("seq")


def paired_mesh():
    return (
        lax.axis_size("dp") == 2 and lax.axis_size("seq") == 2 and lax.axis_size("fsdp") % 2 == 0
    )


def swap(values, axis):
    size = lax.axis_size(axis)
    return lax.ppermute(values, axis, [(place, place ^ 1) for place in range(size)])


def shift(values, step):
    size = lax.axis_size("fsdp")
    moves = [
        (place, place + 2 * step) for place in range(size) if 0 <= place + 2 * step < size
    ]
    return lax.ppermute(values, "fsdp", moves)


def choose(flag, if_set, if_clear):
    return jnp.where(flag == 1, if_set, if_clear)


def pick(values, place, axis):
    return lax.dynamic_index_in_dim(values, place, axis, False)


def narrow(values):
    return values.astype(jnp.bfloat16)


def wide(values):
    return values.astype(jnp.float32)


def placed(relative, first, second):
    def at(row, column):
        here = choose(second, relative[row][1 - column], relative[row][column])
        there = choose(second, relative[1 - row][1 - column], relative[1 - row][column])
        return choose(first, there, here)

    return [[at(0, 0), at(0, 1)], [at(1, 0), at(1, 1)]]


def own_weights(master):
    share = master.shape[0] // replica_count()
    if master.shape[0] % (2 * replica_count()) == 0:
        master = lax.dynamic_slice_in_dim(master, replica_rank() * share, share, 0)
    return as_pairs(as_blocks(master.astype(jnp.bfloat16)))


def hold(values):
    return lax.optimization_barrier(values)


def chip_groups():
    return [list(range(core, lax.axis_size("fsdp"), 2)) for core in range(2)]


def along_line(own):
    n_chips = lax.axis_size("fsdp") // 2
    copies = jnp.broadcast_to(own[None], (n_chips,) + own.shape)
    return lax.all_to_all(copies, "fsdp", 0, 0, axis_index_groups=chip_groups(), tiled=True)


def exchange_near(line):
    mid = BLOCK // 2
    upper, lower = (line[:, :, :mid], line[:, :, mid:])
    return [upper, lower, swap(upper, "seq"), swap(lower, "dp")]


def exchange_far(near):
    upper, lower, upper_half, lower_side = near
    return [
        swap(jnp.stack([lower, lower_side]), "seq"),
        swap(jnp.stack([upper, upper_half]), "dp"),
    ]


def swap_cores(pieces):
    return [swap(piece, "fsdp") for piece in pieces]


def assemble_kernel(place_ref, *refs, shapes):
    outs = refs[12 : 12 + len(shapes)]
    buffer, in_sems, out_sems = refs[12 + len(shapes) :]
    core, side, half = (place_ref[0], place_ref[1], place_ref[2])
    n_chips, quarter, mid, _ = refs[0].shape
    copies = []
    for other in range(2):
        upper, lower, upper_half, lower_side, by_half, by_side = refs[6 * other : 6 * other + 6]
        pieces = [
            (upper, lower),
            (upper_half, by_half.at[0]),
            (by_side.at[0], lower_side),
            (by_side.at[1], by_half.at[1]),
        ]
        for place, both in enumerate(pieces):
            owner = ((side ^ (place // 2)) * 2 + (half ^ (place % 2))) * quarter
            for low, piece in enumerate(both):
                for chip in range(n_chips):
                    first = (2 * chip + (core ^ other)) * (4 * quarter) + owner
                    copies.append(
                        pltpu.make_async_copy(
                            piece.at[chip],
                            buffer.at[pl.ds(first, quarter), pl.ds(low * mid, mid), :],
                            in_sems.at[len(copies)],
                        )
                    )
    for copy in copies:
        copy.start()
    for copy in copies:
        copy.wait()
    copies = []
    for out_ref, (height, breadth) in zip(outs, shapes):
        for row in range(height // BLOCK):
            for column in range(breadth // PAIR):
                copies.append(
                    pltpu.make_async_copy(
                        buffer.at[len(copies)],
                        out_ref.at[pl.ds(row * BLOCK, BLOCK), pl.ds(column * PAIR, PAIR)],
                        out_sems.at[len(copies)],
                    )
                )
    for copy in copies:
        copy.start()
    for copy in copies:
        copy.wait()


def assembled(pieces, shapes):
    n_chips, quarter, mid, _ = pieces[0].shape
    total = 8 * n_chips * quarter
    return pl.pallas_call(
        functools.partial(assemble_kernel, shapes=shapes),
        out_shape=[jax.ShapeDtypeStruct(shape, jnp.bfloat16) for shape in shapes],
        in_specs=[pl.BlockSpec(memory_space=pltpu.SMEM)]
        + [pl.BlockSpec(memory_space=pl.ANY)] * len(pieces),
        out_specs=[pl.BlockSpec(memory_space=pl.ANY)] * len(shapes),
        scratch_shapes=[
            pltpu.VMEM((total, BLOCK, PAIR), jnp.bfloat16),
            pltpu.SemaphoreType.DMA((16 * n_chips,)),
            pltpu.SemaphoreType.DMA((total,)),
        ],
        cost_estimate=pl.CostEstimate(
            flops=0, bytes_accessed=4 * total * BLOCK * PAIR, transcendentals=0
        ),
        compiler_params=pltpu.CompilerParams(vmem_limit_bytes=30 << 20),
    )(own_place(), *pieces)


def gathered_weights(pairs, amount):
    split = amount % (2 * replica_count()) == 0
    return lax.all_gather(pairs, EVERYWHERE if split else "fsdp", axis=0, tiled=True)


def own_place():
    return jnp.stack(
        [lax.axis_index("fsdp") % 2, lax.axis_index("dp"), lax.axis_index("seq")]
    ).astype(jnp.int32)


def fold_kernel(place_ref, own_ref, got_ref, keep_up, send_up, keep_low, send_low):
    total = wide(own_ref[0]) + wide(got_ref[0])
    mid = BLOCK // 2
    upper, lower = (total[:, :mid], total[:, mid:])
    other_side, other_half = (pl.program_id(1), pl.program_id(2))

    @pl.when(other_half == 0)
    def _():
        keep_up[0, 0] = upper

    @pl.when(other_half == 1)
    def _():
        send_up[0, 0] = narrow(upper)

    @pl.when(other_side == 0)
    def _():
        keep_low[0, 0] = lower

    @pl.when(other_side == 1)
    def _():
        send_low[0, 0] = narrow(lower)


def fold_cores(pairs, got, n_chips, quarter):
    mid = BLOCK // 2

    def quarter_of(place, other_side, other_half):
        return (place[1] ^ other_side) * 2 + (place[2] ^ other_half)

    whole = (1, quarter, BLOCK, PAIR)
    part = (1, 1, quarter, mid, PAIR)
    halves = (n_chips, 2, quarter, mid, PAIR)

    def up_at(chip, other_side, other_half, place):
        return (chip, place[1] ^ other_side, 0, 0, 0)

    def keep_low_at(chip, other_side, other_half, place):
        return (chip, jnp.where(other_side == 0, place[2] ^ other_half, place[2] ^ 1), 0, 0, 0)

    def send_low_at(chip, other_side, other_half, place):
        return (chip, jnp.where(other_side == 1, place[2] ^ other_half, place[2]), 0, 0, 0)

    return pl.pallas_call(
        fold_kernel,
        out_shape=[
            jax.ShapeDtypeStruct(halves, kind)
            for kind in (jnp.float32, jnp.bfloat16, jnp.float32, jnp.bfloat16)
        ],
        grid_spec=pltpu.PrefetchScalarGridSpec(
            num_scalar_prefetch=1,
            grid=(n_chips, 2, 2),
            in_specs=[
                pl.BlockSpec(
                    whole,
                    lambda chip, side, half, place: (
                        (2 * chip + place[0]) * 4 + quarter_of(place, side, half),
                        0,
                        0,
                        0,
                    ),
                ),
                pl.BlockSpec(
                    whole,
                    lambda chip, side, half, place: (
                        chip * 4 + quarter_of(place, side, half),
                        0,
                        0,
                        0,
                    ),
                ),
            ],
            out_specs=[
                pl.BlockSpec(part, up_at),
                pl.BlockSpec(part, up_at),
                pl.BlockSpec(part, keep_low_at),
                pl.BlockSpec(part, send_low_at),
            ],
        ),
        cost_estimate=pl.CostEstimate(
            flops=pairs.size // 2, bytes_accessed=5 * pairs.size, transcendentals=0
        ),
        compiler_params=pltpu.CompilerParams(vmem_limit_bytes=32 << 20),
    )(
        own_place(),
        pairs.reshape(-1, quarter, BLOCK, PAIR),
        got.reshape(-1, quarter, BLOCK, PAIR),
    )


def sum_replicas(values):
    values = values + swap(values, "seq")
    return values + swap(values, "dp")


def sum_line(values):
    size = lax.axis_size("fsdp")
    if size & (size - 1):
        return lax.psum(values, "fsdp")
    step = 1
    while step < size:
        moves = [(place, place ^ step) for place in range(size)]
        values = values + lax.ppermute(values, "fsdp", moves)
        step *= 2
    return values


def summed_blocks(pairs):
    shard = lax.psum_scatter(wide(pairs), "fsdp", scatter_dimension=0, tiled=True)
    return lax.psum(shard, REPLICAS)


def swap_halves(pairs):
    n_chips = lax.axis_size("fsdp") // 2
    core = lax.axis_index("fsdp") % 2
    split = pairs.reshape(n_chips, 2, -1, BLOCK, PAIR)
    return swap(pick(split, 1 - core, 1), "fsdp")


def fold_blocks(pairs, got):
    n_chips = lax.axis_size("fsdp") // 2
    return fold_cores(pairs, got, n_chips, pairs.shape[0] // (8 * n_chips))


def near_sums(folded):
    return [folded[0], swap(folded[1], "seq"), folded[2], swap(folded[3], "dp")]


def far_sums(near):
    side, half = (lax.axis_index("dp"), lax.axis_index("seq"))
    upper = near[0] + wide(near[1])
    lower = near[2] + wide(near[3])
    return [
        pick(upper, side, 1),
        swap(narrow(pick(upper, 1 - side, 1)), "dp"),
        pick(lower, half, 1),
        swap(narrow(pick(lower, 1 - half, 1)), "seq"),
    ]


def line_sums(far):
    line = narrow(jnp.concatenate([far[0] + wide(far[1]), far[2] + wide(far[3])], axis=2))
    return lax.all_to_all(line, "fsdp", 0, 0, axis_index_groups=chip_groups(), tiled=True)


def line_total(arrived):
    return jnp.sum(wide(arrived), axis=0)


def share_blocks(own):
    return lax.all_gather(narrow(own), REPLICAS, axis=0, tiled=True)


def window_rows(half_rows):
    return -(-half_rows // 16) * 8


def half_lanes(values, place):
    return lax.dynamic_slice_in_dim(values, place * (D // 2), D // 2, 1)


SCALE_ROWS = 8


def scale_of(power):
    return jnp.exp2(power.astype(jnp.float32))


def message_of(values, power):
    mark = jnp.full((SCALE_ROWS, values.shape[1]), power, jnp.float16)
    return jnp.concatenate([values.astype(jnp.float16), mark], axis=0)


def scaled_swap(message, axis):
    got = swap(message, axis)
    return got[:-SCALE_ROWS], got[-1, 0].astype(jnp.float32)


def joined(values, power, got):
    others, other_power = got
    least = jnp.minimum(power, other_power)
    return (
        values * scale_of(least - power) + wide(others) * scale_of(least - other_power),
        least,
    )


def near_parts(partial, bound):
    side, half = (lax.axis_index("dp"), lax.axis_index("seq"))
    half_rows = partial.shape[0] // 2
    window = window_rows(half_rows)
    power = jnp.clip(12.0 - jnp.ceil(jnp.log2(jnp.maximum(bound, 1e-37))), -120.0, 120.0)

    def rows_of(first, place):
        start = first + place * (half_rows - window)
        return lax.dynamic_slice_in_dim(partial, start, window, 0) * scale_of(power)

    return [
        rows_of(0, half),
        message_of(rows_of(0, 1 - half), power),
        rows_of(half_rows, side),
        message_of(rows_of(half_rows, 1 - side), power),
        power,
    ]


def near_table(parts):
    top, top_sent, low, low_sent, power = parts
    return [top, scaled_swap(top_sent, "seq"), low, scaled_swap(low_sent, "dp"), power]


def far_table(near):
    side, half = (lax.axis_index("dp"), lax.axis_index("seq"))
    top, top_power = joined(near[0], near[4], near[1])
    low, low_power = joined(near[2], near[4], near[3])
    return [
        half_lanes(top, side),
        top_power,
        scaled_swap(message_of(half_lanes(top, 1 - side), top_power), "dp"),
        half_lanes(low, half),
        low_power,
        scaled_swap(message_of(half_lanes(low, 1 - half), low_power), "seq"),
    ]


def table_total(far):
    top, power = joined(*far[:3])
    low, _ = joined(*far[3:])
    return top, low, scale_of(power)


def table_squares(top, low, half_rows):
    side, half = (lax.axis_index("dp"), lax.axis_index("seq"))
    again = 2 * window_rows(half_rows) - half_rows
    row = lax.broadcasted_iota(jnp.int32, (top.shape[0], 1), 0)
    return jnp.sum(jnp.where(row >= again * half, top * top, 0.0)) + jnp.sum(
        jnp.where(row >= again * side, low * low, 0.0)
    )


def share_near(top, low):
    top = hold(top.astype(jnp.float16))
    low = hold(low.astype(jnp.float16))
    return [jnp.stack([top, swap(top, "dp")]), jnp.stack([low, swap(low, "seq")])]


def share_far(near):
    return [swap(near[0], "seq"), swap(near[1], "dp")]


def placed_table(near, far, scale, half_rows):
    side, half = (lax.axis_index("dp"), lax.axis_index("seq"))
    again = 2 * window_rows(half_rows) - half_rows
    top_all = placed([near[0], far[0]], half, side)
    low_all = placed([near[1], far[1]], side, half)
    rows = []
    for first, second in (top_all, low_all):
        rows.append(jnp.concatenate(first, axis=1))
        rows.append(jnp.concatenate(second, axis=1)[again:])
    return wide(jnp.concatenate(rows, axis=0)) * (1.0 / scale)


def adam_update(weight, gradient, moment, second):
    moment = beta_first * moment + (1 - beta_first) * gradient
    second = beta_second * second + (1 - beta_second) * gradient * gradient
    corrected = moment / (1 - beta_first**STEP)
    scaled = second / (1 - beta_second**STEP)
    weight = weight - adam_rate * (
        corrected / (jnp.sqrt(scaled) + adam_eps) + weight_decay * weight
    )
    return (weight, moment, second)


def shampoo_update(weight, moment, left, right, ahead, products, factor):
    gradient, turned, left_square, right_square = products
    direction = beta_first * ahead + ((1 - beta_first) * factor) * turned
    square = (1 - stat_decay) * factor * factor
    return (
        weight - shampoo_rate * (direction + weight_decay * weight),
        beta_first * moment + ((1 - beta_first) * factor) * gradient,
        stat_decay * left + square * left_square,
        stat_decay * right + square * right_square,
    )


def on_device(
    enc_ids,
    span_mask,
    segments,
    targets,
    loss_weights,
    target_segments,
    embedding,
    emb_m,
    emb_v,
    gains,
    gain_m,
    gain_v,
    rel_bias,
    rel_m,
    rel_v,
    enc_w,
    enc_m,
    enc_left,
    enc_right,
    enc_lroot,
    enc_rroot,
    dec_w,
    dec_m,
    dec_left,
    dec_right,
    dec_lroot,
    dec_rroot,
):
    fsdp_rank = lax.axis_index("fsdp")
    seq_rank = lax.axis_index("seq")
    n_fsdp = lax.axis_size("fsdp")
    n_seq = lax.axis_size("seq")
    half_len = enc_ids.shape[1]
    rows, dec_len = targets.shape
    enc_len = half_len * n_seq
    enc_in = jnp.where(span_mask == 1, VOCAB - sentinel_offset, enc_ids)
    dec_in = jnp.concatenate([jnp.zeros((rows, 1), jnp.int32), targets[:, :-1]], axis=1)

    paired = paired_mesh()

    halves = jnp.stack([enc_in, segments]).reshape(2, n_seq, rows, half_len)
    enc_own, dec_own, table = (own_weights(enc_w), own_weights(dec_w), narrow(embedding))
    if n_seq == 2:
        kept = pick(halves, seq_rank, 1)
        got = swap(pick(halves, 1 - seq_rank, 1), "seq")
        got, enc_own, dec_own = hold((got, enc_own, dec_own))
        parts = (choose(seq_rank, got, kept), choose(seq_rank, kept, got))
        row_words = jnp.stack(parts, axis=2)
    else:
        row_words = lax.all_to_all(halves, "seq", 1, 1, tiled=True).transpose(0, 2, 1, 3)
    row_words = row_words.reshape(2, rows, enc_len)
    row_segments = row_words[1]
    message = jnp.concatenate(
        [
            row_words[0].reshape(-1),
            dec_in.reshape(-1),
            targets.reshape(-1),
            loss_weights.reshape(-1),
        ]
    ).reshape(1, -1)
    enc_pairs = gathered_weights(enc_own, enc_w.shape[0])
    gathered = lax.all_gather(message, "fsdp", axis=0, tiled=True)
    gathered, dec_own = hold((gathered, dec_own))
    if paired:
        dec_line = along_line(dec_own)
    all_enc = gathered[:, : rows * enc_len]
    rest = gathered[:, rows * enc_len :].reshape(n_fsdp, 3, rows * dec_len)
    all_dec, all_targets, all_weights = (rest[:, 0], rest[:, 1], rest[:, 2])
    all_tokens = jnp.concatenate([all_enc, all_dec], axis=1)
    vocab_local = table.shape[0]
    vocab_first = fsdp_rank * vocab_local
    found = table_rows(table, all_tokens, vocab_first)
    enc_roots = (enc_m, enc_lroot, enc_rroot)
    dec_roots = (dec_m, dec_lroot, dec_rroot)
    found, enc_roots = hold((found, enc_roots))
    enc_ready = shampoo_ahead(*enc_roots)
    enc_ready, dec_roots = hold((enc_ready, dec_roots))
    dec_ready = shampoo_ahead(*dec_roots)
    enc_onehot = tile_onehot(enc_len // TILE, False)
    dec_onehot = tile_onehot(dec_len // TILE, True)
    if paired:
        found, enc_pairs, enc_ready, dec_line, rel_tiles, dec_ready = hold(
            (found, enc_pairs, enc_ready, dec_line, rel_bias, dec_ready)
        )
    else:
        found, enc_pairs, rel_tiles = hold((found, enc_pairs, rel_bias))
    looked_up = lax.psum_scatter(found, "fsdp", scatter_dimension=0, tiled=True).reshape(-1, D)
    enc_mats = matrices_of(enc_pairs, layer_shapes(False))
    enc_bias = tile_bias(enc_onehot, rel_tiles[0])
    dec_bias = tile_bias(dec_onehot, rel_tiles[1])
    if paired:
        dec_near = exchange_near(dec_line)
        enc_ahead, dec_ahead = (as_rows(enc_ready[0]), as_rows(dec_ready[0]))
        dec_near, enc_mats, enc_bias, dec_bias, enc_ahead = hold(
            (dec_near, enc_mats, enc_bias, dec_bias, enc_ahead)
        )
        dec_far = exchange_far(dec_near)
        dec_cores = swap_cores(dec_near)
        looked_up, dec_far, dec_cores, dec_ahead = hold((looked_up, dec_far, dec_cores, dec_ahead))
        dec_cores = dec_cores + swap_cores(dec_far)
    else:
        dec_mats = matrices_of(gathered_weights(dec_own, dec_w.shape[0]), layer_shapes(True))
        enc_ahead, dec_ahead = (as_rows(enc_ready[0]), as_rows(dec_ready[0]))
    hidden0 = looked_up[: rows * enc_len].reshape(rows, enc_len, D).astype(jnp.float32)
    state0 = looked_up[rows * enc_len :].reshape(rows, dec_len, D).astype(jnp.float32)

    tile_at = D // LANES
    self_places = (0, tile_at, 2 * tile_at)
    cross_places = (0, 0, tile_at)

    normed0 = rms(hidden0, gains[0]).astype(jnp.bfloat16)
    enc_qkv = project(normed0, enc_mats[0]).astype(jnp.bfloat16)
    enc_attended = attend(
        enc_qkv, enc_qkv, self_places, enc_bias, row_segments, row_segments, False
    )
    hidden1 = hidden0 + project(enc_attended, enc_mats[1])
    hidden2, enc_cache = ff_forward(hidden1, gains[1], enc_mats[2], enc_mats[3])
    encoded = rms(hidden2, gains[2]).astype(jnp.bfloat16)
    if paired:
        encoded, dec_cores = hold((encoded, dec_cores))
        dec_mats = assembled(dec_near + dec_far + dec_cores, layer_shapes(True))
    pairs = project(encoded, dec_mats[3]).astype(jnp.bfloat16)

    normed3 = rms(state0, gains[3]).astype(jnp.bfloat16)
    self_qkv = project(normed3, dec_mats[0]).astype(jnp.bfloat16)
    self_attended = attend(
        self_qkv, self_qkv, self_places, dec_bias, target_segments, target_segments, True
    )
    state1 = state0 + project(self_attended, dec_mats[1])
    normed4 = rms(state1, gains[4]).astype(jnp.bfloat16)
    cross_query = project(normed4, dec_mats[2]).astype(jnp.bfloat16)
    cross_attended = attend(
        cross_query, pairs, cross_places, None, target_segments, row_segments, False
    )
    state2 = state1 + project(cross_attended, dec_mats[4])
    state3, dec_cache = ff_forward(state2, gains[5], dec_mats[5], dec_mats[6])
    out_scale = D ** (-0.5)
    final = (rms(state3, gains[6]) * out_scale).astype(jnp.bfloat16)

    count = jnp.sum(all_weights).astype(jnp.float32)
    final, count = hold((final, count))
    all_final = lax.all_gather(final.reshape(rows * dec_len, D), "fsdp", axis=0, tiled=True)
    if paired:
        count = count + swap(count, "seq")
        count = count + swap(count, "dp")
    else:
        count = lax.psum(count, REPLICAS)
    all_final, count = hold((all_final, count))
    share = 1.0 / jnp.maximum(count, 1.0)
    logits = jnp.einsum("nd,vd->nv", all_final, table, preferred_element_type=jnp.float32)
    local_ids = all_targets.reshape(-1) - vocab_first
    target_hot = local_ids[:, None] == jnp.arange(vocab_local, dtype=jnp.int32)[None, :]
    local_top = jnp.max(logits, axis=1)
    local_sum = jnp.sum(jnp.exp(logits - local_top[:, None]), axis=1)
    local_pick = jnp.sum(jnp.where(target_hot, logits, 0.0), axis=1)
    stats = lax.all_gather(
        jnp.stack([local_top, local_sum, local_pick])[None], "fsdp", axis=0, tiled=True
    )
    top_all = jnp.max(stats[:, 0], axis=0)
    sum_all = jnp.sum(stats[:, 1] * jnp.exp(stats[:, 0] - top_all), axis=0)
    pick_all = jnp.sum(stats[:, 2], axis=0)
    lse = top_all + jnp.log(sum_all)
    token_weights = all_weights.reshape(-1).astype(jnp.float32)
    group_loss = jnp.sum(token_weights * (lse - pick_all))
    grad_logits = (
        token_weights[:, None] * (jnp.exp(logits - lse[:, None]) - target_hot.astype(jnp.float32))
    ).astype(jnp.bfloat16)
    grad_final = lax.psum_scatter(
        jnp.dot(grad_logits, table, preferred_element_type=jnp.float32),
        "fsdp",
        scatter_dimension=0,
        tiled=True,
    ).reshape(rows, dec_len, D)
    dense_grad = jnp.einsum("nv,nd->vd", grad_logits, all_final, preferred_element_type=jnp.float32)
    grad_final, dense_grad, dense_bound = hold(
        (grad_final, dense_grad, jnp.max(jnp.abs(dense_grad)))
    )

    grad_state3, gain_six = rms_back(state3, gains[6], grad_final * out_scale)
    grad_state2, gain_five, dec_in_grad, dec_down_grad = ff_back(
        state2, gains[5], dec_mats[5], dec_mats[6], dec_cache, grad_state3
    )
    branch_grad = grad_state2.astype(jnp.bfloat16)
    cross_out_grad = (cross_attended, branch_grad)
    grad_cross = project_back(branch_grad, dec_mats[4]).astype(jnp.bfloat16)
    grad_cq, grad_ck, grad_cv = attend_back(
        cross_query, pairs, cross_places, None, target_segments, row_segments, False, grad_cross
    )
    grad_pairs = jnp.concatenate([grad_ck, grad_cv], axis=-1)
    cross_query_grad = (normed4, grad_cq)
    grad_state1_part, gain_four = rms_back(state1, gains[4], project_back(grad_cq, dec_mats[2]))
    grad_state1 = grad_state2 + grad_state1_part
    cross_pair_grad = (encoded, grad_pairs)
    grad_encoded = project_back(grad_pairs, dec_mats[3])
    branch_grad = grad_state1.astype(jnp.bfloat16)
    self_out_grad = (self_attended, branch_grad)
    grad_self = project_back(branch_grad, dec_mats[1]).astype(jnp.bfloat16)
    grad_sq, grad_sk, grad_sv, dec_bias_grad = attend_back(
        self_qkv, self_qkv, self_places, dec_bias, target_segments, target_segments, True, grad_self
    )
    grad_sqkv = jnp.concatenate([grad_sq, grad_sk, grad_sv], axis=-1)
    self_qkv_grad = (normed3, grad_sqkv)
    grad_state0_part, gain_three = rms_back(state0, gains[3], project_back(grad_sqkv, dec_mats[0]))
    grad_state0 = grad_state1 + grad_state0_part
    decoder_portion = weight_grads(
        [
            self_qkv_grad,
            self_out_grad,
            cross_query_grad,
            cross_pair_grad,
            cross_out_grad,
            dec_in_grad,
            dec_down_grad,
        ]
    )
    if paired:
        dec_got = swap_halves(decoder_portion)

    grad_hidden2, gain_two = rms_back(hidden2, gains[2], grad_encoded)
    grad_hidden1, gain_one, encoder_input_gradient, encoder_down_gradient = ff_back(
        hidden1, gains[1], enc_mats[2], enc_mats[3], enc_cache, grad_hidden2
    )
    branch_grad = grad_hidden1.astype(jnp.bfloat16)
    encoder_output_gradient = (enc_attended, branch_grad)
    grad_attn = project_back(branch_grad, enc_mats[1]).astype(jnp.bfloat16)
    if paired:
        dec_got, decoder_portion, grad_attn = hold((dec_got, decoder_portion, grad_attn))
        dec_folded = fold_blocks(decoder_portion, dec_got)
        dec_folded, grad_attn = hold((dec_folded, grad_attn))
        dec_close = near_sums(dec_folded)
    grad_eq, grad_ek, grad_ev, enc_bias_grad = attend_back(
        enc_qkv, enc_qkv, self_places, enc_bias, row_segments, row_segments, False, grad_attn
    )
    grad_eqkv = jnp.concatenate([grad_eq, grad_ek, grad_ev], axis=-1)
    encoder_qkv_gradient = (normed0, grad_eqkv)
    grad_hidden0_part, gain_zero = rms_back(hidden0, gains[0], project_back(grad_eqkv, enc_mats[0]))
    grad_hidden0 = grad_hidden1 + grad_hidden0_part
    back_rows = jnp.concatenate(
        [grad_hidden0.reshape(-1, D), grad_state0.reshape(-1, D)], axis=0
    ).astype(jnp.bfloat16)
    if paired:
        dec_close, back_rows, grad_eqkv = hold((dec_close, back_rows, grad_eqkv))
        encoder_qkv_gradient = (normed0, grad_eqkv)
        dec_far_sums = far_sums(dec_close)
    back_all = lax.all_gather(back_rows, "fsdp", axis=0, tiled=True)
    encoder_portion = weight_grads(
        [
            encoder_qkv_gradient,
            encoder_output_gradient,
            encoder_input_gradient,
            encoder_down_gradient,
        ]
    )
    if paired:
        encoder_portion, dec_far_sums = hold((encoder_portion, dec_far_sums))
        enc_got = swap_halves(encoder_portion)
        enc_got, encoder_portion = hold((enc_got, encoder_portion))
        enc_folded = hold(fold_blocks(encoder_portion, enc_got))
        enc_close = near_sums(enc_folded)
        back_all, enc_folded, dec_far_sums = hold((back_all, enc_folded, dec_far_sums))
        dec_arrived = line_sums(dec_far_sums)
        bound = dense_bound + back_all.shape[0] * jnp.max(jnp.abs(back_all)).astype(jnp.float32)
    emb_grad = table_grads(back_all, all_tokens, vocab_first, dense_grad)
    gain_part = jnp.stack(
        [gain_zero, gain_one, gain_two, gain_three, gain_four, gain_five, gain_six]
    )
    rel_part = jnp.stack(
        [tile_bias_grad(enc_onehot, enc_bias_grad), tile_bias_grad(dec_onehot, dec_bias_grad)]
    )
    small = jnp.concatenate(
        [
            gain_part.reshape(-1),
            rel_part.reshape(-1),
            jnp.where(fsdp_rank == 0, group_loss, 0.0).reshape(1),
        ]
    )
    if paired:
        half_rows = vocab_local // 2
        dec_arrived, enc_close, emb_grad, bound = hold((dec_arrived, enc_close, emb_grad, bound))
        enc_far_sums = far_sums(enc_close)
        dec_own_sum = line_total(dec_arrived)
        dec_grad = share_blocks(dec_own_sum)
        table_parts = near_parts(emb_grad, bound)
        enc_far_sums, table_parts = hold((enc_far_sums, table_parts))
        table_close = near_table(table_parts)
        enc_arrived = line_sums(enc_far_sums)
        table_close, dec_grad, small = hold((table_close, dec_grad, small))
        table_far = far_table(table_close)
        dec_products = shampoo_products(dec_grad, share, *dec_ready[1:])
        table_far, dec_products, enc_arrived = hold((table_far, dec_products, enc_arrived))
        enc_own_sum = line_total(enc_arrived)
        enc_grad = share_blocks(enc_own_sum)
        top, low, scale = table_total(table_far)
        squares = (
            jnp.sum(jnp.square(enc_own_sum * share))
            + jnp.sum(jnp.square(dec_own_sum * share))
            + table_squares(top * (share / scale), low * (share / scale), half_rows)
        )
    else:
        dec_sum = summed_blocks(decoder_portion)
        enc_sum = summed_blocks(encoder_portion)
        dec_products = rows_of_all(shampoo_products(narrow(dec_sum), share, *dec_ready[1:]))
        enc_products = rows_of_all(shampoo_products(narrow(enc_sum), share, *enc_ready[1:]))
        table_grad = lax.psum(emb_grad, REPLICAS) * share
        squares = (
            jnp.sum(jnp.square(enc_sum * share))
            + jnp.sum(jnp.square(dec_sum * share))
            + jnp.sum(jnp.square(table_grad))
        ) / replica_count()
    small = jnp.concatenate([small, squares.reshape(1), jnp.zeros(126, jnp.float32)])
    small = small.reshape(-1, LANES)
    if paired:
        small, top, low, dec_products = hold((sum_replicas(small), top, low, dec_products))
        table_near = share_near(top, low)
        small = sum_line(small)
        dec_products, enc_grad = hold((rows_of_all(dec_products), enc_grad))
        enc_products = shampoo_products(enc_grad, share, *enc_ready[1:])
        table_near, small, enc_products = hold((table_near, small, enc_products))
        enc_products = hold(rows_of_all(enc_products))
        table_grad = placed_table(table_near, share_far(table_near), scale, half_rows) * share
    else:
        small = lax.psum(small, EVERYWHERE)
    small = small.reshape(-1)
    gain_grad = small[: 7 * D].reshape(7, D) * share
    rel_grad = small[7 * D : 7 * D + 2 * NBK * H].reshape(2, NBK, H) * share
    loss_sum = small[7 * D + 2 * NBK * H]
    squares_all = small[7 * D + 2 * NBK * H + 1]
    loss_count = jnp.maximum(count, 1.0)
    if not paired:
        dec_products, enc_products = hold((dec_products, enc_products))
    grad_norm = jnp.sqrt(
        squares_all + jnp.sum(gain_grad * gain_grad) + jnp.sum(rel_grad * rel_grad)
    )
    factor = jnp.minimum(1.0, clip_limit / grad_norm)
    new_emb = adam_update(embedding, table_grad * factor, emb_m, emb_v)
    new_gain = adam_update(gains, gain_grad * factor, gain_m, gain_v)
    new_rel = adam_update(rel_bias, rel_grad * factor, rel_m, rel_v)
    new_enc = shampoo_update(enc_w, enc_m, enc_left, enc_right, enc_ahead, enc_products, factor)
    new_dec = shampoo_update(dec_w, dec_m, dec_left, dec_right, dec_ahead, dec_products, factor)
    return (
        loss_sum,
        loss_count,
        grad_norm,
        *new_emb,
        *new_gain,
        *new_rel,
        *new_enc,
        *new_dec,
    )


def solution(mesh):
    in_specs = (
        P(("dp", "fsdp"), "seq"),
        P(("dp", "fsdp"), "seq"),
        P(("dp", "fsdp"), "seq"),
        P(("dp", "fsdp", "seq"), None),
        P(("dp", "fsdp", "seq"), None),
        P(("dp", "fsdp", "seq"), None),
        P("fsdp", None),
        P("fsdp", None),
        P("fsdp", None),
        P(),
        P(),
        P(),
        P(),
        P(),
        P(),
        P("fsdp", None),
        P("fsdp", None),
        P("fsdp", None),
        P("fsdp", None),
        P("fsdp", None),
        P("fsdp", None),
        P("fsdp", None),
        P("fsdp", None),
        P("fsdp", None),
        P("fsdp", None),
        P("fsdp", None),
        P("fsdp", None),
    )
    out_specs = (
        P(),
        P(),
        P(),
        P("fsdp", None),
        P("fsdp", None),
        P("fsdp", None),
        P(),
        P(),
        P(),
        P(),
        P(),
        P(),
        P("fsdp", None),
        P("fsdp", None),
        P("fsdp", None),
        P("fsdp", None),
        P("fsdp", None),
        P("fsdp", None),
        P("fsdp", None),
        P("fsdp", None),
    )
    return jax.shard_map(
        on_device, mesh=mesh, in_specs=in_specs, out_specs=out_specs, check_vma=False
    )
```

```python
import functools
import math

import jax
import jax.numpy as jnp
from jax import lax
from jax.experimental import pallas as pl
from jax.experimental.pallas import tpu as pltpu
from jax.sharding import PartitionSpec as P

D = 768
H = 12
DH = 64
FF = 3072
VOCAB = 32128
NBK = 32
REACH = 128
BLOCK = 192
STEP = 10
PAIR = 2 * BLOCK
TILE = 128
LANES = 128


norm_eps = 1e-06
neg_fill = -1000000000.0
sentinel_offset = 29
beta_first = 0.9
beta_second = 0.999
adam_eps = 1e-08
adam_rate = 0.5
shampoo_rate = 0.01
stat_decay = 0.999
weight_decay = 0.01
clip_limit = 0.05
highest = lax.Precision.HIGHEST


def bucket_edges(buckets, exact, reach):
    edges = list(range(1, exact))
    spread = buckets - exact
    for place in range(spread):
        edges.append(int(math.ceil(exact * (reach / exact) ** (place / spread) - 1e-09)))
    return edges


def offset_buckets(offset, causal):
    if causal:
        distance = jnp.maximum(-offset, 0)
        result = jnp.zeros(offset.shape, jnp.int32)
        edges = bucket_edges(NBK, NBK // 2, REACH)
    else:
        distance = jnp.abs(offset)
        result = jnp.where(offset > 0, NBK // 2, 0).astype(jnp.int32)
        edges = bucket_edges(NBK // 2, NBK // 4, REACH)
    for edge in edges:
        result = result + (distance >= edge).astype(jnp.int32)
    return result


def tile_reach(blocks):
    return min(blocks - 1, 2)


def tile_onehot(blocks, causal):
    reach = tile_reach(blocks)
    place = jnp.arange(TILE, dtype=jnp.int32)
    shift = jnp.arange(-reach, reach + 1, dtype=jnp.int32) * TILE
    offset = shift[:, None, None] + place[None, None, :] - place[None, :, None]
    buckets = offset_buckets(offset, causal).reshape(-1)
    return (jnp.arange(NBK, dtype=jnp.int32)[:, None] == buckets[None, :]).astype(jnp.float32)


def tile_bias(onehot, rel):
    flat = jnp.einsum("nh,np->hp", rel, onehot, precision=highest)
    return flat.reshape(H, -1, TILE, TILE)


def tile_bias_grad(onehot, grads):
    return jnp.einsum("np,hp->nh", onehot, grads.reshape(H, -1), precision=highest)


def head_lanes(half):
    lane = lax.broadcasted_iota(jnp.int32, (1, LANES), 1)
    return (lane // DH) == half


def both_heads(values):
    return jnp.concatenate([jnp.where(head_lanes(half), values, 0) for half in range(2)], axis=0)


def own_lanes(stacked):
    return jnp.where(head_lanes(0), stacked[:TILE], stacked[TILE:])


def block_probs(stacked, keys, bias_ref, row, row_segs, key_segs, causal):
    scores = lax.dot_general(
        stacked, keys, (((1,), (1,)), ((), ())), preferred_element_type=jnp.float32
    )
    width = keys.shape[0]
    mask = row_segs == key_segs
    if causal:
        at_row = row * TILE + lax.broadcasted_iota(jnp.int32, (TILE, width), 0)
        at_key = lax.broadcasted_iota(jnp.int32, (TILE, width), 1)
        mask = mask & (at_row >= at_key)
    probs = []
    for half in range(2):
        own = scores[half * TILE : (half + 1) * TILE]
        if bias_ref is not None:
            reach = tile_reach(width // TILE)
            tiles = []
            for column in range(width // TILE):
                tiles.append(bias_ref[half, min(max(column - row, -reach), reach) + reach])
            own = own + (jnp.concatenate(tiles, axis=1) if len(tiles) > 1 else tiles[0])
        own = jnp.where(mask, own, neg_fill)
        raised = jnp.exp(own - jnp.max(own, axis=-1, keepdims=True))
        probs.append(raised * (1.0 / jnp.sum(raised, axis=-1, keepdims=True)))
    return jnp.concatenate(probs, axis=0)


def attend_kernel(q_ref, k_ref, v_ref, *rest, biased, causal):
    bias_ref = rest[0] if biased else None
    sq_ref, sk_ref, o_ref = rest[-3:]
    keys = k_ref[0]
    values = v_ref[0]
    key_segs = sk_ref[0]
    for row in range(q_ref.shape[1] // TILE):
        part = pl.ds(row * TILE, TILE)
        probs = block_probs(
            both_heads(q_ref[0, part, :]), keys, bias_ref, row, sq_ref[0, part, :], key_segs, causal
        )
        output = jnp.dot(probs.astype(jnp.bfloat16), values, preferred_element_type=jnp.float32)
        o_ref[0, part, :] = own_lanes(output).astype(jnp.bfloat16)


def attend_back_kernel(q_ref, k_ref, v_ref, g_ref, *rest, biased, causal):
    if biased:
        bias_ref, sq_ref, sk_ref, dq_ref, dk_ref, dv_ref, db_ref = rest
    else:
        sq_ref, sk_ref, dq_ref, dk_ref, dv_ref = rest
        bias_ref = db_ref = None
    keys = k_ref[0]
    values = v_ref[0]
    key_segs = sk_ref[0]
    width = keys.shape[0]
    if biased:

        @pl.when(pl.program_id(1) == 0)
        def _():
            db_ref[...] = jnp.zeros_like(db_ref)

    grad_keys = None
    grad_values = None
    down = (((0,), (0,)), ((), ()))
    for row in range(q_ref.shape[1] // TILE):
        part = pl.ds(row * TILE, TILE)
        query = both_heads(q_ref[0, part, :])
        grad_out = both_heads(g_ref[0, part, :])
        probs = block_probs(
            query, keys, bias_ref, row, sq_ref[0, part, :], key_segs, causal
        )
        grad_probs = lax.dot_general(
            grad_out, values, (((1,), (1,)), ((), ())), preferred_element_type=jnp.float32
        )
        drop = jnp.sum(probs * grad_probs, axis=-1, keepdims=True)
        grad_scores = (probs * (grad_probs - drop)).astype(jnp.bfloat16)
        part_values = lax.dot_general(
            probs.astype(jnp.bfloat16), grad_out, down, preferred_element_type=jnp.float32
        )
        part_keys = lax.dot_general(grad_scores, query, down, preferred_element_type=jnp.float32)
        grad_values = part_values if grad_values is None else grad_values + part_values
        grad_keys = part_keys if grad_keys is None else grad_keys + part_keys
        grad_query = jnp.dot(grad_scores, keys, preferred_element_type=jnp.float32)
        dq_ref[0, part, :] = own_lanes(grad_query).astype(jnp.bfloat16)
        if biased:
            broad = grad_scores.astype(jnp.float32)
            reach = tile_reach(width // TILE)
            for half in range(2):
                for column in range(width // TILE):
                    slot = min(max(column - row, -reach), reach) + reach
                    db_ref[half, slot] += broad[
                        half * TILE : (half + 1) * TILE, column * TILE : (column + 1) * TILE
                    ]
    dk_ref[0] = grad_keys.astype(jnp.bfloat16)
    dv_ref[0] = grad_values.astype(jnp.bfloat16)


def attention_specs(query, keys, places, bias, row_segs, key_segs):
    q_at, k_at, v_at = places
    rows, nq = row_segs.shape
    nk = key_segs.shape[1]

    def panel(length, first):
        return pl.BlockSpec((1, length, LANES), lambda pair, row: (row, 0, first + pair))

    operands = [query, keys, keys]
    specs = [panel(nq, q_at), panel(nk, k_at), panel(nk, v_at)]
    tail = []
    tail_specs = []
    if bias is not None:
        tail.append(bias)
        tail_specs.append(
            pl.BlockSpec((2,) + bias.shape[1:], lambda pair, row: (pair, 0, 0, 0))
        )
    tail += [row_segs[:, :, None], key_segs[:, None, :]]
    tail_specs += [
        pl.BlockSpec((1, nq, 1), lambda pair, row: (row, 0, 0)),
        pl.BlockSpec((1, 1, nk), lambda pair, row: (row, 0, 0)),
    ]
    return operands, specs, tail, tail_specs, panel


def attention_cost(rows, nq, nk, products):
    return pl.CostEstimate(
        flops=2 * products * rows * H * nq * nk * LANES,
        bytes_accessed=2 * products * rows * (nq + nk) * D,
        transcendentals=rows * H * nq * nk,
    )


def attend(query, keys, places, bias, row_segs, key_segs, causal):
    rows, nq = row_segs.shape
    nk = key_segs.shape[1]
    operands, specs, tail, tail_specs, panel = attention_specs(
        query, keys, places, bias, row_segs, key_segs
    )
    return pl.pallas_call(
        functools.partial(attend_kernel, biased=bias is not None, causal=causal),
        out_shape=jax.ShapeDtypeStruct((rows, nq, D), jnp.bfloat16),
        grid=(H // 2, rows),
        in_specs=specs + tail_specs,
        out_specs=panel(nq, 0),
        cost_estimate=attention_cost(rows, nq, nk, 2),
        compiler_params=pltpu.CompilerParams(vmem_limit_bytes=32 << 20),
    )(*operands, *tail)


def attend_back(query, keys, places, bias, row_segs, key_segs, causal, grad_out):
    rows, nq = row_segs.shape
    nk = key_segs.shape[1]
    operands, specs, tail, tail_specs, panel = attention_specs(
        query, keys, places, bias, row_segs, key_segs
    )
    outs = [
        jax.ShapeDtypeStruct((rows, nq, D), jnp.bfloat16),
        jax.ShapeDtypeStruct((rows, nk, D), jnp.bfloat16),
        jax.ShapeDtypeStruct((rows, nk, D), jnp.bfloat16),
    ]
    out_specs = [panel(nq, 0), panel(nk, 0), panel(nk, 0)]
    if bias is not None:
        outs.append(jax.ShapeDtypeStruct(bias.shape, jnp.float32))
        out_specs.append(
            pl.BlockSpec((2,) + bias.shape[1:], lambda pair, row: (pair, 0, 0, 0))
        )
    return pl.pallas_call(
        functools.partial(attend_back_kernel, biased=bias is not None, causal=causal),
        out_shape=outs,
        grid=(H // 2, rows),
        in_specs=specs + [panel(nq, 0)] + tail_specs,
        out_specs=out_specs,
        cost_estimate=attention_cost(rows, nq, nk, 5),
        compiler_params=pltpu.CompilerParams(vmem_limit_bytes=32 << 20),
    )(*operands, grad_out, *tail)


def layer_shapes(decoder):
    if decoder:
        return [(D, 3 * D), (D, D), (D, D), (D, 2 * D), (D, D), (D, FF), (FF, D)]
    return [(D, 3 * D), (D, D), (D, FF), (FF, D)]


def as_blocks(flat):
    if flat.ndim == 3:
        return flat
    return flat.reshape(flat.shape[0], BLOCK, BLOCK)


def as_rows(blocks):
    return blocks.reshape(blocks.shape[0], BLOCK * BLOCK)


def as_pairs(blocks):
    amount = blocks.shape[0] // 2
    split = blocks.reshape(amount, 2, BLOCK, BLOCK)
    return jnp.concatenate([split[:, 0], split[:, 1]], axis=-1)


def unpack_kernel(pairs_ref, out_ref):
    across = out_ref.shape[1] // PAIR
    for row in range(out_ref.shape[0] // BLOCK):
        for column in range(across):
            out_ref[row * BLOCK : (row + 1) * BLOCK, column * PAIR : (column + 1) * PAIR] = (
                pairs_ref[row * across + column]
            )


def matrices_of(pairs, shapes):
    matrix_list = []
    place = 0
    for height, breadth in shapes:
        group = 2 * breadth // PAIR
        first = place // group
        matrix_list.append(
            pl.pallas_call(
                unpack_kernel,
                out_shape=jax.ShapeDtypeStruct((height, breadth), pairs.dtype),
                grid=(height // PAIR,),
                in_specs=[
                    pl.BlockSpec(
                        (group, BLOCK, PAIR), lambda step, first=first: (first + step, 0, 0)
                    )
                ],
                out_specs=pl.BlockSpec((PAIR, breadth), lambda step: (step, 0)),
                cost_estimate=pl.CostEstimate(
                    flops=0, bytes_accessed=4 * height * breadth, transcendentals=0
                ),
                compiler_params=pltpu.CompilerParams(vmem_limit_bytes=32 << 20),
            )(pairs)
        )
        place += group * (height // PAIR)
    return matrix_list


def weight_grad_kernel(x_ref, g_ref, *rest):
    out_ref = rest[-1]
    across = out_ref.shape[0] // 2
    for column in range(across):
        product = lax.dot_general(
            x_ref[...],
            g_ref[:, column * PAIR : (column + 1) * PAIR],
            (((0,), (0,)), ((), ())),
            preferred_element_type=jnp.float32,
        )
        product = product.astype(jnp.bfloat16)
        out_ref[column] = product[:BLOCK]
        out_ref[across + column] = product[BLOCK:]


def weight_grads(operands):
    total = sum(x.shape[-1] * g.shape[-1] for x, g in operands) // (BLOCK * PAIR)
    pairs = None
    place = 0
    for x, g in operands:
        x = x.reshape(-1, x.shape[-1])
        g = g.reshape(-1, g.shape[-1])
        count, height = x.shape
        breadth = g.shape[1]
        group = 2 * breadth // PAIR
        first = place // group
        given = [] if pairs is None else [pairs]
        pairs = pl.pallas_call(
            weight_grad_kernel,
            out_shape=jax.ShapeDtypeStruct((total, BLOCK, PAIR), jnp.bfloat16),
            grid=(height // PAIR,),
            in_specs=[
                pl.BlockSpec((count, PAIR), lambda step: (0, step)),
                pl.BlockSpec((count, breadth), lambda step: (0, 0)),
            ]
            + [pl.BlockSpec(memory_space=pl.ANY)] * len(given),
            out_specs=pl.BlockSpec(
                (group, BLOCK, PAIR), lambda step, first=first: (first + step, 0, 0)
            ),
            input_output_aliases={2: 0} if given else {},
            cost_estimate=pl.CostEstimate(
                flops=2 * count * height * breadth,
                bytes_accessed=2 * (count * (height + breadth) + height * breadth),
                transcendentals=0,
            ),
            compiler_params=pltpu.CompilerParams(vmem_limit_bytes=40 << 20),
        )(x, g, *given)
        place += group * (height // PAIR)
    return pairs


def split_float(values):
    high = values.astype(jnp.bfloat16)
    return high, (values - high.astype(jnp.float32)).astype(jnp.bfloat16)


def full_product(left, right, contract):
    def part(first, second):
        return lax.dot_general(
            first, second, (contract, ((), ())), preferred_element_type=jnp.float32
        )

    return (
        part(left[0], right[1]) + part(left[1], right[0]) + part(left[0], right[0])
    )


ROW_COL = ((1,), (0,))
ROW_ROW = ((1,), (1,))
COL_COL = ((0,), (0,))


def turned_product(left_root, middle, right_root):
    shaped = full_product(split_float(left_root), middle, ROW_COL)
    return full_product(split_float(shaped), split_float(right_root), ROW_COL)


def ahead_kernel(m_ref, lr_ref, rr_ref, o_ref):
    for place in range(m_ref.shape[0]):
        o_ref[place] = turned_product(lr_ref[place], split_float(m_ref[place]), rr_ref[place])


def products_kernel(rest_ref, g_ref, lr_ref, rr_ref, g_out, turned_out, left_out, right_out):
    rest = rest_ref[0]

    def single(first, second, contract):
        return lax.dot_general(
            first, second, (contract, ((), ())), preferred_element_type=jnp.float32
        )

    for place in range(g_out.shape[0]):
        first = place % 2 * BLOCK
        block = g_ref[place // 2, :, first : first + BLOCK]
        g_out[place] = block.astype(jnp.float32) * rest
        high, low = split_float(lr_ref[place])
        shaped = single(low, block, ROW_COL) + single(high, block, ROW_COL)
        turned_out[place] = rest * full_product(
            split_float(shaped), split_float(rr_ref[place]), ROW_COL
        )
        left_out[place] = (rest * rest) * single(block, block, ROW_ROW)
        right_out[place] = (rest * rest) * single(block, block, COL_COL)


def block_cost(amount, products, arrays):
    return pl.CostEstimate(
        flops=6 * products * amount * BLOCK**3,
        bytes_accessed=4 * arrays * amount * BLOCK * BLOCK,
        transcendentals=0,
    )


def shampoo_ahead(moment, left_root, right_root):
    blocks = [as_blocks(member) for member in (moment, left_root, right_root)]
    amount = moment.shape[0]
    spec = pl.BlockSpec((2, BLOCK, BLOCK), lambda pair: (pair, 0, 0))
    ahead = pl.pallas_call(
        ahead_kernel,
        out_shape=jax.ShapeDtypeStruct((amount, BLOCK, BLOCK), jnp.float32),
        grid=(amount // 2,),
        in_specs=[spec] * 3,
        out_specs=spec,
        cost_estimate=block_cost(amount, 2, 4),
        compiler_params=pltpu.CompilerParams(vmem_limit_bytes=52 << 20),
    )(*blocks)
    return ahead, blocks[1], blocks[2]


def shampoo_products(pairs, share, left_root, right_root):
    amount = left_root.shape[0]
    power = jnp.exp2(jnp.floor(jnp.log2(share)))
    pairs = narrow(wide(pairs) * power)
    group = 4 if amount % 4 == 0 else 2
    spec = pl.BlockSpec((group, BLOCK, BLOCK), lambda step: (step, 0, 0))
    results = pl.pallas_call(
        products_kernel,
        out_shape=[jax.ShapeDtypeStruct((amount, BLOCK, BLOCK), jnp.float32)] * 4,
        grid=(amount // group,),
        in_specs=[
            pl.BlockSpec(memory_space=pltpu.SMEM),
            pl.BlockSpec((group // 2, BLOCK, PAIR), lambda step: (step, 0, 0)),
            spec,
            spec,
        ],
        out_specs=[spec] * 4,
        cost_estimate=block_cost(amount, 3, 7),
        compiler_params=pltpu.CompilerParams(vmem_limit_bytes=52 << 20),
    )((share / power).reshape(1), pairs, left_root, right_root)
    return results


def rows_of_all(results):
    return [as_rows(result) for result in results]


def project(left, right):
    return jnp.matmul(left, right, preferred_element_type=jnp.float32)


def project_back(left, right):
    return jnp.einsum("btf,df->btd", left, right, preferred_element_type=jnp.float32)


def rms(values, gain):
    return values * lax.rsqrt(jnp.mean(values * values, axis=-1, keepdims=True) + norm_eps) * gain


def rms_back(values, gain, grad_out):
    inverse = lax.rsqrt(jnp.mean(values * values, axis=-1, keepdims=True) + norm_eps)
    normed = values * inverse
    grad_gain = jnp.sum(grad_out * normed, axis=(0, 1))
    grad_normed = grad_out * gain
    grad_values = inverse * (
        grad_normed - normed * jnp.mean(grad_normed * normed, axis=-1, keepdims=True)
    )
    return (grad_values, grad_gain)


def ff_forward(hidden, gain, w_in, w_down):
    normed = rms(hidden, gain).astype(jnp.bfloat16)
    inner = project(normed, w_in)
    active = jax.nn.gelu(inner).astype(jnp.bfloat16)
    return (hidden + project(active, w_down), (normed, inner, active))


def ff_back(hidden, gain, w_in, w_down, cache, grad_out):
    normed, inner, active = cache
    branch_grad = grad_out.astype(jnp.bfloat16)
    grad_active = project_back(branch_grad, w_down)
    unused, gelu_back = jax.vjp(jax.nn.gelu, inner)
    grad_inner = gelu_back(grad_active)[0].astype(jnp.bfloat16)
    grad_part, grad_gain = rms_back(hidden, gain, project_back(grad_inner, w_in))
    return (grad_out + grad_part, grad_gain, (normed, grad_inner), (active, branch_grad))


def table_rows(table, token_ids, vocab_first):
    local_ids = token_ids - vocab_first
    inside = (local_ids >= 0) & (local_ids < table.shape[0])
    picked = jnp.take(table, jnp.clip(local_ids, 0, table.shape[0] - 1), axis=0)
    return jnp.where(inside[..., None], picked, jnp.zeros((), table.dtype))


def table_grads(grads, token_ids, vocab_first, dense):
    vocab_local = dense.shape[0]
    local_ids = token_ids.reshape(-1) - vocab_first
    inside = (local_ids >= 0) & (local_ids < vocab_local)
    slots = jnp.where(inside, local_ids, vocab_local)
    return dense.at[slots].add(grads.astype(jnp.float32), mode="drop")


REPLICAS = ("dp", "seq")
EVERYWHERE = ("fsdp", "dp", "seq")


def replica_rank():
    return lax.axis_index("dp") * lax.axis_size("seq") + lax.axis_index("seq")


def replica_count():
    return lax.axis_size("dp") * lax.axis_size("seq")


def paired_mesh():
    return (
        lax.axis_size("dp") == 2 and lax.axis_size("seq") == 2 and lax.axis_size("fsdp") % 2 == 0
    )


def swap(values, axis):
    size = lax.axis_size(axis)
    return lax.ppermute(values, axis, [(place, place ^ 1) for place in range(size)])


def shift(values, step):
    size = lax.axis_size("fsdp")
    moves = [
        (place, place + 2 * step) for place in range(size) if 0 <= place + 2 * step < size
    ]
    return lax.ppermute(values, "fsdp", moves)


def choose(flag, if_set, if_clear):
    return jnp.where(flag == 1, if_set, if_clear)


def pick(values, place, axis):
    return lax.dynamic_index_in_dim(values, place, axis, False)


def narrow(values):
    return values.astype(jnp.bfloat16)


def wide(values):
    return values.astype(jnp.float32)


def placed(relative, first, second):
    def at(row, column):
        here = choose(second, relative[row][1 - column], relative[row][column])
        there = choose(second, relative[1 - row][1 - column], relative[1 - row][column])
        return choose(first, there, here)

    return [[at(0, 0), at(0, 1)], [at(1, 0), at(1, 1)]]


def own_weights(master):
    share = master.shape[0] // replica_count()
    if master.shape[0] % (2 * replica_count()) == 0:
        master = lax.dynamic_slice_in_dim(master, replica_rank() * share, share, 0)
    return as_pairs(as_blocks(master.astype(jnp.bfloat16)))


def hold(values):
    return lax.optimization_barrier(values)


def chip_groups():
    return [list(range(core, lax.axis_size("fsdp"), 2)) for core in range(2)]


def along_line(own):
    n_chips = lax.axis_size("fsdp") // 2
    copies = jnp.broadcast_to(own[None], (n_chips,) + own.shape)
    return lax.all_to_all(copies, "fsdp", 0, 0, axis_index_groups=chip_groups(), tiled=True)


def exchange_near(line):
    mid = BLOCK // 2
    upper, lower = (line[:, :, :mid], line[:, :, mid:])
    return [upper, lower, swap(upper, "seq"), swap(lower, "dp")]


def exchange_far(near):
    upper, lower, upper_half, lower_side = near
    return [
        swap(jnp.stack([lower, lower_side]), "seq"),
        swap(jnp.stack([upper, upper_half]), "dp"),
    ]


def swap_cores(pieces):
    return [swap(piece, "fsdp") for piece in pieces]


def assemble_kernel(place_ref, *refs, shapes):
    outs = refs[12 : 12 + len(shapes)]
    buffer, in_sems, out_sems = refs[12 + len(shapes) :]
    core, side, half = (place_ref[0], place_ref[1], place_ref[2])
    n_chips, quarter, mid, _ = refs[0].shape
    copies = []
    for other in range(2):
        upper, lower, upper_half, lower_side, by_half, by_side = refs[6 * other : 6 * other + 6]
        pieces = [
            (upper, lower),
            (upper_half, by_half.at[0]),
            (by_side.at[0], lower_side),
            (by_side.at[1], by_half.at[1]),
        ]
        for place, both in enumerate(pieces):
            owner = ((side ^ (place // 2)) * 2 + (half ^ (place % 2))) * quarter
            for low, piece in enumerate(both):
                for chip in range(n_chips):
                    first = (2 * chip + (core ^ other)) * (4 * quarter) + owner
                    copies.append(
                        pltpu.make_async_copy(
                            piece.at[chip],
                            buffer.at[pl.ds(first, quarter), pl.ds(low * mid, mid), :],
                            in_sems.at[len(copies)],
                        )
                    )
    for copy in copies:
        copy.start()
    for copy in copies:
        copy.wait()
    copies = []
    for out_ref, (height, breadth) in zip(outs, shapes):
        for row in range(height // BLOCK):
            for column in range(breadth // PAIR):
                copies.append(
                    pltpu.make_async_copy(
                        buffer.at[len(copies)],
                        out_ref.at[pl.ds(row * BLOCK, BLOCK), pl.ds(column * PAIR, PAIR)],
                        out_sems.at[len(copies)],
                    )
                )
    for copy in copies:
        copy.start()
    for copy in copies:
        copy.wait()


def assembled(pieces, shapes):
    n_chips, quarter, mid, _ = pieces[0].shape
    total = 8 * n_chips * quarter
    return pl.pallas_call(
        functools.partial(assemble_kernel, shapes=shapes),
        out_shape=[jax.ShapeDtypeStruct(shape, jnp.bfloat16) for shape in shapes],
        in_specs=[pl.BlockSpec(memory_space=pltpu.SMEM)]
        + [pl.BlockSpec(memory_space=pl.ANY)] * len(pieces),
        out_specs=[pl.BlockSpec(memory_space=pl.ANY)] * len(shapes),
        scratch_shapes=[
            pltpu.VMEM((total, BLOCK, PAIR), jnp.bfloat16),
            pltpu.SemaphoreType.DMA((16 * n_chips,)),
            pltpu.SemaphoreType.DMA((total,)),
        ],
        cost_estimate=pl.CostEstimate(
            flops=0, bytes_accessed=4 * total * BLOCK * PAIR, transcendentals=0
        ),
        compiler_params=pltpu.CompilerParams(vmem_limit_bytes=30 << 20),
    )(own_place(), *pieces)


def gathered_weights(pairs, amount):
    split = amount % (2 * replica_count()) == 0
    return lax.all_gather(pairs, EVERYWHERE if split else "fsdp", axis=0, tiled=True)


def own_place():
    return jnp.stack(
        [lax.axis_index("fsdp") % 2, lax.axis_index("dp"), lax.axis_index("seq")]
    ).astype(jnp.int32)


def fold_kernel(place_ref, own_ref, got_ref, keep_up, send_up, keep_low, send_low):
    total = wide(own_ref[0]) + wide(got_ref[0])
    mid = BLOCK // 2
    upper, lower = (total[:, :mid], total[:, mid:])
    other_side, other_half = (pl.program_id(1), pl.program_id(2))

    @pl.when(other_half == 0)
    def _():
        keep_up[0, 0] = upper

    @pl.when(other_half == 1)
    def _():
        send_up[0, 0] = narrow(upper)

    @pl.when(other_side == 0)
    def _():
        keep_low[0, 0] = lower

    @pl.when(other_side == 1)
    def _():
        send_low[0, 0] = narrow(lower)


def fold_cores(pairs, got, n_chips, quarter):
    mid = BLOCK // 2

    def quarter_of(place, other_side, other_half):
        return (place[1] ^ other_side) * 2 + (place[2] ^ other_half)

    whole = (1, quarter, BLOCK, PAIR)
    part = (1, 1, quarter, mid, PAIR)
    halves = (n_chips, 2, quarter, mid, PAIR)

    def up_at(chip, other_side, other_half, place):
        return (chip, place[1] ^ other_side, 0, 0, 0)

    def keep_low_at(chip, other_side, other_half, place):
        return (chip, jnp.where(other_side == 0, place[2] ^ other_half, place[2] ^ 1), 0, 0, 0)

    def send_low_at(chip, other_side, other_half, place):
        return (chip, jnp.where(other_side == 1, place[2] ^ other_half, place[2]), 0, 0, 0)

    return pl.pallas_call(
        fold_kernel,
        out_shape=[
            jax.ShapeDtypeStruct(halves, kind)
            for kind in (jnp.float32, jnp.bfloat16, jnp.float32, jnp.bfloat16)
        ],
        grid_spec=pltpu.PrefetchScalarGridSpec(
            num_scalar_prefetch=1,
            grid=(n_chips, 2, 2),
            in_specs=[
                pl.BlockSpec(
                    whole,
                    lambda chip, side, half, place: (
                        (2 * chip + place[0]) * 4 + quarter_of(place, side, half),
                        0,
                        0,
                        0,
                    ),
                ),
                pl.BlockSpec(
                    whole,
                    lambda chip, side, half, place: (
                        chip * 4 + quarter_of(place, side, half),
                        0,
                        0,
                        0,
                    ),
                ),
            ],
            out_specs=[
                pl.BlockSpec(part, up_at),
                pl.BlockSpec(part, up_at),
                pl.BlockSpec(part, keep_low_at),
                pl.BlockSpec(part, send_low_at),
            ],
        ),
        cost_estimate=pl.CostEstimate(
            flops=pairs.size // 2, bytes_accessed=5 * pairs.size, transcendentals=0
        ),
        compiler_params=pltpu.CompilerParams(vmem_limit_bytes=32 << 20),
    )(
        own_place(),
        pairs.reshape(-1, quarter, BLOCK, PAIR),
        got.reshape(-1, quarter, BLOCK, PAIR),
    )


def sum_replicas(values):
    values = values + swap(values, "seq")
    return values + swap(values, "dp")


def sum_line(values):
    size = lax.axis_size("fsdp")
    if size & (size - 1):
        return lax.psum(values, "fsdp")
    step = 1
    while step < size:
        moves = [(place, place ^ step) for place in range(size)]
        values = values + lax.ppermute(values, "fsdp", moves)
        step *= 2
    return values


def summed_blocks(pairs):
    shard = lax.psum_scatter(wide(pairs), "fsdp", scatter_dimension=0, tiled=True)
    return lax.psum(shard, REPLICAS)


def swap_halves(pairs):
    n_chips = lax.axis_size("fsdp") // 2
    core = lax.axis_index("fsdp") % 2
    split = pairs.reshape(n_chips, 2, -1, BLOCK, PAIR)
    return swap(pick(split, 1 - core, 1), "fsdp")


def fold_blocks(pairs, got):
    n_chips = lax.axis_size("fsdp") // 2
    return fold_cores(pairs, got, n_chips, pairs.shape[0] // (8 * n_chips))


def near_sums(folded):
    return [folded[0], swap(folded[1], "seq"), folded[2], swap(folded[3], "dp")]


def far_sums(near):
    side, half = (lax.axis_index("dp"), lax.axis_index("seq"))
    upper = near[0] + wide(near[1])
    lower = near[2] + wide(near[3])
    return [
        pick(upper, side, 1),
        swap(narrow(pick(upper, 1 - side, 1)), "dp"),
        pick(lower, half, 1),
        swap(narrow(pick(lower, 1 - half, 1)), "seq"),
    ]


def line_sums(far):
    line = narrow(jnp.concatenate([far[0] + wide(far[1]), far[2] + wide(far[3])], axis=2))
    return lax.all_to_all(line, "fsdp", 0, 0, axis_index_groups=chip_groups(), tiled=True)


def line_total(arrived):
    return jnp.sum(wide(arrived), axis=0)


def share_blocks(own):
    return lax.all_gather(narrow(own), REPLICAS, axis=0, tiled=True)


def window_rows(half_rows):
    return -(-half_rows // 16) * 8


def half_lanes(values, place):
    return lax.dynamic_slice_in_dim(values, place * (D // 2), D // 2, 1)


SCALE_ROWS = 8


def scale_of(power):
    return jnp.exp2(power.astype(jnp.float32))


def message_of(values, power):
    mark = jnp.full((SCALE_ROWS, values.shape[1]), power, jnp.float16)
    return jnp.concatenate([values.astype(jnp.float16), mark], axis=0)


def scaled_swap(message, axis):
    got = swap(message, axis)
    return got[:-SCALE_ROWS], got[-1, 0].astype(jnp.float32)


def joined(values, power, got):
    others, other_power = got
    least = jnp.minimum(power, other_power)
    return (
        values * scale_of(least - power) + wide(others) * scale_of(least - other_power),
        least,
    )


def near_parts(partial, bound):
    side, half = (lax.axis_index("dp"), lax.axis_index("seq"))
    half_rows = partial.shape[0] // 2
    window = window_rows(half_rows)
    power = jnp.clip(12.0 - jnp.ceil(jnp.log2(jnp.maximum(bound, 1e-37))), -120.0, 120.0)

    def rows_of(first, place):
        start = first + place * (half_rows - window)
        return lax.dynamic_slice_in_dim(partial, start, window, 0) * scale_of(power)

    return [
        rows_of(0, half),
        message_of(rows_of(0, 1 - half), power),
        rows_of(half_rows, side),
        message_of(rows_of(half_rows, 1 - side), power),
        power,
    ]


def near_table(parts):
    top, top_sent, low, low_sent, power = parts
    return [top, scaled_swap(top_sent, "seq"), low, scaled_swap(low_sent, "dp"), power]


def far_table(near):
    side, half = (lax.axis_index("dp"), lax.axis_index("seq"))
    top, top_power = joined(near[0], near[4], near[1])
    low, low_power = joined(near[2], near[4], near[3])
    return [
        half_lanes(top, side),
        top_power,
        scaled_swap(message_of(half_lanes(top, 1 - side), top_power), "dp"),
        half_lanes(low, half),
        low_power,
        scaled_swap(message_of(half_lanes(low, 1 - half), low_power), "seq"),
    ]


def table_total(far):
    top, power = joined(*far[:3])
    low, _ = joined(*far[3:])
    return top, low, scale_of(power)


def table_squares(top, low, half_rows):
    side, half = (lax.axis_index("dp"), lax.axis_index("seq"))
    again = 2 * window_rows(half_rows) - half_rows
    row = lax.broadcasted_iota(jnp.int32, (top.shape[0], 1), 0)
    return jnp.sum(jnp.where(row >= again * half, top * top, 0.0)) + jnp.sum(
        jnp.where(row >= again * side, low * low, 0.0)
    )


def share_near(top, low):
    top = hold(top.astype(jnp.float16))
    low = hold(low.astype(jnp.float16))
    return [jnp.stack([top, swap(top, "dp")]), jnp.stack([low, swap(low, "seq")])]


def share_far(near):
    return [swap(near[0], "seq"), swap(near[1], "dp")]


def placed_table(near, far, scale, half_rows):
    side, half = (lax.axis_index("dp"), lax.axis_index("seq"))
    again = 2 * window_rows(half_rows) - half_rows
    top_all = placed([near[0], far[0]], half, side)
    low_all = placed([near[1], far[1]], side, half)
    rows = []
    for first, second in (top_all, low_all):
        rows.append(jnp.concatenate(first, axis=1))
        rows.append(jnp.concatenate(second, axis=1)[again:])
    return wide(jnp.concatenate(rows, axis=0)) * (1.0 / scale)


def adam_update(weight, gradient, moment, second):
    moment = beta_first * moment + (1 - beta_first) * gradient
    second = beta_second * second + (1 - beta_second) * gradient * gradient
    corrected = moment / (1 - beta_first**STEP)
    scaled = second / (1 - beta_second**STEP)
    weight = weight - adam_rate * (
        corrected / (jnp.sqrt(scaled) + adam_eps) + weight_decay * weight
    )
    return (weight, moment, second)


def shampoo_update(weight, moment, left, right, ahead, products, factor):
    gradient, turned, left_square, right_square = products
    direction = beta_first * ahead + ((1 - beta_first) * factor) * turned
    square = (1 - stat_decay) * factor * factor
    return (
        weight - shampoo_rate * (direction + weight_decay * weight),
        beta_first * moment + ((1 - beta_first) * factor) * gradient,
        stat_decay * left + square * left_square,
        stat_decay * right + square * right_square,
    )


def on_device(
    enc_ids,
    span_mask,
    segments,
    targets,
    loss_weights,
    target_segments,
    embedding,
    emb_m,
    emb_v,
    gains,
    gain_m,
    gain_v,
    rel_bias,
    rel_m,
    rel_v,
    enc_w,
    enc_m,
    enc_left,
    enc_right,
    enc_lroot,
    enc_rroot,
    dec_w,
    dec_m,
    dec_left,
    dec_right,
    dec_lroot,
    dec_rroot,
):
    fsdp_rank = lax.axis_index("fsdp")
    seq_rank = lax.axis_index("seq")
    n_fsdp = lax.axis_size("fsdp")
    n_seq = lax.axis_size("seq")
    half_len = enc_ids.shape[1]
    rows, dec_len = targets.shape
    enc_len = half_len * n_seq
    enc_in = jnp.where(span_mask == 1, VOCAB - sentinel_offset, enc_ids)
    dec_in = jnp.concatenate([jnp.zeros((rows, 1), jnp.int32), targets[:, :-1]], axis=1)

    paired = paired_mesh()

    halves = jnp.stack([enc_in, segments]).reshape(2, n_seq, rows, half_len)
    enc_own, dec_own, table = (own_weights(enc_w), own_weights(dec_w), narrow(embedding))
    if n_seq == 2:
        kept = pick(halves, seq_rank, 1)
        got = swap(pick(halves, 1 - seq_rank, 1), "seq")
        got, enc_own, dec_own = hold((got, enc_own, dec_own))
        parts = (choose(seq_rank, got, kept), choose(seq_rank, kept, got))
        row_words = jnp.stack(parts, axis=2)
    else:
        row_words = lax.all_to_all(halves, "seq", 1, 1, tiled=True).transpose(0, 2, 1, 3)
    row_words = row_words.reshape(2, rows, enc_len)
    row_segments = row_words[1]
    message = jnp.concatenate(
        [
            row_words[0].reshape(-1),
            dec_in.reshape(-1),
            targets.reshape(-1),
            loss_weights.reshape(-1),
        ]
    ).reshape(1, -1)
    enc_pairs = gathered_weights(enc_own, enc_w.shape[0])
    gathered = lax.all_gather(message, "fsdp", axis=0, tiled=True)
    gathered, dec_own = hold((gathered, dec_own))
    if paired:
        dec_line = along_line(dec_own)
    all_enc = gathered[:, : rows * enc_len]
    rest = gathered[:, rows * enc_len :].reshape(n_fsdp, 3, rows * dec_len)
    all_dec, all_targets, all_weights = (rest[:, 0], rest[:, 1], rest[:, 2])
    all_tokens = jnp.concatenate([all_enc, all_dec], axis=1)
    vocab_local = table.shape[0]
    vocab_first = fsdp_rank * vocab_local
    found = table_rows(table, all_tokens, vocab_first)
    enc_roots = (enc_m, enc_lroot, enc_rroot)
    dec_roots = (dec_m, dec_lroot, dec_rroot)
    found, enc_roots = hold((found, enc_roots))
    enc_ready = shampoo_ahead(*enc_roots)
    enc_ready, dec_roots = hold((enc_ready, dec_roots))
    dec_ready = shampoo_ahead(*dec_roots)
    enc_onehot = tile_onehot(enc_len // TILE, False)
    dec_onehot = tile_onehot(dec_len // TILE, True)
    if paired:
        found, enc_pairs, enc_ready, dec_line, rel_tiles, dec_ready = hold(
            (found, enc_pairs, enc_ready, dec_line, rel_bias, dec_ready)
        )
    else:
        found, enc_pairs, rel_tiles = hold((found, enc_pairs, rel_bias))
    looked_up = lax.psum_scatter(found, "fsdp", scatter_dimension=0, tiled=True).reshape(-1, D)
    enc_mats = matrices_of(enc_pairs, layer_shapes(False))
    enc_bias = tile_bias(enc_onehot, rel_tiles[0])
    dec_bias = tile_bias(dec_onehot, rel_tiles[1])
    if paired:
        dec_near = exchange_near(dec_line)
        enc_ahead, dec_ahead = (as_rows(enc_ready[0]), as_rows(dec_ready[0]))
        dec_near, enc_mats, enc_bias, dec_bias, enc_ahead = hold(
            (dec_near, enc_mats, enc_bias, dec_bias, enc_ahead)
        )
        dec_far = exchange_far(dec_near)
        dec_cores = swap_cores(dec_near)
        looked_up, dec_far, dec_cores, dec_ahead = hold((looked_up, dec_far, dec_cores, dec_ahead))
        dec_cores = dec_cores + swap_cores(dec_far)
    else:
        dec_mats = matrices_of(gathered_weights(dec_own, dec_w.shape[0]), layer_shapes(True))
        enc_ahead, dec_ahead = (as_rows(enc_ready[0]), as_rows(dec_ready[0]))
    hidden0 = looked_up[: rows * enc_len].reshape(rows, enc_len, D).astype(jnp.float32)
    state0 = looked_up[rows * enc_len :].reshape(rows, dec_len, D).astype(jnp.float32)

    tile_at = D // LANES
    self_places = (0, tile_at, 2 * tile_at)
    cross_places = (0, 0, tile_at)

    normed0 = rms(hidden0, gains[0]).astype(jnp.bfloat16)
    enc_qkv = project(normed0, enc_mats[0]).astype(jnp.bfloat16)
    enc_attended = attend(
        enc_qkv, enc_qkv, self_places, enc_bias, row_segments, row_segments, False
    )
    hidden1 = hidden0 + project(enc_attended, enc_mats[1])
    hidden2, enc_cache = ff_forward(hidden1, gains[1], enc_mats[2], enc_mats[3])
    encoded = rms(hidden2, gains[2]).astype(jnp.bfloat16)
    if paired:
        encoded, dec_cores = hold((encoded, dec_cores))
        dec_mats = assembled(dec_near + dec_far + dec_cores, layer_shapes(True))
    pairs = project(encoded, dec_mats[3]).astype(jnp.bfloat16)

    normed3 = rms(state0, gains[3]).astype(jnp.bfloat16)
    self_qkv = project(normed3, dec_mats[0]).astype(jnp.bfloat16)
    self_attended = attend(
        self_qkv, self_qkv, self_places, dec_bias, target_segments, target_segments, True
    )
    state1 = state0 + project(self_attended, dec_mats[1])
    normed4 = rms(state1, gains[4]).astype(jnp.bfloat16)
    cross_query = project(normed4, dec_mats[2]).astype(jnp.bfloat16)
    cross_attended = attend(
        cross_query, pairs, cross_places, None, target_segments, row_segments, False
    )
    state2 = state1 + project(cross_attended, dec_mats[4])
    state3, dec_cache = ff_forward(state2, gains[5], dec_mats[5], dec_mats[6])
    out_scale = D ** (-0.5)
    final = (rms(state3, gains[6]) * out_scale).astype(jnp.bfloat16)

    count = jnp.sum(all_weights).astype(jnp.float32)
    final, count = hold((final, count))
    all_final = lax.all_gather(final.reshape(rows * dec_len, D), "fsdp", axis=0, tiled=True)
    if paired:
        count = count + swap(count, "seq")
        count = count + swap(count, "dp")
    else:
        count = lax.psum(count, REPLICAS)
    all_final, count = hold((all_final, count))
    share = 1.0 / jnp.maximum(count, 1.0)
    logits = jnp.einsum("nd,vd->nv", all_final, table, preferred_element_type=jnp.float32)
    local_ids = all_targets.reshape(-1) - vocab_first
    target_hot = local_ids[:, None] == jnp.arange(vocab_local, dtype=jnp.int32)[None, :]
    local_top = jnp.max(logits, axis=1)
    local_sum = jnp.sum(jnp.exp(logits - local_top[:, None]), axis=1)
    local_pick = jnp.sum(jnp.where(target_hot, logits, 0.0), axis=1)
    stats = lax.all_gather(
        jnp.stack([local_top, local_sum, local_pick])[None], "fsdp", axis=0, tiled=True
    )
    top_all = jnp.max(stats[:, 0], axis=0)
    sum_all = jnp.sum(stats[:, 1] * jnp.exp(stats[:, 0] - top_all), axis=0)
    pick_all = jnp.sum(stats[:, 2], axis=0)
    lse = top_all + jnp.log(sum_all)
    token_weights = all_weights.reshape(-1).astype(jnp.float32)
    group_loss = jnp.sum(token_weights * (lse - pick_all))
    grad_logits = (
        token_weights[:, None] * (jnp.exp(logits - lse[:, None]) - target_hot.astype(jnp.float32))
    ).astype(jnp.bfloat16)
    grad_final = lax.psum_scatter(
        jnp.dot(grad_logits, table, preferred_element_type=jnp.float32),
        "fsdp",
        scatter_dimension=0,
        tiled=True,
    ).reshape(rows, dec_len, D)
    dense_grad = jnp.einsum("nv,nd->vd", grad_logits, all_final, preferred_element_type=jnp.float32)
    grad_final, dense_grad, dense_bound = hold(
        (grad_final, dense_grad, jnp.max(jnp.abs(dense_grad)))
    )

    grad_state3, gain_six = rms_back(state3, gains[6], grad_final * out_scale)
    grad_state2, gain_five, dec_in_grad, dec_down_grad = ff_back(
        state2, gains[5], dec_mats[5], dec_mats[6], dec_cache, grad_state3
    )
    branch_grad = grad_state2.astype(jnp.bfloat16)
    cross_out_grad = (cross_attended, branch_grad)
    grad_cross = project_back(branch_grad, dec_mats[4]).astype(jnp.bfloat16)
    grad_cq, grad_ck, grad_cv = attend_back(
        cross_query, pairs, cross_places, None, target_segments, row_segments, False, grad_cross
    )
    grad_pairs = jnp.concatenate([grad_ck, grad_cv], axis=-1)
    cross_query_grad = (normed4, grad_cq)
    grad_state1_part, gain_four = rms_back(state1, gains[4], project_back(grad_cq, dec_mats[2]))
    grad_state1 = grad_state2 + grad_state1_part
    cross_pair_grad = (encoded, grad_pairs)
    grad_encoded = project_back(grad_pairs, dec_mats[3])
    branch_grad = grad_state1.astype(jnp.bfloat16)
    self_out_grad = (self_attended, branch_grad)
    grad_self = project_back(branch_grad, dec_mats[1]).astype(jnp.bfloat16)
    grad_sq, grad_sk, grad_sv, dec_bias_grad = attend_back(
        self_qkv, self_qkv, self_places, dec_bias, target_segments, target_segments, True, grad_self
    )
    grad_sqkv = jnp.concatenate([grad_sq, grad_sk, grad_sv], axis=-1)
    self_qkv_grad = (normed3, grad_sqkv)
    grad_state0_part, gain_three = rms_back(state0, gains[3], project_back(grad_sqkv, dec_mats[0]))
    grad_state0 = grad_state1 + grad_state0_part
    decoder_portion = weight_grads(
        [
            self_qkv_grad,
            self_out_grad,
            cross_query_grad,
            cross_pair_grad,
            cross_out_grad,
            dec_in_grad,
            dec_down_grad,
        ]
    )
    if paired:
        dec_got = swap_halves(decoder_portion)

    grad_hidden2, gain_two = rms_back(hidden2, gains[2], grad_encoded)
    grad_hidden1, gain_one, encoder_input_gradient, encoder_down_gradient = ff_back(
        hidden1, gains[1], enc_mats[2], enc_mats[3], enc_cache, grad_hidden2
    )
    branch_grad = grad_hidden1.astype(jnp.bfloat16)
    encoder_output_gradient = (enc_attended, branch_grad)
    grad_attn = project_back(branch_grad, enc_mats[1]).astype(jnp.bfloat16)
    if paired:
        dec_got, decoder_portion, grad_attn = hold((dec_got, decoder_portion, grad_attn))
        dec_folded = fold_blocks(decoder_portion, dec_got)
        dec_folded, grad_attn = hold((dec_folded, grad_attn))
        dec_close = near_sums(dec_folded)
    grad_eq, grad_ek, grad_ev, enc_bias_grad = attend_back(
        enc_qkv, enc_qkv, self_places, enc_bias, row_segments, row_segments, False, grad_attn
    )
    grad_eqkv = jnp.concatenate([grad_eq, grad_ek, grad_ev], axis=-1)
    encoder_qkv_gradient = (normed0, grad_eqkv)
    grad_hidden0_part, gain_zero = rms_back(hidden0, gains[0], project_back(grad_eqkv, enc_mats[0]))
    grad_hidden0 = grad_hidden1 + grad_hidden0_part
    back_rows = jnp.concatenate(
        [grad_hidden0.reshape(-1, D), grad_state0.reshape(-1, D)], axis=0
    ).astype(jnp.bfloat16)
    if paired:
        dec_close, back_rows, grad_eqkv = hold((dec_close, back_rows, grad_eqkv))
        encoder_qkv_gradient = (normed0, grad_eqkv)
        dec_far_sums = far_sums(dec_close)
    back_all = lax.all_gather(back_rows, "fsdp", axis=0, tiled=True)
    encoder_portion = weight_grads(
        [
            encoder_qkv_gradient,
            encoder_output_gradient,
            encoder_input_gradient,
            encoder_down_gradient,
        ]
    )
    if paired:
        encoder_portion, dec_far_sums = hold((encoder_portion, dec_far_sums))
        enc_got = swap_halves(encoder_portion)
        enc_got, encoder_portion = hold((enc_got, encoder_portion))
        enc_folded = hold(fold_blocks(encoder_portion, enc_got))
        enc_close = near_sums(enc_folded)
        back_all, enc_folded, dec_far_sums = hold((back_all, enc_folded, dec_far_sums))
        dec_arrived = line_sums(dec_far_sums)
        bound = dense_bound + back_all.shape[0] * jnp.max(jnp.abs(back_all)).astype(jnp.float32)
    emb_grad = table_grads(back_all, all_tokens, vocab_first, dense_grad)
    gain_part = jnp.stack(
        [gain_zero, gain_one, gain_two, gain_three, gain_four, gain_five, gain_six]
    )
    rel_part = jnp.stack(
        [tile_bias_grad(enc_onehot, enc_bias_grad), tile_bias_grad(dec_onehot, dec_bias_grad)]
    )
    small = jnp.concatenate(
        [
            gain_part.reshape(-1),
            rel_part.reshape(-1),
            jnp.where(fsdp_rank == 0, group_loss, 0.0).reshape(1),
        ]
    )
    if paired:
        half_rows = vocab_local // 2
        dec_arrived, enc_close, emb_grad, bound = hold((dec_arrived, enc_close, emb_grad, bound))
        enc_far_sums = far_sums(enc_close)
        dec_own_sum = line_total(dec_arrived)
        dec_grad = share_blocks(dec_own_sum)
        table_parts = near_parts(emb_grad, bound)
        enc_far_sums, table_parts = hold((enc_far_sums, table_parts))
        table_close = near_table(table_parts)
        enc_arrived = line_sums(enc_far_sums)
        table_close, dec_grad, small = hold((table_close, dec_grad, small))
        table_far = far_table(table_close)
        dec_products = shampoo_products(dec_grad, share, *dec_ready[1:])
        table_far, dec_products, enc_arrived = hold((table_far, dec_products, enc_arrived))
        enc_own_sum = line_total(enc_arrived)
        enc_grad = share_blocks(enc_own_sum)
        top, low, scale = table_total(table_far)
        squares = (
            jnp.sum(jnp.square(enc_own_sum * share))
            + jnp.sum(jnp.square(dec_own_sum * share))
            + table_squares(top * (share / scale), low * (share / scale), half_rows)
        )
    else:
        dec_sum = summed_blocks(decoder_portion)
        enc_sum = summed_blocks(encoder_portion)
        dec_products = rows_of_all(shampoo_products(narrow(dec_sum), share, *dec_ready[1:]))
        enc_products = rows_of_all(shampoo_products(narrow(enc_sum), share, *enc_ready[1:]))
        table_grad = lax.psum(emb_grad, REPLICAS) * share
        squares = (
            jnp.sum(jnp.square(enc_sum * share))
            + jnp.sum(jnp.square(dec_sum * share))
            + jnp.sum(jnp.square(table_grad))
        ) / replica_count()
    small = jnp.concatenate([small, squares.reshape(1), jnp.zeros(126, jnp.float32)])
    small = small.reshape(-1, LANES)
    if paired:
        small, top, low, dec_products = hold((sum_replicas(small), top, low, dec_products))
        table_near = share_near(top, low)
        small = sum_line(small)
        dec_products, enc_grad = hold((rows_of_all(dec_products), enc_grad))
        enc_products = shampoo_products(enc_grad, share, *enc_ready[1:])
        table_near, small, enc_products = hold((table_near, small, enc_products))
        enc_products = hold(rows_of_all(enc_products))
        table_grad = placed_table(table_near, share_far(table_near), scale, half_rows) * share
    else:
        small = lax.psum(small, EVERYWHERE)
    small = small.reshape(-1)
    gain_grad = small[: 7 * D].reshape(7, D) * share
    rel_grad = small[7 * D : 7 * D + 2 * NBK * H].reshape(2, NBK, H) * share
    loss_sum = small[7 * D + 2 * NBK * H]
    squares_all = small[7 * D + 2 * NBK * H + 1]
    loss_count = jnp.maximum(count, 1.0)
    if not paired:
        dec_products, enc_products = hold((dec_products, enc_products))
    grad_norm = jnp.sqrt(
        squares_all + jnp.sum(gain_grad * gain_grad) + jnp.sum(rel_grad * rel_grad)
    )
    factor = jnp.minimum(1.0, clip_limit / grad_norm)
    new_emb = adam_update(embedding, table_grad * factor, emb_m, emb_v)
    new_gain = adam_update(gains, gain_grad * factor, gain_m, gain_v)
    new_rel = adam_update(rel_bias, rel_grad * factor, rel_m, rel_v)
    new_enc = shampoo_update(enc_w, enc_m, enc_left, enc_right, enc_ahead, enc_products, factor)
    new_dec = shampoo_update(dec_w, dec_m, dec_left, dec_right, dec_ahead, dec_products, factor)
    return (
        loss_sum,
        loss_count,
        grad_norm,
        *new_emb,
        *new_gain,
        *new_rel,
        *new_enc,
        *new_dec,
    )


def solution(mesh):
    in_specs = (
        P(("dp", "fsdp"), "seq"),
        P(("dp", "fsdp"), "seq"),
        P(("dp", "fsdp"), "seq"),
        P(("dp", "fsdp", "seq"), None),
        P(("dp", "fsdp", "seq"), None),
        P(("dp", "fsdp", "seq"), None),
        P("fsdp", None),
        P("fsdp", None),
        P("fsdp", None),
        P(),
        P(),
        P(),
        P(),
        P(),
        P(),
        P("fsdp", None),
        P("fsdp", None),
        P("fsdp", None),
        P("fsdp", None),
        P("fsdp", None),
        P("fsdp", None),
        P("fsdp", None),
        P("fsdp", None),
        P("fsdp", None),
        P("fsdp", None),
        P("fsdp", None),
        P("fsdp", None),
    )
    out_specs = (
        P(),
        P(),
        P(),
        P("fsdp", None),
        P("fsdp", None),
        P("fsdp", None),
        P(),
        P(),
        P(),
        P(),
        P(),
        P(),
        P("fsdp", None),
        P("fsdp", None),
        P("fsdp", None),
        P("fsdp", None),
        P("fsdp", None),
        P("fsdp", None),
        P("fsdp", None),
        P("fsdp", None),
    )
    return jax.shard_map(
        on_device, mesh=mesh, in_specs=in_specs, out_specs=out_specs, check_vma=False
    )
```
